32 devices in a mesh: dp: 4 (over z), expert: 8 (over y, x, core).
Axes of the slice: x: 2, y: 2, z: 4, core: 2. Of those that a mesh axis runs over, the one named last changes fastest.
Arguments:
- tokens: bfloat16 [32, 256, 1152], P(('dp', 'expert')), may hold values from -6 to 6
- lengths: int32 [32], P(('dp', 'expert')), may hold values from 128 to 256, as said below
- routes: int32 [32, 256], P(('dp', 'expert')), may hold values from 0 to 7, as said below
- slot_index: int32 [32, 256], P(('dp', 'expert')), may hold values from 0 to 64, as said below
- mixer_norm: bfloat16 [1152], P('expert'), may hold values from 0.5 to 1.5
- in_weight: bfloat16 [1152, 4608], P(None, 'expert'), may hold values from -0.1875 to 0.1875
- conv_weight: bfloat16 [4, 2304], P(None, 'expert'), may hold values from -3 to 3
- conv_bias: bfloat16 [2304], P('expert'), may hold values from -3 to 3
- scan_weight: bfloat16 [2304, 104], P('expert'), may hold values from -0.125 to 0.125
- step_weight: bfloat16 [72, 2304], P(None, 'expert'), may hold values from -0.75 to 0.75
- step_bias: bfloat16 [2304], P('expert'), may hold values from -6 to -1
- decay_log: bfloat16 [2304, 16], P('expert'), may hold values from -1 to 2.796875
- skip_gain: bfloat16 [2304], P('expert'), may hold values from 0.5 to 1.5
- out_weight: bfloat16 [2304, 1152], P('expert'), may hold values from -0.25 to 0.25
- moe_norm: bfloat16 [1152], P('expert'), may hold values from 0.5 to 1.5
- router_weight: bfloat16 [1152, 8], P('expert'), may hold values from -0.09375 to 0.09375
- up_weight: bfloat16 [8, 1152, 3072], P('expert'), may hold values from -0.1875 to 0.1875
- down_weight: bfloat16 [8, 3072, 1152], P('expert'), may hold values from -0.875 to 0.875
- cotangent: bfloat16 [32, 256, 1152], P(('dp', 'expert')), may hold values from -6 to 6
Outputs:
- layer_out: bfloat16 [32, 256, 1152], P(('dp', 'expert'))
- tokens_grad: float32 [32, 256, 1152], P(('dp', 'expert'))
- mixer_norm_grad: float32 [1152], P('expert')
- in_weight_grad: float32 [1152, 4608], P(None, 'expert')
- conv_weight_grad: float32 [4, 2304], P(None, 'expert')
- conv_bias_grad: float32 [2304], P('expert')
- scan_weight_grad: float32 [2304, 104], P('expert')
- step_weight_grad: float32 [72, 2304], P(None, 'expert')
- step_bias_grad: float32 [2304], P('expert')
- decay_log_grad: float32 [2304, 16], P('expert')
- skip_gain_grad: float32 [2304], P('expert')
- out_weight_grad: float32 [2304, 1152], P('expert')
- moe_norm_grad: float32 [1152], P('expert')
- router_weight_grad: float32 [1152, 8], P('expert')
- up_weight_grad: float32 [8, 1152, 3072], P('expert')
- down_weight_grad: float32 [8, 3072, 1152], P('expert')
The draws below stay inside these ranges and needn't reach their ends.
Inputs may be any that keep to these rules, and one draw needn't show every extreme that they name: `lengths`: each device holds one sequence of this many real tokens followed by padding; some device's sequence fills all 256 rows. Padding rows carry routes too. `slot_index`: within one device, the kept tokens of one route have slots 0, 1, 2, ... in order of position; 64 marks a dropped token or a padding row; on every device some expert fills all 64 slots and drops further tokens.
All inputs are finite; a program needn't handle non-finite values.
Results may differ from the reference program's by a relative error of at most 0.019.
Values may be sent and summed in bfloat16 or wider, within the bound.
A program may use at most 768 MiB of HBM per device.

```python
import math
from functools import partial
import jax
import jax.numpy as jnp
from jax import lax

D = 1152
DI = 2304
DT_RANK = 72
STATE = 16
CONV = 4
EXPERTS = 8
EH = 3072
TOK_DEV = 256
CAP = 64
SCAN_BLOCK = 16
SPLIT = 1
PIECES = 8
HP = 3072
BATCH = 32


def shuffled(subkey):
    return jax.random.permutation(subkey, TOK_DEV // 2)


def routing_tables(key):
    key_len, key_full, key_hot, key_order, key_rest = jax.random.split(key, 5)
    lengths = jax.random.randint(key_len, (BATCH,), TOK_DEV // 2, TOK_DEV + 1)
    fullest = jax.random.randint(key_full, (), 0, BATCH)
    lengths = jnp.where(jnp.arange(BATCH) == fullest, TOK_DEV, lengths).astype(jnp.int32)
    hottest = jax.random.randint(key_hot, (), 0, EXPERTS)
    routes = jax.random.randint(key_rest, (BATCH, TOK_DEV), 0, EXPERTS)
    orders = jax.vmap(shuffled)(jax.random.split(key_order, BATCH))
    marked = jnp.zeros((BATCH, TOK_DEV), jnp.int32).at[jnp.arange(BATCH)[:, None], orders[:, :CAP + CAP // 4]].set(1)
    routes = jnp.where(marked > 0, hottest, routes).astype(jnp.int32)
    inside = jnp.arange(TOK_DEV)[None, :] < lengths[:, None]
    chosen = ((routes[:, :, None] == jnp.arange(EXPERTS)[None, None, :]) & inside[:, :, None]).astype(jnp.int32)
    rank_of = jnp.sum((jnp.cumsum(chosen, 1) - 1) * chosen, 2)
    slot_ids = jnp.where(inside & (rank_of < CAP), rank_of, CAP).astype(jnp.int32)
    return (lengths, routes, slot_ids)


def draw_lengths(key, part):
    tables = routing_tables(key)
    return tables[0]


def draw_routes(key, part):
    tables = routing_tables(key)
    return tables[1]


def draw_slot_index(key, part):
    tables = routing_tables(key)
    return tables[2]


def shard_levels(rng, shape, pieces, smallest, largest):
    gain = 1.0
    for position, parts in pieces:
        draws = jax.random.uniform(jax.random.fold_in(jax.random.fold_in(rng, 6), position), (parts,), jnp.float32, smallest / len(pieces), largest / len(pieces))
        gain = gain * jnp.repeat(jnp.exp(draws), shape[position] // parts).reshape((-1,) + (1,) * (len(shape) - 1 - position))
    return gain


def centred(key, dims, width, reach, cuts=(), kind=jnp.bfloat16):
    entries = width * jax.random.normal(key, dims, jnp.float32)
    if cuts:
        entries = entries * shard_levels(key, dims, cuts, -0.22, 0.18)
    return jnp.clip(entries, -reach, reach).astype(kind)


def setup_inputs(seed: int = 0) -> dict:
    keys = jax.random.split(jax.random.key(seed), 20)
    return {
        "tokens": centred(keys[0], (BATCH, TOK_DEV, D), 1.0, 6.0, ((0, 32),)),
        "lengths": draw_lengths(jax.random.fold_in(keys[19], 71), 0),
        "routes": draw_routes(jax.random.fold_in(keys[19], 71), 0),
        "slot_index": draw_slot_index(jax.random.fold_in(keys[19], 71), 0),
        "mixer_norm": jnp.clip(1.0 + 0.1 * jax.random.normal(keys[4], (D,), jnp.float32), 0.5, 1.5).astype(jnp.bfloat16),
        "in_weight": centred(keys[5], (D, 2 * DI), D ** -0.5, 0.1875, ((1, 8),)),
        "conv_weight": centred(keys[6], (CONV, DI), CONV ** -0.5, 3.0, ((1, 8),)),
        "conv_bias": centred(keys[7], (DI,), 0.5, 3.0, ((0, 8),)),
        "scan_weight": centred(keys[8], (DI, DT_RANK + 2 * STATE), DI ** -0.5, 0.125, ((0, 8),)),
        "step_weight": centred(keys[9], (DT_RANK, DI), DT_RANK ** -0.5, 0.75, ((1, 8),)),
        "step_bias": jnp.clip(-6.0 + 5.0 * jax.random.uniform(keys[10], (DI,), jnp.float32) ** shard_levels(keys[10], (DI,), ((0, 8),), -0.2, 0.2), -6.0, -1.0).astype(jnp.bfloat16),
        "decay_log": jnp.clip(-1.0 + 3.796875 * jax.random.uniform(keys[11], (DI, STATE), jnp.float32) ** shard_levels(keys[11], (DI, STATE), ((0, 8),), -0.2, 0.2), -1.0, 2.796875).astype(jnp.bfloat16),
        "skip_gain": jnp.clip(0.5 + 1.0 * jax.random.uniform(keys[12], (DI,), jnp.float32) ** shard_levels(keys[12], (DI,), ((0, 8),), -0.2, 0.2), 0.5, 1.5).astype(jnp.bfloat16),
        "out_weight": centred(keys[13], (DI, D), (DI // 4) ** -0.5, 0.25, ((0, 8),)),
        "moe_norm": jnp.clip(1.0 + 0.1 * jax.random.normal(keys[14], (D,), jnp.float32), 0.5, 1.5).astype(jnp.bfloat16),
        "router_weight": centred(keys[15], (D, EXPERTS), (4 * D) ** -0.5, 0.09375, ((0, 8),)),
        "up_weight": centred(keys[16], (PIECES, D, HP), D ** -0.5, 0.1875, ((0, 8),)),
        "down_weight": centred(keys[17], (PIECES, HP, D), (EH // 64) ** -0.5, 0.875, ((0, 8),)),
        "cotangent": centred(keys[18], (BATCH, TOK_DEV, D), 1.0, 6.0, ((0, 32),)),
    }


@jax.custom_vjp
def low(v):
    return lax.optimization_barrier(v.astype(jnp.bfloat16)).astype(jnp.float32)

@jax.custom_vjp
def low_back(v):
    return v

def low_keep(v):
    return (low(v), None)

def low_pass(kept, grad):
    return (grad,)

def back_keep(v):
    return (v, None)

def back_low(kept, grad):
    return (low(grad),)
low.defvjp(low_keep, low_pass)
low_back.defvjp(back_keep, back_low)

def matmul(left, right):
    return jnp.dot(left, right, precision=lax.Precision.HIGHEST, preferred_element_type=jnp.float32)

def rms_scale(values, gain_vec):
    return values * lax.rsqrt(lax.optimization_barrier(jnp.mean(values * values, -1, keepdims=True)) + 1e-05) * gain_vec

def conv_front(x_inner, conv_kernel, conv_offset):
    length = x_inner.shape[0]
    tap_count = conv_kernel.shape[0]
    padded = jnp.pad(x_inner, ((tap_count - 1, 0), (0, 0)))
    summed = conv_offset + conv_kernel[0] * padded[0:length]
    for offset in range(1, tap_count):
        summed = summed + conv_kernel[offset] * padded[offset:offset + length]
    return jax.nn.silu(summed)

def block_scan(u_act, step_size, b_mat, c_mat, a_mat):
    length, channels = u_act.shape
    blocks = length // SCAN_BLOCK

    def arrange(values):
        return values.reshape(blocks, SCAN_BLOCK, values.shape[1]).transpose(1, 0, 2)
    seq_u, seq_step, seq_b, seq_c = (arrange(u_act), arrange(step_size), arrange(b_mat), arrange(c_mat))

    def advance(carry_state, u_now, step_now, b_now):
        return jnp.exp(step_now[:, :, None] * a_mat[None]) * carry_state + (step_now * u_now)[:, :, None] * b_now[:, None, :]

    def local_step(carry_state, inputs):
        return (advance(carry_state, inputs[0], inputs[1], inputs[2]), None)
    zeros_state = jnp.zeros((blocks, channels, a_mat.shape[1]), jnp.float32)
    block_ends, _ = lax.scan(local_step, zeros_state, (seq_u, seq_step, seq_b))
    block_decay = jnp.exp(lax.optimization_barrier(jnp.sum(seq_step, 0))[:, :, None] * a_mat[None])

    def combine(earlier, later):
        return (earlier[0] * later[0], later[0] * earlier[1] + later[1])
    _, carried = lax.associative_scan(combine, (block_decay, block_ends))
    starts = jnp.concatenate([zeros_state[:1], carried[:-1]], 0)

    def out_step(carry_state, inputs):
        carry_state = advance(carry_state, inputs[0], inputs[1], inputs[2])
        return (carry_state, lax.optimization_barrier(jnp.sum(carry_state * inputs[3][:, None, :], 2)))
    _, scanned = lax.scan(out_step, starts, (seq_u, seq_step, seq_b, seq_c))
    return scanned.transpose(1, 0, 2).reshape(length, channels)

def channel_scan(u_act, step_size, b_mat, c_mat, a_mat):
    length, channels = u_act.shape
    groups = 4
    group_width = channels // groups

    def stacked(values):
        return values.reshape(length, groups, group_width).transpose(1, 0, 2)

    def per_group(inputs):
        return block_scan(inputs[0], inputs[1], b_mat, c_mat, inputs[2])
    outputs = lax.map(jax.checkpoint(per_group), (stacked(u_act), stacked(step_size), a_mat.reshape(groups, group_width, a_mat.shape[1])))
    return outputs.transpose(1, 0, 2).reshape(length, channels)

def mixer_tail(step_proj, u_act, b_mat, c_mat, gate_in, step_bias, decay_log, skip_gain):
    step_size = jax.nn.softplus(step_proj + step_bias)
    scanned = channel_scan(u_act, step_size, b_mat, c_mat, -jnp.exp(decay_log))
    return (scanned + skip_gain * u_act) * jax.nn.silu(gate_in)

def mixer(tokens, weights):
    mixer_norm, in_weight, conv_weight, conv_bias, scan_weight, step_weight, step_bias, decay_log, skip_gain, out_weight = weights
    inner_width = out_weight.shape[0]
    dt_rank = step_weight.shape[0]
    state_size = decay_log.shape[1]
    normed = low(rms_scale(tokens, mixer_norm))
    projected_in = low_back(matmul(normed, in_weight))
    u_act = conv_front(projected_in[:, :inner_width], conv_weight, conv_bias)
    projected_x = low_back(matmul(low(u_act), scan_weight))
    step_proj = low_back(matmul(low(projected_x[:, :dt_rank]), step_weight))
    gated_out = mixer_tail(step_proj, u_act, projected_x[:, dt_rank:dt_rank + state_size], projected_x[:, dt_rank + state_size:], projected_in[:, inner_width:], step_bias, decay_log, skip_gain)
    return tokens + low_back(matmul(low(gated_out), out_weight))

def expert_apply(arguments):
    expert_in, up_pieces, down_pieces = arguments
    summed = jnp.zeros((expert_in.shape[0], down_pieces.shape[2]), jnp.float32)
    for piece_id in range(up_pieces.shape[0]):
        copied = low_back(expert_in)
        hidden = low_back(matmul(copied, up_pieces[piece_id]))
        summed = summed + low(matmul(low(jax.nn.gelu(hidden, approximate=False)), down_pieces[piece_id]))
    return summed

def reference(tokens, lengths, routes, slot_index, mixer_norm, in_weight, conv_weight, conv_bias, scan_weight, step_weight, step_bias, decay_log, skip_gain, out_weight, moe_norm, router_weight, up_weight, down_weight, cotangent):
    live_rows = (jnp.arange(TOK_DEV, dtype=jnp.int32)[None, :] < lengths[:, None]).astype(jnp.float32)
    kept_rows = slot_index < CAP
    target = jnp.where(kept_rows, routes * CAP + slot_index, EXPERTS * CAP).astype(jnp.int32)
    batch_index = jnp.arange(BATCH, dtype=jnp.int32)[:, None]
    positions = jnp.broadcast_to(jnp.arange(TOK_DEV, dtype=jnp.int32)[None, :], (BATCH, TOK_DEV))
    source_row = jnp.zeros((BATCH, EXPERTS * CAP + 1), jnp.int32).at[batch_index, target].set(positions)[:, :EXPERTS * CAP]
    filled = jnp.zeros((BATCH, EXPERTS * CAP + 1), jnp.float32).at[batch_index, target].set(1.0)[:, :EXPERTS * CAP]
    chosen = (routes[:, :, None] == jnp.arange(EXPERTS, dtype=jnp.int32)[None, None, :]).astype(jnp.float32)
    grouping = math.gcd(BATCH, max(1, 4096 // TOK_DEV))

    def forward(tokens_f, mixer_norm_f, in_weight_f, conv_weight_f, conv_bias_f, scan_weight_f, step_weight_f, step_bias_f, decay_log_f, skip_gain_f, out_weight_f, moe_norm_f, router_f, up_f, down_f):
        mixer_weights = (mixer_norm_f, in_weight_f, conv_weight_f, conv_bias_f, scan_weight_f, step_weight_f, step_bias_f, decay_log_f, skip_gain_f, out_weight_f)

        def mix_group(group_tokens):
            return jax.vmap(partial(mixer, weights=mixer_weights))(group_tokens)
        grouped = tokens_f.reshape(BATCH // grouping, grouping, TOK_DEV, D)
        mid_tokens = lax.map(jax.checkpoint(mix_group), grouped).reshape(BATCH, TOK_DEV, D)
        normed_two = low(rms_scale(mid_tokens, moe_norm_f))
        logits = low_back(matmul(normed_two.reshape(BATCH * TOK_DEV, D), router_f)).reshape(BATCH, TOK_DEV, EXPERTS)
        router_probs = jax.nn.softmax(logits, -1)
        gate_value = lax.optimization_barrier(jnp.sum(router_probs * chosen, -1))
        buffer = normed_two[batch_index, source_row] * filled[:, :, None]
        by_expert = buffer.reshape(BATCH, EXPERTS, CAP, D).transpose(1, 0, 2, 3).reshape(EXPERTS, BATCH * CAP, D)
        expert_rows = lax.map(jax.checkpoint(expert_apply), (by_expert, up_f.reshape(EXPERTS, SPLIT, D, HP), down_f.reshape(EXPERTS, SPLIT, HP, D)))
        returned = expert_rows.reshape(EXPERTS, BATCH, CAP, D).transpose(1, 0, 2, 3).reshape(BATCH, EXPERTS * CAP, D)
        returned = jnp.concatenate([returned, jnp.zeros((BATCH, 1, D), jnp.float32)], 1)
        expert_sum = returned[batch_index, target]
        return live_rows[:, :, None] * (mid_tokens + gate_value[:, :, None] * low_back(expert_sum))
    primals = (tokens.astype(jnp.float32), mixer_norm.astype(jnp.float32), in_weight.astype(jnp.float32), conv_weight.astype(jnp.float32), conv_bias.astype(jnp.float32), scan_weight.astype(jnp.float32), step_weight.astype(jnp.float32), step_bias.astype(jnp.float32), decay_log.astype(jnp.float32), skip_gain.astype(jnp.float32), out_weight.astype(jnp.float32), moe_norm.astype(jnp.float32), router_weight.astype(jnp.float32), up_weight.astype(jnp.float32), down_weight.astype(jnp.float32))
    layer_out, pullback = jax.vjp(forward, *primals)
    gradients = pullback(cotangent.astype(jnp.float32))
    return (layer_out.astype(jnp.bfloat16), gradients[0], gradients[1], gradients[2], gradients[3], gradients[4], gradients[5], gradients[6], gradients[7], gradients[8], gradients[9], gradients[10], gradients[11], gradients[12], gradients[13], gradients[14])
```

```python
from functools import partial

import jax
import jax.numpy as jnp
from jax import lax
from jax.experimental import pallas as pl
from jax.experimental.pallas import tpu as pltpu
from jax.sharding import PartitionSpec as P

CAP = 64
BLOCK = 16
LOG2E = 1.4426950408889634
F32 = jnp.float32
BF16 = jnp.bfloat16
VMEM_LIMIT = 56 * 1024 * 1024


def product(left, right):
    return jnp.dot(left, right, preferred_element_type=F32)


def contract_rows(left, right):
    return lax.dot_general(left, right, (((0,), (0,)), ((), ())), preferred_element_type=F32)


def times_transpose(left, right):
    return lax.dot_general(left, right, (((1,), (1,)), ((), ())), preferred_element_type=F32)


def exact_product(left, right):
    return jnp.dot(left, right, preferred_element_type=F32, precision=lax.Precision.HIGHEST)


def iota(shape, axis):
    return lax.broadcasted_iota(jnp.int32, shape, axis)


def sigmoid(values):
    return 1.0 / (1.0 + jnp.exp(-values))


def softplus(values):
    return jnp.maximum(values, 0.0) + jnp.log1p(jnp.exp(-jnp.abs(values)))


def shift_rows(values, offset):
    rows = values.shape[0]
    if offset == 0:
        return values
    rolled = pltpu.roll(values, offset % rows, 0)
    row = iota(values.shape, 0)
    keep = row >= offset if offset > 0 else row < rows + offset
    return jnp.where(keep, rolled, 0.0)


def two_parts(values):
    high = values.astype(BF16)
    low = (values - high.astype(F32)).astype(BF16)
    return high, low


def spread_rows(proj_block, first, state):
    rows, width = proj_block.shape
    big = rows * state
    pick = (iota((big, rows), 0) // state == iota((big, rows), 1)).astype(F32)
    copied = exact_product(pick, proj_block)
    lane = iota((big, width), 1)
    own = lane == first + iota((big, width), 0) % state
    column = jnp.sum(jnp.where(own, copied, 0.0), axis=1, keepdims=True)
    return jnp.broadcast_to(column, (big, 128))


def diagonal_blocks(proj_block, first, state):
    rows, width = proj_block.shape
    big = rows * state
    place = (iota((width, big), 0) == first + iota((width, big), 1) % state).astype(BF16)
    own = iota((rows, big), 0) == iota((rows, big), 1) // state
    parts = [
        jnp.where(own, product(part, place), 0.0).astype(BF16) for part in two_parts(proj_block)
    ]
    return jnp.concatenate(parts, 0)


def front_kernel(
    tokens_ref, gain_ref, wx_ref, wg_ref, conv_ref, bias_ref, scanw_ref,
    normed_ref, xin_ref, u_ref, gate_ref, proj_ref,
):
    step = pl.program_id(0)

    @pl.when(step == 0)
    def _():
        values = tokens_ref[...].astype(F32)
        scale = lax.rsqrt(jnp.mean(values * values, -1, keepdims=True) + 1e-05)
        normed_ref[...] = (values * scale * gain_ref[...]).astype(BF16)
        proj_ref[...] = jnp.zeros_like(proj_ref)

    normed = normed_ref[...]
    x_inner = times_transpose(normed, wx_ref[...])
    gate_ref[...] = times_transpose(normed, wg_ref[...])
    xin_ref[...] = x_inner
    taps = conv_ref.shape[0]
    summed = bias_ref[...] + conv_ref[taps - 1 : taps, :] * x_inner
    for back in range(1, taps):
        tap = taps - 1 - back
        summed = summed + conv_ref[tap : tap + 1, :] * shift_rows(x_inner, back)
    u_act = summed * sigmoid(summed)
    u_ref[...] = u_act
    proj_ref[...] += product(u_act.astype(BF16), scanw_ref[...])


def front(tokens, gain, in_t, conv, bias, scan_w, tile):
    rows, width = tokens.shape
    channels = scan_w.shape[0]
    cols = scan_w.shape[1]
    steps = channels // tile
    return pl.pallas_call(
        front_kernel,
        grid=(steps,),
        in_specs=[
            pl.BlockSpec((rows, width), lambda i: (0, 0)),
            pl.BlockSpec((1, width), lambda i: (0, 0)),
            pl.BlockSpec((tile, width), lambda i: (i, 0)),
            pl.BlockSpec((tile, width), lambda i: (i + steps, 0)),
            pl.BlockSpec((conv.shape[0], tile), lambda i: (0, i)),
            pl.BlockSpec((1, tile), lambda i: (0, i)),
            pl.BlockSpec((tile, cols), lambda i: (i, 0)),
        ],
        out_specs=[
            pl.BlockSpec((rows, width), lambda i: (0, 0)),
            pl.BlockSpec((rows, tile), lambda i: (0, i)),
            pl.BlockSpec((rows, tile), lambda i: (0, i)),
            pl.BlockSpec((rows, tile), lambda i: (0, i)),
            pl.BlockSpec((rows, cols), lambda i: (0, 0)),
        ],
        out_shape=[
            jax.ShapeDtypeStruct((rows, width), BF16),
            jax.ShapeDtypeStruct((rows, channels), F32),
            jax.ShapeDtypeStruct((rows, channels), F32),
            jax.ShapeDtypeStruct((rows, channels), F32),
            jax.ShapeDtypeStruct((rows, cols), F32),
        ],
        compiler_params=pltpu.CompilerParams(vmem_limit_bytes=VMEM_LIMIT),
        name="mixer_front",
    )(tokens, gain, in_t, in_t, conv, bias, scan_w)


def scan_kernel(
    proj_ref, stepw_ref, dbias_ref, decay_ref, skip_ref, u_ref, gate_ref, outw_ref, tokens_ref,
    step_ref, mixed_ref, gated_ref, hist_ref, mid_ref,
    b_wide, c_blocks, du, scanned,
):
    tile_id = pl.program_id(0)
    rank = stepw_ref.shape[0]
    state = decay_ref.shape[0]
    rows = u_ref.shape[0]
    blocks = rows // BLOCK
    big = BLOCK * state

    @pl.when(tile_id == 0)
    def _():
        mid_ref[...] = tokens_ref[...].astype(F32)

        def build(block, carry):
            part = proj_ref[pl.ds(pl.multiple_of(block * BLOCK, BLOCK), BLOCK), :]
            b_wide[pl.ds(pl.multiple_of(block * big, big), big), :] = spread_rows(part, rank, state)
            c_blocks[pl.ds(pl.multiple_of(block * 2 * BLOCK, 2 * BLOCK), 2 * BLOCK), :] = (
                diagonal_blocks(part, rank + state, state)
            )
            return carry

        lax.fori_loop(0, blocks, build, 0)

    u_act = u_ref[...]
    step_size = softplus(
        product(proj_ref[:, :rank].astype(BF16), stepw_ref[...]) + dbias_ref[...]
    )
    step_ref[...] = step_size
    du[...] = step_size * u_act
    decay = decay_ref[...] * LOG2E
    tile = u_act.shape[1]
    hist_ref[0:state, :] = jnp.zeros((state, tile), BF16)

    def run_block(block, held):
        base = pl.multiple_of(block * BLOCK, BLOCK)
        steps_now = step_ref[pl.ds(base, BLOCK), :]
        du_now = du[pl.ds(base, BLOCK), :]
        wide_base = pl.multiple_of(block * big, big)
        for t in range(BLOCK):
            b_now = b_wide[pl.ds(wide_base + t * state, state), :]
            fade = jnp.exp2(steps_now[t : t + 1, :] * decay)
            fresh = du_now[t : t + 1, :] * jnp.concatenate([b_now] * (tile // 128), 1)
            held = fade * held + fresh
            hist_ref[pl.ds(wide_base + (t + 1) * state, state), :] = held.astype(BF16)
        weights = c_blocks[pl.ds(pl.multiple_of(block * 2 * BLOCK, 2 * BLOCK), 2 * BLOCK), :]
        both = product(weights, hist_ref[pl.ds(wide_base + state, big), :])
        scanned[pl.ds(base, BLOCK), :] = both[:BLOCK] + both[BLOCK:]
        return held

    lax.fori_loop(0, blocks, run_block, jnp.zeros((state, tile), F32))
    mixed = scanned[...] + skip_ref[...] * u_act
    mixed_ref[...] = mixed
    gate_in = gate_ref[...]
    gated = (mixed * (gate_in * sigmoid(gate_in))).astype(BF16)
    gated_ref[...] = gated
    mid_ref[...] += product(gated, outw_ref[...])


def scan_forward(proj, step_w, dbias, decay, skip, u_act, gate_in, out_w, tokens, tile):
    rows, channels = u_act.shape
    width = tokens.shape[1]
    cols = proj.shape[1]
    rank, state = step_w.shape[0], decay.shape[0]
    steps = channels // tile
    hist_rows = (rows + 1) * state
    column = lambda i: (0, i)
    fixed = lambda i: (0, 0)
    return pl.pallas_call(
        scan_kernel,
        grid=(steps,),
        in_specs=[
            pl.BlockSpec((rows, cols), fixed),
            pl.BlockSpec((rank, tile), column),
            pl.BlockSpec((1, tile), column),
            pl.BlockSpec((state, tile), column),
            pl.BlockSpec((1, tile), column),
            pl.BlockSpec((rows, tile), column),
            pl.BlockSpec((rows, tile), column),
            pl.BlockSpec((tile, width), lambda i: (i, 0)),
            pl.BlockSpec((rows, width), fixed),
        ],
        out_specs=[
            pl.BlockSpec((rows, tile), column),
            pl.BlockSpec((rows, tile), column),
            pl.BlockSpec((rows, tile), column),
            pl.BlockSpec((hist_rows, tile), column),
            pl.BlockSpec((rows, width), fixed),
        ],
        out_shape=[
            jax.ShapeDtypeStruct((rows, channels), F32),
            jax.ShapeDtypeStruct((rows, channels), F32),
            jax.ShapeDtypeStruct((rows, channels), BF16),
            jax.ShapeDtypeStruct((hist_rows, channels), BF16),
            jax.ShapeDtypeStruct((rows, width), F32),
        ],
        scratch_shapes=[
            pltpu.VMEM((rows * state, 128), F32),
            pltpu.VMEM((rows * 2, BLOCK * state), BF16),
            pltpu.VMEM((rows, tile), F32),
            pltpu.VMEM((rows, tile), F32),
        ],
        compiler_params=pltpu.CompilerParams(vmem_limit_bytes=VMEM_LIMIT),
        name="scan_forward",
    )(proj, step_w, dbias, decay, skip, u_act, gate_in, out_w, tokens)


def scan_back_kernel(
    proj_ref, stepw_ref, dbias_ref, decay_ref, skip_ref, u_ref, gate_ref, outw_ref, gradmix_ref,
    step_ref, mixed_ref, hist_ref,
    gradu_ref, gradgate_ref, gradstepw_ref, gradbias_ref, gradskip_ref, gradlog_ref, gradproj_ref,
    c_wide, b_blocks, b_sums, c_sums, gy, du, g_hist, w_hist, grad_du, grad_step,
):
    tile_id = pl.program_id(0)
    cols, rank = proj_ref.shape[1], stepw_ref.shape[0]
    state = decay_ref.shape[0]
    rows, tile = u_ref.shape
    blocks = rows // BLOCK
    big = BLOCK * state

    @pl.when(tile_id == 0)
    def _():
        gradproj_ref[...] = jnp.zeros_like(gradproj_ref)
        b_sums[...] = jnp.zeros_like(b_sums)
        c_sums[...] = jnp.zeros_like(c_sums)

        def build(block, carry):
            part = proj_ref[pl.ds(pl.multiple_of(block * BLOCK, BLOCK), BLOCK), :]
            c_wide[pl.ds(pl.multiple_of(block * big, big), big), :] = spread_rows(
                part, rank + state, state
            )
            b_blocks[pl.ds(pl.multiple_of(block * 2 * BLOCK, 2 * BLOCK), 2 * BLOCK), :] = (
                diagonal_blocks(part, rank, state)
            )
            return carry

        lax.fori_loop(0, blocks, build, 0)

    grad_gated = times_transpose(gradmix_ref[...], outw_ref[...])
    gate_in = gate_ref[...]
    gate_sig = sigmoid(gate_in)
    grad_mixed = grad_gated * (gate_in * gate_sig)
    gradgate_ref[...] = (
        grad_gated * mixed_ref[...] * (gate_sig * (1.0 + gate_in * (1.0 - gate_sig)))
    ).astype(BF16)
    u_act = u_ref[...]
    step_size = step_ref[...]
    gy[...] = grad_mixed
    du[...] = step_size * u_act
    gradskip_ref[...] = jnp.sum(grad_mixed * u_act, 0, keepdims=True)
    rate = decay_ref[...]
    decay = rate * LOG2E
    sums = (iota((BLOCK, big), 0) == iota((BLOCK, big), 1) // state).astype(BF16)

    def run_block(turn, carry):
        carried, log_sum = carry
        block = blocks - 1 - turn
        base = pl.multiple_of(block * BLOCK, BLOCK)
        wide_base = pl.multiple_of(block * big, big)
        steps_now = step_ref[pl.ds(base, BLOCK), :]
        gy_now = gy[pl.ds(base, BLOCK), :]
        for t in range(BLOCK - 1, -1, -1):
            c_now = c_wide[pl.ds(wide_base + t * state, state), :]
            step_now = steps_now[t : t + 1, :]
            fade = jnp.exp2(step_now * decay)
            grad = gy_now[t : t + 1, :] * jnp.concatenate([c_now] * (tile // 128), 1) + carried
            g_hist[t * state : (t + 1) * state, :] = grad.astype(BF16)
            carried = fade * grad
            before = hist_ref[pl.ds(wide_base + t * state, state), :].astype(F32)
            weighted = carried * before * rate
            w_hist[t * state : (t + 1) * state, :] = weighted.astype(BF16)
            log_sum = log_sum + weighted * step_now
        grads = g_hist[...]
        both = product(
            b_blocks[pl.ds(pl.multiple_of(block * 2 * BLOCK, 2 * BLOCK), 2 * BLOCK), :], grads
        )
        grad_du[pl.ds(base, BLOCK), :] = both[:BLOCK] + both[BLOCK:]
        grad_step[pl.ds(base, BLOCK), :] = product(sums, w_hist[...])
        b_sums[pl.ds(base, BLOCK), :] += times_transpose(
            du[pl.ds(base, BLOCK), :].astype(BF16), grads
        )
        c_sums[pl.ds(base, BLOCK), :] += times_transpose(
            gy_now.astype(BF16), hist_ref[pl.ds(wide_base + state, big), :]
        )
        return carried, log_sum

    zeros = jnp.zeros((state, tile), F32)
    _, log_sum = lax.fori_loop(0, blocks, run_block, (zeros, zeros))
    gradlog_ref[...] = log_sum
    full_du = grad_du[...]
    gradu_ref[...] = full_du * step_size + skip_ref[...] * gy[...]
    grad_size = grad_step[...] + full_du * u_act
    grad_pre = grad_size * (1.0 - jnp.exp(-step_size))
    gradbias_ref[...] = jnp.sum(grad_pre, 0, keepdims=True)
    grad_low = grad_pre.astype(BF16)
    gradstepw_ref[...] = contract_rows(proj_ref[:, :rank].astype(BF16), grad_low)
    gradproj_ref[:, :rank] += times_transpose(grad_low, stepw_ref[...])

    @pl.when(tile_id == pl.num_programs(0) - 1)
    def _():
        own = iota((rows, big), 0) % BLOCK == iota((rows, big), 1) // state
        lane = iota((big, cols), 1)
        slot = iota((big, cols), 0) % state
        total = gradproj_ref[...]
        for sums_ref, first in ((b_sums, rank), (c_sums, rank + state)):
            place = (lane == first + slot).astype(F32)
            total = total + exact_product(jnp.where(own, sums_ref[...], 0.0), place)
        gradproj_ref[...] = total


def scan_backward(
    proj, step_w, dbias, decay, skip, u_act, gate_in, out_w, grad_mix, step_size, mixed, hist, tile
):
    rows, channels = u_act.shape
    width = grad_mix.shape[1]
    cols = proj.shape[1]
    rank, state = step_w.shape[0], decay.shape[0]
    steps = channels // tile
    big = BLOCK * state
    column = lambda i: (0, i)
    fixed = lambda i: (0, 0)
    return pl.pallas_call(
        scan_back_kernel,
        grid=(steps,),
        in_specs=[
            pl.BlockSpec((rows, cols), fixed),
            pl.BlockSpec((rank, tile), column),
            pl.BlockSpec((1, tile), column),
            pl.BlockSpec((state, tile), column),
            pl.BlockSpec((1, tile), column),
            pl.BlockSpec((rows, tile), column),
            pl.BlockSpec((rows, tile), column),
            pl.BlockSpec((tile, width), lambda i: (i, 0)),
            pl.BlockSpec((rows, width), fixed),
            pl.BlockSpec((rows, tile), column),
            pl.BlockSpec((rows, tile), column),
            pl.BlockSpec((hist.shape[0], tile), column),
        ],
        out_specs=[
            pl.BlockSpec((rows, tile), column),
            pl.BlockSpec((rows, tile), column),
            pl.BlockSpec((rank, tile), column),
            pl.BlockSpec((1, tile), column),
            pl.BlockSpec((1, tile), column),
            pl.BlockSpec((state, tile), column),
            pl.BlockSpec((rows, cols), fixed),
        ],
        out_shape=[
            jax.ShapeDtypeStruct((rows, channels), F32),
            jax.ShapeDtypeStruct((rows, channels), BF16),
            jax.ShapeDtypeStruct((rank, channels), F32),
            jax.ShapeDtypeStruct((1, channels), F32),
            jax.ShapeDtypeStruct((1, channels), F32),
            jax.ShapeDtypeStruct((state, channels), F32),
            jax.ShapeDtypeStruct((rows, cols), F32),
        ],
        scratch_shapes=[
            pltpu.VMEM((rows * state, 128), F32),
            pltpu.VMEM((rows * 2, big), BF16),
            pltpu.VMEM((rows, big), F32),
            pltpu.VMEM((rows, big), F32),
            pltpu.VMEM((rows, tile), F32),
            pltpu.VMEM((rows, tile), F32),
            pltpu.VMEM((big, tile), BF16),
            pltpu.VMEM((big, tile), BF16),
            pltpu.VMEM((rows, tile), F32),
            pltpu.VMEM((rows, tile), F32),
        ],
        compiler_params=pltpu.CompilerParams(vmem_limit_bytes=VMEM_LIMIT),
        name="scan_backward",
    )(proj, step_w, dbias, decay, skip, u_act, gate_in, out_w, grad_mix, step_size, mixed, hist)


def back_kernel(
    gradproj_ref, scanw_ref, gradu_ref, xin_ref, conv_ref, bias_ref, gradgate_ref, wx_ref, wg_ref,
    u_ref, tokens_ref, gain_ref, gradmid_ref,
    gradx_ref, gradconv_ref, gradbias_ref, gradscanw_ref, gradtok_ref, gradgain_ref,
    total,
):
    tile_id = pl.program_id(0)

    @pl.when(tile_id == 0)
    def _():
        total[...] = jnp.zeros_like(total)

    grad_proj = gradproj_ref[...].astype(BF16)
    grad_u = gradu_ref[...] + times_transpose(grad_proj, scanw_ref[...])
    gradscanw_ref[...] = contract_rows(u_ref[...].astype(BF16), grad_proj)
    x_inner = xin_ref[...]
    taps = conv_ref.shape[0]
    shifted = [shift_rows(x_inner, taps - 1 - tap) for tap in range(taps)]
    summed = bias_ref[...]
    for tap in range(taps):
        summed = summed + conv_ref[tap : tap + 1, :] * shifted[tap]
    sig = sigmoid(summed)
    grad_sum = grad_u * (sig * (1.0 + summed * (1.0 - sig)))
    gradbias_ref[...] = jnp.sum(grad_sum, 0, keepdims=True)
    grad_x = jnp.zeros_like(x_inner)
    for tap in range(taps):
        gradconv_ref[tap : tap + 1, :] = jnp.sum(grad_sum * shifted[tap], 0, keepdims=True)
        grad_x = grad_x + conv_ref[tap : tap + 1, :] * shift_rows(grad_sum, tap + 1 - taps)
    grad_x = grad_x.astype(BF16)
    gradx_ref[...] = grad_x
    total[...] += product(grad_x, wx_ref[...]) + product(gradgate_ref[...], wg_ref[...])

    @pl.when(tile_id == pl.num_programs(0) - 1)
    def _():
        values = tokens_ref[...].astype(F32)
        scale = lax.rsqrt(jnp.mean(values * values, -1, keepdims=True) + 1e-05)
        unit = values * scale
        grad = total[...]
        gradgain_ref[...] = jnp.sum(grad * unit, 0, keepdims=True)
        inner = grad * gain_ref[...]
        gradtok_ref[...] = gradmid_ref[...] + scale * (
            inner - unit * jnp.mean(inner * unit, -1, keepdims=True)
        )


def mixer_back(
    grad_proj, scan_w, grad_u, x_inner, conv, bias, grad_gate, in_t, u_act, tokens, gain, grad_mid,
    tile,
):
    rows, channels = u_act.shape
    width = tokens.shape[1]
    cols = scan_w.shape[1]
    taps = conv.shape[0]
    steps = channels // tile
    column = lambda i: (0, i)
    fixed = lambda i: (0, 0)
    return pl.pallas_call(
        back_kernel,
        grid=(steps,),
        in_specs=[
            pl.BlockSpec((rows, cols), fixed),
            pl.BlockSpec((tile, cols), lambda i: (i, 0)),
            pl.BlockSpec((rows, tile), column),
            pl.BlockSpec((rows, tile), column),
            pl.BlockSpec((taps, tile), column),
            pl.BlockSpec((1, tile), column),
            pl.BlockSpec((rows, tile), column),
            pl.BlockSpec((tile, width), lambda i: (i, 0)),
            pl.BlockSpec((tile, width), lambda i: (i + steps, 0)),
            pl.BlockSpec((rows, tile), column),
            pl.BlockSpec((rows, width), fixed),
            pl.BlockSpec((1, width), fixed),
            pl.BlockSpec((rows, width), fixed),
        ],
        out_specs=[
            pl.BlockSpec((rows, tile), column),
            pl.BlockSpec((taps, tile), column),
            pl.BlockSpec((1, tile), column),
            pl.BlockSpec((tile, cols), lambda i: (i, 0)),
            pl.BlockSpec((rows, width), fixed),
            pl.BlockSpec((1, width), fixed),
        ],
        out_shape=[
            jax.ShapeDtypeStruct((rows, channels), BF16),
            jax.ShapeDtypeStruct((taps, channels), F32),
            jax.ShapeDtypeStruct((1, channels), F32),
            jax.ShapeDtypeStruct((channels, cols), F32),
            jax.ShapeDtypeStruct((rows, width), F32),
            jax.ShapeDtypeStruct((1, width), F32),
        ],
        scratch_shapes=[pltpu.VMEM((rows, width), F32)],
        compiler_params=pltpu.CompilerParams(vmem_limit_bytes=VMEM_LIMIT),
        name="mixer_back",
    )(
        grad_proj, scan_w, grad_u, x_inner, conv, bias, grad_gate, in_t, in_t, u_act, tokens, gain,
        grad_mid,
    )


def gelu_parts(values):
    weight = jnp.exp(values * values * -0.5)
    scaled = jnp.abs(values) * 0.7071067811865476
    ratio = 1.0 / (1.0 + 0.3275911 * scaled)
    series = 1.061405429 * ratio - 1.453152027
    series = series * ratio + 1.421413741
    series = series * ratio - 0.284496736
    series = series * ratio + 0.254829592
    tail = (0.5 * ratio) * series * weight
    below = jnp.where(values >= 0.0, 1.0 - tail, tail)
    return values * below, below + values * weight * 0.3989422804014327


def router_kernel(
    mid_ref, gain_ref, router_ref, routes_col_ref, routes_row_ref, slots_row_ref, live_ref, cot_ref,
    send_ref, normed_ref, probs_ref,
):
    mid = mid_ref[...]
    rows = mid.shape[0]
    experts = router_ref.shape[1]
    scale = lax.rsqrt(jnp.mean(mid * mid, -1, keepdims=True) + 1e-05)
    normed = (mid * scale * gain_ref[...]).astype(BF16)
    normed_ref[...] = normed
    logits = product(normed, router_ref[...])
    weights = jnp.exp(logits - jnp.max(logits, -1, keepdims=True))
    probs = weights / jnp.sum(weights, -1, keepdims=True)
    probs_ref[...] = probs
    chosen = (routes_col_ref[...] == iota((rows, experts), 1)).astype(F32)
    gate = jnp.sum(probs * chosen, 1, keepdims=True)
    grads = (gate * (cot_ref[...].astype(F32) * live_ref[...])).astype(BF16)
    slot = iota((experts * CAP, rows), 0)
    dispatch = (
        (routes_row_ref[...] == slot // CAP) & (slots_row_ref[...] == slot % CAP)
    ).astype(BF16)
    width = mid.shape[1]
    send_ref[:, :CAP, :] = product(dispatch, normed).astype(BF16).reshape(experts, CAP, width)
    send_ref[:, CAP:, :] = product(dispatch, grads).astype(BF16).reshape(experts, CAP, width)


def router_step(mid, gain, router, routes_col, routes_row, slots_row, live, cotangent):
    rows, width = mid.shape
    experts = router.shape[1]
    return pl.pallas_call(
        router_kernel,
        out_shape=[
            jax.ShapeDtypeStruct((experts, 2 * CAP, width), BF16),
            jax.ShapeDtypeStruct((rows, width), BF16),
            jax.ShapeDtypeStruct((rows, experts), F32),
        ],
        compiler_params=pltpu.CompilerParams(vmem_limit_bytes=VMEM_LIMIT),
        name="router_step",
    )(mid, gain, router, routes_col, routes_row, slots_row, live, cotangent)


def expert_kernel(got_ref, up_ref, down_ref, back_ref, out_sum, in_sum):
    step = pl.program_id(0)
    pieces, double, width = got_ref.shape
    rows = got_ref[:, :CAP, :].reshape(pieces * CAP, width)
    grads = got_ref[:, CAP:, :].reshape(pieces * CAP, width)

    @pl.when(step == 0)
    def _():
        out_sum[...] = jnp.zeros_like(out_sum)
        in_sum[...] = jnp.zeros_like(in_sum)

    activated, slope = gelu_parts(product(rows, up_ref[...]))
    out_sum[...] += product(activated.astype(BF16), down_ref[...])
    grad_pre = (times_transpose(grads, down_ref[...]) * slope).astype(BF16)
    in_sum[...] += times_transpose(grad_pre, up_ref[...])

    @pl.when(step == pl.num_programs(0) - 1)
    def _():
        back_ref[:, :CAP, :] = out_sum[...].astype(BF16).reshape(pieces, CAP, width)
        back_ref[:, CAP:, :] = in_sum[...].astype(BF16).reshape(pieces, CAP, width)


def expert_step(got, up, down, tile):
    pieces, double, width = got.shape
    hidden = up.shape[1]
    fixed = lambda i: (0, 0, 0)
    return pl.pallas_call(
        expert_kernel,
        grid=(hidden // tile,),
        in_specs=[
            pl.BlockSpec(got.shape, fixed),
            pl.BlockSpec((width, tile), lambda i: (0, i)),
            pl.BlockSpec((tile, width), lambda i: (i, 0)),
        ],
        out_specs=pl.BlockSpec(got.shape, fixed),
        out_shape=jax.ShapeDtypeStruct(got.shape, BF16),
        scratch_shapes=[pltpu.VMEM((pieces * CAP, width), F32)] * 2,
        compiler_params=pltpu.CompilerParams(vmem_limit_bytes=VMEM_LIMIT),
        name="expert_step",
    )(got, up, down)


def expert_grads_kernel(chunks, all_ref, up_ref, down_ref, gup_ref, gdown_ref, rows_t):
    chunk = pl.program_id(1)
    groups, pieces, double, width = all_ref.shape
    count = groups * pieces * CAP
    rows = all_ref[:, :, :CAP, :].reshape(count, width)
    grads = all_ref[:, :, CAP:, :].reshape(count, width)

    @pl.when((pl.program_id(0) == 0) | (chunks > 1))
    def _():
        rows_t[...] = rows.T

    activated, slope = gelu_parts(product(rows, up_ref[...]))
    grad_pre = (times_transpose(grads, down_ref[...]) * slope).astype(BF16)
    grad_up = product(rows_t[...], grad_pre)
    grad_down = contract_rows(activated.astype(BF16), grads)

    @pl.when(chunk == 0)
    def _():
        gup_ref[...] = grad_up
        gdown_ref[...] = grad_down

    if chunks > 1:

        @pl.when(chunk > 0)
        def _():
            gup_ref[...] += grad_up
            gdown_ref[...] += grad_down


def expert_grads(gathered, up, down, tile):
    groups, pieces, double, width = gathered.shape
    hidden = up.shape[1]
    together = max(1, min(groups, 32 // pieces))
    chunks = groups // together
    return pl.pallas_call(
        partial(expert_grads_kernel, chunks),
        grid=(hidden // tile, chunks),
        in_specs=[
            pl.BlockSpec((together, pieces, double, width), lambda i, j: (j, 0, 0, 0)),
            pl.BlockSpec((width, tile), lambda i, j: (0, i)),
            pl.BlockSpec((tile, width), lambda i, j: (i, 0)),
        ],
        out_specs=[
            pl.BlockSpec((width, tile), lambda i, j: (0, i)),
            pl.BlockSpec((tile, width), lambda i, j: (i, 0)),
        ],
        out_shape=[
            jax.ShapeDtypeStruct((width, hidden), F32),
            jax.ShapeDtypeStruct((hidden, width), F32),
        ],
        scratch_shapes=[pltpu.VMEM((width, together * pieces * CAP), BF16)],
        compiler_params=pltpu.CompilerParams(vmem_limit_bytes=VMEM_LIMIT),
        name="expert_grads",
    )(gathered, up, down)


def combine_kernel(
    mid_ref, gain_ref, router_ref, routes_ref, slots_ref, live_ref, cot_ref, probs_ref, normed_ref,
    back_ref, out_ref, gradmid_ref, gradmix_ref, gradrouter_ref, gradgain_ref,
):
    mid = mid_ref[...]
    rows, width = mid.shape
    experts = router_ref.shape[1]
    routes = routes_ref[...]
    chosen = (routes == iota((rows, experts), 1)).astype(F32)
    probs = probs_ref[...]
    gate = jnp.sum(probs * chosen, 1, keepdims=True)
    live = live_ref[...]
    slot = iota((rows, experts * CAP), 1)
    collect = ((routes == slot // CAP) & (slots_ref[...] == slot % CAP)).astype(BF16)
    expert_sum = product(collect, back_ref[:, :CAP, :].reshape(experts * CAP, width))
    out_ref[...] = (live * (mid + gate * expert_sum)).astype(BF16)
    grad_out = cot_ref[...].astype(F32) * live
    grad_gate = jnp.sum(grad_out * expert_sum, 1, keepdims=True)
    grad_logits = (probs * (chosen * grad_gate - gate * grad_gate)).astype(BF16)
    gradrouter_ref[...] = contract_rows(normed_ref[...], grad_logits)
    grad = product(collect, back_ref[:, CAP:, :].reshape(experts * CAP, width))
    grad = grad + times_transpose(grad_logits, router_ref[...])
    scale = lax.rsqrt(jnp.mean(mid * mid, -1, keepdims=True) + 1e-05)
    unit = mid * scale
    gradgain_ref[...] = jnp.sum(grad * unit, 0, keepdims=True)
    inner = grad * gain_ref[...]
    grad_mid = grad_out + scale * (inner - unit * jnp.mean(inner * unit, -1, keepdims=True))
    gradmid_ref[...] = grad_mid
    gradmix_ref[...] = grad_mid.astype(BF16)


def combine_step(mid, gain, router, routes, slots, live, cotangent, probs, normed, back):
    rows, width = mid.shape
    return pl.pallas_call(
        combine_kernel,
        out_shape=[
            jax.ShapeDtypeStruct((rows, width), BF16),
            jax.ShapeDtypeStruct((rows, width), F32),
            jax.ShapeDtypeStruct((rows, width), BF16),
            jax.ShapeDtypeStruct(router.shape, F32),
            jax.ShapeDtypeStruct((1, width), F32),
        ],
        compiler_params=pltpu.CompilerParams(vmem_limit_bytes=VMEM_LIMIT),
        name="combine_step",
    )(mid, gain, router, routes, slots, live, cotangent, probs, normed, back)


def gather(value):
    return lax.all_gather(value, "expert", axis=0, tiled=True)


def exchange(value):
    return lax.all_to_all(value, "expert", split_axis=0, concat_axis=0, tiled=True)


def shards(
    tokens, lengths, routes, slot_index, mixer_norm, in_weight, conv_weight, conv_bias,
    scan_weight, step_weight, step_bias, decay_log, skip_gain, out_weight, moe_norm, router_weight,
    up_weight, down_weight, cotangent,
):
    devices = lax.axis_size("expert")
    rows, width = tokens.shape[1:]
    part = out_weight.shape[0]
    channels = part * devices
    cols = scan_weight.shape[1]
    rank, state, taps = step_weight.shape[0], decay_log.shape[1], conv_weight.shape[0]
    experts = router_weight.shape[1]
    split = devices // experts
    slice_w = width // devices
    tile = 768

    in_t = gather(in_weight.T)
    by_column = jnp.concatenate(
        [step_weight, decay_log.T, conv_weight, conv_bias[None], step_bias[None], skip_gain[None]], 0
    )
    by_width = jnp.concatenate([mixer_norm[:, None], moe_norm[:, None], router_weight], 1)
    small = jnp.concatenate(
        [by_column.reshape(-1), scan_weight.reshape(-1), by_width.reshape(-1)]
    )
    small = gather(small[None])
    first = by_column.size
    second = first + scan_weight.size
    columns = (
        small[:, :first].reshape(devices, by_column.shape[0], part)
        .transpose(1, 0, 2).reshape(by_column.shape[0], channels)
    )
    scan_full = small[:, first:second].reshape(channels, cols)
    widths = small[:, second:].reshape(width, experts + 2)
    out_full = gather(out_weight)
    step_full = columns[:rank]
    rest = columns[rank:].astype(F32)
    rate = -jnp.exp(rest[:state])
    conv_full = rest[state : state + taps]
    bias_full, dbias_full, skip_full = (
        rest[state + taps + k : state + taps + k + 1] for k in range(3)
    )
    gain_first = widths[:, 0].astype(F32)[None]
    gain_second = widths[:, 1].astype(F32)[None]
    router = widths[:, 2:]
    up, down = up_weight[0], down_weight[0]
    live = (jnp.arange(rows, dtype=jnp.int32) < lengths[0]).astype(F32)[:, None]
    routes_col, slots_col = routes[0][:, None], slot_index[0][:, None]

    normed_low, x_inner, u_act, gate_in, proj = front(
        tokens[0], gain_first, in_t, conv_full, bias_full, scan_full, tile
    )
    step_size, mixed, gated, hist, mid = scan_forward(
        proj, step_full, dbias_full, rate, skip_full, u_act, gate_in, out_full, tokens[0], tile
    )
    send, normed_two, probs = router_step(
        mid, gain_second, router, routes_col, routes, slot_index, live, cotangent[0]
    )
    wide = jnp.broadcast_to(send[:, None], (experts, split) + send.shape[1:])
    got = exchange(wide.reshape(devices, 2 * CAP, width))
    everyone = lax.all_gather(got, "dp")
    pieces_back = exchange(expert_step(got, up, down, min(512, up.shape[1] // 3)))
    pieces_back = pieces_back.reshape(experts, split, 2 * CAP, width)
    back = pieces_back[:, 0]
    if split > 1:
        back = jnp.sum(pieces_back.astype(F32), 1).astype(BF16)
    layer_out, grad_mid, grad_mix, grad_router, grad_gain_second = combine_step(
        mid, gain_second, router, routes_col, slots_col, live, cotangent[0], probs, normed_two, back
    )
    grad_u, grad_gate, grad_step_w, grad_dbias, grad_skip, grad_log, grad_proj = scan_backward(
        proj, step_full, dbias_full, rate, skip_full, u_act, gate_in, out_full, grad_mix, step_size,
        mixed, hist, tile,
    )
    grad_x, grad_conv, grad_bias, grad_scan_w, tokens_grad, grad_gain_first = mixer_back(
        grad_proj, scan_full, grad_u, x_inner, conv_full, bias_full, grad_gate, in_t, u_act,
        tokens[0], gain_first, grad_mid, tile,
    )

    grad_in = jnp.concatenate([grad_x, grad_gate], 1)
    grad_in_parts = exchange(grad_in.reshape(rows, devices, 2 * part).transpose(1, 0, 2))
    normed_all = gather(normed_low)
    grad_in_w = contract_rows(normed_all, grad_in_parts.reshape(devices * rows, 2 * part))
    gated_parts = exchange(gated.reshape(rows, devices, part).transpose(1, 0, 2))
    grad_mix_all = gather(grad_mix)
    grad_out_w = contract_rows(gated_parts.reshape(devices * rows, part), grad_mix_all)

    grad_columns = jnp.concatenate(
        [grad_step_w, grad_log, grad_conv, grad_bias, grad_dbias, grad_skip], 0
    ).astype(BF16)
    count = grad_columns.shape[0]
    grad_columns = grad_columns.reshape(count, devices, part).transpose(1, 0, 2)
    grad_widths = jnp.concatenate([grad_gain_first.T, grad_gain_second.T, grad_router], 1)
    grad_small = jnp.concatenate(
        [
            grad_columns.reshape(devices, -1),
            grad_scan_w.astype(BF16).reshape(devices, -1),
            grad_widths.astype(BF16).reshape(devices, -1),
        ],
        1,
    )
    grad_small = jnp.sum(exchange(grad_small).astype(F32), 0)
    flat = jnp.concatenate(
        [grad_in_w.astype(BF16).reshape(-1), grad_out_w.astype(BF16).reshape(-1), grad_small.astype(BF16)]
    )
    flat = lax.psum(flat, "dp").astype(F32)
    grad_up, grad_down = expert_grads(everyone, up, down, min(256, up.shape[1]))

    in_size = in_weight.size
    out_size = in_size + out_weight.size
    in_total = flat[:in_size].reshape(in_weight.shape)
    out_total = flat[in_size:out_size].reshape(out_weight.shape)
    tail = flat[out_size:]
    columns_total = tail[:first].reshape(by_column.shape)
    scan_total = tail[first:second].reshape(scan_weight.shape)
    widths_total = tail[second:].reshape(slice_w, experts + 2)
    return (
        layer_out[None],
        tokens_grad[None],
        widths_total[:, 0],
        in_total,
        columns_total[rank + state : rank + state + taps],
        columns_total[rank + state + taps],
        scan_total,
        columns_total[:rank],
        columns_total[rank + state + taps + 1],
        columns_total[rank : rank + state].T,
        columns_total[rank + state + taps + 2],
        out_total,
        widths_total[:, 1],
        widths_total[:, 2:],
        grad_up[None],
        grad_down[None],
    )


def solution(mesh):
    in_specs = (
        P(("dp", "expert"), None, None),
        P(("dp", "expert")),
        P(("dp", "expert"), None),
        P(("dp", "expert"), None),
        P("expert"),
        P(None, "expert"),
        P(None, "expert"),
        P("expert"),
        P("expert", None),
        P(None, "expert"),
        P("expert"),
        P("expert", None),
        P("expert"),
        P("expert", None),
        P("expert"),
        P("expert", None),
        P("expert", None, None),
        P("expert", None, None),
        P(("dp", "expert"), None, None),
    )
    out_specs = (
        P(("dp", "expert"), None, None),
        P(("dp", "expert"), None, None),
        P("expert"),
        P(None, "expert"),
        P(None, "expert"),
        P("expert"),
        P("expert", None),
        P(None, "expert"),
        P("expert"),
        P("expert", None),
        P("expert"),
        P("expert", None),
        P("expert"),
        P("expert", None),
        P("expert", None, None),
        P("expert", None, None),
    )
    return jax.shard_map(shards, mesh=mesh, in_specs=in_specs, out_specs=out_specs, check_vma=False)
```

```python
from functools import partial

import jax
import jax.numpy as jnp
from jax import lax
from jax.experimental import pallas as pl
from jax.experimental.pallas import tpu as pltpu
from jax.sharding import PartitionSpec as P

CAP = 64
BLOCK = 16
LOG2E = 1.4426950408889634
F32 = jnp.float32
BF16 = jnp.bfloat16
VMEM_LIMIT = 56 * 1024 * 1024


def product(left, right):
    return jnp.dot(left, right, preferred_element_type=F32)


def contract_rows(left, right):
    return lax.dot_general(left, right, (((0,), (0,)), ((), ())), preferred_element_type=F32)


def times_transpose(left, right):
    return lax.dot_general(left, right, (((1,), (1,)), ((), ())), preferred_element_type=F32)


def exact_product(left, right):
    return jnp.dot(left, right, preferred_element_type=F32, precision=lax.Precision.HIGHEST)


def iota(shape, axis):
    return lax.broadcasted_iota(jnp.int32, shape, axis)


def sigmoid(values):
    return 1.0 / (1.0 + jnp.exp(-values))


def softplus(values):
    return jnp.maximum(values, 0.0) + jnp.log1p(jnp.exp(-jnp.abs(values)))


def split_lanes(out_ref, value):
    parts, _, width = out_ref.shape
    for part in range(parts):
        out_ref[part] = value[:, part * width : (part + 1) * width]


def shift_rows(values, offset):
    rows = values.shape[0]
    if offset == 0:
        return values
    rolled = pltpu.roll(values, offset % rows, 0)
    row = iota(values.shape, 0)
    keep = row >= offset if offset > 0 else row < rows + offset
    return jnp.where(keep, rolled, 0.0)


def two_parts(values):
    high = values.astype(BF16)
    low = (values - high.astype(F32)).astype(BF16)
    return high, low


def spread_rows(proj_block, first, state):
    rows, width = proj_block.shape
    big = rows * state
    pick = (iota((big, rows), 0) // state == iota((big, rows), 1)).astype(F32)
    copied = exact_product(pick, proj_block)
    lane = iota((big, width), 1)
    own = lane == first + iota((big, width), 0) % state
    column = jnp.sum(jnp.where(own, copied, 0.0), axis=1, keepdims=True)
    return jnp.broadcast_to(column, (big, 128))


def diagonal_blocks(proj_block, first, state):
    rows, width = proj_block.shape
    big = rows * state
    place = (iota((width, big), 0) == first + iota((width, big), 1) % state).astype(BF16)
    own = iota((rows, big), 0) == iota((rows, big), 1) // state
    parts = [
        jnp.where(own, product(part, place), 0.0).astype(BF16) for part in two_parts(proj_block)
    ]
    return jnp.concatenate(parts, 0)


def front_kernel(
    tokens_ref, gain_ref, wx_ref, wg_ref, conv_ref, bias_ref, scanw_ref,
    normed_ref, xin_ref, u_ref, gate_ref, proj_ref,
):
    step = pl.program_id(0)

    @pl.when(step == 0)
    def _():
        values = tokens_ref[...].astype(F32)
        scale = lax.rsqrt(jnp.mean(values * values, -1, keepdims=True) + 1e-05)
        normed_ref[...] = (values * scale * gain_ref[...]).astype(BF16)
        proj_ref[...] = jnp.zeros_like(proj_ref)

    normed = normed_ref[...]
    x_inner = times_transpose(normed, wx_ref[...])
    gate_ref[...] = times_transpose(normed, wg_ref[...])
    xin_ref[...] = x_inner
    taps = conv_ref.shape[0]
    summed = bias_ref[...] + conv_ref[taps - 1 : taps, :] * x_inner
    for back in range(1, taps):
        tap = taps - 1 - back
        summed = summed + conv_ref[tap : tap + 1, :] * shift_rows(x_inner, back)
    u_act = summed * sigmoid(summed)
    u_ref[...] = u_act
    proj_ref[...] += product(u_act.astype(BF16), scanw_ref[...])


def front(tokens, gain, in_t, conv, bias, scan_w, tile):
    rows, width = tokens.shape
    channels = scan_w.shape[0]
    cols = scan_w.shape[1]
    steps = channels // tile
    return pl.pallas_call(
        front_kernel,
        grid=(steps,),
        in_specs=[
            pl.BlockSpec((rows, width), lambda i: (0, 0)),
            pl.BlockSpec((1, width), lambda i: (0, 0)),
            pl.BlockSpec((tile, width), lambda i: (i, 0)),
            pl.BlockSpec((tile, width), lambda i: (i + steps, 0)),
            pl.BlockSpec((conv.shape[0], tile), lambda i: (0, i)),
            pl.BlockSpec((1, tile), lambda i: (0, i)),
            pl.BlockSpec((tile, cols), lambda i: (i, 0)),
        ],
        out_specs=[
            pl.BlockSpec((rows, width), lambda i: (0, 0)),
            pl.BlockSpec((rows, tile), lambda i: (0, i)),
            pl.BlockSpec((rows, tile), lambda i: (0, i)),
            pl.BlockSpec((rows, tile), lambda i: (0, i)),
            pl.BlockSpec((rows, cols), lambda i: (0, 0)),
        ],
        out_shape=[
            jax.ShapeDtypeStruct((rows, width), BF16),
            jax.ShapeDtypeStruct((rows, channels), F32),
            jax.ShapeDtypeStruct((rows, channels), F32),
            jax.ShapeDtypeStruct((rows, channels), F32),
            jax.ShapeDtypeStruct((rows, cols), F32),
        ],
        compiler_params=pltpu.CompilerParams(vmem_limit_bytes=VMEM_LIMIT),
        name="mixer_front",
    )(tokens, gain, in_t, in_t, conv, bias, scan_w)


def scan_prepare(proj_ref, b_wide, c_blocks, b_first, c_first, state):
    blocks = proj_ref.shape[0] // BLOCK
    big = BLOCK * state

    def build(block, carry):
        part = proj_ref[pl.ds(pl.multiple_of(block * BLOCK, BLOCK), BLOCK), :]
        b_wide[pl.ds(pl.multiple_of(block * big, big), big), :] = spread_rows(part, b_first, state)
        c_blocks[pl.ds(pl.multiple_of(block * 2 * BLOCK, 2 * BLOCK), 2 * BLOCK), :] = (
            diagonal_blocks(part, c_first, state)
        )
        return carry

    lax.fori_loop(0, blocks, build, 0)


def scan_tile(
    proj_ref, stepw_ref, dbias_ref, decay_ref, skip_ref, u_ref, gate_ref, step_ref, mixed_ref,
    hist_ref, b_wide, c_blocks, du, scanned, between,
):
    rank, state = stepw_ref.shape[0], decay_ref.shape[0]
    rows, tile = u_ref.shape
    blocks = rows // BLOCK
    big = BLOCK * state
    u_act = u_ref[...]
    step_size = softplus(
        product(proj_ref[:, :rank].astype(BF16), stepw_ref[...]) + dbias_ref[...]
    )
    step_ref[...] = step_size
    du[...] = step_size * u_act
    decay = decay_ref[...] * LOG2E
    hist_ref[0:state, :] = jnp.zeros((state, tile), BF16)

    def run_block(block, held):
        base = pl.multiple_of(block * BLOCK, BLOCK)
        steps_now = step_ref[pl.ds(base, BLOCK), :]
        du_now = du[pl.ds(base, BLOCK), :]
        wide_base = pl.multiple_of(block * big, big)
        for t in range(BLOCK):
            b_now = b_wide[pl.ds(wide_base + t * state, state), :]
            fade = jnp.exp2(steps_now[t : t + 1, :] * decay)
            fresh = du_now[t : t + 1, :] * jnp.concatenate([b_now] * (tile // 128), 1)
            held = fade * held + fresh
            hist_ref[pl.ds(wide_base + (t + 1) * state, state), :] = held.astype(BF16)
        weights = c_blocks[pl.ds(pl.multiple_of(block * 2 * BLOCK, 2 * BLOCK), 2 * BLOCK), :]
        both = product(weights, hist_ref[pl.ds(wide_base + state, big), :])
        scanned[pl.ds(base, BLOCK), :] = both[:BLOCK] + both[BLOCK:]
        return held

    held = jnp.zeros((state, tile), F32)
    held = lax.fori_loop(0, blocks // 2, run_block, held)
    between(0)
    lax.fori_loop(blocks // 2, blocks, run_block, held)
    between(1)
    mixed = scanned[...] + skip_ref[...] * u_act
    mixed_ref[...] = mixed
    gate_in = gate_ref[...]
    return (mixed * (gate_in * sigmoid(gate_in))).astype(BF16)


def scan_kernel(
    proj_ref, stepw_ref, dbias_ref, decay_ref, skip_ref, u_ref, gate_ref, outw_ref, tokens_ref,
    step_ref, mixed_ref, gated_ref, hist_ref, mid_ref,
    b_wide, c_blocks, du, scanned,
):
    rank, state = stepw_ref.shape[0], decay_ref.shape[0]

    @pl.when(pl.program_id(0) == 0)
    def _():
        mid_ref[...] = tokens_ref[...].astype(F32)
        scan_prepare(proj_ref, b_wide, c_blocks, rank, rank + state, state)

    gated = scan_tile(
        proj_ref, stepw_ref, dbias_ref, decay_ref, skip_ref, u_ref, gate_ref, step_ref, mixed_ref,
        hist_ref, b_wide, c_blocks, du, scanned, lambda half: None,
    )
    gated_ref[...] = gated
    mid_ref[...] += product(gated, outw_ref[...])


def scan_forward(proj, step_w, dbias, decay, skip, u_act, gate_in, out_w, tokens, tile):
    rows, channels = u_act.shape
    width = tokens.shape[1]
    cols = proj.shape[1]
    rank, state = step_w.shape[0], decay.shape[0]
    steps = channels // tile
    hist_rows = (rows + 1) * state
    column = lambda i: (0, i)
    fixed = lambda i: (0, 0)
    return pl.pallas_call(
        scan_kernel,
        grid=(steps,),
        in_specs=[
            pl.BlockSpec((rows, cols), fixed),
            pl.BlockSpec((rank, tile), column),
            pl.BlockSpec((1, tile), column),
            pl.BlockSpec((state, tile), column),
            pl.BlockSpec((1, tile), column),
            pl.BlockSpec((rows, tile), column),
            pl.BlockSpec((rows, tile), column),
            pl.BlockSpec((tile, width), lambda i: (i, 0)),
            pl.BlockSpec((rows, width), fixed),
        ],
        out_specs=[
            pl.BlockSpec((rows, tile), column),
            pl.BlockSpec((rows, tile), column),
            pl.BlockSpec((rows, tile), column),
            pl.BlockSpec((hist_rows, tile), column),
            pl.BlockSpec((rows, width), fixed),
        ],
        out_shape=[
            jax.ShapeDtypeStruct((rows, channels), F32),
            jax.ShapeDtypeStruct((rows, channels), F32),
            jax.ShapeDtypeStruct((rows, channels), BF16),
            jax.ShapeDtypeStruct((hist_rows, channels), BF16),
            jax.ShapeDtypeStruct((rows, width), F32),
        ],
        scratch_shapes=[
            pltpu.VMEM((rows * state, 128), F32),
            pltpu.VMEM((rows * 2, BLOCK * state), BF16),
            pltpu.VMEM((rows, tile), F32),
            pltpu.VMEM((rows, tile), F32),
        ],
        compiler_params=pltpu.CompilerParams(vmem_limit_bytes=VMEM_LIMIT),
        name="scan_forward",
    )(proj, step_w, dbias, decay, skip, u_act, gate_in, out_w, tokens)


def scan_back_kernel(*refs, between=lambda half: None):
    scan_back_tile(between, *refs)


def scan_back_tile(
    between, proj_ref, stepw_ref, dbias_ref, decay_ref, skip_ref, u_ref, gate_ref, outw_ref, gradmix_ref,
    step_ref, mixed_ref, hist_ref,
    gradu_ref, gradgate_ref, pack_ref, gradproj_ref,
    c_wide, b_blocks, b_sums, c_sums, gy, du, g_hist, w_hist, grad_du, grad_step,
):
    tile_id = pl.program_id(0)
    cols, rank = proj_ref.shape[1], stepw_ref.shape[0]
    state = decay_ref.shape[0]
    rows, tile = u_ref.shape
    blocks = rows // BLOCK
    big = BLOCK * state

    @pl.when(tile_id == 0)
    def _():
        gradproj_ref[...] = jnp.zeros_like(gradproj_ref)
        b_sums[...] = jnp.zeros_like(b_sums)
        c_sums[...] = jnp.zeros_like(c_sums)
        scan_prepare(proj_ref, c_wide, b_blocks, rank + state, rank, state)

    grad_gated = times_transpose(gradmix_ref[...], outw_ref[...])
    gate_in = gate_ref[...]
    gate_sig = sigmoid(gate_in)
    grad_mixed = grad_gated * (gate_in * gate_sig)
    split_lanes(
        gradgate_ref,
        (grad_gated * mixed_ref[...] * (gate_sig * (1.0 + gate_in * (1.0 - gate_sig)))).astype(BF16),
    )
    u_act = u_ref[...]
    step_size = step_ref[...]
    gy[...] = grad_mixed
    du[...] = step_size * u_act
    grad_skip = jnp.sum(grad_mixed * u_act, 0, keepdims=True)
    rate = decay_ref[...]
    decay = rate * LOG2E
    sums = (iota((BLOCK, big), 0) == iota((BLOCK, big), 1) // state).astype(BF16)

    def run_block(turn, carry):
        carried, log_sum = carry
        block = blocks - 1 - turn
        base = pl.multiple_of(block * BLOCK, BLOCK)
        wide_base = pl.multiple_of(block * big, big)
        steps_now = step_ref[pl.ds(base, BLOCK), :]
        gy_now = gy[pl.ds(base, BLOCK), :]
        for t in range(BLOCK - 1, -1, -1):
            c_now = c_wide[pl.ds(wide_base + t * state, state), :]
            step_now = steps_now[t : t + 1, :]
            fade = jnp.exp2(step_now * decay)
            grad = gy_now[t : t + 1, :] * jnp.concatenate([c_now] * (tile // 128), 1) + carried
            g_hist[t * state : (t + 1) * state, :] = grad.astype(BF16)
            carried = fade * grad
            before = hist_ref[pl.ds(wide_base + t * state, state), :].astype(F32)
            weighted = carried * before * rate
            w_hist[t * state : (t + 1) * state, :] = weighted.astype(BF16)
            log_sum = log_sum + weighted * step_now
        grads = g_hist[...]
        both = product(
            b_blocks[pl.ds(pl.multiple_of(block * 2 * BLOCK, 2 * BLOCK), 2 * BLOCK), :], grads
        )
        grad_du[pl.ds(base, BLOCK), :] = both[:BLOCK] + both[BLOCK:]
        grad_step[pl.ds(base, BLOCK), :] = product(sums, w_hist[...])
        b_sums[pl.ds(base, BLOCK), :] += times_transpose(
            du[pl.ds(base, BLOCK), :].astype(BF16), grads
        )
        c_sums[pl.ds(base, BLOCK), :] += times_transpose(
            gy_now.astype(BF16), hist_ref[pl.ds(wide_base + state, big), :]
        )
        return carried, log_sum

    zeros = jnp.zeros((state, tile), F32)
    held = lax.fori_loop(0, blocks // 2, run_block, (zeros, zeros))
    between(0)
    _, log_sum = lax.fori_loop(blocks // 2, blocks, run_block, held)
    between(1)
    full_du = grad_du[...]
    gradu_ref[...] = full_du * step_size + skip_ref[...] * gy[...]
    grad_size = grad_step[...] + full_du * u_act
    grad_pre = grad_size * (1.0 - jnp.exp(-step_size))
    grad_low = grad_pre.astype(BF16)
    grad_step_w = contract_rows(proj_ref[:, :rank].astype(BF16), grad_low)
    packed = jnp.concatenate(
        [grad_step_w, log_sum, jnp.sum(grad_pre, 0, keepdims=True), grad_skip, zeros[:6]], 0
    )
    split_lanes(pack_ref, packed.astype(BF16))
    gradproj_ref[:, :rank] += times_transpose(grad_low, stepw_ref[...])

    @pl.when(tile_id == pl.num_programs(0) - 1)
    def _():
        own = iota((rows, big), 0) % BLOCK == iota((rows, big), 1) // state
        lane = iota((big, cols), 1)
        slot = iota((big, cols), 0) % state
        total = gradproj_ref[...]
        for sums_ref, first in ((b_sums, rank), (c_sums, rank + state)):
            place = (lane == first + slot).astype(F32)
            total = total + exact_product(jnp.where(own, sums_ref[...], 0.0), place)
        gradproj_ref[...] = total


def scan_backward(
    proj, step_w, dbias, decay, skip, u_act, gate_in, out_w, grad_mix, step_size, mixed, hist, tile,
    devices,
):
    rows, channels = u_act.shape
    gate_parts = tile * devices // (2 * channels)
    pack_parts = tile * devices // channels
    pack_rows = step_w.shape[0] + decay.shape[0] + 8
    width = grad_mix.shape[1]
    cols = proj.shape[1]
    rank, state = step_w.shape[0], decay.shape[0]
    steps = channels // tile
    big = BLOCK * state
    column = lambda i: (0, i)
    fixed = lambda i: (0, 0)
    return pl.pallas_call(
        scan_back_kernel,
        grid=(steps,),
        in_specs=[
            pl.BlockSpec((rows, cols), fixed),
            pl.BlockSpec((rank, tile), column),
            pl.BlockSpec((1, tile), column),
            pl.BlockSpec((state, tile), column),
            pl.BlockSpec((1, tile), column),
            pl.BlockSpec((rows, tile), column),
            pl.BlockSpec((rows, tile), column),
            pl.BlockSpec((tile, width), lambda i: (i, 0)),
            pl.BlockSpec((rows, width), fixed),
            pl.BlockSpec((rows, tile), column),
            pl.BlockSpec((rows, tile), column),
            pl.BlockSpec((hist.shape[0], tile), column),
        ],
        out_specs=[
            pl.BlockSpec((rows, tile), column),
            pl.BlockSpec((gate_parts, rows, tile // gate_parts), lambda i: (i, 0, 0)),
            pl.BlockSpec((pack_parts, pack_rows, tile // pack_parts), lambda i: (i, 0, 0)),
            pl.BlockSpec((rows, cols), fixed),
        ],
        out_shape=[
            jax.ShapeDtypeStruct((rows, channels), F32),
            jax.ShapeDtypeStruct((devices // 2, rows, 2 * channels // devices), BF16),
            jax.ShapeDtypeStruct((devices, pack_rows, channels // devices), BF16),
            jax.ShapeDtypeStruct((rows, cols), F32),
        ],
        scratch_shapes=[
            pltpu.VMEM((rows * state, 128), F32),
            pltpu.VMEM((rows * 2, big), BF16),
            pltpu.VMEM((rows, big), F32),
            pltpu.VMEM((rows, big), F32),
            pltpu.VMEM((rows, tile), F32),
            pltpu.VMEM((rows, tile), F32),
            pltpu.VMEM((big, tile), BF16),
            pltpu.VMEM((big, tile), BF16),
            pltpu.VMEM((rows, tile), F32),
            pltpu.VMEM((rows, tile), F32),
        ],
        compiler_params=pltpu.CompilerParams(vmem_limit_bytes=VMEM_LIMIT),
        name="scan_backward",
    )(proj, step_w, dbias, decay, skip, u_act, gate_in, out_w, grad_mix, step_size, mixed, hist)


def back_kernel(
    gradproj_ref, scanw_ref, gradu_ref, xin_ref, conv_ref, bias_ref, gradgate_ref, wx_ref, wg_ref,
    u_ref, tokens_ref, gain_ref, gradmid_ref, widths_ref,
    gradx_ref, pack_ref, tail_ref, gradtok_ref,
    total,
):
    tile_id = pl.program_id(0)

    @pl.when(tile_id == 0)
    def _():
        total[...] = jnp.zeros_like(total)

    grad_proj = gradproj_ref[...].astype(BF16)
    grad_u = gradu_ref[...] + times_transpose(grad_proj, scanw_ref[...])
    pieces = [contract_rows(grad_proj, u_ref[...].astype(BF16))]
    x_inner = xin_ref[...]
    taps = conv_ref.shape[0]
    shifted = [shift_rows(x_inner, taps - 1 - tap) for tap in range(taps)]
    summed = bias_ref[...]
    for tap in range(taps):
        summed = summed + conv_ref[tap : tap + 1, :] * shifted[tap]
    sig = sigmoid(summed)
    grad_sum = grad_u * (sig * (1.0 + summed * (1.0 - sig)))
    grad_x = jnp.zeros_like(x_inner)
    for tap in range(taps):
        pieces.append(jnp.sum(grad_sum * shifted[tap], 0, keepdims=True))
        grad_x = grad_x + conv_ref[tap : tap + 1, :] * shift_rows(grad_sum, tap + 1 - taps)
    pieces.append(jnp.sum(grad_sum, 0, keepdims=True))
    pieces.append(jnp.zeros((pack_ref.shape[1] - grad_proj.shape[1] - taps - 1, x_inner.shape[1]), F32))
    split_lanes(pack_ref, jnp.concatenate(pieces, 0).astype(BF16))
    grad_x = grad_x.astype(BF16)
    split_lanes(gradx_ref, grad_x)
    grad_gate = jnp.concatenate([gradgate_ref[k] for k in range(gradgate_ref.shape[0])], 1)
    total[...] += product(grad_x, wx_ref[...]) + product(grad_gate, wg_ref[...])

    @pl.when(tile_id == pl.num_programs(0) - 1)
    def _():
        values = tokens_ref[...].astype(F32)
        scale = lax.rsqrt(jnp.mean(values * values, -1, keepdims=True) + 1e-05)
        unit = values * scale
        grad = total[...]
        widths = jnp.concatenate([widths_ref[...], jnp.sum(grad * unit, 0, keepdims=True)], 0)
        widths = jnp.concatenate(
            [widths, jnp.zeros((tail_ref.shape[1] - widths.shape[0], widths.shape[1]), F32)], 0
        )
        split_lanes(tail_ref, widths.astype(BF16))
        inner = grad * gain_ref[...]
        gradtok_ref[...] = gradmid_ref[...] + scale * (
            inner - unit * jnp.mean(inner * unit, -1, keepdims=True)
        )


def mixer_back(
    grad_proj, scan_w, grad_u, x_inner, conv, bias, grad_gate, in_t, u_act, tokens, gain, grad_mid,
    grad_widths, tile, devices,
):
    rows, channels = u_act.shape
    gate_parts = tile * devices // (2 * channels)
    pack_parts = tile * devices // channels
    pack_rows = scan_w.shape[1] + 8
    tail_rows = grad_widths.shape[0] + 7
    width = tokens.shape[1]
    cols = scan_w.shape[1]
    taps = conv.shape[0]
    steps = channels // tile
    column = lambda i: (0, i)
    fixed = lambda i: (0, 0)
    return pl.pallas_call(
        back_kernel,
        grid=(steps,),
        in_specs=[
            pl.BlockSpec((rows, cols), fixed),
            pl.BlockSpec((tile, cols), lambda i: (i, 0)),
            pl.BlockSpec((rows, tile), column),
            pl.BlockSpec((rows, tile), column),
            pl.BlockSpec((taps, tile), column),
            pl.BlockSpec((1, tile), column),
            pl.BlockSpec((gate_parts, rows, tile // gate_parts), lambda i: (i, 0, 0)),
            pl.BlockSpec((tile, width), lambda i: (i, 0)),
            pl.BlockSpec((tile, width), lambda i: (i + steps, 0)),
            pl.BlockSpec((rows, tile), column),
            pl.BlockSpec((rows, width), fixed),
            pl.BlockSpec((1, width), fixed),
            pl.BlockSpec((rows, width), fixed),
            pl.BlockSpec(grad_widths.shape, fixed),
        ],
        out_specs=[
            pl.BlockSpec((gate_parts, rows, tile // gate_parts), lambda i: (i, 0, 0)),
            pl.BlockSpec((pack_parts, pack_rows, tile // pack_parts), lambda i: (i, 0, 0)),
            pl.BlockSpec((devices, tail_rows, width // devices), lambda i: (0, 0, 0)),
            pl.BlockSpec((rows, width), fixed),
        ],
        out_shape=[
            jax.ShapeDtypeStruct((devices // 2, rows, 2 * channels // devices), BF16),
            jax.ShapeDtypeStruct((devices, pack_rows, channels // devices), BF16),
            jax.ShapeDtypeStruct((devices, tail_rows, width // devices), BF16),
            jax.ShapeDtypeStruct((rows, width), F32),
        ],
        scratch_shapes=[pltpu.VMEM((rows, width), F32)],
        compiler_params=pltpu.CompilerParams(vmem_limit_bytes=VMEM_LIMIT),
        name="mixer_back",
    )(
        grad_proj, scan_w, grad_u, x_inner, conv, bias, grad_gate, in_t, in_t, u_act, tokens, gain,
        grad_mid, grad_widths,
    )


def gelu_parts(values):
    weight = jnp.exp(values * values * -0.5)
    scaled = jnp.abs(values) * 0.7071067811865476
    ratio = 1.0 / (1.0 + 0.3275911 * scaled)
    series = 1.061405429 * ratio - 1.453152027
    series = series * ratio + 1.421413741
    series = series * ratio - 0.284496736
    series = series * ratio + 0.254829592
    tail = (0.5 * ratio) * series * weight
    below = jnp.where(values >= 0.0, 1.0 - tail, tail)
    return values * below, below + values * weight * 0.3989422804014327


def router_kernel(
    mid_ref, gain_ref, router_ref, routes_col_ref, routes_row_ref, slots_row_ref, live_ref, cot_ref,
    sendr_ref, sendg_ref, normed_ref, probs_ref,
):
    mid = mid_ref[...]
    rows = mid.shape[0]
    experts = router_ref.shape[1]
    scale = lax.rsqrt(jnp.mean(mid * mid, -1, keepdims=True) + 1e-05)
    normed = (mid * scale * gain_ref[...]).astype(BF16)
    normed_ref[...] = normed
    logits = product(normed, router_ref[...])
    weights = jnp.exp(logits - jnp.max(logits, -1, keepdims=True))
    probs = weights / jnp.sum(weights, -1, keepdims=True)
    probs_ref[...] = probs
    chosen = (routes_col_ref[...] == iota((rows, experts), 1)).astype(F32)
    gate = jnp.sum(probs * chosen, 1, keepdims=True)
    grads = (gate * (cot_ref[...].astype(F32) * live_ref[...])).astype(BF16)
    slot = iota((experts * CAP, rows), 0)
    dispatch = (
        (routes_row_ref[...] == slot // CAP) & (slots_row_ref[...] == slot % CAP)
    ).astype(BF16)
    width = mid.shape[1]
    sendr_ref[...] = product(dispatch, normed).astype(BF16).reshape(experts, CAP, width)
    sendg_ref[...] = product(dispatch, grads).astype(BF16).reshape(experts, CAP, width)


def router_step(mid, gain, router, routes_col, routes_row, slots_row, live, cotangent):
    rows, width = mid.shape
    experts = router.shape[1]
    return pl.pallas_call(
        router_kernel,
        out_shape=[
            jax.ShapeDtypeStruct((experts, CAP, width), BF16),
            jax.ShapeDtypeStruct((experts, CAP, width), BF16),
            jax.ShapeDtypeStruct((rows, width), BF16),
            jax.ShapeDtypeStruct((rows, experts), F32),
        ],
        compiler_params=pltpu.CompilerParams(vmem_limit_bytes=VMEM_LIMIT),
        name="router_step",
    )(mid, gain, router, routes_col, routes_row, slots_row, live, cotangent)


def expert_out_kernel(rows_ref, up_ref, down_ref, out_ref, slope_ref, total):
    step = pl.program_id(0)
    pieces, cap, width = rows_ref.shape
    rows = rows_ref[...].reshape(pieces * cap, width)

    @pl.when(step == 0)
    def _():
        total[...] = jnp.zeros_like(total)

    activated, slope = gelu_parts(product(rows, up_ref[...]))
    slope_ref[...] = slope.astype(BF16)
    total[...] += product(activated.astype(BF16), down_ref[...])

    @pl.when(step == pl.num_programs(0) - 1)
    def _():
        out_ref[...] = total[...].astype(BF16).reshape(pieces, cap, width)


def expert_out(rows, up, down, tile):
    pieces, cap, width = rows.shape
    hidden = up.shape[1]
    fixed = lambda i: (0, 0, 0)
    return pl.pallas_call(
        expert_out_kernel,
        grid=(hidden // tile,),
        in_specs=[
            pl.BlockSpec(rows.shape, fixed),
            pl.BlockSpec((width, tile), lambda i: (0, i)),
            pl.BlockSpec((tile, width), lambda i: (i, 0)),
        ],
        out_specs=[
            pl.BlockSpec(rows.shape, fixed),
            pl.BlockSpec((pieces * cap, tile), lambda i: (0, i)),
        ],
        out_shape=[
            jax.ShapeDtypeStruct(rows.shape, BF16),
            jax.ShapeDtypeStruct((pieces * cap, hidden), BF16),
        ],
        scratch_shapes=[pltpu.VMEM((pieces * cap, width), F32)],
        compiler_params=pltpu.CompilerParams(vmem_limit_bytes=VMEM_LIMIT),
        name="expert_out",
    )(rows, up, down)


def expert_back_kernel(grads_ref, up_ref, down_ref, slope_ref, out_ref, total):
    step = pl.program_id(0)
    pieces, cap, width = grads_ref.shape
    grads = grads_ref[...].reshape(pieces * cap, width)

    @pl.when(step == 0)
    def _():
        total[...] = jnp.zeros_like(total)

    slope = slope_ref[...].astype(F32)
    grad_pre = (times_transpose(grads, down_ref[...]) * slope).astype(BF16)
    total[...] += times_transpose(grad_pre, up_ref[...])

    @pl.when(step == pl.num_programs(0) - 1)
    def _():
        out_ref[...] = total[...].astype(BF16).reshape(pieces, cap, width)


def expert_back(grads, up, down, slope, tile):
    pieces, cap, width = grads.shape
    hidden = up.shape[1]
    fixed = lambda i: (0, 0, 0)
    return pl.pallas_call(
        expert_back_kernel,
        grid=(hidden // tile,),
        in_specs=[
            pl.BlockSpec(grads.shape, fixed),
            pl.BlockSpec((width, tile), lambda i: (0, i)),
            pl.BlockSpec((tile, width), lambda i: (i, 0)),
            pl.BlockSpec((pieces * cap, tile), lambda i: (0, i)),
        ],
        out_specs=pl.BlockSpec(grads.shape, fixed),
        out_shape=jax.ShapeDtypeStruct(grads.shape, BF16),
        scratch_shapes=[pltpu.VMEM((pieces * cap, width), F32)],
        compiler_params=pltpu.CompilerParams(vmem_limit_bytes=VMEM_LIMIT),
        name="expert_back",
    )(grads, up, down, slope)


def expert_grads_kernel(chunks, rows_ref, grads_ref, up_ref, down_ref, gup_ref, gdown_ref, rows_t):
    chunk = pl.program_id(1)
    groups, pieces, cap, width = rows_ref.shape
    count = groups * pieces * cap
    rows = rows_ref[...].reshape(count, width)
    grads = grads_ref[...].reshape(count, width)

    @pl.when((pl.program_id(0) == 0) | (chunks > 1))
    def _():
        rows_t[...] = rows.T

    activated, slope = gelu_parts(product(rows, up_ref[...]))
    grad_pre = (times_transpose(grads, down_ref[...]) * slope).astype(BF16)
    grad_up = product(rows_t[...], grad_pre)
    grad_down = contract_rows(activated.astype(BF16), grads)

    @pl.when(chunk == 0)
    def _():
        gup_ref[...] = grad_up
        gdown_ref[...] = grad_down

    if chunks > 1:

        @pl.when(chunk > 0)
        def _():
            gup_ref[...] += grad_up
            gdown_ref[...] += grad_down


def expert_grads(rows, grads, up, down, tile):
    groups, pieces, cap, width = rows.shape
    hidden = up.shape[1]
    together = max(1, min(groups, 32 // pieces))
    chunks = groups // together
    some = pl.BlockSpec((together, pieces, cap, width), lambda i, j: (j, 0, 0, 0))
    return pl.pallas_call(
        partial(expert_grads_kernel, chunks),
        grid=(hidden // tile, chunks),
        in_specs=[
            some,
            some,
            pl.BlockSpec((width, tile), lambda i, j: (0, i)),
            pl.BlockSpec((tile, width), lambda i, j: (i, 0)),
        ],
        out_specs=[
            pl.BlockSpec((width, tile), lambda i, j: (0, i)),
            pl.BlockSpec((tile, width), lambda i, j: (i, 0)),
        ],
        out_shape=[
            jax.ShapeDtypeStruct((width, hidden), F32),
            jax.ShapeDtypeStruct((hidden, width), F32),
        ],
        scratch_shapes=[pltpu.VMEM((width, together * pieces * cap), BF16)],
        compiler_params=pltpu.CompilerParams(vmem_limit_bytes=VMEM_LIMIT),
        name="expert_grads",
    )(rows, grads, up, down)


def combine_kernel(
    mid_ref, gain_ref, router_ref, routes_ref, slots_ref, live_ref, cot_ref, probs_ref, normed_ref,
    backr_ref, backg_ref, out_ref, gradmid_ref, gradmix_ref, widths_ref,
):
    mid = mid_ref[...]
    rows, width = mid.shape
    experts = router_ref.shape[1]
    routes = routes_ref[...]
    chosen = (routes == iota((rows, experts), 1)).astype(F32)
    probs = probs_ref[...]
    gate = jnp.sum(probs * chosen, 1, keepdims=True)
    live = live_ref[...]
    slot = iota((rows, experts * CAP), 1)
    collect = ((routes == slot // CAP) & (slots_ref[...] == slot % CAP)).astype(BF16)
    expert_sum = product(collect, backr_ref[...].reshape(experts * CAP, width))
    out_ref[...] = (live * (mid + gate * expert_sum)).astype(BF16)
    grad_out = cot_ref[...].astype(F32) * live
    grad_gate = jnp.sum(grad_out * expert_sum, 1, keepdims=True)
    grad_logits = (probs * (chosen * grad_gate - gate * grad_gate)).astype(BF16)
    grad_router = contract_rows(grad_logits, normed_ref[...])
    grad = product(collect, backg_ref[...].reshape(experts * CAP, width))
    grad = grad + times_transpose(grad_logits, router_ref[...])
    scale = lax.rsqrt(jnp.mean(mid * mid, -1, keepdims=True) + 1e-05)
    unit = mid * scale
    widths_ref[...] = jnp.concatenate([grad_router, jnp.sum(grad * unit, 0, keepdims=True)], 0)
    inner = grad * gain_ref[...]
    grad_mid = grad_out + scale * (inner - unit * jnp.mean(inner * unit, -1, keepdims=True))
    gradmid_ref[...] = grad_mid
    gradmix_ref[...] = grad_mid.astype(BF16)


def combine_step(mid, gain, router, routes, slots, live, cotangent, probs, normed, backr, backg):
    rows, width = mid.shape
    return pl.pallas_call(
        combine_kernel,
        out_shape=[
            jax.ShapeDtypeStruct((rows, width), BF16),
            jax.ShapeDtypeStruct((rows, width), F32),
            jax.ShapeDtypeStruct((rows, width), BF16),
            jax.ShapeDtypeStruct((router.shape[1] + 1, width), F32),
        ],
        compiler_params=pltpu.CompilerParams(vmem_limit_bytes=VMEM_LIMIT),
        name="combine_step",
    )(mid, gain, router, routes, slots, live, cotangent, probs, normed, backr, backg)


MESH = pl.DeviceIdType.MESH


def neighbour(bit):
    me = lax.axis_index("expert")
    return me + (1 - 2 * ((me // bit) % 2)) * bit


def greet(line=True):
    devices, copies = lax.axis_size("expert"), lax.axis_size("dp")
    me, place = lax.axis_index("expert"), lax.axis_index("dp")
    barrier = pltpu.get_barrier_semaphore()
    for k in range(1, devices):
        pl.semaphore_signal(
            barrier, inc=1, device_id={"expert": (me + k) % devices}, device_id_type=MESH
        )
    if line:

        @pl.when(place < copies - 1)
        def _():
            pl.semaphore_signal(barrier, inc=1, device_id={"dp": place + 1}, device_id_type=MESH)

        @pl.when(place > 0)
        def _():
            pl.semaphore_signal(barrier, inc=1, device_id={"dp": place - 1}, device_id_type=MESH)

    ends = (place == 0) | (place == copies - 1)
    if line:
        pl.when(ends)(lambda: pl.semaphore_wait(barrier, devices))
        pl.when(jnp.logical_not(ends))(lambda: pl.semaphore_wait(barrier, devices + 1))
    else:
        pl.semaphore_wait(barrier, devices - 1)


class Exchange:
    def __init__(self, source, target, send_sems, recv_sems, local_sem):
        devices, me = lax.axis_size("expert"), lax.axis_index("expert")
        self.copies = []
        for k in range(1, devices):
            peer = (me + k) % devices
            self.copies.append(
                pltpu.make_async_remote_copy(
                    source.at[peer], target.at[me], send_sems.at[k], recv_sems.at[k],
                    device_id={"expert": peer}, device_id_type=MESH,
                )
            )
        self.local = pltpu.make_async_copy(source.at[me], target.at[me], local_sem)

    def start(self):
        for copy in self.copies:
            copy.start()
        self.local.start()

    def wait(self):
        self.local.wait()
        for copy in self.copies:
            copy.wait()


class Line:
    def __init__(self, stage, from_left, from_right, next_left, next_right, send_sems, recv_sems):
        place = lax.axis_index("dp")
        last = lax.axis_size("dp") - 1
        self.right = pltpu.make_async_remote_copy(
            from_left, next_left, send_sems.at[0], recv_sems.at[0],
            device_id={"dp": jnp.minimum(place + 1, last)}, device_id_type=MESH,
        )
        self.left = pltpu.make_async_remote_copy(
            from_right, next_right, send_sems.at[1], recv_sems.at[1],
            device_id={"dp": jnp.maximum(place - 1, 0)}, device_id_type=MESH,
        )
        self.send_right = (place >= stage - 1) & (place < last)
        self.send_left = (last - place >= stage - 1) & (place > 0)
        self.get_left = place >= stage
        self.get_right = last - place >= stage

    def start(self):
        pl.when(self.send_right)(lambda: self.right.start())
        pl.when(self.send_left)(lambda: self.left.start())

    def wait(self):
        pl.when(self.send_right)(lambda: self.right.wait_send())
        pl.when(self.send_left)(lambda: self.left.wait_send())
        pl.when(self.get_left)(lambda: self.right.wait_recv())
        pl.when(self.get_right)(lambda: self.left.wait_recv())


def expert_layer_kernel(
    mid_ref, gain_ref, router_ref, routes_col_ref, routes_row_ref, slots_col_ref, slots_row_ref,
    live_ref, cot_ref, up_hbm, down_hbm,
    out_ref, gradmid_ref, gradmix_ref, widths_ref, rows_out, grads_out, left_rows, right_rows,
    up_ref, down_ref, normed_ref, send_r, send_g, got_r, got_g, slope_ref, total, give_r, give_g,
    back_r, back_g, probs_ref, weight_sems, send_sems, recv_sems, local_sems, line_send, line_recv,
    out_sems,
):
    tile = 512
    rows, width = mid_ref.shape
    experts = router_ref.shape[1]
    hidden = up_ref.shape[1]
    load_up = pltpu.make_async_copy(up_hbm, up_ref, weight_sems.at[0])
    load_down = pltpu.make_async_copy(down_hbm, down_ref, weight_sems.at[1])
    load_up.start()
    load_down.start()
    greet()

    ways = [
        Exchange(source, target, send_sems.at[k], recv_sems.at[k], local_sems.at[k])
        for k, (source, target) in enumerate(
            [(send_r, got_r), (send_g, got_g), (give_r, back_r), (give_g, back_g)]
        )
    ]
    mid = mid_ref[...]
    scale = lax.rsqrt(jnp.mean(mid * mid, -1, keepdims=True) + 1e-05)
    normed = (mid * scale * gain_ref[...]).astype(BF16)
    normed_ref[...] = normed
    slot = iota((experts * CAP, rows), 0)
    dispatch = (
        (routes_row_ref[...] == slot // CAP) & (slots_row_ref[...] == slot % CAP)
    ).astype(BF16)
    send_r[...] = product(dispatch, normed).astype(BF16).reshape(experts, CAP, width)
    ways[0].start()
    logits = product(normed, router_ref[...])
    weights = jnp.exp(logits - jnp.max(logits, -1, keepdims=True))
    probs = weights / jnp.sum(weights, -1, keepdims=True)
    probs_ref[...] = probs
    chosen = (routes_col_ref[...] == iota((rows, experts), 1)).astype(F32)
    gate = jnp.sum(probs * chosen, 1, keepdims=True)
    grads = (gate * (cot_ref[...].astype(F32) * live_ref[...])).astype(BF16)
    send_g[...] = product(dispatch, grads).astype(BF16).reshape(experts, CAP, width)
    ways[1].start()

    load_up.wait()
    load_down.wait()
    ways[0].wait()
    line = Line(1, got_r, got_r, left_rows, right_rows, line_send, line_recv)
    line.start()
    keep_rows = pltpu.make_async_copy(got_r, rows_out, out_sems.at[0])
    keep_rows.start()
    total[...] = jnp.zeros_like(total)

    def forward(step, carry):
        at = pl.ds(pl.multiple_of(step * tile, tile), tile)
        inputs = got_r[...].reshape(experts * CAP, width)
        activated, slope = gelu_parts(product(inputs, up_ref[:, at]))
        slope_ref[:, at] = slope.astype(BF16)
        total[...] += product(activated.astype(BF16), down_ref[at, :])
        return carry

    lax.fori_loop(0, hidden // tile, forward, 0)
    give_r[...] = total[...].astype(BF16).reshape(experts, CAP, width)
    ways[2].start()
    ways[1].wait()
    keep_grads = pltpu.make_async_copy(got_g, grads_out, out_sems.at[1])
    keep_grads.start()
    total[...] = jnp.zeros_like(total)

    def backward(step, carry):
        at = pl.ds(pl.multiple_of(step * tile, tile), tile)
        outputs = got_g[...].reshape(experts * CAP, width)
        slope = slope_ref[:, at].astype(F32)
        grad_pre = (times_transpose(outputs, down_ref[at, :]) * slope).astype(BF16)
        total[...] += times_transpose(grad_pre, up_ref[:, at])
        return carry

    lax.fori_loop(0, hidden // tile, backward, 0)
    give_g[...] = total[...].astype(BF16).reshape(experts, CAP, width)
    ways[3].start()

    routes = routes_col_ref[...]
    chosen = (routes == iota((rows, experts), 1)).astype(F32)
    probs = probs_ref[...]
    gate = jnp.sum(probs * chosen, 1, keepdims=True)
    live = live_ref[...]
    slot = iota((rows, experts * CAP), 1)
    collect = ((routes == slot // CAP) & (slots_col_ref[...] == slot % CAP)).astype(BF16)
    ways[2].wait()
    expert_sum = product(collect, back_r[...].reshape(experts * CAP, width))
    mid = mid_ref[...]
    out_ref[...] = (live * (mid + gate * expert_sum)).astype(BF16)
    grad_out = cot_ref[...].astype(F32) * live
    grad_gate = jnp.sum(grad_out * expert_sum, 1, keepdims=True)
    grad_logits = (probs * (chosen * grad_gate - gate * grad_gate)).astype(BF16)
    grad_router = contract_rows(grad_logits, normed_ref[...])
    from_logits = times_transpose(grad_logits, router_ref[...])
    scale = lax.rsqrt(jnp.mean(mid * mid, -1, keepdims=True) + 1e-05)
    unit = mid * scale
    ways[3].wait()
    grad = product(collect, back_g[...].reshape(experts * CAP, width)) + from_logits
    widths_ref[...] = jnp.concatenate([grad_router, jnp.sum(grad * unit, 0, keepdims=True)], 0)
    inner = grad * gain_ref[...]
    grad_mid = grad_out + scale * (inner - unit * jnp.mean(inner * unit, -1, keepdims=True))
    gradmid_ref[...] = grad_mid
    gradmix_ref[...] = grad_mid.astype(BF16)
    keep_rows.wait()
    keep_grads.wait()
    line.wait()


def expert_layer(
    mid, gain, router, routes_col, routes_row, slots_col, slots_row, live, cotangent, up, down
):
    rows, width = mid.shape
    experts = router.shape[1]
    hidden = up.shape[1]
    buffer = (experts, CAP, width)
    here = pl.BlockSpec(memory_space=pltpu.VMEM)
    far = pl.BlockSpec(memory_space=pl.ANY)
    slots = jax.ShapeDtypeStruct(buffer, BF16)
    dma = pltpu.SemaphoreType.DMA
    return pl.pallas_call(
        expert_layer_kernel,
        in_specs=[here] * 9 + [far] * 2,
        out_specs=[here] * 4 + [far] * 4,
        out_shape=[
            jax.ShapeDtypeStruct((rows, width), BF16),
            jax.ShapeDtypeStruct((rows, width), F32),
            jax.ShapeDtypeStruct((rows, width), BF16),
            jax.ShapeDtypeStruct((experts + 1, width), F32),
        ] + [slots] * 4,
        scratch_shapes=[
            pltpu.VMEM(up.shape, BF16),
            pltpu.VMEM(down.shape, BF16),
            pltpu.VMEM((rows, width), BF16),
        ] + [pltpu.VMEM(buffer, BF16)] * 4 + [
            pltpu.VMEM((experts * CAP, hidden), BF16),
            pltpu.VMEM((experts * CAP, width), F32),
        ] + [pltpu.VMEM(buffer, BF16)] * 4 + [
            pltpu.VMEM((rows, experts), F32),
            dma((2,)), dma((4, experts)), dma((4, experts)), dma((4,)), dma((2,)), dma((2,)),
            dma((2,)),
        ],
        compiler_params=pltpu.CompilerParams(
            vmem_limit_bytes=VMEM_LIMIT, collective_id=1, has_side_effects=True
        ),
        name="expert_layer",
    )(mid, gain, router, routes_col, routes_row, slots_col, slots_row, live, cotangent, up, down)


class PlaneGather:
    def __init__(self, source, target, send_sems, recv_sems, local_sem):
        me = lax.axis_index("expert")
        core, side, above = neighbour(1), neighbour(2), neighbour(4)
        far = side + above - me
        rows = target.shape[1]
        first, second = pl.ds(0, rows // 2), pl.ds(rows // 2, rows - rows // 2)
        every = pl.ds(0, rows)

        def send(k, block, owner, part, device):
            return pltpu.make_async_remote_copy(
                block, target.at[owner, part], send_sems.at[k], recv_sems.at[k],
                device_id={"expert": device}, device_id_type=MESH,
            )

        self.copies = [
            send(0, source.at[first], me, first, side),
            send(1, source.at[second], me, second, side),
            send(2, source.at[first], me, first, above),
            send(3, source.at[second], me, second, above),
            send(4, target.at[side, first], side, first, above),
            send(5, target.at[above, second], above, second, side),
            send(6, source, me, every, core),
            send(7, target.at[side], side, every, core),
            send(8, target.at[above], above, every, core),
            send(9, target.at[far], far, every, core),
        ]
        self.local = pltpu.make_async_copy(source, target.at[me], local_sem)

    def step(self, number):
        copies = self.copies
        for k in ((), (0, 3), (1, 2), (4, 5), (6, 7, 8, 9))[number]:
            copies[k].wait_recv()
        for k in ((0, 3, 1, 2, 6), (4, 5), (7, 8), (9,), ())[number]:
            copies[k].start()
        if number == 0:
            self.local.start()
        if number == 4:
            self.local.wait()
            for copy in copies:
                copy.wait_send()


class Spread:
    def __init__(self, source, target, send_sems, recv_sems, local_sem):
        devices, me = lax.axis_size("expert"), lax.axis_index("expert")
        self.copies = [
            pltpu.make_async_remote_copy(
                source, target.at[me], send_sems.at[k], recv_sems.at[k],
                device_id={"expert": (me + k) % devices}, device_id_type=MESH,
            )
            for k in range(1, devices)
        ]
        self.local = pltpu.make_async_copy(source, target.at[me], local_sem)

    start, wait = Exchange.start, Exchange.wait


DMA = pltpu.SemaphoreType.DMA
FAR = pl.BlockSpec(memory_space=pl.ANY)


def remote_params(collective_id):
    return pltpu.CompilerParams(
        vmem_limit_bytes=VMEM_LIMIT, collective_id=collective_id, has_side_effects=True
    )


def gather_kernel(in_ref, *refs):
    small = len(refs) // 2 - 3
    sources, targets = refs[:small], refs[small + 1 : 2 * small + 1]
    in_full = refs[small]
    big_send, big_recv, small_send, small_recv, local_sems = refs[2 * small + 1 :]
    greet(line=False)
    big = PlaneGather(in_ref, in_full, big_send, big_recv, local_sems.at[small])
    spreads = [
        Spread(sources[k], targets[k], small_send.at[k], small_recv.at[k], local_sems.at[k])
        for k in range(small)
    ]
    big.step(0)
    for spread in spreads:
        spread.start()
    for number in range(1, 5):
        big.step(number)
    for spread in spreads:
        spread.wait()


def gather_weights(in_t, *small):
    devices = lax.axis_size("expert")
    count = len(small)
    full = [jax.ShapeDtypeStruct((devices,) + v.shape, v.dtype) for v in (in_t,) + small]
    return pl.pallas_call(
        gather_kernel,
        in_specs=[FAR] * (count + 1),
        out_specs=[FAR] * (count + 1),
        out_shape=full,
        scratch_shapes=[
            DMA((10,)), DMA((10,)), DMA((count, devices)), DMA((count, devices)), DMA((count + 1,)),
        ],
        compiler_params=remote_params(2),
        name="gather_weights",
    )(in_t, *small)


def scan_plane_kernel(
    proj_ref, stepw_ref, dbias_ref, decay_ref, skip_ref, u_ref, gate_ref, tokens_ref, outw_ref,
    step_ref, mixed_ref, gated_ref, hist_ref, mid_ref, outw_all,
    b_wide, c_blocks, du, scanned, gated_all, outw_here, send_sems, recv_sems, local_sems,
):
    tile_id = pl.program_id(0)
    rank, state = stepw_ref.shape[0], decay_ref.shape[0]
    tile = u_ref.shape[1]
    gather = PlaneGather(outw_ref, outw_here, send_sems, recv_sems, local_sems.at[0])
    keep = pltpu.make_async_copy(outw_here, outw_all, local_sems.at[1])

    @pl.when(tile_id == 0)
    def _():
        greet(line=False)
        gather.step(0)
        scan_prepare(proj_ref, b_wide, c_blocks, rank, rank + state, state)

    def between(half):
        for turn in range(2):

            @pl.when(tile_id == turn)
            def _():
                gather.step(2 * turn + half + 1)
                if turn + half == 2:
                    keep.start()

    gated = scan_tile(
        proj_ref, stepw_ref, dbias_ref, decay_ref, skip_ref, u_ref, gate_ref, step_ref, mixed_ref,
        hist_ref, b_wide, c_blocks, du, scanned, between,
    )
    split_lanes(gated_ref, gated)
    gated_all[:, pl.ds(pl.multiple_of(tile_id * tile, tile), tile)] = gated

    @pl.when(tile_id == 1)
    def _():
        devices, part, width = outw_here.shape
        weights = outw_here[...].reshape(devices * part, width)
        mid_ref[...] = tokens_ref[...].astype(F32) + product(gated_all[...], weights)
        keep.wait()


def scan_forward_plane(proj, step_w, dbias, decay, skip, u_act, gate_in, out_w, tokens):
    rows, channels = u_act.shape
    width = tokens.shape[1]
    cols = proj.shape[1]
    rank, state = step_w.shape[0], decay.shape[0]
    devices = lax.axis_size("expert")
    tile = channels // 2
    part = channels // devices
    hist_rows = (rows + 1) * state
    column = lambda i: (0, i)
    fixed = lambda i: (0, 0)
    return pl.pallas_call(
        scan_plane_kernel,
        grid=(2,),
        in_specs=[
            pl.BlockSpec((rows, cols), fixed),
            pl.BlockSpec((rank, tile), column),
            pl.BlockSpec((1, tile), column),
            pl.BlockSpec((state, tile), column),
            pl.BlockSpec((1, tile), column),
            pl.BlockSpec((rows, tile), column),
            pl.BlockSpec((rows, tile), column),
            pl.BlockSpec((rows, width), fixed),
            FAR,
        ],
        out_specs=[
            pl.BlockSpec((rows, tile), column),
            pl.BlockSpec((rows, tile), column),
            pl.BlockSpec((devices // 2, rows, part), lambda i: (i, 0, 0)),
            pl.BlockSpec((hist_rows, tile), column),
            pl.BlockSpec((rows, width), fixed),
            FAR,
        ],
        out_shape=[
            jax.ShapeDtypeStruct((rows, channels), F32),
            jax.ShapeDtypeStruct((rows, channels), F32),
            jax.ShapeDtypeStruct((devices, rows, part), BF16),
            jax.ShapeDtypeStruct((hist_rows, channels), BF16),
            jax.ShapeDtypeStruct((rows, width), F32),
            jax.ShapeDtypeStruct((devices, part, width), BF16),
        ],
        scratch_shapes=[
            pltpu.VMEM((rows * state, 128), F32),
            pltpu.VMEM((rows * 2, BLOCK * state), BF16),
            pltpu.VMEM((rows, tile), F32),
            pltpu.VMEM((rows, tile), F32),
            pltpu.VMEM((rows, channels), BF16),
            pltpu.VMEM((devices, part, width), BF16),
            DMA((10,)), DMA((10,)), DMA((2,)),
        ],
        compiler_params=remote_params(3),
        name="scan_forward_plane",
    )(proj, step_w, dbias, decay, skip, u_act, gate_in, tokens, out_w)


def scan_back_plane_kernel(*refs):
    inputs, refs = refs[:12], refs[12:]
    (mix_ref, normed_ref, gated_ref, own_grads, left_rows, right_rows), refs = refs[:6], refs[6:]
    outputs, refs = refs[:4], refs[4:]
    (mix_all, normed_all, gated_all, left_grads, right_grads, next_left, next_right), refs = (
        refs[:7], refs[7:]
    )
    scratch, refs = refs[:10], refs[10:]
    g_send, g_recv, x_send, x_recv, l_send, l_recv, local_sems = refs
    tile_id = pl.program_id(0)
    mix = PlaneGather(mix_ref, mix_all, g_send.at[0], g_recv.at[0], local_sems.at[0])
    normed = PlaneGather(normed_ref, normed_all, g_send.at[1], g_recv.at[1], local_sems.at[1])
    gated = Exchange(gated_ref, gated_all, x_send, x_recv, local_sems.at[2])
    line_g = Line(
        1, own_grads, own_grads, left_grads, right_grads, l_send.at[0], l_recv.at[0]
    )
    line_r = Line(
        2, left_rows, right_rows, next_left, next_right, l_send.at[1], l_recv.at[1]
    )

    @pl.when(tile_id == 0)
    def _():
        greet()
        line_g.start()
        line_r.start()
        mix.step(0)
        gated.start()
        normed.step(0)

    def between(half):
        for turn in range(2):

            @pl.when(tile_id == turn)
            def _():
                mix.step(2 * turn + half + 1)
                normed.step(2 * turn + half + 1)
                if turn + half == 2:
                    gated.wait()
                    line_g.wait()
                    line_r.wait()

    scan_back_tile(between, *inputs, *outputs, *scratch)


def scan_backward_plane(
    proj, step_w, dbias, decay, skip, u_act, gate_in, out_w, grad_mix, step_size, mixed, hist,
    normed_low, gated, own_grads, left_rows, right_rows,
):
    rows, channels = u_act.shape
    width = grad_mix.shape[1]
    cols = proj.shape[1]
    rank, state = step_w.shape[0], decay.shape[0]
    devices = lax.axis_size("expert")
    tile = channels // 2
    gate_parts, pack_parts = devices // 4, devices // 2
    pack_rows = rank + state + 8
    big = BLOCK * state
    column = lambda i: (0, i)
    fixed = lambda i: (0, 0)
    slots = jax.ShapeDtypeStruct(own_grads.shape, BF16)
    everyone = jax.ShapeDtypeStruct((devices, rows, width), BF16)
    return pl.pallas_call(
        scan_back_plane_kernel,
        grid=(2,),
        in_specs=[
            pl.BlockSpec((rows, cols), fixed),
            pl.BlockSpec((rank, tile), column),
            pl.BlockSpec((1, tile), column),
            pl.BlockSpec((state, tile), column),
            pl.BlockSpec((1, tile), column),
            pl.BlockSpec((rows, tile), column),
            pl.BlockSpec((rows, tile), column),
            pl.BlockSpec((tile, width), lambda i: (i, 0)),
            pl.BlockSpec((rows, width), fixed),
            pl.BlockSpec((rows, tile), column),
            pl.BlockSpec((rows, tile), column),
            pl.BlockSpec((hist.shape[0], tile), column),
        ] + [FAR] * 6,
        out_specs=[
            pl.BlockSpec((rows, tile), column),
            pl.BlockSpec((gate_parts, rows, tile // gate_parts), lambda i: (i, 0, 0)),
            pl.BlockSpec((pack_parts, pack_rows, tile // pack_parts), lambda i: (i, 0, 0)),
            pl.BlockSpec((rows, cols), fixed),
        ] + [FAR] * 7,
        out_shape=[
            jax.ShapeDtypeStruct((rows, channels), F32),
            jax.ShapeDtypeStruct((devices // 2, rows, 2 * channels // devices), BF16),
            jax.ShapeDtypeStruct((devices, pack_rows, channels // devices), BF16),
            jax.ShapeDtypeStruct((rows, cols), F32),
            everyone,
            everyone,
            jax.ShapeDtypeStruct(gated.shape, BF16),
        ] + [slots] * 4,
        scratch_shapes=[
            pltpu.VMEM((rows * state, 128), F32),
            pltpu.VMEM((rows * 2, big), BF16),
            pltpu.VMEM((rows, big), F32),
            pltpu.VMEM((rows, big), F32),
            pltpu.VMEM((rows, tile), F32),
            pltpu.VMEM((rows, tile), F32),
            pltpu.VMEM((big, tile), BF16),
            pltpu.VMEM((big, tile), BF16),
            pltpu.VMEM((rows, tile), F32),
            pltpu.VMEM((rows, tile), F32),
            DMA((2, 10)), DMA((2, 10)), DMA((devices,)), DMA((devices,)), DMA((2, 2)), DMA((2, 2)),
            DMA((3,)),
        ],
        compiler_params=remote_params(4),
        name="scan_backward_plane",
    )(
        proj, step_w, dbias, decay, skip, u_act, gate_in, out_w, grad_mix, step_size, mixed, hist,
        grad_mix, normed_low, gated, own_grads, left_rows, right_rows,
    )


def back_plane_kernel(
    gradproj_ref, scanw_ref, gradu_ref, xin_ref, conv_ref, bias_ref, wx_ref, wg_ref, u_ref,
    tokens_ref, gain_ref, gradmid_ref, widths_ref,
    gate_hbm, scan_parts, normed_hbm, mix_hbm, gated_hbm, left_grads, right_grads,
    gradtok_ref, gradin_ref, gradout_ref, scan_ref, back_ref, tail_ref, next_left, next_right,
    total, send_in, got_in, normed_all, mix_all, gated_all, got_scan, send_back, got_back,
    send_tail, got_tail, x_send, x_recv, l_send, l_recv, local_sems, load_sems,
):
    tile_id = pl.program_id(0)
    devices, me = lax.axis_size("expert"), lax.axis_index("expert")
    half = devices // 2
    gates = send_in.shape[0] // 4
    ways = [
        Exchange(source, target, x_send.at[k], x_recv.at[k], local_sems.at[k])
        for k, (source, target) in enumerate(
            [
                (send_in, got_in), (scan_parts, got_scan), (send_back, got_back),
                (send_tail, got_tail),
            ]
        )
    ]
    line = Line(2, left_grads, right_grads, next_left, next_right, l_send, l_recv)
    loads = [
        pltpu.make_async_copy(source, target, load_sems.at[k])
        for k, (source, target) in enumerate(
            [
                (gate_hbm, send_in.at[pl.ds(half, half)]), (normed_hbm, normed_all),
                (mix_hbm, mix_all), (gated_hbm, gated_all),
            ]
        )
    ]

    def start_inputs(late):
        for k, copy in enumerate(ways[0].copies):
            peer = (me + k + 1) % devices
            pl.when((peer < half) if late else (peer >= half))(lambda copy=copy: copy.start())
        pl.when((me < half) if late else (me >= half))(lambda: ways[0].local.start())

    @pl.when(tile_id == 0)
    def _():
        total[...] = jnp.zeros_like(total)
        for load in loads:
            load.start()
        greet()
        line.start()
        ways[1].start()
        loads[0].wait()
        start_inputs(False)

    grad_proj = gradproj_ref[...].astype(BF16)
    grad_u = gradu_ref[...] + times_transpose(grad_proj, scanw_ref[...])
    pieces = [contract_rows(grad_proj, u_ref[...].astype(BF16))]
    x_inner = xin_ref[...]
    taps = conv_ref.shape[0]
    shifted = [shift_rows(x_inner, taps - 1 - tap) for tap in range(taps)]
    summed = bias_ref[...]
    for tap in range(taps):
        summed = summed + conv_ref[tap : tap + 1, :] * shifted[tap]
    sig = sigmoid(summed)
    grad_sum = grad_u * (sig * (1.0 + summed * (1.0 - sig)))
    grad_x = jnp.zeros_like(x_inner)
    for tap in range(taps):
        pieces.append(jnp.sum(grad_sum * shifted[tap], 0, keepdims=True))
        grad_x = grad_x + conv_ref[tap : tap + 1, :] * shift_rows(grad_sum, tap + 1 - taps)
    pieces.append(jnp.sum(grad_sum, 0, keepdims=True))
    spare = send_back.shape[1] - grad_proj.shape[1] - taps - 1
    pieces.append(jnp.zeros((spare, x_inner.shape[1]), F32))
    packed = jnp.concatenate(pieces, 0).astype(BF16)
    grad_x = grad_x.astype(BF16)
    for turn in range(2):

        @pl.when(tile_id == turn)
        def _():
            split_lanes(send_back.at[pl.ds(turn * half, half)], packed)
            split_lanes(send_in.at[pl.ds(turn * gates, gates)], grad_x)

    @pl.when(tile_id == 1)
    def _():
        start_inputs(True)
        ways[2].start()

    for turn in range(2):

        @pl.when(tile_id == turn)
        def _():
            first = half + turn * gates
            grad_gate = jnp.concatenate([send_in[first + k] for k in range(gates)], 1)
            total[...] += product(grad_x, wx_ref[...]) + product(grad_gate, wg_ref[...])

    @pl.when(tile_id == 1)
    def _():
        values = tokens_ref[...].astype(F32)
        scale = lax.rsqrt(jnp.mean(values * values, -1, keepdims=True) + 1e-05)
        unit = values * scale
        grad = total[...]
        widths = jnp.concatenate([widths_ref[...], jnp.sum(grad * unit, 0, keepdims=True)], 0)
        widths = jnp.concatenate(
            [widths, jnp.zeros((send_tail.shape[1] - widths.shape[0], widths.shape[1]), F32)], 0
        )
        split_lanes(send_tail, widths.astype(BF16))
        ways[3].start()
        inner = grad * gain_ref[...]
        gradtok_ref[...] = gradmid_ref[...] + scale * (
            inner - unit * jnp.mean(inner * unit, -1, keepdims=True)
        )
        for load in loads[1:]:
            load.wait()
        rows, part = gated_all.shape[1:]
        width = mix_all.shape[2]
        gradout_ref[...] = contract_rows(
            gated_all[...].reshape(devices * rows, part), mix_all[...].reshape(devices * rows, width)
        ).astype(BF16)
        ways[0].wait()
        gradin_ref[...] = contract_rows(
            normed_all[...].reshape(devices * rows, width),
            got_in[...].reshape(devices * rows, got_in.shape[2]),
        ).astype(BF16)
        for way, got, out in (
            (ways[1], got_scan, scan_ref), (ways[2], got_back, back_ref), (ways[3], got_tail, tail_ref),
        ):
            way.wait()
            out[...] = jnp.sum(got[...].astype(F32), 0).astype(BF16)
        line.wait()


def mixer_back_plane(
    grad_proj, scan_w, grad_u, x_inner, conv, bias, in_t, u_act, tokens, gain, grad_mid,
    grad_widths, grad_gate, scan_parts, normed_all, mix_all, gated_all, left_grads, right_grads,
):
    rows, channels = u_act.shape
    width = tokens.shape[1]
    cols = scan_w.shape[1]
    taps = conv.shape[0]
    devices = lax.axis_size("expert")
    part = channels // devices
    tile = channels // 2
    pack_rows = cols + 8
    tail_rows = grad_widths.shape[0] + 7
    column = lambda i: (0, i)
    fixed = lambda i: (0, 0)
    slots = jax.ShapeDtypeStruct(left_grads.shape, BF16)
    return pl.pallas_call(
        back_plane_kernel,
        grid=(2,),
        in_specs=[
            pl.BlockSpec((rows, cols), fixed),
            pl.BlockSpec((tile, cols), lambda i: (i, 0)),
            pl.BlockSpec((rows, tile), column),
            pl.BlockSpec((rows, tile), column),
            pl.BlockSpec((taps, tile), column),
            pl.BlockSpec((1, tile), column),
            pl.BlockSpec((tile, width), lambda i: (i, 0)),
            pl.BlockSpec((tile, width), lambda i: (i + 2, 0)),
            pl.BlockSpec((rows, tile), column),
            pl.BlockSpec((rows, width), fixed),
            pl.BlockSpec((1, width), fixed),
            pl.BlockSpec((rows, width), fixed),
            pl.BlockSpec(grad_widths.shape, fixed),
        ] + [FAR] * 7,
        out_specs=[
            pl.BlockSpec((rows, width), fixed),
            pl.BlockSpec((width, 2 * part), fixed),
            pl.BlockSpec((part, width), fixed),
            pl.BlockSpec(scan_parts.shape[1:], fixed),
            pl.BlockSpec((pack_rows, part), fixed),
            pl.BlockSpec((tail_rows, width // devices), fixed),
            FAR,
            FAR,
        ],
        out_shape=[
            jax.ShapeDtypeStruct((rows, width), F32),
            jax.ShapeDtypeStruct((width, 2 * part), BF16),
            jax.ShapeDtypeStruct((part, width), BF16),
            jax.ShapeDtypeStruct(scan_parts.shape[1:], BF16),
            jax.ShapeDtypeStruct((pack_rows, part), BF16),
            jax.ShapeDtypeStruct((tail_rows, width // devices), BF16),
            slots,
            slots,
        ],
        scratch_shapes=[
            pltpu.VMEM((rows, width), F32),
            pltpu.VMEM((devices, rows, 2 * part), BF16),
            pltpu.VMEM((devices, rows, 2 * part), BF16),
            pltpu.VMEM(normed_all.shape, BF16),
            pltpu.VMEM(mix_all.shape, BF16),
            pltpu.VMEM(gated_all.shape, BF16),
            pltpu.VMEM(scan_parts.shape, BF16),
            pltpu.VMEM((devices, pack_rows, part), BF16),
            pltpu.VMEM((devices, pack_rows, part), BF16),
            pltpu.VMEM((devices, tail_rows, width // devices), BF16),
            pltpu.VMEM((devices, tail_rows, width // devices), BF16),
            DMA((4, devices)), DMA((4, devices)), DMA((2,)), DMA((2,)), DMA((4,)), DMA((4,)),
        ],
        compiler_params=remote_params(5),
        name="mixer_back_plane",
    )(
        grad_proj, scan_w, grad_u, x_inner, conv, bias, in_t, in_t, u_act, tokens, gain, grad_mid,
        grad_widths, grad_gate, scan_parts, normed_all, mix_all, gated_all, left_grads, right_grads,
    )


def add_groups(rows, grads, rows_t, up_ref, down_ref):
    activated, slope = gelu_parts(product(rows, up_ref[...]))
    grad_pre = (times_transpose(grads, down_ref[...]) * slope).astype(BF16)
    return product(rows_t, grad_pre), contract_rows(activated.astype(BF16), grads)


def first_grads_kernel(
    up_ref, down_ref, rows_0, grads_0, rows_l1, rows_r1, grads_l1, grads_r1, rows_l2, rows_r2,
    grads_l2, grads_r2,
    gup_ref, gdown_ref, rows_l3, rows_r3, grads_l3, grads_r3,
    rows_ref, grads_ref, rows_t, l_send, l_recv, load_sems,
):
    step = pl.program_id(0)
    place = lax.axis_index("dp")
    count, width = rows_ref.shape[0] * rows_ref.shape[1] * rows_ref.shape[2], rows_ref.shape[3]
    lines = [
        Line(3, rows_l2, rows_r2, rows_l3, rows_r3, l_send.at[0], l_recv.at[0]),
        Line(3, grads_l2, grads_r2, grads_l3, grads_r3, l_send.at[1], l_recv.at[1]),
    ]

    @pl.when(step == 0)
    def _():
        greet()
        for line in lines:
            line.start()
        own = [
            pltpu.make_async_copy(rows_0, rows_ref.at[0], load_sems.at[0]),
            pltpu.make_async_copy(grads_0, grads_ref.at[0], load_sems.at[1]),
        ]
        for copy in own:
            copy.start()
        for condition, rows_1, grads_1 in (
            (place >= 1, rows_l1, grads_l1), (place < 1, rows_r1, grads_r1),
        ):

            @pl.when(condition)
            def _():
                next_to = [
                    pltpu.make_async_copy(rows_1, rows_ref.at[1], load_sems.at[2]),
                    pltpu.make_async_copy(grads_1, grads_ref.at[1], load_sems.at[3]),
                ]
                for copy in next_to:
                    copy.start()
                for copy in next_to:
                    copy.wait()

        for copy in own:
            copy.wait()
        rows_t[...] = rows_ref[...].reshape(count, width).T

    gup_ref[...], gdown_ref[...] = add_groups(
        rows_ref[...].reshape(count, width), grads_ref[...].reshape(count, width), rows_t[...],
        up_ref, down_ref,
    )

    @pl.when(step == pl.num_programs(0) - 1)
    def _():
        for line in lines:
            line.wait()


def last_grads_kernel(
    up_ref, down_ref, gup_in, gdown_in, *refs
):
    choices, (gup_ref, gdown_ref, rows_ref, grads_ref, rows_t, load_sems) = refs[:10], refs[10:]
    rows_l2, rows_l3, rows_r1, rows_r2, rows_r3 = choices[:5]
    grads_l2, grads_l3, grads_r1, grads_r2, grads_r3 = choices[5:]
    step = pl.program_id(0)
    place = lax.axis_index("dp")
    count, width = rows_ref.shape[0] * rows_ref.shape[1] * rows_ref.shape[2], rows_ref.shape[3]

    @pl.when(step == 0)
    def _():
        for spot, pairs in enumerate(
            (
                ((rows_r2, grads_r2), (rows_r1, grads_r1), (rows_l2, grads_l2), (rows_l2, grads_l2)),
                ((rows_r3, grads_r3), (rows_r2, grads_r2), (rows_r1, grads_r1), (rows_l3, grads_l3)),
            )
        ):
            for where, (rows_1, grads_1) in enumerate(pairs):

                @pl.when(place == where)
                def _():
                    copies = [
                        pltpu.make_async_copy(rows_1, rows_ref.at[spot], load_sems.at[0]),
                        pltpu.make_async_copy(grads_1, grads_ref.at[spot], load_sems.at[1]),
                    ]
                    for copy in copies:
                        copy.start()
                    for copy in copies:
                        copy.wait()

        rows_t[...] = rows_ref[...].reshape(count, width).T

    grad_up, grad_down = add_groups(
        rows_ref[...].reshape(count, width), grads_ref[...].reshape(count, width), rows_t[...],
        up_ref, down_ref,
    )
    gup_ref[...] = gup_in[...] + grad_up
    gdown_ref[...] = gdown_in[...] + grad_down


def expert_grads_plane(up, down, rows, grads, tile):
    width, hidden = up.shape
    slots = jax.ShapeDtypeStruct(rows[0].shape, BF16)
    pair = (2,) + rows[0].shape
    count = pair[0] * pair[1] * pair[2]
    across = pl.BlockSpec((width, tile), lambda i: (0, i))
    along = pl.BlockSpec((tile, width), lambda i: (i, 0))
    shapes = [
        jax.ShapeDtypeStruct((width, hidden), F32), jax.ShapeDtypeStruct((hidden, width), F32)
    ]
    buffers = [pltpu.VMEM(pair, BF16), pltpu.VMEM(pair, BF16), pltpu.VMEM((width, count), BF16)]
    grad_up, grad_down, rows_l3, rows_r3, grads_l3, grads_r3 = pl.pallas_call(
        first_grads_kernel,
        grid=(hidden // tile,),
        in_specs=[across, along] + [FAR] * 10,
        out_specs=[across, along] + [FAR] * 4,
        out_shape=shapes + [slots] * 4,
        scratch_shapes=buffers + [DMA((2, 2)), DMA((2, 2)), DMA((4,))],
        compiler_params=remote_params(6),
        name="expert_grads_first",
    )(
        up, down, rows[0], grads[0], rows[1], rows[2], grads[1], grads[2], rows[3], rows[4],
        grads[3], grads[4],
    )
    return pl.pallas_call(
        last_grads_kernel,
        grid=(hidden // tile,),
        in_specs=[across, along, across, along] + [FAR] * 10,
        out_specs=[across, along],
        out_shape=shapes,
        scratch_shapes=buffers + [DMA((2,))],
        compiler_params=pltpu.CompilerParams(vmem_limit_bytes=VMEM_LIMIT),
        name="expert_grads_last",
    )(
        up, down, grad_up, grad_down, rows[3], rows_l3, rows[2], rows[4], rows_r3, grads[3],
        grads_l3, grads[2], grads[4], grads_r3,
    )


def gather(value):
    return lax.all_gather(value, "expert", axis=0, tiled=True)


def exchange(value):
    return lax.all_to_all(value, "expert", split_axis=0, concat_axis=0, tiled=True)


def shards(
    tokens, lengths, routes, slot_index, mixer_norm, in_weight, conv_weight, conv_bias,
    scan_weight, step_weight, step_bias, decay_log, skip_gain, out_weight, moe_norm, router_weight,
    up_weight, down_weight, cotangent,
):
    devices = lax.axis_size("expert")
    rows, width = tokens.shape[1:]
    part = out_weight.shape[0]
    channels = part * devices
    cols = scan_weight.shape[1]
    rank, state, taps = step_weight.shape[0], decay_log.shape[1], conv_weight.shape[0]
    experts = router_weight.shape[1]
    split = devices // experts
    slice_w = width // devices
    tile = channels // 2

    on_plane = devices == 8 and split == 1 and lax.axis_size("dp") == 4
    by_column = jnp.concatenate(
        [
            step_weight, decay_log.T, conv_weight, conv_bias[None], step_bias[None],
            skip_gain[None], jnp.zeros_like(skip_gain)[None],
        ],
        0,
    )
    by_width = jnp.concatenate(
        [router_weight.T, mixer_norm[None], moe_norm[None], jnp.zeros((6, slice_w), BF16)], 0
    )
    in_t = in_weight.T
    if on_plane:
        in_t, by_column, scan_full, by_width = gather_weights(in_t, by_column, scan_weight, by_width)
    else:
        in_t, by_column, scan_full, by_width = (
            lax.all_gather(value, "expert") for value in (in_t, by_column, scan_weight, by_width)
        )
    in_t = in_t.reshape(2 * channels, width)
    scan_full = scan_full.reshape(channels, cols)
    columns = by_column.transpose(1, 0, 2).reshape(by_column.shape[1], channels)
    widths = by_width.transpose(1, 0, 2).reshape(by_width.shape[1], width)
    step_full = columns[:rank]
    rest = columns[rank:].astype(F32)
    rate = -jnp.exp(rest[:state])
    conv_full = rest[state : state + taps]
    bias_full, dbias_full, skip_full = (
        rest[state + taps + k : state + taps + k + 1] for k in range(3)
    )
    router = widths[:experts].T
    gain_first = widths[experts : experts + 1].astype(F32)
    gain_second = widths[experts + 1 : experts + 2].astype(F32)
    up, down = up_weight[0], down_weight[0]
    live = (jnp.arange(rows, dtype=jnp.int32) < lengths[0]).astype(F32)[:, None]
    routes_col, slots_col = routes[0][:, None], slot_index[0][:, None]

    normed_low, x_inner, u_act, gate_in, proj = front(
        tokens[0], gain_first, in_t, conv_full, bias_full, scan_full, tile
    )
    hidden = up.shape[1]
    if on_plane:
        step_size, mixed, gated, hist, mid, out_full = scan_forward_plane(
            proj, step_full, dbias_full, rate, skip_full, u_act, gate_in, out_weight, tokens[0]
        )
        out_full = out_full.reshape(channels, width)
        (
            layer_out, grad_mid, grad_mix, grad_widths, rows_0, grads_0, rows_l1, rows_r1
        ) = expert_layer(
            mid, gain_second, router, routes_col, routes, slots_col, slot_index, live, cotangent[0],
            up, down,
        )
        (
            grad_u, grad_gate, scan_parts, grad_proj, mix_all, normed_all, gated_all, grads_l1,
            grads_r1, rows_l2, rows_r2,
        ) = scan_backward_plane(
            proj, step_full, dbias_full, rate, skip_full, u_act, gate_in, out_full, grad_mix,
            step_size, mixed, hist, normed_low, gated, grads_0, rows_l1, rows_r1,
        )
        tokens_grad, *totals, grads_l2, grads_r2 = mixer_back_plane(
            grad_proj, scan_full, grad_u, x_inner, conv_full, bias_full, in_t, u_act, tokens[0],
            gain_first, grad_mid, grad_widths, grad_gate, scan_parts, normed_all, mix_all,
            gated_all, grads_l1, grads_r1,
        )
        totals = lax.psum(tuple(totals), "dp")
        grad_up, grad_down = expert_grads_plane(
            up, down, (rows_0, rows_l1, rows_r1, rows_l2, rows_r2),
            (grads_0, grads_l1, grads_r1, grads_l2, grads_r2), min(256, hidden),
        )
        in_total, out_total, scan_small, back_small, width_small = (t.astype(F32) for t in totals)
    else:
        out_full = gather(out_weight)
        step_size, mixed, gated, hist, mid = scan_forward(
            proj, step_full, dbias_full, rate, skip_full, u_act, gate_in, out_full, tokens[0], tile
        )
        send_rows, send_grads, normed_two, probs = router_step(
            mid, gain_second, router, routes_col, routes, slot_index, live, cotangent[0]
        )

        def to_pieces(value):
            wide = jnp.broadcast_to(value[:, None], (experts, split) + value.shape[1:])
            return exchange(wide.reshape(devices, CAP, width))

        def from_pieces(value):
            value = exchange(value).reshape(experts, split, CAP, width)
            if split == 1:
                return value[:, 0]
            return jnp.sum(value.astype(F32), 1).astype(BF16)

        some = min(512, hidden // 3)
        rows_in = to_pieces(send_rows)
        grads_in = to_pieces(send_grads)
        partial_out, slope = expert_out(rows_in, up, down, some)
        back_rows = from_pieces(partial_out)
        back_grads = from_pieces(expert_back(grads_in, up, down, slope, some))
        all_rows = lax.all_gather(rows_in, "dp")
        layer_out, grad_mid, grad_mix, grad_widths = combine_step(
            mid, gain_second, router, routes_col, slots_col, live, cotangent[0], probs, normed_two,
            back_rows, back_grads,
        )
        grad_mix, all_rows = lax.optimization_barrier((grad_mix, all_rows))
        all_grads = lax.all_gather(grads_in, "dp")
        out_parts = contract_rows(gated, grad_mix).astype(BF16).reshape(devices, part, width)
        grad_out_w = jnp.sum(exchange(out_parts).astype(F32), 0).astype(BF16)
        grad_u, grad_gate, scan_parts, grad_proj = scan_backward(
            proj, step_full, dbias_full, rate, skip_full, u_act, gate_in, out_full, grad_mix, step_size,
            mixed, hist, tile, devices,
        )
        scan_small = jnp.sum(exchange(scan_parts).astype(F32), 0).astype(BF16)
        grad_x, back_parts, width_parts, tokens_grad = mixer_back(
            grad_proj, scan_full, grad_u, x_inner, conv_full, bias_full, grad_gate, in_t, u_act,
            tokens[0], gain_first, grad_mid, grad_widths, tile, devices,
        )
        back_small = jnp.sum(exchange(back_parts).astype(F32), 0).astype(BF16)
        width_small = jnp.sum(exchange(width_parts).astype(F32), 0).astype(BF16)
        normed_all = gather(normed_low)
        grad_in_parts = exchange(jnp.concatenate([grad_x, grad_gate], 0))
        grad_in_w = contract_rows(
            grad_in_parts.reshape(devices * rows, 2 * part), normed_all
        ).astype(BF16)
        totals = (grad_in_w, grad_out_w, scan_small, back_small, width_small)
        totals, all_grads = lax.optimization_barrier((totals, all_grads))
        totals = lax.psum(totals, "dp")
        in_total, out_total, scan_small, back_small, width_small = (
            t.astype(F32) for t in totals
        )
        in_total = in_total.T
        grad_up, grad_down = expert_grads(all_rows, all_grads, up, down, min(256, hidden))
    return (
        layer_out[None],
        tokens_grad[None],
        width_small[experts + 1],
        in_total,
        back_small[cols : cols + taps],
        back_small[cols + taps],
        back_small[:cols].T,
        scan_small[:rank],
        scan_small[rank + state],
        scan_small[rank : rank + state].T,
        scan_small[rank + state + 1],
        out_total,
        width_small[experts],
        width_small[:experts].T,
        grad_up[None],
        grad_down[None],
    )


def solution(mesh):
    in_specs = (
        P(("dp", "expert"), None, None),
        P(("dp", "expert")),
        P(("dp", "expert"), None),
        P(("dp", "expert"), None),
        P("expert"),
        P(None, "expert"),
        P(None, "expert"),
        P("expert"),
        P("expert", None),
        P(None, "expert"),
        P("expert"),
        P("expert", None),
        P("expert"),
        P("expert", None),
        P("expert"),
        P("expert", None),
        P("expert", None, None),
        P("expert", None, None),
        P(("dp", "expert"), None, None),
    )
    out_specs = (
        P(("dp", "expert"), None, None),
        P(("dp", "expert"), None, None),
        P("expert"),
        P(None, "expert"),
        P(None, "expert"),
        P("expert"),
        P("expert", None),
        P(None, "expert"),
        P("expert"),
        P("expert", None),
        P("expert"),
        P("expert", None),
        P("expert"),
        P("expert", None),
        P("expert", None, None),
        P("expert", None, None),
    )
    return jax.shard_map(shards, mesh=mesh, in_specs=in_specs, out_specs=out_specs, check_vma=False)
```

```python
from functools import partial

import jax
import jax.numpy as jnp
from jax import lax
from jax.experimental import pallas as pl
from jax.experimental.pallas import tpu as pltpu
from jax.sharding import PartitionSpec as P

CAP = 64
BLOCK = 16
LOG2E = 1.4426950408889634
F32 = jnp.float32
BF16 = jnp.bfloat16
VMEM_LIMIT = 56 * 1024 * 1024


def product(left, right):
    return jnp.dot(left, right, preferred_element_type=F32)


def contract_rows(left, right):
    return lax.dot_general(left, right, (((0,), (0,)), ((), ())), preferred_element_type=F32)


def times_transpose(left, right):
    return lax.dot_general(left, right, (((1,), (1,)), ((), ())), preferred_element_type=F32)


def exact_product(left, right):
    return jnp.dot(left, right, preferred_element_type=F32, precision=lax.Precision.HIGHEST)


def iota(shape, axis):
    return lax.broadcasted_iota(jnp.int32, shape, axis)


def sigmoid(values):
    return 1.0 / (1.0 + jnp.exp(-values))


def softplus(values):
    return jnp.maximum(values, 0.0) + jnp.log1p(jnp.exp(-jnp.abs(values)))


class Rows:
    def __init__(self, ref, first, count):
        self.ref, self.first = ref, first
        self.shape = (count, ref.shape[1])

    def __getitem__(self, index):
        low, high = (0, self.shape[0]) if index is Ellipsis else (index[0].start, index[0].stop)
        return self.ref[self.first + low : self.first + high, :]


def conv_rows(misc_ref):
    return Rows(misc_ref, 0, 4), Rows(misc_ref, 4, 1)


def scan_rows(misc_ref):
    return Rows(misc_ref, 5, 1), Rows(misc_ref, 6, 1)


def split_lanes(out_ref, value):
    parts, _, width = out_ref.shape
    for part in range(parts):
        out_ref[part] = value[:, part * width : (part + 1) * width]


def shift_rows(values, offset):
    rows = values.shape[0]
    if offset == 0:
        return values
    rolled = pltpu.roll(values, offset % rows, 0)
    row = iota(values.shape, 0)
    keep = row >= offset if offset > 0 else row < rows + offset
    return jnp.where(keep, rolled, 0.0)


def two_parts(values):
    high = values.astype(BF16)
    low = (values - high.astype(F32)).astype(BF16)
    return high, low


def spread_rows(proj_block, first, state):
    rows, width = proj_block.shape
    big = rows * state
    pick = (iota((big, rows), 0) // state == iota((big, rows), 1)).astype(F32)
    copied = exact_product(pick, proj_block)
    lane = iota((big, width), 1)
    own = lane == first + iota((big, width), 0) % state
    column = jnp.sum(jnp.where(own, copied, 0.0), axis=1, keepdims=True)
    return jnp.broadcast_to(column, (big, 128))


def diagonal_blocks(proj_block, first, state):
    rows, width = proj_block.shape
    big = rows * state
    place = (iota((width, big), 0) == first + iota((width, big), 1) % state).astype(BF16)
    own = iota((rows, big), 0) == iota((rows, big), 1) // state
    parts = [
        jnp.where(own, product(part, place), 0.0).astype(BF16) for part in two_parts(proj_block)
    ]
    return jnp.concatenate(parts, 0)


def front_kernel(
    tokens_ref, gain_ref, wx_ref, wg_ref, misc_ref, scanw_ref,
    normed_ref, xin_ref, u_ref, gate_ref, proj_ref,
):
    step = pl.program_id(0)
    conv_ref, bias_ref = conv_rows(misc_ref)

    @pl.when(step == 0)
    def _():
        values = tokens_ref[...].astype(F32)
        scale = lax.rsqrt(jnp.mean(values * values, -1, keepdims=True) + 1e-05)
        normed_ref[...] = (values * scale * gain_ref[0:1, :]).astype(BF16)
        proj_ref[...] = jnp.zeros_like(proj_ref)

    normed = normed_ref[...]
    x_inner = times_transpose(normed, wx_ref[...])
    gate_ref[...] = times_transpose(normed, wg_ref[...])
    xin_ref[...] = x_inner
    taps = conv_ref.shape[0]
    summed = bias_ref[...] + conv_ref[taps - 1 : taps, :] * x_inner
    for back in range(1, taps):
        tap = taps - 1 - back
        summed = summed + conv_ref[tap : tap + 1, :] * shift_rows(x_inner, back)
    u_act = summed * sigmoid(summed)
    u_ref[...] = u_act
    proj_ref[...] += product(u_act.astype(BF16), scanw_ref[...])


def front(tokens, gains, in_t, vec, scan_w, tile):
    rows, width = tokens.shape
    channels = scan_w.shape[0]
    cols = scan_w.shape[1]
    steps = channels // tile
    return pl.pallas_call(
        front_kernel,
        grid=(steps,),
        in_specs=[
            pl.BlockSpec((rows, width), lambda i: (0, 0)),
            pl.BlockSpec(gains.shape, lambda i: (0, 0)),
            pl.BlockSpec((tile, width), lambda i: (i, 0)),
            pl.BlockSpec((tile, width), lambda i: (i + steps, 0)),
            pl.BlockSpec((8, tile), lambda i: ((vec.shape[0] - 8) // 8, i)),
            pl.BlockSpec((tile, cols), lambda i: (i, 0)),
        ],
        out_specs=[
            pl.BlockSpec((rows, width), lambda i: (0, 0)),
            pl.BlockSpec((rows, tile), lambda i: (0, i)),
            pl.BlockSpec((rows, tile), lambda i: (0, i)),
            pl.BlockSpec((rows, tile), lambda i: (0, i)),
            pl.BlockSpec((rows, cols), lambda i: (0, 0)),
        ],
        out_shape=[
            jax.ShapeDtypeStruct((rows, width), BF16),
            jax.ShapeDtypeStruct((rows, channels), F32),
            jax.ShapeDtypeStruct((rows, channels), F32),
            jax.ShapeDtypeStruct((rows, channels), F32),
            jax.ShapeDtypeStruct((rows, cols), F32),
        ],
        compiler_params=pltpu.CompilerParams(vmem_limit_bytes=VMEM_LIMIT),
        name="mixer_front",
    )(tokens, gains, in_t, in_t, vec, scan_w)


def scan_prepare(proj_ref, b_wide, c_blocks, b_first, c_first, state):
    blocks = proj_ref.shape[0] // BLOCK
    big = BLOCK * state

    def build(block, carry):
        part = proj_ref[pl.ds(pl.multiple_of(block * BLOCK, BLOCK), BLOCK), :]
        b_wide[pl.ds(pl.multiple_of(block * big, big), big), :] = spread_rows(part, b_first, state)
        c_blocks[pl.ds(pl.multiple_of(block * 2 * BLOCK, 2 * BLOCK), 2 * BLOCK), :] = (
            diagonal_blocks(part, c_first, state)
        )
        return carry

    lax.fori_loop(0, blocks, build, 0)


def scan_tile(
    proj_ref, stepw_ref, decay_ref, misc_ref, u_ref, gate_ref, step_ref, mixed_ref, hist_ref,
    b_wide, c_blocks, du, scanned, between,
):
    rank, state = stepw_ref.shape[0], decay_ref.shape[0]
    rows, tile = u_ref.shape
    blocks = rows // BLOCK
    big = BLOCK * state
    dbias_ref, skip_ref = scan_rows(misc_ref)
    u_act = u_ref[...]
    step_size = softplus(
        product(proj_ref[:, :rank].astype(BF16), stepw_ref[...]) + dbias_ref[...]
    )
    step_ref[...] = step_size
    du[...] = step_size * u_act
    decay = decay_ref[...] * LOG2E
    hist_ref[0:state, :] = jnp.zeros((state, tile), BF16)

    def run_block(block, held):
        base = pl.multiple_of(block * BLOCK, BLOCK)
        steps_now = step_ref[pl.ds(base, BLOCK), :]
        du_now = du[pl.ds(base, BLOCK), :]
        wide_base = pl.multiple_of(block * big, big)
        for t in range(BLOCK):
            b_now = b_wide[pl.ds(wide_base + t * state, state), :]
            fade = jnp.exp2(steps_now[t : t + 1, :] * decay)
            fresh = du_now[t : t + 1, :] * jnp.concatenate([b_now] * (tile // 128), 1)
            held = fade * held + fresh
            hist_ref[pl.ds(wide_base + (t + 1) * state, state), :] = held.astype(BF16)
        weights = c_blocks[pl.ds(pl.multiple_of(block * 2 * BLOCK, 2 * BLOCK), 2 * BLOCK), :]
        both = product(weights, hist_ref[pl.ds(wide_base + state, big), :])
        scanned[pl.ds(base, BLOCK), :] = both[:BLOCK] + both[BLOCK:]
        return held

    held = jnp.zeros((state, tile), F32)
    held = lax.fori_loop(0, blocks // 2, run_block, held)
    between(0)
    lax.fori_loop(blocks // 2, blocks, run_block, held)
    between(1)
    mixed = scanned[...] + skip_ref[...] * u_act
    mixed_ref[...] = mixed
    gate_in = gate_ref[...]
    return (mixed * (gate_in * sigmoid(gate_in))).astype(BF16)


def scan_kernel(
    proj_ref, stepw_ref, decay_ref, misc_ref, u_ref, gate_ref, outw_ref, tokens_ref,
    step_ref, mixed_ref, gated_ref, hist_ref, mid_ref,
    b_wide, c_blocks, du, scanned,
):
    rank, state = stepw_ref.shape[0], decay_ref.shape[0]

    @pl.when(pl.program_id(0) == 0)
    def _():
        mid_ref[...] = tokens_ref[...].astype(F32)
        scan_prepare(proj_ref, b_wide, c_blocks, rank, rank + state, state)

    gated = scan_tile(
        proj_ref, stepw_ref, decay_ref, misc_ref, u_ref, gate_ref, step_ref, mixed_ref, hist_ref,
        b_wide, c_blocks, du, scanned, lambda half: None,
    )
    gated_ref[...] = gated
    mid_ref[...] += product(gated, outw_ref[...])


def scan_forward(proj, step_w, vec, u_act, gate_in, out_w, tokens, tile):
    rows, channels = u_act.shape
    width = tokens.shape[1]
    cols = proj.shape[1]
    rank, state = step_w.shape[0], vec.shape[0] - 8
    steps = channels // tile
    hist_rows = (rows + 1) * state
    column = lambda i: (0, i)
    fixed = lambda i: (0, 0)
    return pl.pallas_call(
        scan_kernel,
        grid=(steps,),
        in_specs=[
            pl.BlockSpec((rows, cols), fixed),
            pl.BlockSpec((rank, tile), column),
            pl.BlockSpec((state, tile), column),
            pl.BlockSpec((8, tile), lambda i: ((vec.shape[0] - 8) // 8, i)),
            pl.BlockSpec((rows, tile), column),
            pl.BlockSpec((rows, tile), column),
            pl.BlockSpec((tile, width), lambda i: (i, 0)),
            pl.BlockSpec((rows, width), fixed),
        ],
        out_specs=[
            pl.BlockSpec((rows, tile), column),
            pl.BlockSpec((rows, tile), column),
            pl.BlockSpec((rows, tile), column),
            pl.BlockSpec((hist_rows, tile), column),
            pl.BlockSpec((rows, width), fixed),
        ],
        out_shape=[
            jax.ShapeDtypeStruct((rows, channels), F32),
            jax.ShapeDtypeStruct((rows, channels), F32),
            jax.ShapeDtypeStruct((rows, channels), BF16),
            jax.ShapeDtypeStruct((hist_rows, channels), BF16),
            jax.ShapeDtypeStruct((rows, width), F32),
        ],
        scratch_shapes=[
            pltpu.VMEM((rows * state, 128), F32),
            pltpu.VMEM((rows * 2, BLOCK * state), BF16),
            pltpu.VMEM((rows, tile), F32),
            pltpu.VMEM((rows, tile), F32),
        ],
        compiler_params=pltpu.CompilerParams(vmem_limit_bytes=VMEM_LIMIT),
        name="scan_forward",
    )(proj, step_w, vec, vec, u_act, gate_in, out_w, tokens)


def scan_back_kernel(*refs):
    scan_back_tile(lambda half: None, split_lanes, *refs)


def scan_back_tile(
    between, put_gate, proj_ref, stepw_ref, decay_ref, misc_ref, u_ref, gate_ref, outw_ref, gradmix_ref,
    step_ref, mixed_ref, hist_ref,
    gradu_ref, gradgate_ref, pack_ref, gradproj_ref,
    c_wide, b_blocks, b_sums, c_sums, gy, du, g_hist, w_hist, grad_du, grad_step,
):
    tile_id = pl.program_id(0)
    cols, rank = proj_ref.shape[1], stepw_ref.shape[0]
    state = decay_ref.shape[0]
    rows, tile = u_ref.shape
    blocks = rows // BLOCK
    big = BLOCK * state

    @pl.when(tile_id == 0)
    def _():
        gradproj_ref[...] = jnp.zeros_like(gradproj_ref)
        b_sums[...] = jnp.zeros_like(b_sums)
        c_sums[...] = jnp.zeros_like(c_sums)
        scan_prepare(proj_ref, c_wide, b_blocks, rank + state, rank, state)

    skip_ref = scan_rows(misc_ref)[1]
    grad_gated = times_transpose(gradmix_ref[...], outw_ref[...])
    gate_in = gate_ref[...]
    gate_sig = sigmoid(gate_in)
    grad_mixed = grad_gated * (gate_in * gate_sig)
    put_gate(
        gradgate_ref,
        (grad_gated * mixed_ref[...] * (gate_sig * (1.0 + gate_in * (1.0 - gate_sig)))).astype(BF16),
    )
    u_act = u_ref[...]
    step_size = step_ref[...]
    gy[...] = grad_mixed
    du[...] = step_size * u_act
    grad_skip = jnp.sum(grad_mixed * u_act, 0, keepdims=True)
    rate = decay_ref[...]
    decay = rate * LOG2E
    sums = (iota((BLOCK, big), 0) == iota((BLOCK, big), 1) // state).astype(BF16)

    def run_block(turn, carry):
        carried, log_sum = carry
        block = blocks - 1 - turn
        base = pl.multiple_of(block * BLOCK, BLOCK)
        wide_base = pl.multiple_of(block * big, big)
        steps_now = step_ref[pl.ds(base, BLOCK), :]
        gy_now = gy[pl.ds(base, BLOCK), :]
        for t in range(BLOCK - 1, -1, -1):
            c_now = c_wide[pl.ds(wide_base + t * state, state), :]
            step_now = steps_now[t : t + 1, :]
            fade = jnp.exp2(step_now * decay)
            grad = gy_now[t : t + 1, :] * jnp.concatenate([c_now] * (tile // 128), 1) + carried
            g_hist[t * state : (t + 1) * state, :] = grad.astype(BF16)
            carried = fade * grad
            before = hist_ref[pl.ds(wide_base + t * state, state), :].astype(F32)
            weighted = carried * before * rate
            w_hist[t * state : (t + 1) * state, :] = weighted.astype(BF16)
            log_sum = log_sum + weighted * step_now
        grads = g_hist[...]
        both = product(
            b_blocks[pl.ds(pl.multiple_of(block * 2 * BLOCK, 2 * BLOCK), 2 * BLOCK), :], grads
        )
        grad_du[pl.ds(base, BLOCK), :] = both[:BLOCK] + both[BLOCK:]
        grad_step[pl.ds(base, BLOCK), :] = product(sums, w_hist[...])
        b_sums[pl.ds(base, BLOCK), :] += times_transpose(
            du[pl.ds(base, BLOCK), :].astype(BF16), grads
        )
        c_sums[pl.ds(base, BLOCK), :] += times_transpose(
            gy_now.astype(BF16), hist_ref[pl.ds(wide_base + state, big), :]
        )
        return carried, log_sum

    zeros = jnp.zeros((state, tile), F32)
    held = lax.fori_loop(0, blocks // 2, run_block, (zeros, zeros))
    between(0)
    _, log_sum = lax.fori_loop(blocks // 2, blocks, run_block, held)
    between(1)
    full_du = grad_du[...]
    gradu_ref[...] = full_du * step_size + skip_ref[...] * gy[...]
    grad_size = grad_step[...] + full_du * u_act
    grad_pre = grad_size * (1.0 - jnp.exp(-step_size))
    grad_low = grad_pre.astype(BF16)
    grad_step_w = contract_rows(proj_ref[:, :rank].astype(BF16), grad_low)
    packed = jnp.concatenate(
        [grad_step_w, log_sum, jnp.sum(grad_pre, 0, keepdims=True), grad_skip, zeros[:6]], 0
    )
    split_lanes(pack_ref, packed.astype(BF16))
    gradproj_ref[:, :rank] += times_transpose(grad_low, stepw_ref[...])

    @pl.when(tile_id == pl.num_programs(0) - 1)
    def _():
        own = iota((rows, big), 0) % BLOCK == iota((rows, big), 1) // state
        lane = iota((big, cols), 1)
        slot = iota((big, cols), 0) % state
        total = gradproj_ref[...]
        for sums_ref, first in ((b_sums, rank), (c_sums, rank + state)):
            place = (lane == first + slot).astype(F32)
            total = total + exact_product(jnp.where(own, sums_ref[...], 0.0), place)
        gradproj_ref[...] = total


def scan_backward(
    proj, step_w, vec, u_act, gate_in, out_w, grad_mix, step_size, mixed, hist, tile, devices
):
    rows, channels = u_act.shape
    gate_parts = tile * devices // (2 * channels)
    pack_parts = tile * devices // channels
    pack_rows = step_w.shape[0] + vec.shape[0]
    width = grad_mix.shape[1]
    cols = proj.shape[1]
    rank, state = step_w.shape[0], vec.shape[0] - 8
    steps = channels // tile
    big = BLOCK * state
    column = lambda i: (0, i)
    fixed = lambda i: (0, 0)
    return pl.pallas_call(
        scan_back_kernel,
        grid=(steps,),
        in_specs=[
            pl.BlockSpec((rows, cols), fixed),
            pl.BlockSpec((rank, tile), column),
            pl.BlockSpec((state, tile), column),
            pl.BlockSpec((8, tile), lambda i: ((vec.shape[0] - 8) // 8, i)),
            pl.BlockSpec((rows, tile), column),
            pl.BlockSpec((rows, tile), column),
            pl.BlockSpec((tile, width), lambda i: (i, 0)),
            pl.BlockSpec((rows, width), fixed),
            pl.BlockSpec((rows, tile), column),
            pl.BlockSpec((rows, tile), column),
            pl.BlockSpec((hist.shape[0], tile), column),
        ],
        out_specs=[
            pl.BlockSpec((rows, tile), column),
            pl.BlockSpec((gate_parts, rows, tile // gate_parts), lambda i: (i, 0, 0)),
            pl.BlockSpec((pack_parts, pack_rows, tile // pack_parts), lambda i: (i, 0, 0)),
            pl.BlockSpec((rows, cols), fixed),
        ],
        out_shape=[
            jax.ShapeDtypeStruct((rows, channels), F32),
            jax.ShapeDtypeStruct((devices // 2, rows, 2 * channels // devices), BF16),
            jax.ShapeDtypeStruct((devices, pack_rows, channels // devices), BF16),
            jax.ShapeDtypeStruct((rows, cols), F32),
        ],
        scratch_shapes=[
            pltpu.VMEM((rows * state, 128), F32),
            pltpu.VMEM((rows * 2, big), BF16),
            pltpu.VMEM((rows, big), F32),
            pltpu.VMEM((rows, big), F32),
            pltpu.VMEM((rows, tile), F32),
            pltpu.VMEM((rows, tile), F32),
            pltpu.VMEM((big, tile), BF16),
            pltpu.VMEM((big, tile), BF16),
            pltpu.VMEM((rows, tile), F32),
            pltpu.VMEM((rows, tile), F32),
        ],
        compiler_params=pltpu.CompilerParams(vmem_limit_bytes=VMEM_LIMIT),
        name="scan_backward",
    )(proj, step_w, vec, vec, u_act, gate_in, out_w, grad_mix, step_size, mixed, hist)


def back_kernel(
    gradproj_ref, scanw_ref, gradu_ref, xin_ref, misc_ref, gradgate_ref, wx_ref, wg_ref,
    u_ref, tokens_ref, gain_ref, gradmid_ref, widths_ref,
    gradx_ref, pack_ref, tail_ref, gradtok_ref,
    total,
):
    tile_id = pl.program_id(0)

    @pl.when(tile_id == 0)
    def _():
        total[...] = jnp.zeros_like(total)

    conv_ref, bias_ref = conv_rows(misc_ref)
    grad_proj = gradproj_ref[...].astype(BF16)
    grad_u = gradu_ref[...] + times_transpose(grad_proj, scanw_ref[...])
    pieces = [contract_rows(grad_proj, u_ref[...].astype(BF16))]
    x_inner = xin_ref[...]
    taps = conv_ref.shape[0]
    shifted = [shift_rows(x_inner, taps - 1 - tap) for tap in range(taps)]
    summed = bias_ref[...]
    for tap in range(taps):
        summed = summed + conv_ref[tap : tap + 1, :] * shifted[tap]
    sig = sigmoid(summed)
    grad_sum = grad_u * (sig * (1.0 + summed * (1.0 - sig)))
    grad_x = jnp.zeros_like(x_inner)
    for tap in range(taps):
        pieces.append(jnp.sum(grad_sum * shifted[tap], 0, keepdims=True))
        grad_x = grad_x + conv_ref[tap : tap + 1, :] * shift_rows(grad_sum, tap + 1 - taps)
    pieces.append(jnp.sum(grad_sum, 0, keepdims=True))
    pieces.append(jnp.zeros((pack_ref.shape[1] - grad_proj.shape[1] - taps - 1, x_inner.shape[1]), F32))
    split_lanes(pack_ref, jnp.concatenate(pieces, 0).astype(BF16))
    grad_x = grad_x.astype(BF16)
    split_lanes(gradx_ref, grad_x)
    grad_gate = jnp.concatenate([gradgate_ref[k] for k in range(gradgate_ref.shape[0])], 1)
    total[...] += product(grad_x, wx_ref[...]) + product(grad_gate, wg_ref[...])

    @pl.when(tile_id == pl.num_programs(0) - 1)
    def _():
        values = tokens_ref[...].astype(F32)
        scale = lax.rsqrt(jnp.mean(values * values, -1, keepdims=True) + 1e-05)
        unit = values * scale
        grad = total[...]
        widths = jnp.concatenate([widths_ref[...], jnp.sum(grad * unit, 0, keepdims=True)], 0)
        widths = jnp.concatenate(
            [widths, jnp.zeros((tail_ref.shape[1] - widths.shape[0], widths.shape[1]), F32)], 0
        )
        split_lanes(tail_ref, widths.astype(BF16))
        inner = grad * gain_ref[0:1, :]
        gradtok_ref[...] = gradmid_ref[...] + scale * (
            inner - unit * jnp.mean(inner * unit, -1, keepdims=True)
        )


def mixer_back(
    grad_proj, scan_w, grad_u, x_inner, vec, grad_gate, in_t, u_act, tokens, gains, grad_mid,
    grad_widths, tile, devices,
):
    rows, channels = u_act.shape
    gate_parts = tile * devices // (2 * channels)
    pack_parts = tile * devices // channels
    pack_rows = scan_w.shape[1] + 8
    tail_rows = grad_widths.shape[0] + 7
    width = tokens.shape[1]
    cols = scan_w.shape[1]
    steps = channels // tile
    column = lambda i: (0, i)
    fixed = lambda i: (0, 0)
    return pl.pallas_call(
        back_kernel,
        grid=(steps,),
        in_specs=[
            pl.BlockSpec((rows, cols), fixed),
            pl.BlockSpec((tile, cols), lambda i: (i, 0)),
            pl.BlockSpec((rows, tile), column),
            pl.BlockSpec((rows, tile), column),
            pl.BlockSpec((8, tile), lambda i: ((vec.shape[0] - 8) // 8, i)),
            pl.BlockSpec((gate_parts, rows, tile // gate_parts), lambda i: (i, 0, 0)),
            pl.BlockSpec((tile, width), lambda i: (i, 0)),
            pl.BlockSpec((tile, width), lambda i: (i + steps, 0)),
            pl.BlockSpec((rows, tile), column),
            pl.BlockSpec((rows, width), fixed),
            pl.BlockSpec(gains.shape, fixed),
            pl.BlockSpec((rows, width), fixed),
            pl.BlockSpec(grad_widths.shape, fixed),
        ],
        out_specs=[
            pl.BlockSpec((gate_parts, rows, tile // gate_parts), lambda i: (i, 0, 0)),
            pl.BlockSpec((pack_parts, pack_rows, tile // pack_parts), lambda i: (i, 0, 0)),
            pl.BlockSpec((devices, tail_rows, width // devices), lambda i: (0, 0, 0)),
            pl.BlockSpec((rows, width), fixed),
        ],
        out_shape=[
            jax.ShapeDtypeStruct((devices // 2, rows, 2 * channels // devices), BF16),
            jax.ShapeDtypeStruct((devices, pack_rows, channels // devices), BF16),
            jax.ShapeDtypeStruct((devices, tail_rows, width // devices), BF16),
            jax.ShapeDtypeStruct((rows, width), F32),
        ],
        scratch_shapes=[pltpu.VMEM((rows, width), F32)],
        compiler_params=pltpu.CompilerParams(vmem_limit_bytes=VMEM_LIMIT),
        name="mixer_back",
    )(
        grad_proj, scan_w, grad_u, x_inner, vec, grad_gate, in_t, in_t, u_act, tokens, gains,
        grad_mid, grad_widths,
    )


def gelu_parts(values):
    weight = jnp.exp(values * values * -0.5)
    scaled = jnp.abs(values) * 0.7071067811865476
    ratio = 1.0 / (1.0 + 0.3275911 * scaled)
    series = 1.061405429 * ratio - 1.453152027
    series = series * ratio + 1.421413741
    series = series * ratio - 0.284496736
    series = series * ratio + 0.254829592
    tail = (0.5 * ratio) * series * weight
    below = jnp.where(values >= 0.0, 1.0 - tail, tail)
    return values * below, below + values * weight * 0.3989422804014327


def router_kernel(
    mid_ref, gain_ref, router_ref, routes_col_ref, routes_row_ref, slots_row_ref, live_ref, cot_ref,
    sendr_ref, sendg_ref, normed_ref, probs_ref,
):
    mid = mid_ref[...]
    rows = mid.shape[0]
    experts = router_ref.shape[1]
    scale = lax.rsqrt(jnp.mean(mid * mid, -1, keepdims=True) + 1e-05)
    normed = (mid * scale * gain_ref[...]).astype(BF16)
    normed_ref[...] = normed
    logits = product(normed, router_ref[...])
    weights = jnp.exp(logits - jnp.max(logits, -1, keepdims=True))
    probs = weights / jnp.sum(weights, -1, keepdims=True)
    probs_ref[...] = probs
    chosen = (routes_col_ref[...] == iota((rows, experts), 1)).astype(F32)
    gate = jnp.sum(probs * chosen, 1, keepdims=True)
    grads = (gate * (cot_ref[...].astype(F32) * live_ref[...])).astype(BF16)
    slot = iota((experts * CAP, rows), 0)
    dispatch = (
        (routes_row_ref[...] == slot // CAP) & (slots_row_ref[...] == slot % CAP)
    ).astype(BF16)
    width = mid.shape[1]
    sendr_ref[...] = product(dispatch, normed).astype(BF16).reshape(experts, CAP, width)
    sendg_ref[...] = product(dispatch, grads).astype(BF16).reshape(experts, CAP, width)


def router_step(mid, gain, router, routes_col, routes_row, slots_row, live, cotangent):
    rows, width = mid.shape
    experts = router.shape[1]
    return pl.pallas_call(
        router_kernel,
        out_shape=[
            jax.ShapeDtypeStruct((experts, CAP, width), BF16),
            jax.ShapeDtypeStruct((experts, CAP, width), BF16),
            jax.ShapeDtypeStruct((rows, width), BF16),
            jax.ShapeDtypeStruct((rows, experts), F32),
        ],
        compiler_params=pltpu.CompilerParams(vmem_limit_bytes=VMEM_LIMIT),
        name="router_step",
    )(mid, gain, router, routes_col, routes_row, slots_row, live, cotangent)


def expert_out_kernel(rows_ref, up_ref, down_ref, out_ref, slope_ref, total):
    step = pl.program_id(0)
    pieces, cap, width = rows_ref.shape
    rows = rows_ref[...].reshape(pieces * cap, width)

    @pl.when(step == 0)
    def _():
        total[...] = jnp.zeros_like(total)

    activated, slope = gelu_parts(product(rows, up_ref[...]))
    slope_ref[...] = slope.astype(BF16)
    total[...] += product(activated.astype(BF16), down_ref[...])

    @pl.when(step == pl.num_programs(0) - 1)
    def _():
        out_ref[...] = total[...].astype(BF16).reshape(pieces, cap, width)


def expert_out(rows, up, down, tile):
    pieces, cap, width = rows.shape
    hidden = up.shape[1]
    fixed = lambda i: (0, 0, 0)
    return pl.pallas_call(
        expert_out_kernel,
        grid=(hidden // tile,),
        in_specs=[
            pl.BlockSpec(rows.shape, fixed),
            pl.BlockSpec((width, tile), lambda i: (0, i)),
            pl.BlockSpec((tile, width), lambda i: (i, 0)),
        ],
        out_specs=[
            pl.BlockSpec(rows.shape, fixed),
            pl.BlockSpec((pieces * cap, tile), lambda i: (0, i)),
        ],
        out_shape=[
            jax.ShapeDtypeStruct(rows.shape, BF16),
            jax.ShapeDtypeStruct((pieces * cap, hidden), BF16),
        ],
        scratch_shapes=[pltpu.VMEM((pieces * cap, width), F32)],
        compiler_params=pltpu.CompilerParams(vmem_limit_bytes=VMEM_LIMIT),
        name="expert_out",
    )(rows, up, down)


def expert_back_kernel(grads_ref, up_ref, down_ref, slope_ref, out_ref, total):
    step = pl.program_id(0)
    pieces, cap, width = grads_ref.shape
    grads = grads_ref[...].reshape(pieces * cap, width)

    @pl.when(step == 0)
    def _():
        total[...] = jnp.zeros_like(total)

    slope = slope_ref[...].astype(F32)
    grad_pre = (times_transpose(grads, down_ref[...]) * slope).astype(BF16)
    total[...] += times_transpose(grad_pre, up_ref[...])

    @pl.when(step == pl.num_programs(0) - 1)
    def _():
        out_ref[...] = total[...].astype(BF16).reshape(pieces, cap, width)


def expert_back(grads, up, down, slope, tile):
    pieces, cap, width = grads.shape
    hidden = up.shape[1]
    fixed = lambda i: (0, 0, 0)
    return pl.pallas_call(
        expert_back_kernel,
        grid=(hidden // tile,),
        in_specs=[
            pl.BlockSpec(grads.shape, fixed),
            pl.BlockSpec((width, tile), lambda i: (0, i)),
            pl.BlockSpec((tile, width), lambda i: (i, 0)),
            pl.BlockSpec((pieces * cap, tile), lambda i: (0, i)),
        ],
        out_specs=pl.BlockSpec(grads.shape, fixed),
        out_shape=jax.ShapeDtypeStruct(grads.shape, BF16),
        scratch_shapes=[pltpu.VMEM((pieces * cap, width), F32)],
        compiler_params=pltpu.CompilerParams(vmem_limit_bytes=VMEM_LIMIT),
        name="expert_back",
    )(grads, up, down, slope)


def expert_grads_kernel(chunks, rows_ref, grads_ref, up_ref, down_ref, gup_ref, gdown_ref, rows_t):
    chunk = pl.program_id(1)
    groups, pieces, cap, width = rows_ref.shape
    count = groups * pieces * cap
    rows = rows_ref[...].reshape(count, width)
    grads = grads_ref[...].reshape(count, width)

    @pl.when((pl.program_id(0) == 0) | (chunks > 1))
    def _():
        rows_t[...] = rows.T

    activated, slope = gelu_parts(product(rows, up_ref[...]))
    grad_pre = (times_transpose(grads, down_ref[...]) * slope).astype(BF16)
    grad_up = product(rows_t[...], grad_pre)
    grad_down = contract_rows(activated.astype(BF16), grads)

    @pl.when(chunk == 0)
    def _():
        gup_ref[...] = grad_up
        gdown_ref[...] = grad_down

    if chunks > 1:

        @pl.when(chunk > 0)
        def _():
            gup_ref[...] += grad_up
            gdown_ref[...] += grad_down


def expert_grads(rows, grads, up, down, tile):
    groups, pieces, cap, width = rows.shape
    hidden = up.shape[1]
    together = max(1, min(groups, 32 // pieces))
    chunks = groups // together
    some = pl.BlockSpec((together, pieces, cap, width), lambda i, j: (j, 0, 0, 0))
    return pl.pallas_call(
        partial(expert_grads_kernel, chunks),
        grid=(hidden // tile, chunks),
        in_specs=[
            some,
            some,
            pl.BlockSpec((width, tile), lambda i, j: (0, i)),
            pl.BlockSpec((tile, width), lambda i, j: (i, 0)),
        ],
        out_specs=[
            pl.BlockSpec((width, tile), lambda i, j: (0, i)),
            pl.BlockSpec((tile, width), lambda i, j: (i, 0)),
        ],
        out_shape=[
            jax.ShapeDtypeStruct((width, hidden), F32),
            jax.ShapeDtypeStruct((hidden, width), F32),
        ],
        scratch_shapes=[pltpu.VMEM((width, together * pieces * cap), BF16)],
        compiler_params=pltpu.CompilerParams(vmem_limit_bytes=VMEM_LIMIT),
        name="expert_grads",
    )(rows, grads, up, down)


def combine_kernel(
    mid_ref, gain_ref, router_ref, routes_ref, slots_ref, live_ref, cot_ref, probs_ref, normed_ref,
    backr_ref, backg_ref, out_ref, gradmid_ref, gradmix_ref, widths_ref,
):
    mid = mid_ref[...]
    rows, width = mid.shape
    experts = router_ref.shape[1]
    routes = routes_ref[...]
    chosen = (routes == iota((rows, experts), 1)).astype(F32)
    probs = probs_ref[...]
    gate = jnp.sum(probs * chosen, 1, keepdims=True)
    live = live_ref[...]
    slot = iota((rows, experts * CAP), 1)
    collect = ((routes == slot // CAP) & (slots_ref[...] == slot % CAP)).astype(BF16)
    expert_sum = product(collect, backr_ref[...].reshape(experts * CAP, width))
    out_ref[...] = (live * (mid + gate * expert_sum)).astype(BF16)
    grad_out = cot_ref[...].astype(F32) * live
    grad_gate = jnp.sum(grad_out * expert_sum, 1, keepdims=True)
    grad_logits = (probs * (chosen * grad_gate - gate * grad_gate)).astype(BF16)
    grad_router = contract_rows(grad_logits, normed_ref[...])
    grad = product(collect, backg_ref[...].reshape(experts * CAP, width))
    grad = grad + times_transpose(grad_logits, router_ref[...])
    scale = lax.rsqrt(jnp.mean(mid * mid, -1, keepdims=True) + 1e-05)
    unit = mid * scale
    widths_ref[...] = jnp.concatenate([grad_router, jnp.sum(grad * unit, 0, keepdims=True)], 0)
    inner = grad * gain_ref[...]
    grad_mid = grad_out + scale * (inner - unit * jnp.mean(inner * unit, -1, keepdims=True))
    gradmid_ref[...] = grad_mid
    gradmix_ref[...] = grad_mid.astype(BF16)


def combine_step(mid, gain, router, routes, slots, live, cotangent, probs, normed, backr, backg):
    rows, width = mid.shape
    return pl.pallas_call(
        combine_kernel,
        out_shape=[
            jax.ShapeDtypeStruct((rows, width), BF16),
            jax.ShapeDtypeStruct((rows, width), F32),
            jax.ShapeDtypeStruct((rows, width), BF16),
            jax.ShapeDtypeStruct((router.shape[1] + 1, width), F32),
        ],
        compiler_params=pltpu.CompilerParams(vmem_limit_bytes=VMEM_LIMIT),
        name="combine_step",
    )(mid, gain, router, routes, slots, live, cotangent, probs, normed, backr, backg)


MESH = pl.DeviceIdType.MESH


def neighbour(bit):
    me = lax.axis_index("expert")
    return me + (1 - 2 * ((me // bit) % 2)) * bit


def greet(line=True):
    devices, copies = lax.axis_size("expert"), lax.axis_size("dp")
    me, place = lax.axis_index("expert"), lax.axis_index("dp")
    barrier = pltpu.get_barrier_semaphore()
    for k in range(1, devices):
        pl.semaphore_signal(
            barrier, inc=1, device_id={"expert": (me + k) % devices}, device_id_type=MESH
        )
    if line:

        @pl.when(place < copies - 1)
        def _():
            pl.semaphore_signal(barrier, inc=1, device_id={"dp": place + 1}, device_id_type=MESH)

        @pl.when(place > 0)
        def _():
            pl.semaphore_signal(barrier, inc=1, device_id={"dp": place - 1}, device_id_type=MESH)

    ends = (place == 0) | (place == copies - 1)
    if line:
        pl.when(ends)(lambda: pl.semaphore_wait(barrier, devices))
        pl.when(jnp.logical_not(ends))(lambda: pl.semaphore_wait(barrier, devices + 1))
    else:
        pl.semaphore_wait(barrier, devices - 1)


class Exchange:
    def __init__(self, source, target, send_sems, recv_sems, local_sem):
        devices, me = lax.axis_size("expert"), lax.axis_index("expert")
        self.copies = []
        for k in range(1, devices):
            peer = (me + k) % devices
            self.copies.append(
                pltpu.make_async_remote_copy(
                    source.at[peer], target.at[me], send_sems.at[k], recv_sems.at[k],
                    device_id={"expert": peer}, device_id_type=MESH,
                )
            )
        self.local = pltpu.make_async_copy(source.at[me], target.at[me], local_sem)

    def start(self):
        for copy in self.copies:
            copy.start()
        self.local.start()

    def wait(self):
        self.local.wait()
        for copy in self.copies:
            copy.wait()


class Line:
    def __init__(self, stage, from_left, from_right, next_left, next_right, send_sems, recv_sems):
        place = lax.axis_index("dp")
        last = lax.axis_size("dp") - 1
        self.right = pltpu.make_async_remote_copy(
            from_left, next_left, send_sems.at[0], recv_sems.at[0],
            device_id={"dp": jnp.minimum(place + 1, last)}, device_id_type=MESH,
        )
        self.left = pltpu.make_async_remote_copy(
            from_right, next_right, send_sems.at[1], recv_sems.at[1],
            device_id={"dp": jnp.maximum(place - 1, 0)}, device_id_type=MESH,
        )
        self.send_right = (place >= stage - 1) & (place < last)
        self.send_left = (last - place >= stage - 1) & (place > 0)
        self.get_left = place >= stage
        self.get_right = last - place >= stage

    def start(self):
        pl.when(self.send_right)(lambda: self.right.start())
        pl.when(self.send_left)(lambda: self.left.start())

    def wait(self):
        pl.when(self.send_right)(lambda: self.right.wait_send())
        pl.when(self.send_left)(lambda: self.left.wait_send())
        pl.when(self.get_left)(lambda: self.right.wait_recv())
        pl.when(self.get_right)(lambda: self.left.wait_recv())


def as_column(row):
    return jnp.broadcast_to(row.astype(F32), (8, row.shape[1])).T[:, 0:1].astype(jnp.int32)


def dispatch_matrix(goal, experts):
    slot = iota((experts * CAP, goal.shape[1]), 0)
    return (goal[0:1, :] == slot).astype(BF16)


def expert_layer_kernel(
    length_ref, mid_ref, gains_ref, router_ref, routes_ref, slots_ref, cot_ref, up_hbm, down_hbm,
    out_ref, gradmid_ref, gradmix_ref, widths_ref, rows_out, grads_out,
    left_1, right_1, left_2, right_2, goal_l1, goal_r1, goal_l2, goal_r2, gup_hbm, gdown_hbm,
    raw, goal, up_ref, down_ref, send_r, send_g, got_r, got_g, slope_ref, total, give_r, give_g,
    back_r, back_g, probs_ref, act_ref, rows_t, gup_ref, gdown_ref,
    weight_sems, send_sems, recv_sems, local_sems, line_send, line_recv, out_sems, grad_sems,
):
    tile = 512
    rows, width = mid_ref.shape
    experts = router_ref.shape[0]
    hidden = up_ref.shape[1]
    load_up = pltpu.make_async_copy(up_hbm, up_ref, weight_sems.at[0])
    load_down = pltpu.make_async_copy(down_hbm, down_ref, weight_sems.at[1])
    load_up.start()
    load_down.start()
    greet()

    ways = [
        Exchange(source, target, send_sems.at[k], recv_sems.at[k], local_sems.at[k])
        for k, (source, target) in enumerate(
            [(send_r, got_r), (send_g, got_g), (give_r, back_r), (give_g, back_g)]
        )
    ]
    lines = [
        Line(stage, *buffers, line_send.at[k], line_recv.at[k])
        for k, (stage, buffers) in enumerate(
            [(1, (raw.at[part], raw.at[part], left_1.at[part], right_1.at[part])) for part in (0, 1)]
            + [(1, (goal, goal, goal_l1, goal_r1))]
            + [
                (2, (left_1.at[part], right_1.at[part], left_2.at[part], right_2.at[part]))
                for part in (0, 1)
            ]
            + [(2, (goal_l1, goal_r1, goal_l2, goal_r2))]
        )
    ]
    gain = gains_ref[1:2, :]
    live = (iota((rows, 1), 0) < length_ref[0]).astype(F32)
    routes, slots = as_column(routes_ref[...]), as_column(slots_ref[...])
    mid = mid_ref[...]
    scale = lax.rsqrt(jnp.mean(mid * mid, -1, keepdims=True) + 1e-05)
    normed = (mid * scale * gain).astype(BF16)
    raw[0] = normed
    slots_row = slots_ref[...]
    target = jnp.where(slots_row < CAP, routes_ref[...] * CAP + slots_row, -1)
    goal[...] = jnp.broadcast_to(target, goal.shape)
    dispatch = dispatch_matrix(goal, experts)
    send_r[...] = product(dispatch, normed).astype(BF16).reshape(experts, CAP, width)
    ways[0].start()
    for k in (0, 2):
        lines[k].start()
    logits = times_transpose(normed, router_ref[...])
    weights = jnp.exp(logits - jnp.max(logits, -1, keepdims=True))
    probs = weights / jnp.sum(weights, -1, keepdims=True)
    probs_ref[...] = probs
    chosen = (routes == iota((rows, experts), 1)).astype(F32)
    gate = jnp.sum(probs * chosen, 1, keepdims=True)
    grads = (gate * (cot_ref[...].astype(F32) * live)).astype(BF16)
    raw[1] = grads
    send_g[...] = product(dispatch, grads).astype(BF16).reshape(experts, CAP, width)
    ways[1].start()
    lines[1].start()

    load_up.wait()
    load_down.wait()
    ways[0].wait()
    for k in (0, 2):
        lines[k].wait()
        lines[k + 3].start()
    keep_rows = pltpu.make_async_copy(got_r, rows_out, out_sems.at[0])
    keep_rows.start()
    total[...] = jnp.zeros_like(total)

    def forward(step, carry):
        at = pl.ds(pl.multiple_of(step * tile, tile), tile)
        inputs = got_r[...].reshape(experts * CAP, width)
        activated, slope = gelu_parts(product(inputs, up_ref[:, at]))
        slope_ref[:, at] = slope.astype(BF16)
        activated = activated.astype(BF16)
        act_ref[:, at] = activated
        total[...] += product(activated, down_ref[at, :])
        return carry

    lax.fori_loop(0, hidden // tile, forward, 0)
    give_r[...] = total[...].astype(BF16).reshape(experts, CAP, width)
    ways[2].start()
    ways[1].wait()
    lines[1].wait()
    lines[4].start()
    keep_grads = pltpu.make_async_copy(got_g, grads_out, out_sems.at[1])
    keep_grads.start()
    total[...] = jnp.zeros_like(total)

    def backward(step, carry):
        at = pl.ds(pl.multiple_of(step * tile, tile), tile)
        outputs = got_g[...].reshape(experts * CAP, width)
        slope = slope_ref[:, at].astype(F32)
        grad_pre = (times_transpose(outputs, down_ref[at, :]) * slope).astype(BF16)
        slope_ref[:, at] = grad_pre
        total[...] += times_transpose(grad_pre, up_ref[:, at])
        return carry

    lax.fori_loop(0, hidden // tile, backward, 0)
    give_g[...] = total[...].astype(BF16).reshape(experts, CAP, width)
    ways[3].start()

    rows_t[...] = got_r[...].reshape(experts * CAP, width).T
    stores = []
    for step in range(hidden // tile):
        spot = step % 2
        at = pl.ds(step * tile, tile)
        if step >= 2:
            for store in stores[2 * (step - 2) : 2 * (step - 1)]:
                store.wait()
        gup_ref[spot] = product(rows_t[...], slope_ref[:, at]).astype(BF16)
        gdown_ref[spot] = contract_rows(
            act_ref[:, at], got_g[...].reshape(experts * CAP, width)
        ).astype(BF16)
        stores += [
            pltpu.make_async_copy(gup_ref.at[spot], gup_hbm.at[:, at], grad_sems.at[0, spot]),
            pltpu.make_async_copy(gdown_ref.at[spot], gdown_hbm.at[at], grad_sems.at[1, spot]),
        ]
        for store in stores[-2:]:
            store.start()

    chosen = (routes == iota((rows, experts), 1)).astype(F32)
    probs = probs_ref[...]
    gate = jnp.sum(probs * chosen, 1, keepdims=True)
    slot = iota((rows, experts * CAP), 1)
    collect = ((routes == slot // CAP) & (slots == slot % CAP)).astype(BF16)
    ways[2].wait()
    expert_sum = product(collect, back_r[...].reshape(experts * CAP, width))
    mid = mid_ref[...]
    out_ref[...] = (live * (mid + gate * expert_sum)).astype(BF16)
    grad_out = cot_ref[...].astype(F32) * live
    grad_gate = jnp.sum(grad_out * expert_sum, 1, keepdims=True)
    grad_logits = (probs * (chosen * grad_gate - gate * grad_gate)).astype(BF16)
    grad_router = contract_rows(grad_logits, raw[0])
    from_logits = product(grad_logits, router_ref[...])
    scale = lax.rsqrt(jnp.mean(mid * mid, -1, keepdims=True) + 1e-05)
    unit = mid * scale
    ways[3].wait()
    grad = product(collect, back_g[...].reshape(experts * CAP, width)) + from_logits
    widths_ref[...] = jnp.concatenate([grad_router, jnp.sum(grad * unit, 0, keepdims=True)], 0)
    inner = grad * gain
    grad_mid = grad_out + scale * (inner - unit * jnp.mean(inner * unit, -1, keepdims=True))
    gradmid_ref[...] = grad_mid
    gradmix_ref[...] = grad_mid.astype(BF16)
    for store in stores[-4:]:
        store.wait()
    keep_rows.wait()
    keep_grads.wait()
    for k in (3, 4, 5):
        lines[k].wait()


def expert_layer(lengths, mid, gains, router, routes, slots, cotangent, up, down):
    rows, width = mid.shape
    experts = router.shape[0]
    hidden = up.shape[1]
    buffer = (experts, CAP, width)
    here = pl.BlockSpec(memory_space=pltpu.VMEM)
    far = pl.BlockSpec(memory_space=pl.ANY)
    blocks = jax.ShapeDtypeStruct(buffer, BF16)
    raw = jax.ShapeDtypeStruct((2, rows, width), BF16)
    goal = jax.ShapeDtypeStruct((8, rows), jnp.int32)
    dma = pltpu.SemaphoreType.DMA
    return pl.pallas_call(
        expert_layer_kernel,
        in_specs=[pl.BlockSpec(memory_space=pltpu.SMEM)] + [here] * 6 + [far] * 2,
        out_specs=[here] * 4 + [far] * 12,
        out_shape=[
            jax.ShapeDtypeStruct((rows, width), BF16),
            jax.ShapeDtypeStruct((rows, width), F32),
            jax.ShapeDtypeStruct((rows, width), BF16),
            jax.ShapeDtypeStruct((experts + 1, width), F32),
        ] + [blocks] * 2 + [raw] * 4 + [goal] * 4 + [
            jax.ShapeDtypeStruct(up.shape, BF16),
            jax.ShapeDtypeStruct(down.shape, BF16),
        ],
        scratch_shapes=[
            pltpu.VMEM(raw.shape, BF16),
            pltpu.VMEM(goal.shape, jnp.int32),
            pltpu.VMEM(up.shape, BF16),
            pltpu.VMEM(down.shape, BF16),
        ] + [pltpu.VMEM(buffer, BF16)] * 4 + [
            pltpu.VMEM((experts * CAP, hidden), BF16),
            pltpu.VMEM((experts * CAP, width), F32),
        ] + [pltpu.VMEM(buffer, BF16)] * 4 + [
            pltpu.VMEM((rows, experts), F32),
            pltpu.VMEM((experts * CAP, hidden), BF16),
            pltpu.VMEM((width, experts * CAP), BF16),
            pltpu.VMEM((2, width, 512), BF16),
            pltpu.VMEM((2, 512, width), BF16),
            dma((2,)), dma((4, experts)), dma((4, experts)), dma((4,)), dma((6, 2)), dma((6, 2)),
            dma((2,)), dma((2, 2)),
        ],
        compiler_params=pltpu.CompilerParams(
            vmem_limit_bytes=VMEM_LIMIT, collective_id=1, has_side_effects=True
        ),
        name="expert_layer",
    )(lengths, mid, gains, router, routes, slots, cotangent, up, down)


class PlaneGather:
    def __init__(self, source, target, send_sems, recv_sems, local_sem):
        me = lax.axis_index("expert")
        core, side, above = neighbour(1), neighbour(2), neighbour(4)
        far = side + above - me
        rows = target.shape[1]
        first, second = pl.ds(0, rows // 2), pl.ds(rows // 2, rows - rows // 2)
        every = pl.ds(0, rows)

        def send(k, block, owner, part, device):
            return pltpu.make_async_remote_copy(
                block, target.at[owner, part], send_sems.at[k], recv_sems.at[k],
                device_id={"expert": device}, device_id_type=MESH,
            )

        self.copies = [
            send(0, source.at[first], me, first, side),
            send(1, source.at[second], me, second, side),
            send(2, source.at[first], me, first, above),
            send(3, source.at[second], me, second, above),
            send(4, target.at[side, first], side, first, above),
            send(5, target.at[above, second], above, second, side),
            send(6, source, me, every, core),
            send(7, target.at[side], side, every, core),
            send(8, target.at[above], above, every, core),
            send(9, target.at[far], far, every, core),
        ]
        self.local = pltpu.make_async_copy(source, target.at[me], local_sem)

    def step(self, number):
        copies = self.copies
        for k in ((), (0, 3), (1, 2), (4, 5), (6, 7, 8, 9))[number]:
            copies[k].wait_recv()
        for k in ((0, 3, 1, 2, 6), (4, 5), (7, 8), (9,), ())[number]:
            copies[k].start()
        if number == 0:
            self.local.start()
        if number == 4:
            self.local.wait()
            for copy in copies:
                copy.wait_send()


class Spread:
    def __init__(self, source, target, send_sems, recv_sems, local_sem):
        devices, me = lax.axis_size("expert"), lax.axis_index("expert")
        self.copies = [
            pltpu.make_async_remote_copy(
                source, target.at[me], send_sems.at[k], recv_sems.at[k],
                device_id={"expert": (me + k) % devices}, device_id_type=MESH,
            )
            for k in range(1, devices)
        ]
        self.local = pltpu.make_async_copy(source, target.at[me], local_sem)

    start, wait = Exchange.start, Exchange.wait


class Near:
    def __init__(self, own, target, send_sems, recv_sems):
        self.place = lax.axis_index("dp")
        self.last = lax.axis_size("dp") - 1
        self.right = pltpu.make_async_remote_copy(
            own, target, send_sems.at[0], recv_sems.at[0],
            device_id={"dp": jnp.minimum(self.place + 1, self.last)}, device_id_type=MESH,
        )
        self.left = pltpu.make_async_remote_copy(
            own, target, send_sems.at[1], recv_sems.at[1],
            device_id={"dp": jnp.maximum(self.place - 1, 0)}, device_id_type=MESH,
        )

    def start(self):
        pl.when(self.place < self.last)(lambda: self.right.start())
        pl.when(self.place == 1)(lambda: self.left.start())

    def wait(self):
        pl.when(self.place < self.last)(lambda: self.right.wait_send())
        pl.when(self.place == 1)(lambda: self.left.wait_send())
        pl.when(self.place > 0)(lambda: self.right.wait_recv())
        pl.when(self.place == 0)(lambda: self.left.wait_recv())


DMA = pltpu.SemaphoreType.DMA
FAR = pl.BlockSpec(memory_space=pl.ANY)


def remote_params(collective_id):
    return pltpu.CompilerParams(
        vmem_limit_bytes=VMEM_LIMIT, collective_id=collective_id, has_side_effects=True
    )


def gather_kernel(
    in_ref, scan_ref, step_ref, decay_ref, conv_ref, vectors_ref, norms_ref, router_ref,
    in_full, scan_full, step_full, vec_ref, router_full, gains_ref,
    columns, widths, columns_all, widths_all, send_sems, recv_sems, local_sems,
):
    devices, rank, part = columns_all.shape[0], step_ref.shape[0], step_ref.shape[1]
    state, taps, experts = decay_ref.shape[0], conv_ref.shape[0], router_ref.shape[0]
    slice_w = widths.shape[1]
    greet(line=False)
    spare = columns.shape[0] - rank - state - taps - 3
    columns[...] = jnp.concatenate(
        [
            step_ref[...].astype(F32), decay_ref[...].astype(F32), conv_ref[...].astype(F32),
            vectors_ref[...].astype(F32), jnp.zeros((spare, part), F32),
        ],
        0,
    ).astype(BF16)
    widths[...] = jnp.concatenate(
        [
            router_ref[...].astype(F32), norms_ref[...].astype(F32),
            jnp.zeros((widths.shape[0] - experts - 2, slice_w), F32),
        ],
        0,
    ).astype(BF16)
    small = [
        PlaneGather(source, target, send_sems.at[k], recv_sems.at[k], local_sems.at[k])
        for k, (source, target) in enumerate(
            [(columns, columns_all), (widths, widths_all), (scan_ref, scan_full)]
        )
    ]
    big = PlaneGather(in_ref, in_full, send_sems.at[3], recv_sems.at[3], local_sems.at[3])
    for number in range(3):
        for one in small:
            one.step(number)
        big.step(number)
    for number in (3, 4):
        for one in small:
            one.step(number)
    table = jnp.concatenate([columns_all[k].astype(F32) for k in range(devices)], 1)
    step_full[...] = table[:rank].astype(BF16)
    rest = table[rank:]
    vec_ref[0:state, :] = -jnp.exp(rest[:state])
    vec_ref[state : state + 8, :] = rest[state : state + 8]
    across = jnp.concatenate([widths_all[k].astype(F32) for k in range(devices)], 1)
    router_full[...] = across[:experts].astype(BF16)
    gains_ref[...] = across[experts : experts + 8]
    for number in (3, 4):
        big.step(number)


def gather_weights(in_t, scan_w, step_w, decay_t, conv, vectors, norms, router_t):
    devices = lax.axis_size("expert")
    rank, part = step_w.shape
    state, experts, slice_w = decay_t.shape[0], router_t.shape[0], router_t.shape[1]
    channels = devices * part
    here = pl.BlockSpec(memory_space=pltpu.VMEM)
    return pl.pallas_call(
        gather_kernel,
        in_specs=[here] * 8,
        out_specs=[FAR] * 2 + [here] * 4,
        out_shape=[
            jax.ShapeDtypeStruct((devices,) + in_t.shape, BF16),
            jax.ShapeDtypeStruct((devices,) + scan_w.shape, BF16),
            jax.ShapeDtypeStruct((rank, channels), BF16),
            jax.ShapeDtypeStruct((state + 8, channels), F32),
            jax.ShapeDtypeStruct((experts, devices * slice_w), BF16),
            jax.ShapeDtypeStruct((8, devices * slice_w), F32),
        ],
        scratch_shapes=[
            pltpu.VMEM((rank + state + 8, part), BF16),
            pltpu.VMEM((32, slice_w), BF16),
            pltpu.VMEM((devices, rank + state + 8, part), BF16),
            pltpu.VMEM((devices, 32, slice_w), BF16),
            DMA((4, 10)), DMA((4, 10)), DMA((4,)),
        ],
        compiler_params=remote_params(2),
        name="gather_weights",
    )(in_t, scan_w, step_w, decay_t, conv, vectors, norms, router_t)


def scan_plane_kernel(
    proj_ref, stepw_ref, decay_ref, misc_ref, u_ref, gate_ref, tokens_ref, normed_ref, outw_ref,
    step_ref, mixed_ref, gated_ref, hist_ref, mid_ref, outw_all, normed_all,
    b_wide, c_blocks, du, scanned, gated_all, outw_here, send_sems, recv_sems, local_sems,
):
    tile_id = pl.program_id(0)
    rank, state = stepw_ref.shape[0], decay_ref.shape[0]
    tile = u_ref.shape[1]
    gather = PlaneGather(
        outw_ref, outw_here, send_sems.at[0], recv_sems.at[0], local_sems.at[0]
    )
    normed = PlaneGather(
        normed_ref.at[pl.ds(0, normed_all.shape[1])], normed_all, send_sems.at[1],
        recv_sems.at[1], local_sems.at[2],
    )
    keep = pltpu.make_async_copy(outw_here, outw_all, local_sems.at[1])

    @pl.when(tile_id == 0)
    def _():
        greet(line=False)
        gather.step(0)
        scan_prepare(proj_ref, b_wide, c_blocks, rank, rank + state, state)

    def between(half):
        for turn in range(2):

            @pl.when(tile_id == turn)
            def _():
                gather.step(2 * turn + half + 1)
                normed.step(2 * turn + half)
                if turn + half == 2:
                    keep.start()

    gated = scan_tile(
        proj_ref, stepw_ref, decay_ref, misc_ref, u_ref, gate_ref, step_ref, mixed_ref, hist_ref,
        b_wide, c_blocks, du, scanned, between,
    )
    gated_ref[...] = gated.T.reshape(gated_ref.shape)
    gated_all[:, pl.ds(pl.multiple_of(tile_id * tile, tile), tile)] = gated

    @pl.when(tile_id == 1)
    def _():
        devices, part, width = outw_here.shape
        weights = outw_here[...].reshape(devices * part, width)
        mid_ref[...] = tokens_ref[...].astype(F32) + product(gated_all[...], weights)
        keep.wait()
        normed.step(4)


def scan_forward_plane(proj, step_w, vec, u_act, gate_in, out_w, tokens, normed_low):
    rows, channels = u_act.shape
    width = tokens.shape[1]
    cols = proj.shape[1]
    rank, state = step_w.shape[0], vec.shape[0] - 8
    devices = lax.axis_size("expert")
    tile = channels // 2
    part = channels // devices
    hist_rows = (rows + 1) * state
    column = lambda i: (0, i)
    fixed = lambda i: (0, 0)
    return pl.pallas_call(
        scan_plane_kernel,
        grid=(2,),
        in_specs=[
            pl.BlockSpec((rows, cols), fixed),
            pl.BlockSpec((rank, tile), column),
            pl.BlockSpec((state, tile), column),
            pl.BlockSpec((8, tile), lambda i: (state // 8, i)),
            pl.BlockSpec((rows, tile), column),
            pl.BlockSpec((rows, tile), column),
            pl.BlockSpec((rows, width), fixed),
            pl.BlockSpec((rows, width), fixed),
            FAR,
        ],
        out_specs=[
            pl.BlockSpec((rows, tile), column),
            pl.BlockSpec((rows, tile), column),
            pl.BlockSpec((devices // 2, part, rows), lambda i: (i, 0, 0)),
            pl.BlockSpec((hist_rows, tile), column),
            pl.BlockSpec((rows, width), fixed),
            FAR,
            FAR,
        ],
        out_shape=[
            jax.ShapeDtypeStruct((rows, channels), F32),
            jax.ShapeDtypeStruct((rows, channels), F32),
            jax.ShapeDtypeStruct((devices, part, rows), BF16),
            jax.ShapeDtypeStruct((hist_rows, channels), BF16),
            jax.ShapeDtypeStruct((rows, width), F32),
            jax.ShapeDtypeStruct((devices, part, width), BF16),
            jax.ShapeDtypeStruct((devices, rows // 2, width), BF16),
        ],
        scratch_shapes=[
            pltpu.VMEM((rows * state, 128), F32),
            pltpu.VMEM((rows * 2, BLOCK * state), BF16),
            pltpu.VMEM((rows, tile), F32),
            pltpu.VMEM((rows, tile), F32),
            pltpu.VMEM((rows, channels), BF16),
            pltpu.VMEM((devices, part, width), BF16),
            DMA((2, 10)), DMA((2, 10)), DMA((3,)),
        ],
        compiler_params=remote_params(3),
        name="scan_forward_plane",
    )(proj, step_w, vec, vec, u_act, gate_in, tokens, normed_low, out_w)


class Dispatch:
    def __init__(self, raw, goal, sends, targets, send_sems, recv_sems, local_sems):
        self.raw, self.goal, self.sends = raw, goal, sends
        self.ways = [
            Exchange(sends.at[k], out, send_sems.at[k], recv_sems.at[k], local_sems.at[k])
            for k, out in enumerate(targets)
        ]

    def prepare(self, parts):
        experts, cap, width = self.sends.shape[1:]
        matrix = dispatch_matrix(self.goal, experts)
        for k, part in enumerate(parts):
            values = product(matrix, self.raw[part]).astype(BF16)
            self.sends[k] = values.reshape(experts, cap, width)

    def start(self):
        for way in self.ways:
            way.start()

    def wait(self):
        for way in self.ways:
            way.wait()


def pick(choices, raw, goal, sems):
    place = lax.axis_index("dp")
    for where, (source, source_goal) in enumerate(choices):

        @pl.when(place == where)
        def _():
            copies = [
                pltpu.make_async_copy(source, raw, sems.at[0]),
                pltpu.make_async_copy(source_goal, goal, sems.at[1]),
            ]
            for copy in copies:
                copy.start()
            for copy in copies:
                copy.wait()


def scan_back_plane_kernel(*refs):
    inputs, refs = refs[:11], refs[11:]
    (normed_ref, gated_ref, rows_0, left_2, right_2, goal_l2, goal_r2), refs = refs[:7], refs[7:]
    outputs, refs = refs[:4], refs[4:]
    (parts_ref, mix_all, normed_all, gated_all, rows_1, left_3, right_3, goal_l3, goal_r3), refs = (
        refs[:9], refs[9:]
    )
    scratch, refs = refs[:10], refs[10:]
    g_send, g_recv, x_send, x_recv, l_send, l_recv, local_sems = refs
    mix_ref = inputs[7]
    half_rows = normed_all.shape[1]
    near_rows = rows_1.shape[0]
    tile_id = pl.program_id(0)
    mix = PlaneGather(mix_ref, mix_all, g_send.at[0], g_recv.at[0], local_sems.at[0])
    normed = PlaneGather(
        normed_ref.at[pl.ds(half_rows, half_rows)], normed_all, g_send.at[1], g_recv.at[1],
        local_sems.at[1],
    )
    gated = Exchange(gated_ref, gated_all, x_send, x_recv, local_sems.at[2])
    lines = [
        Line(3, left_2, right_2, left_3, right_3, l_send.at[0], l_recv.at[0]),
        Line(3, goal_l2, goal_r2, goal_l3, goal_r3, l_send.at[1], l_recv.at[1]),
        Near(rows_0.at[pl.ds(0, near_rows)], rows_1, l_send.at[2], l_recv.at[2]),
    ]

    @pl.when(tile_id == 0)
    def _():
        greet()
        for line in lines:
            line.start()
        mix.step(0)

    def between(half):
        @pl.when((tile_id == 0) & (half == 0))
        def _():
            mix.step(1)
            gated.start()

        @pl.when((tile_id == 0) & (half == 1))
        def _():
            mix.step(2)
            normed.step(0)

        @pl.when((tile_id == 1) & (half == 0))
        def _():
            mix.step(3)
            normed.step(1)

        @pl.when((tile_id == 1) & (half == 1))
        def _():
            mix.step(4)
            normed.step(2)
            for line in lines:
                line.wait()
            gated.wait()
            normed.step(3)
            normed.step(4)

    def put_gate(out_ref, value):
        out_ref[...] = value
        parts_ref[...] = value.T.reshape(parts_ref.shape)

    scan_back_tile(between, put_gate, *inputs, *outputs, *scratch)


def scan_backward_plane(
    proj, step_w, vec, u_act, gate_in, out_w, grad_mix, step_size, mixed, hist, normed_low, gated,
    rows_0, raws, goals,
):
    rows, channels = u_act.shape
    width = grad_mix.shape[1]
    cols = proj.shape[1]
    rank, state = step_w.shape[0], vec.shape[0] - 8
    devices = lax.axis_size("expert")
    tile = channels // 2
    gate_parts, pack_parts = devices // 4, devices // 2
    pack_rows = rank + state + 8
    big = BLOCK * state
    column = lambda i: (0, i)
    fixed = lambda i: (0, 0)
    slots = jax.ShapeDtypeStruct((devices // 2, CAP, width), BF16)
    raw = jax.ShapeDtypeStruct(raws[0].shape, BF16)
    goal = jax.ShapeDtypeStruct(goals[0].shape, jnp.int32)
    return pl.pallas_call(
        scan_back_plane_kernel,
        grid=(2,),
        in_specs=[
            pl.BlockSpec((rows, cols), fixed),
            pl.BlockSpec((rank, tile), column),
            pl.BlockSpec((state, tile), column),
            pl.BlockSpec((8, tile), lambda i: (state // 8, i)),
            pl.BlockSpec((rows, tile), column),
            pl.BlockSpec((rows, tile), column),
            pl.BlockSpec((tile, width), lambda i: (i, 0)),
            pl.BlockSpec((rows, width), fixed),
            pl.BlockSpec((rows, tile), column),
            pl.BlockSpec((rows, tile), column),
            pl.BlockSpec((hist.shape[0], tile), column),
            pl.BlockSpec((rows, width), fixed),
            pl.BlockSpec(gated.shape, lambda i: (0, 0, 0)),
        ] + [FAR] * 5,
        out_specs=[
            pl.BlockSpec((rows, tile), column),
            pl.BlockSpec((rows, tile), column),
            pl.BlockSpec((pack_parts, pack_rows, tile // pack_parts), lambda i: (i, 0, 0)),
            pl.BlockSpec((rows, cols), fixed),
            pl.BlockSpec((gate_parts, tile // gate_parts, rows), lambda i: (i, 0, 0)),
        ] + [FAR] * 8,
        out_shape=[
            jax.ShapeDtypeStruct((rows, channels), F32),
            jax.ShapeDtypeStruct((rows, channels), BF16),
            jax.ShapeDtypeStruct((devices, pack_rows, channels // devices), BF16),
            jax.ShapeDtypeStruct((rows, cols), F32),
            jax.ShapeDtypeStruct((devices // 2, 2 * channels // devices, rows), BF16),
            jax.ShapeDtypeStruct((devices, rows, width), BF16),
            jax.ShapeDtypeStruct((devices, rows // 2, width), BF16),
            jax.ShapeDtypeStruct(gated.shape, BF16),
            slots, raw, raw, goal, goal,
        ],
        scratch_shapes=[
            pltpu.VMEM((rows * state, 128), F32),
            pltpu.VMEM((rows * 2, big), BF16),
            pltpu.VMEM((rows, big), F32),
            pltpu.VMEM((rows, big), F32),
            pltpu.VMEM((rows, tile), F32),
            pltpu.VMEM((rows, tile), F32),
            pltpu.VMEM((big, tile), BF16),
            pltpu.VMEM((big, tile), BF16),
            pltpu.VMEM((rows, tile), F32),
            pltpu.VMEM((rows, tile), F32),
            DMA((2, 10)), DMA((2, 10)), DMA((devices,)), DMA((devices,)), DMA((3, 2)), DMA((3, 2)),
            DMA((3,)),
        ],
        compiler_params=remote_params(4),
        name="scan_backward_plane",
    )(
        proj, step_w, vec, vec, u_act, gate_in, out_w, grad_mix, step_size, mixed, hist,
        normed_low, gated, rows_0, raws[2], raws[3], goals[2], goals[3],
    )


def back_plane_kernel(
    gradproj_ref, scanw_ref, gradu_ref, xin_ref, misc_ref, wx_ref, wg_ref, u_ref,
    tokens_ref, gain_ref, gradmid_ref, widths_ref, gradgate_ref,
    gate_hbm, scan_parts, normed_low, normed_high, mix_hbm, gated_hbm, rows_0, grads_0,
    gradtok_ref, totals_ref, rows_1, grads_1,
    total, send_in, got_in, normed_all, mix_all, gated_all, got_scan, send_back, got_back,
    send_tail, got_tail, x_send, x_recv, l_send, l_recv, local_sems, load_sems,
):
    tile_id = pl.program_id(0)
    devices, me = lax.axis_size("expert"), lax.axis_index("expert")
    half = devices // 2
    gates = send_in.shape[0] // 4
    ways = [
        Exchange(source, target, x_send.at[k], x_recv.at[k], local_sems.at[k])
        for k, (source, target) in enumerate(
            [
                (send_in, got_in), (scan_parts, got_scan), (send_back, got_back),
                (send_tail, got_tail),
            ]
        )
    ]
    conv_ref, bias_ref = conv_rows(misc_ref)
    near_rows = rows_1.shape[0]
    half_rows = normed_low.shape[1]
    nears = [
        Near(rows_0.at[pl.ds(near_rows, near_rows)], rows_1, l_send.at[0], l_recv.at[0]),
        Near(grads_0, grads_1, l_send.at[1], l_recv.at[1]),
    ]
    loads = [
        pltpu.make_async_copy(source, target, load_sems.at[k])
        for k, (source, target) in enumerate(
            [
                (gate_hbm, send_in.at[pl.ds(half, half)]),
                (normed_low, normed_all.at[:, pl.ds(0, half_rows)]),
                (normed_high, normed_all.at[:, pl.ds(half_rows, half_rows)]),
                (mix_hbm, mix_all), (gated_hbm, gated_all),
            ]
        )
    ]

    def start_inputs(first, last):
        for k, copy in enumerate(ways[0].copies):
            peer = (me + k + 1) % devices
            pl.when((peer >= first) & (peer < last))(lambda copy=copy: copy.start())
        pl.when((me >= first) & (me < last))(lambda: ways[0].local.start())

    @pl.when(tile_id == 0)
    def _():
        total[...] = jnp.zeros_like(total)
        for load in loads:
            load.start()
        greet()
        for near in nears:
            near.start()
        loads[0].wait()
        start_inputs(half, devices)
        ways[1].start()

    grad_proj = gradproj_ref[...].astype(BF16)
    grad_u = gradu_ref[...] + times_transpose(grad_proj, scanw_ref[...])
    pieces = [contract_rows(grad_proj, u_ref[...].astype(BF16))]
    x_inner = xin_ref[...]
    taps = conv_ref.shape[0]
    shifted = [shift_rows(x_inner, taps - 1 - tap) for tap in range(taps)]
    summed = bias_ref[...]
    for tap in range(taps):
        summed = summed + conv_ref[tap : tap + 1, :] * shifted[tap]
    sig = sigmoid(summed)
    grad_sum = grad_u * (sig * (1.0 + summed * (1.0 - sig)))
    grad_x = jnp.zeros_like(x_inner)
    for tap in range(taps):
        pieces.append(jnp.sum(grad_sum * shifted[tap], 0, keepdims=True))
        grad_x = grad_x + conv_ref[tap : tap + 1, :] * shift_rows(grad_sum, tap + 1 - taps)
    pieces.append(jnp.sum(grad_sum, 0, keepdims=True))
    spare = send_back.shape[1] - grad_proj.shape[1] - taps - 1
    pieces.append(jnp.zeros((spare, x_inner.shape[1]), F32))
    packed = jnp.concatenate(pieces, 0).astype(BF16)
    grad_x = grad_x.astype(BF16)
    for turn in range(2):

        @pl.when(tile_id == turn)
        def _():
            split_lanes(send_back.at[pl.ds(turn * half, half)], packed)
            send_in[turn * gates : (turn + 1) * gates] = grad_x.T.reshape(
                (gates,) + send_in.shape[1:]
            )
            start_inputs(turn * gates, (turn + 1) * gates)

    @pl.when(tile_id == 1)
    def _():
        ways[2].start()

    total[...] += product(grad_x, wx_ref[...]) + product(gradgate_ref[...], wg_ref[...])

    @pl.when(tile_id == 1)
    def _():
        values = tokens_ref[...].astype(F32)
        scale = lax.rsqrt(jnp.mean(values * values, -1, keepdims=True) + 1e-05)
        unit = values * scale
        grad = total[...]
        widths = jnp.concatenate([widths_ref[...], jnp.sum(grad * unit, 0, keepdims=True)], 0)
        widths = jnp.concatenate(
            [widths, jnp.zeros((send_tail.shape[1] - widths.shape[0], widths.shape[1]), F32)], 0
        )
        split_lanes(send_tail, widths.astype(BF16))
        ways[3].start()
        inner = grad * gain_ref[0:1, :]
        gradtok_ref[...] = gradmid_ref[...] + scale * (
            inner - unit * jnp.mean(inner * unit, -1, keepdims=True)
        )
        for load in loads[1:]:
            load.wait()
        rows, width = mix_all.shape[1:]

        def side_by_side(ref):
            return jnp.concatenate([ref[k] for k in range(devices)], 1)

        in_rows, part = got_in.shape[1], gated_all.shape[1]
        totals_ref[in_rows : in_rows + part, :] = product(
            side_by_side(gated_all), mix_all[...].reshape(devices * rows, width)
        ).astype(BF16)
        ways[0].wait()
        totals_ref[0:in_rows, :] = product(
            side_by_side(got_in), normed_all[...].reshape(devices * rows, width)
        ).astype(BF16)
        at = in_rows + part
        for way, got in ((ways[1], got_scan), (ways[2], got_back)):
            way.wait()
            total_here = jnp.sum(got[...].astype(F32), 0)
            quarter = total_here.shape[0] // 4
            folded = jnp.concatenate(
                [total_here[k * quarter : (k + 1) * quarter] for k in range(4)], 1
            )
            padding = jnp.zeros((32 - quarter, width), F32)
            totals_ref[at : at + 32, :] = jnp.concatenate([folded, padding], 0).astype(BF16)
            at += 32
        ways[3].wait()
        tail = jnp.sum(got_tail[...].astype(F32), 0)
        tail = jnp.concatenate(
            [tail, jnp.zeros((tail.shape[0], width - tail.shape[1]), F32)], 1
        )
        totals_ref[at : at + 16, :] = tail.astype(BF16)
        for near in nears:
            near.wait()


def mixer_back_plane(
    grad_proj, scan_w, grad_u, x_inner, vec, in_t, u_act, tokens, gains, grad_mid, grad_widths,
    grad_gate, gate_parts, scan_parts, normed_low, normed_high, mix_all, gated_all, rows_0, grads_0,
):
    rows, channels = u_act.shape
    width = tokens.shape[1]
    cols = scan_w.shape[1]
    devices = lax.axis_size("expert")
    part = channels // devices
    tile = channels // 2
    pack_rows = cols + 8
    tail_rows = grad_widths.shape[0] + 7
    column = lambda i: (0, i)
    fixed = lambda i: (0, 0)
    return pl.pallas_call(
        back_plane_kernel,
        grid=(2,),
        in_specs=[
            pl.BlockSpec((rows, cols), fixed),
            pl.BlockSpec((tile, cols), lambda i: (i, 0)),
            pl.BlockSpec((rows, tile), column),
            pl.BlockSpec((rows, tile), column),
            pl.BlockSpec((8, tile), lambda i: ((vec.shape[0] - 8) // 8, i)),
            pl.BlockSpec((tile, width), lambda i: (i, 0)),
            pl.BlockSpec((tile, width), lambda i: (i + 2, 0)),
            pl.BlockSpec((rows, tile), column),
            pl.BlockSpec((rows, width), fixed),
            pl.BlockSpec(gains.shape, fixed),
            pl.BlockSpec((rows, width), fixed),
            pl.BlockSpec(grad_widths.shape, fixed),
            pl.BlockSpec((rows, tile), column),
        ] + [FAR] * 8,
        out_specs=[
            pl.BlockSpec((rows, width), fixed),
            pl.BlockSpec((3 * part + 80, width), fixed),
            FAR,
            FAR,
        ],
        out_shape=[
            jax.ShapeDtypeStruct((rows, width), F32),
            jax.ShapeDtypeStruct((3 * part + 80, width), BF16),
            jax.ShapeDtypeStruct((devices // 2,) + rows_0.shape[1:], BF16),
            jax.ShapeDtypeStruct(grads_0.shape, BF16),
        ],
        scratch_shapes=[
            pltpu.VMEM((rows, width), F32),
            pltpu.VMEM((devices, 2 * part, rows), BF16),
            pltpu.VMEM((devices, 2 * part, rows), BF16),
            pltpu.VMEM((devices, rows, width), BF16),
            pltpu.VMEM(mix_all.shape, BF16),
            pltpu.VMEM(gated_all.shape, BF16),
            pltpu.VMEM(scan_parts.shape, BF16),
            pltpu.VMEM((devices, pack_rows, part), BF16),
            pltpu.VMEM((devices, pack_rows, part), BF16),
            pltpu.VMEM((devices, tail_rows, width // devices), BF16),
            pltpu.VMEM((devices, tail_rows, width // devices), BF16),
            DMA((4, devices)), DMA((4, devices)), DMA((2, 2)), DMA((2, 2)), DMA((4,)), DMA((5,)),
        ],
        compiler_params=remote_params(5),
        name="mixer_back_plane",
    )(
        grad_proj, scan_w, grad_u, x_inner, vec, in_t, in_t, u_act, tokens, gains, grad_mid,
        grad_widths, grad_gate, gate_parts, scan_parts, normed_low, normed_high, mix_all, gated_all,
        rows_0, grads_0,
    )


def add_groups(rows, grads, rows_t, up_ref, down_ref):
    activated, slope = gelu_parts(product(rows, up_ref[...]))
    grad_pre = (times_transpose(grads, down_ref[...]) * slope).astype(BF16)
    return product(rows_t, grad_pre), contract_rows(activated.astype(BF16), grads)


def flat_rows(refs):
    experts, cap, width = refs[0].shape
    values = [ref[...].reshape(ref.shape[0] * cap, width) for ref in refs]
    return values[0] if len(values) == 1 else jnp.concatenate(values, 0)


def next_grads_kernel(sizes, choices, up_ref, down_ref, gup_in, gdown_in, *refs):
    row_parts, grad_parts, count = sizes
    rows_in, refs = refs[:row_parts], refs[row_parts:]
    grads_in, refs = refs[:grad_parts], refs[grad_parts:]
    raws, goals, refs = refs[:count], refs[count : 2 * count], refs[2 * count :]
    gup_ref, gdown_ref, rows_out, grads_out, refs = *refs[:4], refs[4:]
    rows_t, raw, goal, sends, x_send, x_recv, local_sems, load_sems = refs
    step = pl.program_id(0)
    rows, grads = flat_rows(rows_in), flat_rows(grads_in)
    group = Dispatch(raw, goal, sends, (rows_out, grads_out), x_send, x_recv, local_sems)

    @pl.when(step == 0)
    def _():
        greet(line=False)
        pick([(raws[k], goals[k]) for k in choices], raw, goal, load_sems)
        group.prepare((0, 1))
        group.start()
        rows_t[...] = rows.T

    grad_up, grad_down = add_groups(rows, grads, rows_t[...], up_ref, down_ref)
    gup_ref[...] = (gup_in[...].astype(F32) + grad_up).astype(BF16)
    gdown_ref[...] = (gdown_in[...].astype(F32) + grad_down).astype(BF16)

    @pl.when(step == pl.num_programs(0) - 1)
    def _():
        group.wait()


def last_grads_kernel(
    up_ref, down_ref, gup_in, gdown_in, rows_ref, grads_ref, gup_ref, gdown_ref, rows_t
):
    rows, grads = flat_rows((rows_ref,)), flat_rows((grads_ref,))

    @pl.when(pl.program_id(0) == 0)
    def _():
        rows_t[...] = rows.T

    grad_up, grad_down = add_groups(rows, grads, rows_t[...], up_ref, down_ref)
    gup_ref[...] = gup_in[...].astype(F32) + grad_up
    gdown_ref[...] = gdown_in[...].astype(F32) + grad_down


def expert_grads_plane(up, down, grad_up, grad_down, rows_1, grads_1, raws, goals, tile):
    width, hidden = up.shape
    devices, cap = grads_1.shape[:2]
    slots = jax.ShapeDtypeStruct(grads_1.shape, BF16)
    across = pl.BlockSpec((width, tile), lambda i: (0, i))
    along = pl.BlockSpec((tile, width), lambda i: (i, 0))

    def shapes(kind):
        return [
            jax.ShapeDtypeStruct((width, hidden), kind), jax.ShapeDtypeStruct((hidden, width), kind)
        ]

    def wholes(values):
        return [pl.BlockSpec(value.shape, lambda i: (0, 0, 0)) for value in values]

    left_2, left_3, right_1, right_2, right_3 = range(5)
    rows, grads = rows_1, (grads_1,)
    for turn, choices in enumerate(
        ((right_2, right_1, right_1, left_2), (right_3, right_2, left_2, left_3))
    ):
        grad_up, grad_down, rows_next, grads_next = pl.pallas_call(
            partial(next_grads_kernel, (len(rows), len(grads), len(raws)), choices),
            grid=(hidden // tile,),
            in_specs=[across, along] * 2 + wholes(rows + grads) + [FAR] * (2 * len(raws)),
            out_specs=[across, along, FAR, FAR],
            out_shape=shapes(BF16) + [slots] * 2,
            scratch_shapes=[
                pltpu.VMEM((width, devices * cap), BF16),
                pltpu.VMEM(raws[0].shape, BF16),
                pltpu.VMEM(goals[0].shape, jnp.int32),
                pltpu.VMEM((2,) + slots.shape, BF16),
                DMA((2, devices)), DMA((2, devices)), DMA((2,)), DMA((2,)),
            ],
            compiler_params=remote_params(6 + turn),
            name="expert_grads_" + str(turn + 1),
        )(up, down, grad_up, grad_down, *rows, *grads, *raws, *goals)
        rows, grads = (rows_next,), (grads_next,)
    return pl.pallas_call(
        last_grads_kernel,
        grid=(hidden // tile,),
        in_specs=[across, along] * 2 + wholes(rows + grads),
        out_specs=[across, along],
        out_shape=shapes(F32),
        scratch_shapes=[pltpu.VMEM((width, devices * cap), BF16)],
        compiler_params=pltpu.CompilerParams(vmem_limit_bytes=VMEM_LIMIT),
        name="expert_grads_3",
    )(up, down, grad_up, grad_down, *rows, *grads)


def finish_kernel(
    totals_ref, in_ref, out_ref, scanw_ref, stepw_ref, decay_ref, conv_ref, vectors_ref, norms_ref,
    router_ref,
):
    in_rows, part = in_ref.shape[0], out_ref.shape[0]
    cols, rank, state, taps = (
        scanw_ref.shape[1], stepw_ref.shape[0], decay_ref.shape[0], conv_ref.shape[0]
    )
    experts, slice_w = router_ref.shape
    in_ref[...] = totals_ref[0:in_rows, :].astype(F32)
    out_ref[...] = totals_ref[in_rows : in_rows + part, :].astype(F32)
    at = in_rows + part
    unfolded = []
    for quarter in ((rank + state + 8) // 4, (cols + 8) // 4):
        block = totals_ref[at : at + 32, :].astype(F32)[:quarter]
        unfolded.append(
            jnp.concatenate([block[:, k * part : (k + 1) * part] for k in range(4)], 0)
        )
        at += 32
    scan, back = unfolded
    stepw_ref[...] = scan[:rank]
    decay_ref[...] = scan[rank : rank + state]
    scanw_ref[...] = back[:cols].T
    conv_ref[...] = back[cols : cols + taps]
    vectors_ref[...] = jnp.concatenate(
        [back[cols + taps : cols + taps + 1], scan[rank + state : rank + state + 2]], 0
    )
    tail = totals_ref[at : at + 16, :].astype(F32)[:, :slice_w]
    router_ref[...] = tail[:experts]
    norms_ref[...] = tail[experts : experts + 2]


def finish(totals, in_rows, part, cols, rank, state, taps, experts, slice_w):
    here = pl.BlockSpec(memory_space=pltpu.VMEM)
    return pl.pallas_call(
        finish_kernel,
        in_specs=[here],
        out_specs=[here] * 9,
        out_shape=[
            jax.ShapeDtypeStruct(shape, F32)
            for shape in (
                (in_rows, totals.shape[1]), (part, totals.shape[1]), (part, cols), (rank, part),
                (state, part), (taps, part), (3, part), (2, slice_w), (experts, slice_w),
            )
        ],
        compiler_params=pltpu.CompilerParams(vmem_limit_bytes=VMEM_LIMIT),
        name="finish",
    )(totals)


def gather(value):
    return lax.all_gather(value, "expert", axis=0, tiled=True)


def exchange(value):
    return lax.all_to_all(value, "expert", split_axis=0, concat_axis=0, tiled=True)


def shards(
    tokens, lengths, routes, slot_index, mixer_norm, in_weight, conv_weight, conv_bias,
    scan_weight, step_weight, step_bias, decay_log, skip_gain, out_weight, moe_norm, router_weight,
    up_weight, down_weight, cotangent,
):
    devices = lax.axis_size("expert")
    rows, width = tokens.shape[1:]
    part = out_weight.shape[0]
    channels = part * devices
    cols = scan_weight.shape[1]
    rank, state, taps = step_weight.shape[0], decay_log.shape[1], conv_weight.shape[0]
    experts = router_weight.shape[1]
    split = devices // experts
    slice_w = width // devices
    tile = channels // 2

    on_plane = devices == 8 and split == 1 and lax.axis_size("dp") == 4
    vectors = jnp.stack([conv_bias, step_bias, skip_gain])
    norms = jnp.stack([mixer_norm, moe_norm])
    in_t, decay_t, router_t = in_weight.T, decay_log.T, router_weight.T
    if on_plane:
        in_t, scan_full, step_full, vec, router_t, gains = gather_weights(
            in_t, scan_weight, step_weight, decay_t, conv_weight, vectors, norms, router_t
        )
    else:
        spare = jnp.zeros((8 - taps - 3, part), BF16)
        columns = jnp.concatenate([step_weight, decay_t, conv_weight, vectors, spare], 0)
        across = jnp.concatenate([router_t, norms, jnp.zeros((6, slice_w), BF16)], 0)
        in_t, scan_full, columns, across = (
            lax.all_gather(value, "expert") for value in (in_t, scan_weight, columns, across)
        )
        columns = columns.transpose(1, 0, 2).reshape(columns.shape[1], channels)
        across = across.transpose(1, 0, 2).reshape(across.shape[1], width)
        step_full, rest = columns[:rank], columns[rank:].astype(F32)
        vec = jnp.concatenate([-jnp.exp(rest[:state]), rest[state:]], 0)
        router_t, gains = across[:experts], across[experts:].astype(F32)
    in_t = in_t.reshape(2 * channels, width)
    scan_full = scan_full.reshape(channels, cols)
    up, down = up_weight[0], down_weight[0]
    normed_low, x_inner, u_act, gate_in, proj = front(
        tokens[0], gains, in_t, vec, scan_full, tile
    )
    hidden = up.shape[1]
    if on_plane:
        step_size, mixed, gated, hist, mid, out_full, normed_first = scan_forward_plane(
            proj, step_full, vec, u_act, gate_in, out_weight, tokens[0], normed_low
        )
        out_full = out_full.reshape(channels, width)
        layer_out, grad_mid, grad_mix, grad_widths, rows_0, grads_0, *line = expert_layer(
            lengths, mid, gains, router_t, routes, slot_index, cotangent[0], up, down
        )
        raws, goals, grad_up, grad_down = line[:4], line[4:8], line[8], line[9]
        (
            grad_u, grad_gate, scan_parts, grad_proj, gate_parts, mix_all, normed_last, gated_all,
            rows_1a, left_3, right_3, goal_l3, goal_r3,
        ) = scan_backward_plane(
            proj, step_full, vec, u_act, gate_in, out_full, grad_mix, step_size, mixed, hist,
            normed_low, gated, rows_0, raws, goals,
        )
        tokens_grad, totals, rows_1b, grads_1 = mixer_back_plane(
            grad_proj, scan_full, grad_u, x_inner, vec, in_t, u_act, tokens[0], gains, grad_mid,
            grad_widths, grad_gate, gate_parts, scan_parts, normed_first, normed_last, mix_all,
            gated_all, rows_0, grads_0,
        )
        totals = lax.psum(totals, "dp")
        grad_up, grad_down = expert_grads_plane(
            up, down, grad_up, grad_down, (rows_1a, rows_1b), grads_1,
            (raws[2], left_3, raws[1], raws[3], right_3),
            (goals[2], goal_l3, goals[1], goals[3], goal_r3), 512,
        )
        in_total, out_total, scan_w_total, step_w_total, decay_total, conv_total, *rest = finish(
            totals, 2 * part, part, cols, rank, state, taps, experts, slice_w
        )
        vector_totals, norm_totals, router_total = rest
    else:
        live = (jnp.arange(rows, dtype=jnp.int32) < lengths[0]).astype(F32)[:, None]
        routes_col, slots_col = routes[0][:, None], slot_index[0][:, None]
        router, gain_second = router_t.T, gains[1:2]
        out_full = gather(out_weight)
        step_size, mixed, gated, hist, mid = scan_forward(
            proj, step_full, vec, u_act, gate_in, out_full, tokens[0], tile
        )
        send_rows, send_grads, normed_two, probs = router_step(
            mid, gain_second, router, routes_col, routes, slot_index, live, cotangent[0]
        )

        def to_pieces(value):
            wide = jnp.broadcast_to(value[:, None], (experts, split) + value.shape[1:])
            return exchange(wide.reshape(devices, CAP, width))

        def from_pieces(value):
            value = exchange(value).reshape(experts, split, CAP, width)
            if split == 1:
                return value[:, 0]
            return jnp.sum(value.astype(F32), 1).astype(BF16)

        some = min(512, hidden // 3)
        rows_in = to_pieces(send_rows)
        grads_in = to_pieces(send_grads)
        partial_out, slope = expert_out(rows_in, up, down, some)
        back_rows = from_pieces(partial_out)
        back_grads = from_pieces(expert_back(grads_in, up, down, slope, some))
        all_rows = lax.all_gather(rows_in, "dp")
        layer_out, grad_mid, grad_mix, grad_widths = combine_step(
            mid, gain_second, router, routes_col, slots_col, live, cotangent[0], probs, normed_two,
            back_rows, back_grads,
        )
        grad_mix, all_rows = lax.optimization_barrier((grad_mix, all_rows))
        all_grads = lax.all_gather(grads_in, "dp")
        out_parts = contract_rows(gated, grad_mix).astype(BF16).reshape(devices, part, width)
        grad_out_w = jnp.sum(exchange(out_parts).astype(F32), 0).astype(BF16)
        grad_u, grad_gate, scan_parts, grad_proj = scan_backward(
            proj, step_full, vec, u_act, gate_in, out_full, grad_mix, step_size, mixed, hist, tile,
            devices,
        )
        scan_small = jnp.sum(exchange(scan_parts).astype(F32), 0).astype(BF16)
        grad_x, back_parts, width_parts, tokens_grad = mixer_back(
            grad_proj, scan_full, grad_u, x_inner, vec, grad_gate, in_t, u_act, tokens[0], gains,
            grad_mid, grad_widths, tile, devices,
        )
        back_small = jnp.sum(exchange(back_parts).astype(F32), 0).astype(BF16)
        width_small = jnp.sum(exchange(width_parts).astype(F32), 0).astype(BF16)
        normed_all = gather(normed_low)
        grad_in_parts = exchange(jnp.concatenate([grad_x, grad_gate], 0))
        grad_in_w = contract_rows(
            grad_in_parts.reshape(devices * rows, 2 * part), normed_all
        ).astype(BF16)
        totals = (grad_in_w, grad_out_w, scan_small, back_small, width_small)
        totals, all_grads = lax.optimization_barrier((totals, all_grads))
        totals = lax.psum(totals, "dp")
        in_total, out_total, scan_small, back_small, width_small = (
            t.astype(F32) for t in totals
        )
        grad_up, grad_down = expert_grads(all_rows, all_grads, up, down, min(256, hidden))
        scan_w_total, conv_total = back_small[:cols].T, back_small[cols : cols + taps]
        step_w_total, decay_total = scan_small[:rank], scan_small[rank : rank + state]
        vector_totals = (
            back_small[cols + taps], scan_small[rank + state], scan_small[rank + state + 1]
        )
        router_total = width_small[:experts]
        norm_totals = (width_small[experts], width_small[experts + 1])
    return (
        layer_out[None],
        tokens_grad[None],
        norm_totals[1],
        in_total.T,
        conv_total,
        vector_totals[0],
        scan_w_total,
        step_w_total,
        vector_totals[1],
        decay_total.T,
        vector_totals[2],
        out_total,
        norm_totals[0],
        router_total.T,
        grad_up[None],
        grad_down[None],
    )


def solution(mesh):
    in_specs = (
        P(("dp", "expert"), None, None),
        P(("dp", "expert")),
        P(("dp", "expert"), None),
        P(("dp", "expert"), None),
        P("expert"),
        P(None, "expert"),
        P(None, "expert"),
        P("expert"),
        P("expert", None),
        P(None, "expert"),
        P("expert"),
        P("expert", None),
        P("expert"),
        P("expert", None),
        P("expert"),
        P("expert", None),
        P("expert", None, None),
        P("expert", None, None),
        P(("dp", "expert"), None, None),
    )
    out_specs = (
        P(("dp", "expert"), None, None),
        P(("dp", "expert"), None, None),
        P("expert"),
        P(None, "expert"),
        P(None, "expert"),
        P("expert"),
        P("expert", None),
        P(None, "expert"),
        P("expert"),
        P("expert", None),
        P("expert"),
        P("expert", None),
        P("expert"),
        P("expert", None),
        P("expert", None, None),
        P("expert", None, None),
    )
    return jax.shard_map(shards, mesh=mesh, in_specs=in_specs, out_specs=out_specs, check_vma=False)
```

```python
from functools import partial

import jax
import jax.numpy as jnp
from jax import lax
from jax.experimental import pallas as pl
from jax.experimental.pallas import tpu as pltpu
from jax.sharding import PartitionSpec as P

CAP = 64
BLOCK = 16
LOG2E = 1.4426950408889634
F32 = jnp.float32
BF16 = jnp.bfloat16
VMEM_LIMIT = 56 * 1024 * 1024


def product(left, right):
    return jnp.dot(left, right, preferred_element_type=F32)


def contract_rows(left, right):
    return lax.dot_general(left, right, (((0,), (0,)), ((), ())), preferred_element_type=F32)


def times_transpose(left, right):
    return lax.dot_general(left, right, (((1,), (1,)), ((), ())), preferred_element_type=F32)


def exact_product(left, right):
    return jnp.dot(left, right, preferred_element_type=F32, precision=lax.Precision.HIGHEST)


def iota(shape, axis):
    return lax.broadcasted_iota(jnp.int32, shape, axis)


def sigmoid(values):
    return 1.0 / (1.0 + jnp.exp(-values))


def softplus(values):
    return jnp.maximum(values, 0.0) + jnp.log1p(jnp.exp(-jnp.abs(values)))


class Rows:
    def __init__(self, ref, first, count):
        self.ref, self.first = ref, first
        self.shape = (count, ref.shape[1])

    def __getitem__(self, index):
        low, high = (0, self.shape[0]) if index is Ellipsis else (index[0].start, index[0].stop)
        return self.ref[self.first + low : self.first + high, :]


def conv_rows(misc_ref):
    return Rows(misc_ref, 0, 4), Rows(misc_ref, 4, 1)


def scan_rows(misc_ref):
    return Rows(misc_ref, 5, 1), Rows(misc_ref, 6, 1)


def split_lanes(out_ref, value):
    parts, _, width = out_ref.shape
    for part in range(parts):
        out_ref[part] = value[:, part * width : (part + 1) * width]


def shift_rows(values, offset):
    rows = values.shape[0]
    if offset == 0:
        return values
    rolled = pltpu.roll(values, offset % rows, 0)
    row = iota(values.shape, 0)
    keep = row >= offset if offset > 0 else row < rows + offset
    return jnp.where(keep, rolled, 0.0)


def two_parts(values):
    high = values.astype(BF16)
    low = (values - high.astype(F32)).astype(BF16)
    return high, low


def spread_rows(proj_block, first, state):
    rows, width = proj_block.shape
    big = rows * state
    pick = (iota((big, rows), 0) // state == iota((big, rows), 1)).astype(F32)
    copied = exact_product(pick, proj_block)
    lane = iota((big, width), 1)
    own = lane == first + iota((big, width), 0) % state
    column = jnp.sum(jnp.where(own, copied, 0.0), axis=1, keepdims=True)
    return jnp.broadcast_to(column, (big, 128))


def diagonal_blocks(proj_block, first, state):
    rows, width = proj_block.shape
    big = rows * state
    place = (iota((width, big), 0) == first + iota((width, big), 1) % state).astype(BF16)
    own = iota((rows, big), 0) == iota((rows, big), 1) // state
    parts = [
        jnp.where(own, product(part, place), 0.0).astype(BF16) for part in two_parts(proj_block)
    ]
    return jnp.concatenate(parts, 0)


def front_kernel(
    tokens_ref, gain_ref, wx_ref, wg_ref, misc_ref, scanw_ref,
    normed_ref, xin_ref, u_ref, gate_ref, proj_ref,
):
    step = pl.program_id(0)
    conv_ref, bias_ref = conv_rows(misc_ref)

    @pl.when(step == 0)
    def _():
        values = tokens_ref[...].astype(F32)
        scale = lax.rsqrt(jnp.mean(values * values, -1, keepdims=True) + 1e-05)
        normed_ref[...] = (values * scale * gain_ref[0:1, :]).astype(BF16)
        proj_ref[...] = jnp.zeros_like(proj_ref)

    normed = normed_ref[...]
    x_inner = times_transpose(normed, wx_ref[...])
    gate_ref[...] = times_transpose(normed, wg_ref[...])
    xin_ref[...] = x_inner
    taps = conv_ref.shape[0]
    summed = bias_ref[...] + conv_ref[taps - 1 : taps, :] * x_inner
    for back in range(1, taps):
        tap = taps - 1 - back
        summed = summed + conv_ref[tap : tap + 1, :] * shift_rows(x_inner, back)
    u_act = summed * sigmoid(summed)
    u_ref[...] = u_act
    proj_ref[...] += product(u_act.astype(BF16), scanw_ref[...])


def front(tokens, gains, in_t, vec, scan_w, tile):
    rows, width = tokens.shape
    channels = scan_w.shape[0]
    cols = scan_w.shape[1]
    steps = channels // tile
    return pl.pallas_call(
        front_kernel,
        grid=(steps,),
        in_specs=[
            pl.BlockSpec((rows, width), lambda i: (0, 0)),
            pl.BlockSpec(gains.shape, lambda i: (0, 0)),
            pl.BlockSpec((tile, width), lambda i: (i, 0)),
            pl.BlockSpec((tile, width), lambda i: (i + steps, 0)),
            pl.BlockSpec((8, tile), lambda i: ((vec.shape[0] - 8) // 8, i)),
            pl.BlockSpec((tile, cols), lambda i: (i, 0)),
        ],
        out_specs=[
            pl.BlockSpec((rows, width), lambda i: (0, 0)),
            pl.BlockSpec((rows, tile), lambda i: (0, i)),
            pl.BlockSpec((rows, tile), lambda i: (0, i)),
            pl.BlockSpec((rows, tile), lambda i: (0, i)),
            pl.BlockSpec((rows, cols), lambda i: (0, 0)),
        ],
        out_shape=[
            jax.ShapeDtypeStruct((rows, width), BF16),
            jax.ShapeDtypeStruct((rows, channels), F32),
            jax.ShapeDtypeStruct((rows, channels), F32),
            jax.ShapeDtypeStruct((rows, channels), F32),
            jax.ShapeDtypeStruct((rows, cols), F32),
        ],
        compiler_params=pltpu.CompilerParams(vmem_limit_bytes=VMEM_LIMIT),
        name="mixer_front",
    )(tokens, gains, in_t, in_t, vec, scan_w)


def scan_prepare(proj_ref, b_wide, c_blocks, b_first, c_first, state):
    blocks = proj_ref.shape[0] // BLOCK
    big = BLOCK * state

    def build(block, carry):
        part = proj_ref[pl.ds(pl.multiple_of(block * BLOCK, BLOCK), BLOCK), :]
        b_wide[pl.ds(pl.multiple_of(block * big, big), big), :] = spread_rows(part, b_first, state)
        c_blocks[pl.ds(pl.multiple_of(block * 2 * BLOCK, 2 * BLOCK), 2 * BLOCK), :] = (
            diagonal_blocks(part, c_first, state)
        )
        return carry

    lax.fori_loop(0, blocks, build, 0)


def scan_tile(
    proj_ref, stepw_ref, decay_ref, misc_ref, u_ref, gate_ref, step_ref, mixed_ref, hist_ref,
    b_wide, c_blocks, du, scanned, between,
):
    rank, state = stepw_ref.shape[0], decay_ref.shape[0]
    rows, tile = u_ref.shape
    blocks = rows // BLOCK
    big = BLOCK * state
    dbias_ref, skip_ref = scan_rows(misc_ref)
    u_act = u_ref[...]
    step_size = softplus(
        product(proj_ref[:, :rank].astype(BF16), stepw_ref[...]) + dbias_ref[...]
    )
    step_ref[...] = step_size
    du[...] = step_size * u_act
    decay = decay_ref[...] * LOG2E
    hist_ref[0:state, :] = jnp.zeros((state, tile), BF16)

    def run_block(block, held):
        base = pl.multiple_of(block * BLOCK, BLOCK)
        steps_now = step_ref[pl.ds(base, BLOCK), :]
        du_now = du[pl.ds(base, BLOCK), :]
        wide_base = pl.multiple_of(block * big, big)
        for t in range(BLOCK):
            b_now = b_wide[pl.ds(wide_base + t * state, state), :]
            fade = jnp.exp2(steps_now[t : t + 1, :] * decay)
            fresh = du_now[t : t + 1, :] * jnp.concatenate([b_now] * (tile // 128), 1)
            held = fade * held + fresh
            hist_ref[pl.ds(wide_base + (t + 1) * state, state), :] = held.astype(BF16)
        weights = c_blocks[pl.ds(pl.multiple_of(block * 2 * BLOCK, 2 * BLOCK), 2 * BLOCK), :]
        both = product(weights, hist_ref[pl.ds(wide_base + state, big), :])
        scanned[pl.ds(base, BLOCK), :] = both[:BLOCK] + both[BLOCK:]
        return held

    held = jnp.zeros((state, tile), F32)
    held = lax.fori_loop(0, blocks // 2, run_block, held)
    between(0)
    lax.fori_loop(blocks // 2, blocks, run_block, held)
    between(1)
    mixed = scanned[...] + skip_ref[...] * u_act
    mixed_ref[...] = mixed
    gate_in = gate_ref[...]
    return (mixed * (gate_in * sigmoid(gate_in))).astype(BF16)


def scan_kernel(
    proj_ref, stepw_ref, decay_ref, misc_ref, u_ref, gate_ref, outw_ref, tokens_ref,
    step_ref, mixed_ref, gated_ref, hist_ref, mid_ref,
    b_wide, c_blocks, du, scanned,
):
    rank, state = stepw_ref.shape[0], decay_ref.shape[0]

    @pl.when(pl.program_id(0) == 0)
    def _():
        mid_ref[...] = tokens_ref[...].astype(F32)
        scan_prepare(proj_ref, b_wide, c_blocks, rank, rank + state, state)

    gated = scan_tile(
        proj_ref, stepw_ref, decay_ref, misc_ref, u_ref, gate_ref, step_ref, mixed_ref, hist_ref,
        b_wide, c_blocks, du, scanned, lambda half: None,
    )
    gated_ref[...] = gated
    mid_ref[...] += product(gated, outw_ref[...])


def scan_forward(proj, step_w, vec, u_act, gate_in, out_w, tokens, tile):
    rows, channels = u_act.shape
    width = tokens.shape[1]
    cols = proj.shape[1]
    rank, state = step_w.shape[0], vec.shape[0] - 8
    steps = channels // tile
    hist_rows = (rows + 1) * state
    column = lambda i: (0, i)
    fixed = lambda i: (0, 0)
    return pl.pallas_call(
        scan_kernel,
        grid=(steps,),
        in_specs=[
            pl.BlockSpec((rows, cols), fixed),
            pl.BlockSpec((rank, tile), column),
            pl.BlockSpec((state, tile), column),
            pl.BlockSpec((8, tile), lambda i: ((vec.shape[0] - 8) // 8, i)),
            pl.BlockSpec((rows, tile), column),
            pl.BlockSpec((rows, tile), column),
            pl.BlockSpec((tile, width), lambda i: (i, 0)),
            pl.BlockSpec((rows, width), fixed),
        ],
        out_specs=[
            pl.BlockSpec((rows, tile), column),
            pl.BlockSpec((rows, tile), column),
            pl.BlockSpec((rows, tile), column),
            pl.BlockSpec((hist_rows, tile), column),
            pl.BlockSpec((rows, width), fixed),
        ],
        out_shape=[
            jax.ShapeDtypeStruct((rows, channels), F32),
            jax.ShapeDtypeStruct((rows, channels), F32),
            jax.ShapeDtypeStruct((rows, channels), BF16),
            jax.ShapeDtypeStruct((hist_rows, channels), BF16),
            jax.ShapeDtypeStruct((rows, width), F32),
        ],
        scratch_shapes=[
            pltpu.VMEM((rows * state, 128), F32),
            pltpu.VMEM((rows * 2, BLOCK * state), BF16),
            pltpu.VMEM((rows, tile), F32),
            pltpu.VMEM((rows, tile), F32),
        ],
        compiler_params=pltpu.CompilerParams(vmem_limit_bytes=VMEM_LIMIT),
        name="scan_forward",
    )(proj, step_w, vec, vec, u_act, gate_in, out_w, tokens)


def scan_back_kernel(*refs):
    scan_back_tile(lambda half: None, split_lanes, *refs)


def scan_back_tile(
    between, put_gate, proj_ref, stepw_ref, decay_ref, misc_ref, u_ref, gate_ref, outw_ref, gradmix_ref,
    step_ref, mixed_ref, hist_ref,
    gradu_ref, gradgate_ref, pack_ref, gradproj_ref,
    c_wide, b_blocks, b_sums, c_sums, gy, du, g_hist, w_hist, grad_du, grad_step,
):
    tile_id = pl.program_id(0)
    cols, rank = proj_ref.shape[1], stepw_ref.shape[0]
    state = decay_ref.shape[0]
    rows, tile = u_ref.shape
    blocks = rows // BLOCK
    big = BLOCK * state

    @pl.when(tile_id == 0)
    def _():
        gradproj_ref[...] = jnp.zeros_like(gradproj_ref)
        b_sums[...] = jnp.zeros_like(b_sums)
        c_sums[...] = jnp.zeros_like(c_sums)
        scan_prepare(proj_ref, c_wide, b_blocks, rank + state, rank, state)

    skip_ref = scan_rows(misc_ref)[1]
    grad_gated = times_transpose(gradmix_ref[...], outw_ref[...])
    gate_in = gate_ref[...]
    gate_sig = sigmoid(gate_in)
    grad_mixed = grad_gated * (gate_in * gate_sig)
    put_gate(
        gradgate_ref,
        (grad_gated * mixed_ref[...] * (gate_sig * (1.0 + gate_in * (1.0 - gate_sig)))).astype(BF16),
    )
    u_act = u_ref[...]
    step_size = step_ref[...]
    gy[...] = grad_mixed
    du[...] = step_size * u_act
    grad_skip = jnp.sum(grad_mixed * u_act, 0, keepdims=True)
    rate = decay_ref[...]
    decay = rate * LOG2E
    sums = (iota((BLOCK, big), 0) == iota((BLOCK, big), 1) // state).astype(BF16)

    def run_block(turn, carry):
        carried, log_sum = carry
        block = blocks - 1 - turn
        base = pl.multiple_of(block * BLOCK, BLOCK)
        wide_base = pl.multiple_of(block * big, big)
        steps_now = step_ref[pl.ds(base, BLOCK), :]
        gy_now = gy[pl.ds(base, BLOCK), :]
        for t in range(BLOCK - 1, -1, -1):
            c_now = c_wide[pl.ds(wide_base + t * state, state), :]
            step_now = steps_now[t : t + 1, :]
            fade = jnp.exp2(step_now * decay)
            grad = gy_now[t : t + 1, :] * jnp.concatenate([c_now] * (tile // 128), 1) + carried
            g_hist[t * state : (t + 1) * state, :] = grad.astype(BF16)
            carried = fade * grad
            before = hist_ref[pl.ds(wide_base + t * state, state), :].astype(F32)
            weighted = carried * before * rate
            w_hist[t * state : (t + 1) * state, :] = weighted.astype(BF16)
            log_sum = log_sum + weighted * step_now
        grads = g_hist[...]
        both = product(
            b_blocks[pl.ds(pl.multiple_of(block * 2 * BLOCK, 2 * BLOCK), 2 * BLOCK), :], grads
        )
        grad_du[pl.ds(base, BLOCK), :] = both[:BLOCK] + both[BLOCK:]
        grad_step[pl.ds(base, BLOCK), :] = product(sums, w_hist[...])
        b_sums[pl.ds(base, BLOCK), :] += times_transpose(
            du[pl.ds(base, BLOCK), :].astype(BF16), grads
        )
        c_sums[pl.ds(base, BLOCK), :] += times_transpose(
            gy_now.astype(BF16), hist_ref[pl.ds(wide_base + state, big), :]
        )
        return carried, log_sum

    zeros = jnp.zeros((state, tile), F32)
    held = lax.fori_loop(0, blocks // 2, run_block, (zeros, zeros))
    between(0)
    _, log_sum = lax.fori_loop(blocks // 2, blocks, run_block, held)
    between(1)
    full_du = grad_du[...]
    gradu_ref[...] = full_du * step_size + skip_ref[...] * gy[...]
    grad_size = grad_step[...] + full_du * u_act
    grad_pre = grad_size * (1.0 - jnp.exp(-step_size))
    grad_low = grad_pre.astype(BF16)
    grad_step_w = contract_rows(proj_ref[:, :rank].astype(BF16), grad_low)
    packed = jnp.concatenate(
        [grad_step_w, log_sum, jnp.sum(grad_pre, 0, keepdims=True), grad_skip, zeros[:6]], 0
    )
    split_lanes(pack_ref, packed.astype(BF16))
    gradproj_ref[:, :rank] += times_transpose(grad_low, stepw_ref[...])

    @pl.when(tile_id == pl.num_programs(0) - 1)
    def _():
        own = iota((rows, big), 0) % BLOCK == iota((rows, big), 1) // state
        lane = iota((big, cols), 1)
        slot = iota((big, cols), 0) % state
        total = gradproj_ref[...]
        for sums_ref, first in ((b_sums, rank), (c_sums, rank + state)):
            place = (lane == first + slot).astype(F32)
            total = total + exact_product(jnp.where(own, sums_ref[...], 0.0), place)
        gradproj_ref[...] = total


def scan_backward(
    proj, step_w, vec, u_act, gate_in, out_w, grad_mix, step_size, mixed, hist, tile, devices
):
    rows, channels = u_act.shape
    gate_parts = tile * devices // (2 * channels)
    pack_parts = tile * devices // channels
    pack_rows = step_w.shape[0] + vec.shape[0]
    width = grad_mix.shape[1]
    cols = proj.shape[1]
    rank, state = step_w.shape[0], vec.shape[0] - 8
    steps = channels // tile
    big = BLOCK * state
    column = lambda i: (0, i)
    fixed = lambda i: (0, 0)
    return pl.pallas_call(
        scan_back_kernel,
        grid=(steps,),
        in_specs=[
            pl.BlockSpec((rows, cols), fixed),
            pl.BlockSpec((rank, tile), column),
            pl.BlockSpec((state, tile), column),
            pl.BlockSpec((8, tile), lambda i: ((vec.shape[0] - 8) // 8, i)),
            pl.BlockSpec((rows, tile), column),
            pl.BlockSpec((rows, tile), column),
            pl.BlockSpec((tile, width), lambda i: (i, 0)),
            pl.BlockSpec((rows, width), fixed),
            pl.BlockSpec((rows, tile), column),
            pl.BlockSpec((rows, tile), column),
            pl.BlockSpec((hist.shape[0], tile), column),
        ],
        out_specs=[
            pl.BlockSpec((rows, tile), column),
            pl.BlockSpec((gate_parts, rows, tile // gate_parts), lambda i: (i, 0, 0)),
            pl.BlockSpec((pack_parts, pack_rows, tile // pack_parts), lambda i: (i, 0, 0)),
            pl.BlockSpec((rows, cols), fixed),
        ],
        out_shape=[
            jax.ShapeDtypeStruct((rows, channels), F32),
            jax.ShapeDtypeStruct((devices // 2, rows, 2 * channels // devices), BF16),
            jax.ShapeDtypeStruct((devices, pack_rows, channels // devices), BF16),
            jax.ShapeDtypeStruct((rows, cols), F32),
        ],
        scratch_shapes=[
            pltpu.VMEM((rows * state, 128), F32),
            pltpu.VMEM((rows * 2, big), BF16),
            pltpu.VMEM((rows, big), F32),
            pltpu.VMEM((rows, big), F32),
            pltpu.VMEM((rows, tile), F32),
            pltpu.VMEM((rows, tile), F32),
            pltpu.VMEM((big, tile), BF16),
            pltpu.VMEM((big, tile), BF16),
            pltpu.VMEM((rows, tile), F32),
            pltpu.VMEM((rows, tile), F32),
        ],
        compiler_params=pltpu.CompilerParams(vmem_limit_bytes=VMEM_LIMIT),
        name="scan_backward",
    )(proj, step_w, vec, vec, u_act, gate_in, out_w, grad_mix, step_size, mixed, hist)


def back_kernel(
    gradproj_ref, scanw_ref, gradu_ref, xin_ref, misc_ref, gradgate_ref, wx_ref, wg_ref,
    u_ref, tokens_ref, gain_ref, gradmid_ref, widths_ref,
    gradx_ref, pack_ref, tail_ref, gradtok_ref,
    total,
):
    tile_id = pl.program_id(0)

    @pl.when(tile_id == 0)
    def _():
        total[...] = jnp.zeros_like(total)

    conv_ref, bias_ref = conv_rows(misc_ref)
    grad_proj = gradproj_ref[...].astype(BF16)
    grad_u = gradu_ref[...] + times_transpose(grad_proj, scanw_ref[...])
    pieces = [contract_rows(grad_proj, u_ref[...].astype(BF16))]
    x_inner = xin_ref[...]
    taps = conv_ref.shape[0]
    shifted = [shift_rows(x_inner, taps - 1 - tap) for tap in range(taps)]
    summed = bias_ref[...]
    for tap in range(taps):
        summed = summed + conv_ref[tap : tap + 1, :] * shifted[tap]
    sig = sigmoid(summed)
    grad_sum = grad_u * (sig * (1.0 + summed * (1.0 - sig)))
    grad_x = jnp.zeros_like(x_inner)
    for tap in range(taps):
        pieces.append(jnp.sum(grad_sum * shifted[tap], 0, keepdims=True))
        grad_x = grad_x + conv_ref[tap : tap + 1, :] * shift_rows(grad_sum, tap + 1 - taps)
    pieces.append(jnp.sum(grad_sum, 0, keepdims=True))
    pieces.append(jnp.zeros((pack_ref.shape[1] - grad_proj.shape[1] - taps - 1, x_inner.shape[1]), F32))
    split_lanes(pack_ref, jnp.concatenate(pieces, 0).astype(BF16))
    grad_x = grad_x.astype(BF16)
    split_lanes(gradx_ref, grad_x)
    grad_gate = jnp.concatenate([gradgate_ref[k] for k in range(gradgate_ref.shape[0])], 1)
    total[...] += product(grad_x, wx_ref[...]) + product(grad_gate, wg_ref[...])

    @pl.when(tile_id == pl.num_programs(0) - 1)
    def _():
        values = tokens_ref[...].astype(F32)
        scale = lax.rsqrt(jnp.mean(values * values, -1, keepdims=True) + 1e-05)
        unit = values * scale
        grad = total[...]
        widths = jnp.concatenate([widths_ref[...], jnp.sum(grad * unit, 0, keepdims=True)], 0)
        widths = jnp.concatenate(
            [widths, jnp.zeros((tail_ref.shape[1] - widths.shape[0], widths.shape[1]), F32)], 0
        )
        split_lanes(tail_ref, widths.astype(BF16))
        inner = grad * gain_ref[0:1, :]
        gradtok_ref[...] = gradmid_ref[...] + scale * (
            inner - unit * jnp.mean(inner * unit, -1, keepdims=True)
        )


def mixer_back(
    grad_proj, scan_w, grad_u, x_inner, vec, grad_gate, in_t, u_act, tokens, gains, grad_mid,
    grad_widths, tile, devices,
):
    rows, channels = u_act.shape
    gate_parts = tile * devices // (2 * channels)
    pack_parts = tile * devices // channels
    pack_rows = scan_w.shape[1] + 8
    tail_rows = grad_widths.shape[0] + 7
    width = tokens.shape[1]
    cols = scan_w.shape[1]
    steps = channels // tile
    column = lambda i: (0, i)
    fixed = lambda i: (0, 0)
    return pl.pallas_call(
        back_kernel,
        grid=(steps,),
        in_specs=[
            pl.BlockSpec((rows, cols), fixed),
            pl.BlockSpec((tile, cols), lambda i: (i, 0)),
            pl.BlockSpec((rows, tile), column),
            pl.BlockSpec((rows, tile), column),
            pl.BlockSpec((8, tile), lambda i: ((vec.shape[0] - 8) // 8, i)),
            pl.BlockSpec((gate_parts, rows, tile // gate_parts), lambda i: (i, 0, 0)),
            pl.BlockSpec((tile, width), lambda i: (i, 0)),
            pl.BlockSpec((tile, width), lambda i: (i + steps, 0)),
            pl.BlockSpec((rows, tile), column),
            pl.BlockSpec((rows, width), fixed),
            pl.BlockSpec(gains.shape, fixed),
            pl.BlockSpec((rows, width), fixed),
            pl.BlockSpec(grad_widths.shape, fixed),
        ],
        out_specs=[
            pl.BlockSpec((gate_parts, rows, tile // gate_parts), lambda i: (i, 0, 0)),
            pl.BlockSpec((pack_parts, pack_rows, tile // pack_parts), lambda i: (i, 0, 0)),
            pl.BlockSpec((devices, tail_rows, width // devices), lambda i: (0, 0, 0)),
            pl.BlockSpec((rows, width), fixed),
        ],
        out_shape=[
            jax.ShapeDtypeStruct((devices // 2, rows, 2 * channels // devices), BF16),
            jax.ShapeDtypeStruct((devices, pack_rows, channels // devices), BF16),
            jax.ShapeDtypeStruct((devices, tail_rows, width // devices), BF16),
            jax.ShapeDtypeStruct((rows, width), F32),
        ],
        scratch_shapes=[pltpu.VMEM((rows, width), F32)],
        compiler_params=pltpu.CompilerParams(vmem_limit_bytes=VMEM_LIMIT),
        name="mixer_back",
    )(
        grad_proj, scan_w, grad_u, x_inner, vec, grad_gate, in_t, in_t, u_act, tokens, gains,
        grad_mid, grad_widths,
    )


def gelu_parts(values):
    weight = jnp.exp(values * values * -0.5)
    scaled = jnp.abs(values) * 0.7071067811865476
    ratio = 1.0 / (1.0 + 0.3275911 * scaled)
    series = 1.061405429 * ratio - 1.453152027
    series = series * ratio + 1.421413741
    series = series * ratio - 0.284496736
    series = series * ratio + 0.254829592
    tail = (0.5 * ratio) * series * weight
    below = jnp.where(values >= 0.0, 1.0 - tail, tail)
    return values * below, below + values * weight * 0.3989422804014327


def router_kernel(
    mid_ref, gain_ref, router_ref, routes_col_ref, routes_row_ref, slots_row_ref, live_ref, cot_ref,
    sendr_ref, sendg_ref, normed_ref, probs_ref,
):
    mid = mid_ref[...]
    rows = mid.shape[0]
    experts = router_ref.shape[1]
    scale = lax.rsqrt(jnp.mean(mid * mid, -1, keepdims=True) + 1e-05)
    normed = (mid * scale * gain_ref[...]).astype(BF16)
    normed_ref[...] = normed
    logits = product(normed, router_ref[...])
    weights = jnp.exp(logits - jnp.max(logits, -1, keepdims=True))
    probs = weights / jnp.sum(weights, -1, keepdims=True)
    probs_ref[...] = probs
    chosen = (routes_col_ref[...] == iota((rows, experts), 1)).astype(F32)
    gate = jnp.sum(probs * chosen, 1, keepdims=True)
    grads = (gate * (cot_ref[...].astype(F32) * live_ref[...])).astype(BF16)
    slot = iota((experts * CAP, rows), 0)
    dispatch = (
        (routes_row_ref[...] == slot // CAP) & (slots_row_ref[...] == slot % CAP)
    ).astype(BF16)
    width = mid.shape[1]
    sendr_ref[...] = product(dispatch, normed).astype(BF16).reshape(experts, CAP, width)
    sendg_ref[...] = product(dispatch, grads).astype(BF16).reshape(experts, CAP, width)


def router_step(mid, gain, router, routes_col, routes_row, slots_row, live, cotangent):
    rows, width = mid.shape
    experts = router.shape[1]
    return pl.pallas_call(
        router_kernel,
        out_shape=[
            jax.ShapeDtypeStruct((experts, CAP, width), BF16),
            jax.ShapeDtypeStruct((experts, CAP, width), BF16),
            jax.ShapeDtypeStruct((rows, width), BF16),
            jax.ShapeDtypeStruct((rows, experts), F32),
        ],
        compiler_params=pltpu.CompilerParams(vmem_limit_bytes=VMEM_LIMIT),
        name="router_step",
    )(mid, gain, router, routes_col, routes_row, slots_row, live, cotangent)


def expert_out_kernel(rows_ref, up_ref, down_ref, out_ref, slope_ref, total):
    step = pl.program_id(0)
    pieces, cap, width = rows_ref.shape
    rows = rows_ref[...].reshape(pieces * cap, width)

    @pl.when(step == 0)
    def _():
        total[...] = jnp.zeros_like(total)

    activated, slope = gelu_parts(product(rows, up_ref[...]))
    slope_ref[...] = slope.astype(BF16)
    total[...] += product(activated.astype(BF16), down_ref[...])

    @pl.when(step == pl.num_programs(0) - 1)
    def _():
        out_ref[...] = total[...].astype(BF16).reshape(pieces, cap, width)


def expert_out(rows, up, down, tile):
    pieces, cap, width = rows.shape
    hidden = up.shape[1]
    fixed = lambda i: (0, 0, 0)
    return pl.pallas_call(
        expert_out_kernel,
        grid=(hidden // tile,),
        in_specs=[
            pl.BlockSpec(rows.shape, fixed),
            pl.BlockSpec((width, tile), lambda i: (0, i)),
            pl.BlockSpec((tile, width), lambda i: (i, 0)),
        ],
        out_specs=[
            pl.BlockSpec(rows.shape, fixed),
            pl.BlockSpec((pieces * cap, tile), lambda i: (0, i)),
        ],
        out_shape=[
            jax.ShapeDtypeStruct(rows.shape, BF16),
            jax.ShapeDtypeStruct((pieces * cap, hidden), BF16),
        ],
        scratch_shapes=[pltpu.VMEM((pieces * cap, width), F32)],
        compiler_params=pltpu.CompilerParams(vmem_limit_bytes=VMEM_LIMIT),
        name="expert_out",
    )(rows, up, down)


def expert_back_kernel(grads_ref, up_ref, down_ref, slope_ref, out_ref, total):
    step = pl.program_id(0)
    pieces, cap, width = grads_ref.shape
    grads = grads_ref[...].reshape(pieces * cap, width)

    @pl.when(step == 0)
    def _():
        total[...] = jnp.zeros_like(total)

    slope = slope_ref[...].astype(F32)
    grad_pre = (times_transpose(grads, down_ref[...]) * slope).astype(BF16)
    total[...] += times_transpose(grad_pre, up_ref[...])

    @pl.when(step == pl.num_programs(0) - 1)
    def _():
        out_ref[...] = total[...].astype(BF16).reshape(pieces, cap, width)


def expert_back(grads, up, down, slope, tile):
    pieces, cap, width = grads.shape
    hidden = up.shape[1]
    fixed = lambda i: (0, 0, 0)
    return pl.pallas_call(
        expert_back_kernel,
        grid=(hidden // tile,),
        in_specs=[
            pl.BlockSpec(grads.shape, fixed),
            pl.BlockSpec((width, tile), lambda i: (0, i)),
            pl.BlockSpec((tile, width), lambda i: (i, 0)),
            pl.BlockSpec((pieces * cap, tile), lambda i: (0, i)),
        ],
        out_specs=pl.BlockSpec(grads.shape, fixed),
        out_shape=jax.ShapeDtypeStruct(grads.shape, BF16),
        scratch_shapes=[pltpu.VMEM((pieces * cap, width), F32)],
        compiler_params=pltpu.CompilerParams(vmem_limit_bytes=VMEM_LIMIT),
        name="expert_back",
    )(grads, up, down, slope)


def expert_grads_kernel(chunks, rows_ref, grads_ref, up_ref, down_ref, gup_ref, gdown_ref, rows_t):
    chunk = pl.program_id(1)
    groups, pieces, cap, width = rows_ref.shape
    count = groups * pieces * cap
    rows = rows_ref[...].reshape(count, width)
    grads = grads_ref[...].reshape(count, width)

    @pl.when((pl.program_id(0) == 0) | (chunks > 1))
    def _():
        rows_t[...] = rows.T

    activated, slope = gelu_parts(product(rows, up_ref[...]))
    grad_pre = (times_transpose(grads, down_ref[...]) * slope).astype(BF16)
    grad_up = product(rows_t[...], grad_pre)
    grad_down = contract_rows(activated.astype(BF16), grads)

    @pl.when(chunk == 0)
    def _():
        gup_ref[...] = grad_up
        gdown_ref[...] = grad_down

    if chunks > 1:

        @pl.when(chunk > 0)
        def _():
            gup_ref[...] += grad_up
            gdown_ref[...] += grad_down


def expert_grads(rows, grads, up, down, tile):
    groups, pieces, cap, width = rows.shape
    hidden = up.shape[1]
    together = max(1, min(groups, 32 // pieces))
    chunks = groups // together
    some = pl.BlockSpec((together, pieces, cap, width), lambda i, j: (j, 0, 0, 0))
    return pl.pallas_call(
        partial(expert_grads_kernel, chunks),
        grid=(hidden // tile, chunks),
        in_specs=[
            some,
            some,
            pl.BlockSpec((width, tile), lambda i, j: (0, i)),
            pl.BlockSpec((tile, width), lambda i, j: (i, 0)),
        ],
        out_specs=[
            pl.BlockSpec((width, tile), lambda i, j: (0, i)),
            pl.BlockSpec((tile, width), lambda i, j: (i, 0)),
        ],
        out_shape=[
            jax.ShapeDtypeStruct((width, hidden), F32),
            jax.ShapeDtypeStruct((hidden, width), F32),
        ],
        scratch_shapes=[pltpu.VMEM((width, together * pieces * cap), BF16)],
        compiler_params=pltpu.CompilerParams(vmem_limit_bytes=VMEM_LIMIT),
        name="expert_grads",
    )(rows, grads, up, down)


def combine_kernel(
    mid_ref, gain_ref, router_ref, routes_ref, slots_ref, live_ref, cot_ref, probs_ref, normed_ref,
    backr_ref, backg_ref, out_ref, gradmid_ref, gradmix_ref, widths_ref,
):
    mid = mid_ref[...]
    rows, width = mid.shape
    experts = router_ref.shape[1]
    routes = routes_ref[...]
    chosen = (routes == iota((rows, experts), 1)).astype(F32)
    probs = probs_ref[...]
    gate = jnp.sum(probs * chosen, 1, keepdims=True)
    live = live_ref[...]
    slot = iota((rows, experts * CAP), 1)
    collect = ((routes == slot // CAP) & (slots_ref[...] == slot % CAP)).astype(BF16)
    expert_sum = product(collect, backr_ref[...].reshape(experts * CAP, width))
    out_ref[...] = (live * (mid + gate * expert_sum)).astype(BF16)
    grad_out = cot_ref[...].astype(F32) * live
    grad_gate = jnp.sum(grad_out * expert_sum, 1, keepdims=True)
    grad_logits = (probs * (chosen * grad_gate - gate * grad_gate)).astype(BF16)
    grad_router = contract_rows(grad_logits, normed_ref[...])
    grad = product(collect, backg_ref[...].reshape(experts * CAP, width))
    grad = grad + times_transpose(grad_logits, router_ref[...])
    scale = lax.rsqrt(jnp.mean(mid * mid, -1, keepdims=True) + 1e-05)
    unit = mid * scale
    widths_ref[...] = jnp.concatenate([grad_router, jnp.sum(grad * unit, 0, keepdims=True)], 0)
    inner = grad * gain_ref[...]
    grad_mid = grad_out + scale * (inner - unit * jnp.mean(inner * unit, -1, keepdims=True))
    gradmid_ref[...] = grad_mid
    gradmix_ref[...] = grad_mid.astype(BF16)


def combine_step(mid, gain, router, routes, slots, live, cotangent, probs, normed, backr, backg):
    rows, width = mid.shape
    return pl.pallas_call(
        combine_kernel,
        out_shape=[
            jax.ShapeDtypeStruct((rows, width), BF16),
            jax.ShapeDtypeStruct((rows, width), F32),
            jax.ShapeDtypeStruct((rows, width), BF16),
            jax.ShapeDtypeStruct((router.shape[1] + 1, width), F32),
        ],
        compiler_params=pltpu.CompilerParams(vmem_limit_bytes=VMEM_LIMIT),
        name="combine_step",
    )(mid, gain, router, routes, slots, live, cotangent, probs, normed, backr, backg)


MESH = pl.DeviceIdType.MESH


def neighbour(bit):
    me = lax.axis_index("expert")
    return me + (1 - 2 * ((me // bit) % 2)) * bit


def greet(line=True):
    devices, copies = lax.axis_size("expert"), lax.axis_size("dp")
    me, place = lax.axis_index("expert"), lax.axis_index("dp")
    barrier = pltpu.get_barrier_semaphore()
    for k in range(1, devices):
        pl.semaphore_signal(
            barrier, inc=1, device_id={"expert": (me + k) % devices}, device_id_type=MESH
        )
    if line:

        @pl.when(place < copies - 1)
        def _():
            pl.semaphore_signal(barrier, inc=1, device_id={"dp": place + 1}, device_id_type=MESH)

        @pl.when(place > 0)
        def _():
            pl.semaphore_signal(barrier, inc=1, device_id={"dp": place - 1}, device_id_type=MESH)

    ends = (place == 0) | (place == copies - 1)
    if line:
        pl.when(ends)(lambda: pl.semaphore_wait(barrier, devices))
        pl.when(jnp.logical_not(ends))(lambda: pl.semaphore_wait(barrier, devices + 1))
    else:
        pl.semaphore_wait(barrier, devices - 1)


class Exchange:
    def __init__(self, source, target, send_sems, recv_sems, local_sem):
        devices, me = lax.axis_size("expert"), lax.axis_index("expert")
        self.copies = []
        for k in range(1, devices):
            peer = (me + k) % devices
            self.copies.append(
                pltpu.make_async_remote_copy(
                    source.at[peer], target.at[me], send_sems.at[k], recv_sems.at[k],
                    device_id={"expert": peer}, device_id_type=MESH,
                )
            )
        self.local = pltpu.make_async_copy(source.at[me], target.at[me], local_sem)

    def start(self):
        for copy in self.copies:
            copy.start()
        self.local.start()

    def wait(self):
        self.local.wait()
        for copy in self.copies:
            copy.wait()


class Line:
    def __init__(self, stage, from_left, from_right, next_left, next_right, send_sems, recv_sems):
        place = lax.axis_index("dp")
        last = lax.axis_size("dp") - 1
        self.right = pltpu.make_async_remote_copy(
            from_left, next_left, send_sems.at[0], recv_sems.at[0],
            device_id={"dp": jnp.minimum(place + 1, last)}, device_id_type=MESH,
        )
        self.left = pltpu.make_async_remote_copy(
            from_right, next_right, send_sems.at[1], recv_sems.at[1],
            device_id={"dp": jnp.maximum(place - 1, 0)}, device_id_type=MESH,
        )
        self.send_right = (place >= stage - 1) & (place < last)
        self.send_left = (last - place >= stage - 1) & (place > 0)
        self.get_left = place >= stage
        self.get_right = last - place >= stage

    def start(self):
        pl.when(self.send_right)(lambda: self.right.start())
        pl.when(self.send_left)(lambda: self.left.start())

    def wait(self):
        pl.when(self.send_right)(lambda: self.right.wait_send())
        pl.when(self.send_left)(lambda: self.left.wait_send())
        pl.when(self.get_left)(lambda: self.right.wait_recv())
        pl.when(self.get_right)(lambda: self.left.wait_recv())


def as_column(row):
    return jnp.broadcast_to(row.astype(F32), (8, row.shape[1])).T[:, 0:1].astype(jnp.int32)


def dispatch_matrix(goal, experts):
    slot = iota((experts * CAP, goal.shape[1]), 0)
    return (goal[0:1, :] == slot).astype(BF16)


def expert_layer_kernel(
    length_ref, mid_ref, gains_ref, router_ref, routes_ref, slots_ref, cot_ref, up_hbm, down_hbm,
    out_ref, gradmid_ref, gradmix_ref, widths_ref, rows_out, grads_out,
    left_1, right_1, left_2, right_2, goal_l1, goal_r1, goal_l2, goal_r2, gup_hbm, gdown_hbm,
    raw, goal, up_ref, down_ref, send_r, send_g, got_r, got_g, slope_ref, total, give_r, give_g,
    back_r, back_g, probs_ref, act_ref, rows_t, gup_ref, gdown_ref,
    weight_sems, send_sems, recv_sems, local_sems, line_send, line_recv, out_sems, grad_sems,
):
    tile = 512
    rows, width = mid_ref.shape
    experts = router_ref.shape[0]
    hidden = up_ref.shape[1]
    load_up = pltpu.make_async_copy(up_hbm, up_ref, weight_sems.at[0])
    load_down = pltpu.make_async_copy(down_hbm, down_ref, weight_sems.at[1])
    load_up.start()
    load_down.start()
    greet()

    ways = [
        Exchange(source, target, send_sems.at[k], recv_sems.at[k], local_sems.at[k])
        for k, (source, target) in enumerate(
            [(send_r, got_r), (send_g, got_g), (give_r, back_r), (give_g, back_g)]
        )
    ]
    lines = [
        Line(stage, *buffers, line_send.at[k], line_recv.at[k])
        for k, (stage, buffers) in enumerate(
            [(1, (raw.at[part], raw.at[part], left_1.at[part], right_1.at[part])) for part in (0, 1)]
            + [(1, (goal, goal, goal_l1, goal_r1))]
            + [
                (2, (left_1.at[part], right_1.at[part], left_2.at[part], right_2.at[part]))
                for part in (0, 1)
            ]
            + [(2, (goal_l1, goal_r1, goal_l2, goal_r2))]
        )
    ]
    gain = gains_ref[1:2, :]
    live = (iota((rows, 1), 0) < length_ref[0]).astype(F32)
    routes, slots = as_column(routes_ref[...]), as_column(slots_ref[...])
    mid = mid_ref[...]
    scale = lax.rsqrt(jnp.mean(mid * mid, -1, keepdims=True) + 1e-05)
    normed = (mid * scale * gain).astype(BF16)
    raw[0] = normed
    slots_row = slots_ref[...]
    target = jnp.where(slots_row < CAP, routes_ref[...] * CAP + slots_row, -1)
    goal[...] = jnp.broadcast_to(target, goal.shape)
    dispatch = dispatch_matrix(goal, experts)
    send_r[...] = product(dispatch, normed).astype(BF16).reshape(experts, CAP, width)
    ways[0].start()
    for k in (0, 2):
        lines[k].start()
    logits = times_transpose(normed, router_ref[...])
    weights = jnp.exp(logits - jnp.max(logits, -1, keepdims=True))
    probs = weights / jnp.sum(weights, -1, keepdims=True)
    probs_ref[...] = probs
    chosen = (routes == iota((rows, experts), 1)).astype(F32)
    gate = jnp.sum(probs * chosen, 1, keepdims=True)
    grads = (gate * (cot_ref[...].astype(F32) * live)).astype(BF16)
    raw[1] = grads
    send_g[...] = product(dispatch, grads).astype(BF16).reshape(experts, CAP, width)
    ways[1].start()
    lines[1].start()

    load_up.wait()
    load_down.wait()
    ways[0].wait()
    for k in (0, 2):
        lines[k].wait()
        lines[k + 3].start()
    keep_rows = pltpu.make_async_copy(got_r, rows_out, out_sems.at[0])
    keep_rows.start()
    total[...] = jnp.zeros_like(total)

    def forward(step, carry):
        at = pl.ds(pl.multiple_of(step * tile, tile), tile)
        inputs = got_r[...].reshape(experts * CAP, width)
        activated, slope = gelu_parts(product(inputs, up_ref[:, at]))
        slope_ref[:, at] = slope.astype(BF16)
        activated = activated.astype(BF16)
        act_ref[:, at] = activated
        total[...] += product(activated, down_ref[at, :])
        return carry

    lax.fori_loop(0, hidden // tile, forward, 0)
    give_r[...] = total[...].astype(BF16).reshape(experts, CAP, width)
    ways[2].start()
    ways[1].wait()
    lines[1].wait()
    lines[4].start()
    keep_grads = pltpu.make_async_copy(got_g, grads_out, out_sems.at[1])
    keep_grads.start()
    total[...] = jnp.zeros_like(total)

    def backward(step, carry):
        at = pl.ds(pl.multiple_of(step * tile, tile), tile)
        outputs = got_g[...].reshape(experts * CAP, width)
        slope = slope_ref[:, at].astype(F32)
        grad_pre = (times_transpose(outputs, down_ref[at, :]) * slope).astype(BF16)
        slope_ref[:, at] = grad_pre
        total[...] += times_transpose(grad_pre, up_ref[:, at])
        return carry

    lax.fori_loop(0, hidden // tile, backward, 0)
    give_g[...] = total[...].astype(BF16).reshape(experts, CAP, width)
    ways[3].start()

    rows_t[...] = got_r[...].reshape(experts * CAP, width).T
    stores = []
    for step in range(hidden // tile):
        spot = step % 2
        at = pl.ds(step * tile, tile)
        if step >= 2:
            for store in stores[2 * (step - 2) : 2 * (step - 1)]:
                store.wait()
        gup_ref[spot] = product(rows_t[...], slope_ref[:, at]).astype(BF16)
        gdown_ref[spot] = contract_rows(
            act_ref[:, at], got_g[...].reshape(experts * CAP, width)
        ).astype(BF16)
        stores += [
            pltpu.make_async_copy(gup_ref.at[spot], gup_hbm.at[:, at], grad_sems.at[0, spot]),
            pltpu.make_async_copy(gdown_ref.at[spot], gdown_hbm.at[at], grad_sems.at[1, spot]),
        ]
        for store in stores[-2:]:
            store.start()

    chosen = (routes == iota((rows, experts), 1)).astype(F32)
    probs = probs_ref[...]
    gate = jnp.sum(probs * chosen, 1, keepdims=True)
    slot = iota((rows, experts * CAP), 1)
    collect = ((routes == slot // CAP) & (slots == slot % CAP)).astype(BF16)
    ways[2].wait()
    expert_sum = product(collect, back_r[...].reshape(experts * CAP, width))
    mid = mid_ref[...]
    out_ref[...] = (live * (mid + gate * expert_sum)).astype(BF16)
    grad_out = cot_ref[...].astype(F32) * live
    grad_gate = jnp.sum(grad_out * expert_sum, 1, keepdims=True)
    grad_logits = (probs * (chosen * grad_gate - gate * grad_gate)).astype(BF16)
    grad_router = contract_rows(grad_logits, raw[0])
    from_logits = product(grad_logits, router_ref[...])
    scale = lax.rsqrt(jnp.mean(mid * mid, -1, keepdims=True) + 1e-05)
    unit = mid * scale
    ways[3].wait()
    grad = product(collect, back_g[...].reshape(experts * CAP, width)) + from_logits
    widths_ref[...] = jnp.concatenate([grad_router, jnp.sum(grad * unit, 0, keepdims=True)], 0)
    inner = grad * gain
    grad_mid = grad_out + scale * (inner - unit * jnp.mean(inner * unit, -1, keepdims=True))
    gradmid_ref[...] = grad_mid
    gradmix_ref[...] = grad_mid.astype(BF16)
    for store in stores[-4:]:
        store.wait()
    keep_rows.wait()
    keep_grads.wait()
    for k in (3, 4, 5):
        lines[k].wait()


def expert_layer(lengths, mid, gains, router, routes, slots, cotangent, up, down):
    rows, width = mid.shape
    experts = router.shape[0]
    hidden = up.shape[1]
    buffer = (experts, CAP, width)
    here = pl.BlockSpec(memory_space=pltpu.VMEM)
    far = pl.BlockSpec(memory_space=pl.ANY)
    blocks = jax.ShapeDtypeStruct(buffer, BF16)
    raw = jax.ShapeDtypeStruct((2, rows, width), BF16)
    goal = jax.ShapeDtypeStruct((8, rows), jnp.int32)
    dma = pltpu.SemaphoreType.DMA
    return pl.pallas_call(
        expert_layer_kernel,
        in_specs=[pl.BlockSpec(memory_space=pltpu.SMEM)] + [here] * 6 + [far] * 2,
        out_specs=[here] * 4 + [far] * 12,
        out_shape=[
            jax.ShapeDtypeStruct((rows, width), BF16),
            jax.ShapeDtypeStruct((rows, width), F32),
            jax.ShapeDtypeStruct((rows, width), BF16),
            jax.ShapeDtypeStruct((experts + 1, width), F32),
        ] + [blocks] * 2 + [raw] * 4 + [goal] * 4 + [
            jax.ShapeDtypeStruct(up.shape, BF16),
            jax.ShapeDtypeStruct(down.shape, BF16),
        ],
        scratch_shapes=[
            pltpu.VMEM(raw.shape, BF16),
            pltpu.VMEM(goal.shape, jnp.int32),
            pltpu.VMEM(up.shape, BF16),
            pltpu.VMEM(down.shape, BF16),
        ] + [pltpu.VMEM(buffer, BF16)] * 4 + [
            pltpu.VMEM((experts * CAP, hidden), BF16),
            pltpu.VMEM((experts * CAP, width), F32),
        ] + [pltpu.VMEM(buffer, BF16)] * 4 + [
            pltpu.VMEM((rows, experts), F32),
            pltpu.VMEM((experts * CAP, hidden), BF16),
            pltpu.VMEM((width, experts * CAP), BF16),
            pltpu.VMEM((2, width, 512), BF16),
            pltpu.VMEM((2, 512, width), BF16),
            dma((2,)), dma((4, experts)), dma((4, experts)), dma((4,)), dma((6, 2)), dma((6, 2)),
            dma((2,)), dma((2, 2)),
        ],
        compiler_params=pltpu.CompilerParams(
            vmem_limit_bytes=VMEM_LIMIT, collective_id=1, has_side_effects=True
        ),
        name="expert_layer",
    )(lengths, mid, gains, router, routes, slots, cotangent, up, down)


class PlaneGather:
    def __init__(self, source, target, send_sems, recv_sems, local_sem):
        me = lax.axis_index("expert")
        core, side, above = neighbour(1), neighbour(2), neighbour(4)
        far = side + above - me
        rows = target.shape[1]
        first, second = pl.ds(0, rows // 2), pl.ds(rows // 2, rows - rows // 2)
        every = pl.ds(0, rows)

        def send(k, block, owner, part, device):
            return pltpu.make_async_remote_copy(
                block, target.at[owner, part], send_sems.at[k], recv_sems.at[k],
                device_id={"expert": device}, device_id_type=MESH,
            )

        self.copies = [
            send(0, source.at[first], me, first, side),
            send(1, source.at[second], me, second, side),
            send(2, source.at[first], me, first, above),
            send(3, source.at[second], me, second, above),
            send(4, target.at[side, first], side, first, above),
            send(5, target.at[above, second], above, second, side),
            send(6, source, me, every, core),
            send(7, target.at[side], side, every, core),
            send(8, target.at[above], above, every, core),
            send(9, target.at[far], far, every, core),
        ]
        self.local = pltpu.make_async_copy(source, target.at[me], local_sem)

    def step(self, number):
        copies = self.copies
        for k in ((), (0, 3), (1, 2), (4, 5), (6, 7, 8, 9))[number]:
            copies[k].wait_recv()
        for k in ((0, 3, 1, 2, 6), (4, 5), (7, 8), (9,), ())[number]:
            copies[k].start()
        if number == 0:
            self.local.start()
        if number == 4:
            self.local.wait()
            for copy in copies:
                copy.wait_send()


class WideGather:
    def __init__(self, source, target, send_sems, recv_sems, local_sem):
        me, place = lax.axis_index("expert"), lax.axis_index("dp")
        core, side, above = neighbour(1), neighbour(2), neighbour(4)
        far = side + above - me
        odd = place % 2
        partner = place + 1 - 2 * odd
        rows = target.shape[1]
        unit = rows // 6

        def part(start, count):
            return pl.ds(pl.multiple_of(start * unit, unit), count * unit)

        def send(k, block, owner, where, **device):
            return pltpu.make_async_remote_copy(
                block, target.at[owner, where], send_sems.at[k], recv_sems.at[k],
                device_id=device, device_id_type=MESH,
            )

        def forward(k, owner, where, **device):
            return send(k, target.at[owner, where], owner, where, **device)

        outer, inner = part(4 * odd, 2), part(4 * (1 - odd), 2)
        middle = part(2, 2)
        self.copies = [
            send(0, source.at[outer], me, outer, expert=side),
            send(1, source.at[middle], me, middle, expert=side),
            send(2, source.at[inner], me, inner, expert=above),
            send(3, source.at[middle], me, middle, expert=above),
            forward(4, side, outer, expert=above),
            forward(5, side, part(2 + odd, 1), expert=above),
            forward(6, above, inner, expert=side),
            forward(7, above, part(3 - odd, 1), expert=side),
            forward(8, side, outer, dp=partner),
            forward(9, above, inner, dp=partner),
            send(10, source, me, part(0, 6), expert=core),
            forward(11, side, part(2 * odd, 4), expert=core),
            forward(12, above, part(2 - 2 * odd, 4), expert=core),
            forward(13, side, inner, expert=core),
            forward(14, above, outer, expert=core),
            forward(15, far, part(0, 6), expert=core),
        ]
        self.local = pltpu.make_async_copy(source, target.at[me], local_sem)

    def step(self, number):
        copies = self.copies
        for k in ((), (0, 2), (1, 3), (8, 9), (4, 5, 6, 7), (10, 11, 12, 13, 14, 15))[number]:
            copies[k].wait_recv()
        for k in ((0, 2, 1, 3, 10), (4, 6, 8, 9), (5, 7, 11, 12), (13, 14), (15,), ())[number]:
            copies[k].start()
        if number == 0:
            self.local.start()
        if number == 5:
            self.local.wait()
            for copy in copies:
                copy.wait_send()


class Near:
    def __init__(self, own, target, send_sems, recv_sems):
        self.place = lax.axis_index("dp")
        self.last = lax.axis_size("dp") - 1
        self.right = pltpu.make_async_remote_copy(
            own, target, send_sems.at[0], recv_sems.at[0],
            device_id={"dp": jnp.minimum(self.place + 1, self.last)}, device_id_type=MESH,
        )
        self.left = pltpu.make_async_remote_copy(
            own, target, send_sems.at[1], recv_sems.at[1],
            device_id={"dp": jnp.maximum(self.place - 1, 0)}, device_id_type=MESH,
        )

    def start(self):
        pl.when(self.place < self.last)(lambda: self.right.start())
        pl.when(self.place == 1)(lambda: self.left.start())

    def wait(self):
        pl.when(self.place < self.last)(lambda: self.right.wait_send())
        pl.when(self.place == 1)(lambda: self.left.wait_send())
        pl.when(self.place > 0)(lambda: self.right.wait_recv())
        pl.when(self.place == 0)(lambda: self.left.wait_recv())


DMA = pltpu.SemaphoreType.DMA
FAR = pl.BlockSpec(memory_space=pl.ANY)


def remote_params(collective_id):
    return pltpu.CompilerParams(
        vmem_limit_bytes=VMEM_LIMIT, collective_id=collective_id, has_side_effects=True
    )


def columns_of(proj_ref, first, state, target):
    turned = proj_ref[...].T[first : first + state]
    for block in range(proj_ref.shape[0] // BLOCK):
        target[block * state : (block + 1) * state, 0:BLOCK] = turned[
            :, block * BLOCK : (block + 1) * BLOCK
        ]


def diagonals_of(proj_ref, first, state, high_ref, low_ref):
    rows, width = proj_ref.shape
    big = BLOCK * state
    place = (iota((width, big), 0) == first + iota((width, big), 1) % state).astype(BF16)
    own = iota((rows, big), 0) % BLOCK == iota((rows, big), 1) // state
    for part, target in zip(two_parts(proj_ref[...]), (high_ref, low_ref)):
        target[...] = jnp.where(own, product(part, place), 0.0).astype(BF16)


def block_of(ref, block, size):
    return ref[pl.ds(pl.multiple_of(block * size, size), size), :]


def forward_kernel(
    tokens_ref, in_ref, scan_ref, step_w_ref, decay_ref, conv_ref, vectors_ref, norms_ref,
    router_ref, outw_ref,
    normed_ref, xin_ref, u_out, gate_out, proj_ref, step_ref, mixed_ref, gated_ref, mid_ref,
    step_full, vec_ref, router_full, gains_ref, scan_full, in_full, outw_all, normed_all, hist_hbm,
    columns, widths, columns_all, widths_all, scan_here, in_here, u_all, gate_all, b_cols, c_high, c_low, du,
    scanned, gated_all, outw_here, ring,
    send_sems, recv_sems, local_sems, ring_sems,
):
    step = pl.program_id(0)
    devices, rank, part = columns_all.shape[0], step_w_ref.shape[0], step_w_ref.shape[1]
    state, taps, experts = decay_ref.shape[0], conv_ref.shape[0], router_ref.shape[0]
    slice_w = widths.shape[1]
    rows, tile = xin_ref.shape
    width = tokens_ref.shape[1]
    big = BLOCK * state
    turns = ring.shape[0]
    last = rows // BLOCK - 1
    small = [
        PlaneGather(source, target, send_sems.at[k], recv_sems.at[k], local_sems.at[k])
        for k, (source, target) in enumerate(
            [(columns, columns_all), (widths, widths_all), (scan_ref, scan_here)]
        )
    ]
    big_gather = WideGather(in_ref, in_here, send_sems.at[3], recv_sems.at[3], local_sems.at[3])
    gather = WideGather(outw_ref, outw_here, send_sems.at[4], recv_sems.at[4], local_sems.at[4])
    normed_gather = PlaneGather(
        normed_ref, normed_all, send_sems.at[5], recv_sems.at[5], local_sems.at[5]
    )
    keep = pltpu.make_async_copy(outw_here, outw_all, local_sems.at[6])
    keep_in = pltpu.make_async_copy(in_here, in_full, local_sems.at[7])
    half = step % 2
    lanes = pl.ds(pl.multiple_of(half * tile, tile), tile)

    @pl.when(step == 0)
    def _():
        spare = columns.shape[0] - rank - state - taps - 3
        columns[...] = jnp.concatenate(
            [
                step_w_ref[...].astype(F32), decay_ref[...].astype(F32), conv_ref[...].astype(F32),
                vectors_ref[...].astype(F32), jnp.zeros((spare, part), F32),
            ],
            0,
        ).astype(BF16)
        widths[...] = jnp.concatenate(
            [
                router_ref[...].astype(F32), norms_ref[...].astype(F32),
                jnp.zeros((widths.shape[0] - experts - 2, slice_w), F32),
            ],
            0,
        ).astype(BF16)
        greet()
        for number in range(3):
            for one in small:
                one.step(number)
            big_gather.step(number)
        for number in (3, 4):
            for one in small:
                one.step(number)
        big_gather.step(3)
        table = jnp.concatenate([columns_all[k].astype(F32) for k in range(devices)], 1)
        step_full[...] = table[:rank].astype(BF16)
        scan_full[...] = scan_here[...]
        rest = table[rank:]
        vec_ref[0:state, :] = -jnp.exp(rest[:state])
        vec_ref[state : state + 8, :] = rest[state : state + 8]
        across = jnp.concatenate([widths_all[k].astype(F32) for k in range(devices)], 1)
        router_full[...] = across[:experts].astype(BF16)
        gains_ref[...] = across[experts : experts + 8]
        values = tokens_ref[...].astype(F32)
        scale = lax.rsqrt(jnp.mean(values * values, -1, keepdims=True) + 1e-05)
        normed_ref[...] = (values * scale * gains_ref[0:1, :]).astype(BF16)
        proj_ref[...] = jnp.zeros_like(proj_ref)
        big_gather.step(4)
        gather.step(0)
        big_gather.step(5)
        keep_in.start()

    @pl.when(step < 2)
    def _():
        misc = vec_ref[state : state + 8, lanes]
        normed = normed_ref[...]
        own = devices // 4

        def weights(first):
            rows_here = in_here.shape[1]
            return in_here[pl.ds(first + half * own, own)].reshape(own * rows_here, width)

        x_inner = times_transpose(normed, weights(0))
        gate_in = times_transpose(normed, weights(devices // 2))
        gate_out[...] = gate_in
        gate_all[:, lanes] = gate_in
        xin_ref[...] = x_inner
        summed = misc[taps : taps + 1] + misc[taps - 1 : taps] * x_inner
        for back in range(1, taps):
            tap = taps - 1 - back
            summed = summed + misc[tap : tap + 1] * shift_rows(x_inner, back)
        u_act = summed * sigmoid(summed)
        u_out[...] = u_act
        u_all[:, lanes] = u_act
        parts = devices // 2
        scan_rows_here = scan_here[pl.ds(half * parts, parts)].reshape(tile, scan_here.shape[2])
        proj_ref[...] += product(u_act.astype(BF16), scan_rows_here)

    @pl.when(step == 1)
    def _():
        gather.step(1)
        gather.step(2)
        normed_gather.step(0)
        columns_of(proj_ref, rank, state, b_cols)
        diagonals_of(proj_ref, rank + state, state, c_high, c_low)

    def store(spot, block):
        start = pl.multiple_of((block * BLOCK + 1) * state, state)
        return pltpu.make_async_copy(
            ring.at[spot], hist_hbm.at[pl.ds(start, big), lanes], ring_sems.at[spot]
        )

    def sum_states(spot, block):
        high, low = block_of(c_high, block, BLOCK), block_of(c_low, block, BLOCK)
        both = product(jnp.concatenate([high, low], 0), ring[spot])
        return both[:BLOCK] + both[BLOCK:]

    def between(position):
        if position == 1:
            gather.step(3)
            gather.step(4)
        if position == 4:
            gather.step(5)
            keep.start()
            normed_gather.step(1)
            normed_gather.step(2)
        if position == 7:
            normed_gather.step(3)

    @pl.when(step >= 2)
    def _():
        misc = vec_ref[state : state + 8, lanes]
        u_act = u_all[:, lanes]
        step_size = softplus(
            product(proj_ref[:, :rank].astype(BF16), step_full[:, lanes])
            + misc[taps + 1 : taps + 2]
        )
        step_ref[...] = step_size
        du[...] = step_size * u_act
        decay = vec_ref[0:state, lanes] * LOG2E
        ring[turns - 1] = jnp.zeros((big, tile), BF16)
        zero_row = pltpu.make_async_copy(
            ring.at[turns - 1, pl.ds(0, state)], hist_hbm.at[pl.ds(0, state), lanes],
            ring_sems.at[turns],
        )
        zero_row.start()
        zero_row.wait()

        def run_blocks(quarter, held):
            for spot in range(turns):
                block = quarter * turns + spot
                pl.when(quarter > 0)(lambda: store(spot, block).wait())
                base = pl.multiple_of(block * BLOCK, BLOCK)
                before = (spot - 1) % turns
                scanned[pl.ds(base, BLOCK), :] = sum_states(before, jnp.maximum(block - 1, 0))
                steps_now, du_now = block_of(step_ref, block, BLOCK), block_of(du, block, BLOCK)
                b_now = block_of(b_cols, block, state)
                for t in range(BLOCK):
                    b_wide = jnp.broadcast_to(b_now[:, t : t + 1], (state, tile))
                    fade = jnp.exp2(steps_now[t : t + 1, :] * decay)
                    held = fade * held + du_now[t : t + 1, :] * b_wide
                    ring[spot, t * state : (t + 1) * state, :] = held.astype(BF16)
                store(spot, block).start()
            for turn in range(2):
                for count in range(rows // BLOCK // turns):

                    @pl.when((step == turn + 2) & (quarter == count))
                    def _():
                        between(turn * 4 + count)

            return held

        quarters = rows // BLOCK // turns
        lax.fori_loop(0, quarters, run_blocks, jnp.zeros((state, tile), F32))
        scanned[pl.ds(rows, BLOCK), :] = sum_states(turns - 1, last)
        mixed = scanned[pl.ds(BLOCK, rows), :] + misc[taps + 2 : taps + 3] * u_act
        mixed_ref[...] = mixed
        gate_in = gate_all[:, lanes]
        gated = (mixed * (gate_in * sigmoid(gate_in))).astype(BF16)
        gated_ref[...] = gated.T.reshape(gated_ref.shape)
        gated_all[:, lanes] = gated
        for spot in range(turns):
            store(spot, last - turns + 1 + spot).wait()

    @pl.when(step == 3)
    def _():
        weights = outw_here[...].reshape(devices * part, width)
        mid_ref[...] = tokens_ref[...].astype(F32) + product(gated_all[...], weights)
        keep.wait()
        keep_in.wait()
        normed_gather.step(4)


def forward_plane(
    tokens, in_t, scan_w, step_w, decay_t, conv, vectors, norms, router_t, out_w
):
    rows, width = tokens.shape
    rank, part = step_w.shape
    cols = scan_w.shape[1]
    devices = lax.axis_size("expert")
    channels = devices * part
    state, experts, slice_w = decay_t.shape[0], router_t.shape[0], router_t.shape[1]
    tile = channels // 2
    hist_rows = (rows + 1) * state
    first = lambda i: jnp.minimum(i, 1)
    second = lambda i: jnp.maximum(i - 2, 0)

    def whole(shape):
        return pl.BlockSpec(shape, lambda i: (0,) * len(shape), pipeline_mode=pl.Buffered(1))

    def kept(shape):
        return pl.BlockSpec(shape, lambda i: (0,) * len(shape))

    def halves(index):
        return pl.BlockSpec((rows, tile), lambda i: (0, index(i)))

    inputs = (tokens, in_t, scan_w, step_w, decay_t, conv, vectors, norms, router_t)
    fixed = [
        ((rank, channels), BF16), ((state + 8, channels), F32), ((experts, width), BF16),
        ((8, width), F32), ((devices, part, cols), BF16),
    ]
    return pl.pallas_call(
        forward_kernel,
        grid=(4,),
        in_specs=[whole(value.shape) for value in inputs] + [FAR],
        out_specs=[
            kept((rows, width)),
            halves(first),
            halves(first),
            halves(first),
            kept((rows, cols)),
            halves(second),
            halves(second),
            pl.BlockSpec((devices // 2, part, rows), lambda i: (second(i), 0, 0)),
            kept((rows, width)),
        ] + [kept(shape) for shape, _ in fixed] + [FAR] * 4,
        out_shape=[
            jax.ShapeDtypeStruct((rows, width), BF16),
            jax.ShapeDtypeStruct((rows, channels), F32),
            jax.ShapeDtypeStruct((rows, channels), F32),
            jax.ShapeDtypeStruct((rows, channels), F32),
            jax.ShapeDtypeStruct((rows, cols), F32),
            jax.ShapeDtypeStruct((rows, channels), F32),
            jax.ShapeDtypeStruct((rows, channels), F32),
            jax.ShapeDtypeStruct((devices, part, rows), BF16),
            jax.ShapeDtypeStruct((rows, width), F32),
        ] + [jax.ShapeDtypeStruct(shape, kind) for shape, kind in fixed] + [
            jax.ShapeDtypeStruct((devices,) + in_t.shape, BF16),
            jax.ShapeDtypeStruct((devices, part, width), BF16),
            jax.ShapeDtypeStruct((devices, rows, width), BF16),
            jax.ShapeDtypeStruct((hist_rows, channels), BF16),
        ],
        scratch_shapes=[
            pltpu.VMEM((rank + state + 8, part), BF16),
            pltpu.VMEM((32, slice_w), BF16),
            pltpu.VMEM((devices, rank + state + 8, part), BF16),
            pltpu.VMEM((devices, 32, slice_w), BF16),
            pltpu.VMEM((devices, part, cols), BF16),
            pltpu.VMEM((devices,) + in_t.shape, BF16),
            pltpu.VMEM((rows, channels), F32),
            pltpu.VMEM((rows, channels), F32),
            pltpu.VMEM((rows // BLOCK * state, 128), F32),
            pltpu.VMEM((rows, BLOCK * state), BF16),
            pltpu.VMEM((rows, BLOCK * state), BF16),
            pltpu.VMEM((rows, tile), F32),
            pltpu.VMEM((rows + BLOCK, tile), F32),
            pltpu.VMEM((rows, channels), BF16),
            pltpu.VMEM((devices, part, width), BF16),
            pltpu.VMEM((4, BLOCK * state, tile), BF16),
            DMA((6, 16)), DMA((6, 16)), DMA((8,)), DMA((5,)),
        ],
        compiler_params=remote_params(3),
        name="mixer_forward",
    )(*inputs, out_w)


def prepare_sends(raw, goal, sends):
    experts, cap, width = sends.shape[1:]
    matrix = dispatch_matrix(goal, experts)
    for part in range(2):
        values = product(matrix, raw[part]).astype(BF16)
        sends[part] = values.reshape(experts, cap, width)


def pick(choices, raw, goal, sems):
    place = lax.axis_index("dp")
    for where, (source, source_goal) in enumerate(choices):

        @pl.when(place == where)
        def _():
            copies = [
                pltpu.make_async_copy(source, raw, sems.at[0]),
                pltpu.make_async_copy(source_goal, goal, sems.at[1]),
            ]
            for copy in copies:
                copy.start()
            for copy in copies:
                copy.wait()


def fold_rows(got_ref, width):
    total = jnp.sum(got_ref[...].astype(F32), 0)
    quarter = total.shape[0] // 4
    folded = jnp.concatenate([total[k * quarter : (k + 1) * quarter] for k in range(4)], 1)
    return jnp.concatenate([folded, jnp.zeros((32 - quarter, width), F32)], 0).astype(BF16)


def backward_kernel(
    proj_ref, stepw_ref, decay_ref, misc_ref, u_ref, gate_ref, outw_ref, gradmix_ref, step_ref,
    mixed_ref, scanw_ref, xin_ref, misc_x_ref, wx_ref, wg_ref, u_x_ref, tokens_ref, gains_ref,
    widths_ref,
    gradmid_hbm, gated_hbm, normed_hbm, hist_hbm, rows_0, grads_0, left_2, right_2, right_1,
    goal_l2, goal_r2, goal_r1,
    gradtok_hbm, totals_hbm, rows_1, grads_1, left_3, right_3, goal_l3, goal_r3, sends_hbm,
    c_cols, b_high, b_low, b_sums, c_sums, gy, du, grad_du, grad_step, ring, g_ring, w_ring,
    gradproj, gradu_all, gate_all, send_in, got_in, everyone, gated_all, send_scan, got_scan,
    pack_back, send_back, got_back, send_tail, got_tail, totals, raw, goal,
    g_send, g_recv, x_send, x_recv, l_send, l_recv, local_sems, ring_sems, load_sems,
):
    step = pl.program_id(0)
    devices, me = lax.axis_size("expert"), lax.axis_index("expert")
    half = devices // 2
    rank, state = stepw_ref.shape[0], decay_ref.shape[0]
    rows, cols = proj_ref.shape
    tile, small_tile, width = u_ref.shape[1], xin_ref.shape[1], tokens_ref.shape[1]
    blocks, big = rows // BLOCK, BLOCK * state
    turns = ring.shape[0]
    quarters = blocks // turns
    in_part = send_in.shape[0] // devices
    channels = half * in_part
    steps_x = channels // small_tile
    mix = PlaneGather(gradmix_ref, everyone, g_send, g_recv, local_sems.at[0])
    ways = [
        Exchange(source, target, x_send.at[k], x_recv.at[k], local_sems.at[k + 1])
        for k, (source, target) in enumerate(
            [
                (gated_hbm, gated_all), (send_scan, got_scan), (send_back, got_back),
                (send_tail, got_tail),
            ]
        )
    ]

    def input_part(device):
        return send_in.at[pl.ds(pl.multiple_of(device * in_part, in_part), in_part)]

    input_copies = [
        pltpu.make_async_remote_copy(
            input_part((me + k) % devices), got_in.at[me], x_send.at[4, k], x_recv.at[4, k],
            device_id={"expert": (me + k) % devices}, device_id_type=MESH,
        )
        for k in range(1, devices)
    ]
    input_local = pltpu.make_async_copy(input_part(me), got_in.at[me], local_sems.at[5])

    def start_inputs(first, last):
        for k, copy in enumerate(input_copies):
            peer = (me + k + 1) % devices
            pl.when((peer >= first) & (peer < last))(lambda copy=copy: copy.start())
        pl.when((me >= first) & (me < last))(lambda: input_local.start())

    lines = [
        Line(3, left_2, right_2, left_3, right_3, l_send.at[0], l_recv.at[0]),
        Line(3, goal_l2, goal_r2, goal_l3, goal_r3, l_send.at[1], l_recv.at[1]),
        Near(rows_0, rows_1, l_send.at[2], l_recv.at[2]),
        Near(grads_0, grads_1, l_send.at[3], l_recv.at[3]),
    ]
    load_normed = pltpu.make_async_copy(normed_hbm, everyone, load_sems.at[0])
    load_mid = pltpu.make_async_copy(gradmid_hbm, gy, load_sems.at[1])
    store_sends = [
        pltpu.make_async_copy(source, sends_hbm.at[k], load_sems.at[6 + k])
        for k, source in enumerate((g_ring, w_ring))
    ]
    x_spot = (jnp.maximum(step - 2, 0) % steps_x) // (steps_x // 2)
    x_lanes = pl.ds(
        pl.multiple_of((jnp.maximum(step - 2, 0) % (steps_x // 2)) * small_tile, small_tile),
        small_tile,
    )
    lanes = pl.ds(pl.multiple_of(jnp.minimum(step, 1) * tile, tile), tile)

    def load(spot, block):
        start = pl.multiple_of(block * big, big)
        return pltpu.make_async_copy(
            hist_hbm.at[pl.ds(start, big + state), lanes], ring.at[spot], ring_sems.at[spot]
        )

    @pl.when(step < 2)
    def _():
        for spot in range(turns - 1):
            load(spot, blocks - 1 - spot).start()

    @pl.when(step == 0)
    def _():
        greet()
        mix.step(0)
        for line in lines:
            line.start()
        gradproj[...] = jnp.zeros_like(gradproj)
        b_sums[...] = jnp.zeros_like(b_sums)
        c_sums[...] = jnp.zeros_like(c_sums)
        columns_of(proj_ref, rank + state, state, c_cols)
        diagonals_of(proj_ref, rank, state, b_high, b_low)

    def between(position):
        if position == 2:
            mix.step(1)
            mix.step(2)
            ways[0].start()
        if position == 5:
            mix.step(3)
        if position == 7:
            mix.step(4)
            ways[0].wait()

    @pl.when(step < 2)
    def _():
        skip_ref = scan_rows(misc_ref)[1]
        grad_gated = times_transpose(gradmix_ref[...], outw_ref[...])
        gate_in = gate_ref[...]
        gate_sig = sigmoid(gate_in)
        grad_mixed = grad_gated * (gate_in * gate_sig)
        grad_gate = (
            grad_gated * mixed_ref[...] * (gate_sig * (1.0 + gate_in * (1.0 - gate_sig)))
        ).astype(BF16)
        gate_all[:, lanes] = grad_gate
        start = pl.multiple_of(channels + step * tile, tile)
        send_in[pl.ds(start, tile), :] = grad_gate.T
        u_act = u_ref[...]
        step_size = step_ref[...]
        gy[...] = grad_mixed
        du[0:rows, :] = step_size * u_act
        du[rows:, :] = jnp.zeros((BLOCK, tile), F32)
        grad_skip = jnp.sum(grad_mixed * u_act, 0, keepdims=True)
        rate = decay_ref[...]
        decay = rate * LOG2E
        sums = (iota((BLOCK, big), 0) == iota((BLOCK, big), 1) // state).astype(BF16)
        g_ring[1] = jnp.zeros((big, tile), BF16)
        w_ring[1] = jnp.zeros((big, tile), BF16)

        def reduce_block(spot, block):
            grads = g_ring[spot]
            source = jnp.minimum(block, blocks - 1)
            high, low = block_of(b_high, source, BLOCK), block_of(b_low, source, BLOCK)
            both = product(jnp.concatenate([high, low], 0), grads)
            base = pl.ds(pl.multiple_of(block * BLOCK, BLOCK), BLOCK)
            grad_du[base, :] = both[:BLOCK] + both[BLOCK:]
            grad_step[base, :] = product(sums, w_ring[spot])
            b_sums[base, :] += times_transpose(du[base, :].astype(BF16), grads)

        def run_blocks(quarter, carry):
            carried, log_sum = carry
            for spot in range(turns):
                turn = quarter * turns + spot
                block = blocks - 1 - turn
                later = (spot + turns - 1) % turns
                if spot == 0:
                    load(later, block - turns + 1).start()
                else:
                    pl.when(quarter < quarters - 1)(
                        lambda: load(later, block - turns + 1).start()
                    )
                load(spot, block).wait()
                here, before = spot % 2, (spot + 1) % 2
                reduce_block(before, block + 1)
                base = pl.ds(pl.multiple_of(block * BLOCK, BLOCK), BLOCK)
                steps_now, gy_now = step_ref[base, :], gy[base, :]
                c_now = block_of(c_cols, block, state)
                c_sums[base, :] += times_transpose(gy_now.astype(BF16), ring[spot, state:, :])
                for t in range(BLOCK - 1, -1, -1):
                    at = slice(t * state, (t + 1) * state)
                    c_wide = jnp.broadcast_to(c_now[:, t : t + 1], (state, tile))
                    step_now = steps_now[t : t + 1, :]
                    fade = jnp.exp2(step_now * decay)
                    grad = gy_now[t : t + 1, :] * c_wide + carried
                    g_ring[here, at, :] = grad.astype(BF16)
                    carried = fade * grad
                    weighted = carried * ring[spot, at, :].astype(F32) * rate
                    w_ring[here, at, :] = weighted.astype(BF16)
                    log_sum = log_sum + weighted * step_now
            for turn in range(2):
                for part in range(quarters):

                    @pl.when((step == turn) & (quarter == part))
                    def _():
                        between(turn * 4 + part)

            return carried, log_sum

        zeros = jnp.zeros((state, tile), F32)
        _, log_sum = lax.fori_loop(0, quarters, run_blocks, (zeros, zeros))
        reduce_block(1, 0)
        full_du = grad_du[0:rows, :]
        gradu_all[:, lanes] = full_du * step_size + skip_ref[...] * gy[...]
        grad_size = grad_step[0:rows, :] + full_du * u_act
        grad_pre = grad_size * (1.0 - jnp.exp(-step_size))
        grad_low = grad_pre.astype(BF16)
        grad_step_w = contract_rows(proj_ref[:, :rank].astype(BF16), grad_low)
        packed = jnp.concatenate(
            [grad_step_w, log_sum, jnp.sum(grad_pre, 0, keepdims=True), grad_skip, zeros[:6]], 0
        ).astype(BF16)
        for turn in range(2):

            @pl.when(step == turn)
            def _():
                split_lanes(send_scan.at[pl.ds(turn * half, half)], packed)
                start_inputs(half + turn * half // 2, half + (turn + 1) * half // 2)

        gradproj[:, :rank] += times_transpose(grad_low, stepw_ref[...])

    @pl.when(step == 1)
    def _():
        ways[1].start()
        own = iota((rows, big), 0) % BLOCK == iota((rows, big), 1) // state
        lane = iota((big, cols), 1)
        slot = iota((big, cols), 0) % state
        total = gradproj[...]
        for sums_here, first in ((b_sums[0:rows, :], rank), (c_sums[...], rank + state)):
            place = (lane == first + slot).astype(F32)
            total = total + exact_product(jnp.where(own, sums_here, 0.0), place)
        gradproj[...] = total

    @pl.when(step == 2)
    def _():
        load_mid.start()
        grad_du[...] = jnp.zeros_like(grad_du)

    @pl.when(step == steps_x + 2)
    def _():
        split_lanes(send_back, pack_back[...])
        ways[2].start()
        lhs = jnp.concatenate([gated_all[k] for k in range(devices)], 1)
        totals[2 * gated_all.shape[1] : 3 * gated_all.shape[1], :] = product(
            lhs, everyone[...].reshape(devices * rows, width)
        ).astype(BF16)
        load_normed.start()

    here = pl.ds(
        pl.multiple_of((jnp.maximum(step - 2, 0) % steps_x) * small_tile, small_tile), small_tile
    )

    @pl.when((step >= 2) & (step < steps_x + 2))
    def _():
        conv_ref, bias_ref = conv_rows(misc_x_ref)
        grad_proj = gradproj[...].astype(BF16)
        grad_u = gradu_all[:, here] + times_transpose(grad_proj, scanw_ref[...])
        pieces = [contract_rows(grad_proj, u_x_ref[...].astype(BF16))]
        x_inner = xin_ref[...]
        taps = conv_ref.shape[0]
        shifted = [shift_rows(x_inner, taps - 1 - tap) for tap in range(taps)]
        summed = bias_ref[...]
        for tap in range(taps):
            summed = summed + conv_ref[tap : tap + 1, :] * shifted[tap]
        sig = sigmoid(summed)
        grad_sum = grad_u * (sig * (1.0 + summed * (1.0 - sig)))
        grad_x = jnp.zeros_like(x_inner)
        for tap in range(taps):
            pieces.append(jnp.sum(grad_sum * shifted[tap], 0, keepdims=True))
            grad_x = grad_x + conv_ref[tap : tap + 1, :] * shift_rows(grad_sum, tap + 1 - taps)
        pieces.append(jnp.sum(grad_sum, 0, keepdims=True))
        pieces.append(jnp.zeros((pack_back.shape[0] - cols - taps - 1, small_tile), F32))
        pack_back[:, here] = jnp.concatenate(pieces, 0).astype(BF16)
        grad_x = grad_x.astype(BF16)
        send_in[here, :] = grad_x.T
        ring[x_spot, 0:rows, x_lanes] = grad_x
        for part in range(half):
            done = -(-(part + 1) * in_part // small_tile) + 1
            pl.when(step == done)(lambda: start_inputs(part, part + 1))

    @pl.when(step >= steps_x + 2)
    def _():
        grad_du[0:rows, :] += product(ring[x_spot, 0:rows, x_lanes], wx_ref[...]) + product(
            gate_all[:, here], wg_ref[...]
        )

    @pl.when(step == steps_x + 3)
    def _():
        next_to = [(left_2, goal_l2), (right_2, goal_r2), (right_1, goal_r1)]
        pick(
            (next_to[1], next_to[2], next_to[2], next_to[0]), raw, goal, load_sems.at[pl.ds(4, 2)]
        )
        matrix = dispatch_matrix(goal, devices)
        for part, (target, store) in enumerate(zip((g_ring, w_ring), store_sends)):
            target[...] = product(matrix, raw[part]).astype(BF16).reshape(target.shape)
            store.start()

    @pl.when(step == 2 * steps_x + 1)
    def _():
        values = tokens_ref[...].astype(F32)
        scale = lax.rsqrt(jnp.mean(values * values, -1, keepdims=True) + 1e-05)
        unit = values * scale
        grad = grad_du[0:rows, :]
        widths = jnp.concatenate([widths_ref[...], jnp.sum(grad * unit, 0, keepdims=True)], 0)
        widths = jnp.concatenate(
            [widths, jnp.zeros((send_tail.shape[1] - widths.shape[0], width), F32)], 0
        )
        split_lanes(send_tail, widths.astype(BF16))
        ways[3].start()
        inner = grad * gains_ref[0:1, :]
        load_mid.wait()
        gy[...] += scale * (inner - unit * jnp.mean(inner * unit, -1, keepdims=True))
        store_tokens = pltpu.make_async_copy(gy, gradtok_hbm, load_sems.at[2])
        store_tokens.start()
        at = 3 * gated_all.shape[1]
        for way, got in ((ways[1], got_scan), (ways[2], got_back)):
            way.wait()
            totals[at : at + 32, :] = fold_rows(got, width)
            at += 32
        ways[3].wait()
        tail = jnp.sum(got_tail[...].astype(F32), 0)
        tail = jnp.concatenate([tail, jnp.zeros((tail.shape[0], width - tail.shape[1]), F32)], 1)
        totals[at : at + 16, :] = tail.astype(BF16)
        load_normed.wait()
        input_local.wait()
        for copy in input_copies:
            copy.wait()
        lhs = jnp.concatenate([got_in[k] for k in range(devices)], 1)
        totals[0:in_part, :] = product(
            lhs, everyone[...].reshape(devices * rows, width)
        ).astype(BF16)
        store_totals = pltpu.make_async_copy(totals, totals_hbm, load_sems.at[3])
        store_totals.start()
        for line in lines:
            line.wait()
        store_tokens.wait()
        store_totals.wait()
        for store in store_sends:
            store.wait()


def backward_plane(
    proj, step_w, vec, u_act, gate_in, out_w, grad_mix, step_size, mixed, scan_w, x_inner, in_t,
    tokens, gains, grad_widths, grad_mid, gated, normed_all, hist, rows_0, grads_0, raws, goals,
):
    rows, channels = u_act.shape
    width = grad_mix.shape[1]
    cols = proj.shape[1]
    rank, state = step_w.shape[0], vec.shape[0] - 8
    devices = lax.axis_size("expert")
    part = channels // devices
    tile, small = channels // 2, channels // 6
    big = BLOCK * state
    pack_rows, tail_rows = cols + 8, grad_widths.shape[0] + 7
    fixed = lambda i: (0, 0)
    first = lambda i: jnp.minimum(i, 1)
    second = lambda i: jnp.clip(i - 2, 0, 5)
    once = pl.Buffered(1)
    slots = jax.ShapeDtypeStruct(rows_0.shape, BF16)
    raw = jax.ShapeDtypeStruct(raws[0].shape, BF16)
    goal = jax.ShapeDtypeStruct(goals[0].shape, jnp.int32)
    total_rows = 3 * part + 80
    pair = jax.ShapeDtypeStruct((2, 2, big, tile), BF16)
    third = lambda i: jnp.maximum(i - 8, 0)
    packs = [
        pltpu.VMEM((devices, count, lanes), BF16)
        for count, lanes in (
            (rank + state + 8, part), (pack_rows, part), (tail_rows, width // devices)
        )
        for _ in range(2)
    ]
    return pl.pallas_call(
        backward_kernel,
        grid=(14,),
        in_specs=[
            pl.BlockSpec((rows, cols), fixed),
            pl.BlockSpec((rank, tile), lambda i: (0, first(i))),
            pl.BlockSpec((state, tile), lambda i: (0, first(i))),
            pl.BlockSpec((8, tile), lambda i: (state // 8, first(i))),
            pl.BlockSpec((rows, tile), lambda i: (0, first(i))),
            pl.BlockSpec((rows, tile), lambda i: (0, first(i))),
            pl.BlockSpec((tile, width), lambda i: (first(i), 0), pipeline_mode=once),
            pl.BlockSpec((rows, width), fixed, pipeline_mode=once),
            pl.BlockSpec((rows, tile), lambda i: (0, first(i))),
            pl.BlockSpec((rows, tile), lambda i: (0, first(i))),
            pl.BlockSpec((small, cols), lambda i: (second(i), 0)),
            pl.BlockSpec((rows, small), lambda i: (0, second(i))),
            pl.BlockSpec((8, small), lambda i: (state // 8, second(i))),
            pl.BlockSpec((small, width), lambda i: (third(i), 0)),
            pl.BlockSpec((small, width), lambda i: (third(i) + 6, 0)),
            pl.BlockSpec((rows, small), lambda i: (0, second(i))),
            pl.BlockSpec((rows, width), fixed, pipeline_mode=once),
            pl.BlockSpec(gains.shape, fixed),
            pl.BlockSpec(grad_widths.shape, fixed),
        ] + [FAR] * 12,
        out_specs=[FAR] * 9,
        out_shape=[
            jax.ShapeDtypeStruct((rows, width), F32),
            jax.ShapeDtypeStruct((total_rows, width), BF16),
            slots, slots, raw, raw, goal, goal, pair,
        ],
        scratch_shapes=[
            pltpu.VMEM((rows // BLOCK * state, 128), F32),
            pltpu.VMEM((rows, big), BF16),
            pltpu.VMEM((rows, big), BF16),
            pltpu.VMEM((rows + BLOCK, big), F32),
            pltpu.VMEM((rows, big), F32),
            pltpu.VMEM((rows, tile), F32),
            pltpu.VMEM((rows + BLOCK, tile), F32),
            pltpu.VMEM((rows + BLOCK, tile), F32),
            pltpu.VMEM((rows + BLOCK, tile), F32),
            pltpu.VMEM((4, big + state, tile), BF16),
            pltpu.VMEM((2, big, tile), BF16),
            pltpu.VMEM((2, big, tile), BF16),
            pltpu.VMEM((rows, cols), F32),
            pltpu.VMEM((rows, channels), F32),
            pltpu.VMEM((rows, channels), BF16),
            pltpu.VMEM((2 * channels, rows), BF16),
            pltpu.VMEM((devices, 2 * part, rows), BF16),
            pltpu.VMEM((devices, rows, width), BF16),
            pltpu.VMEM(gated.shape, BF16),
            packs[0],
            packs[1],
            pltpu.VMEM((pack_rows, channels), BF16),
            *packs[2:],
            pltpu.VMEM((total_rows, width), BF16),
            pltpu.VMEM(raw.shape, BF16),
            pltpu.VMEM(goal.shape, jnp.int32),
            DMA((10,)), DMA((10,)), DMA((5, devices)), DMA((5, devices)), DMA((4, 2)), DMA((4, 2)),
            DMA((6,)), DMA((4,)), DMA((8,)),
        ],
        compiler_params=pltpu.CompilerParams(
            vmem_limit_bytes=VMEM_LIMIT, collective_id=4, has_side_effects=True
        ),
        name="mixer_backward",
    )(
        proj, step_w, vec, vec, u_act, gate_in, out_w, grad_mix, step_size, mixed, scan_w, x_inner,
        vec, in_t, in_t, u_act, tokens, gains, grad_widths, grad_mid, gated, normed_all, hist,
        rows_0, grads_0, raws[2], raws[3], raws[1], goals[2], goals[3], goals[1],
    )


def add_groups(rows, grads, rows_t, up_ref, down_ref):
    activated, slope = gelu_parts(product(rows, up_ref[...]))
    grad_pre = (times_transpose(grads, down_ref[...]) * slope).astype(BF16)
    return product(rows_t, grad_pre), contract_rows(activated.astype(BF16), grads)


def flat_rows(refs):
    experts, cap, width = refs[0].shape
    values = [ref[...].reshape(ref.shape[0] * cap, width) for ref in refs]
    return values[0] if len(values) == 1 else jnp.concatenate(values, 0)


def next_grads_kernel(
    last, up_ref, down_ref, gup_in, gdown_in, rows_ref, grads_ref, sends_in, *refs
):
    if not last:
        raws, goals, refs = refs[:4], refs[4:8], refs[8:]
    gup_ref, gdown_ref, rows_out, grads_out, refs = *refs[:4], refs[4:]
    if not last:
        sends_out, refs = refs[0], refs[1:]
    rows_t, x_send, x_recv, local_sems, refs = *refs[:4], refs[4:]
    step = pl.program_id(0)
    rows, grads = flat_rows((rows_ref,)), flat_rows((grads_ref,))
    ways = [
        Exchange(sends_in.at[k], out, x_send.at[k], x_recv.at[k], local_sems.at[k])
        for k, out in enumerate((rows_out, grads_out))
    ]

    @pl.when(step == 0)
    def _():
        greet(line=False)
        for way in ways:
            way.start()
        rows_t[...] = rows.T

    grad_up, grad_down = add_groups(rows, grads, rows_t[...], up_ref, down_ref)
    gup_ref[...] = (gup_in[...].astype(F32) + grad_up).astype(BF16)
    gdown_ref[...] = (gdown_in[...].astype(F32) + grad_down).astype(BF16)
    if not last:
        raw, goal, sends, load_sems = refs
        left_2, left_3, right_2, right_3 = zip(raws, goals)
        store = pltpu.make_async_copy(sends, sends_out, load_sems.at[2])

        @pl.when(step == 1)
        def _():
            pick((right_3, right_2, left_2, left_3), raw, goal, load_sems)
            prepare_sends(raw, goal, sends)
            store.start()

    @pl.when(step == pl.num_programs(0) - 1)
    def _():
        for way in ways:
            way.wait()
        if not last:
            store.wait()


def last_grads_kernel(
    up_ref, down_ref, gup_in, gdown_in, rows_ref, grads_ref, gup_ref, gdown_ref, rows_t
):
    rows, grads = flat_rows((rows_ref,)), flat_rows((grads_ref,))

    @pl.when(pl.program_id(0) == 0)
    def _():
        rows_t[...] = rows.T

    grad_up, grad_down = add_groups(rows, grads, rows_t[...], up_ref, down_ref)
    gup_ref[...] = gup_in[...].astype(F32) + grad_up
    gdown_ref[...] = gdown_in[...].astype(F32) + grad_down


def expert_grads_plane(up, down, grad_up, grad_down, rows, grads, sends, raws, goals, tile):
    width, hidden = up.shape
    devices, cap = grads.shape[:2]
    slots = jax.ShapeDtypeStruct(grads.shape, BF16)
    pair = jax.ShapeDtypeStruct(sends.shape, BF16)
    whole = pl.BlockSpec(grads.shape, lambda i: (0, 0, 0))

    def tiles(size):
        return [
            pl.BlockSpec((width, size), lambda i: (0, i)),
            pl.BlockSpec((size, width), lambda i: (i, 0)),
        ]

    def shapes(kind):
        return [
            jax.ShapeDtypeStruct((width, hidden), kind), jax.ShapeDtypeStruct((hidden, width), kind)
        ]

    turned = pltpu.VMEM((width, devices * cap), BF16)
    sems = [DMA((2, devices)), DMA((2, devices)), DMA((2,))]
    for last in (False, True):
        extra = () if last else (*raws, *goals)
        grad_up, grad_down, rows, grads, *more = pl.pallas_call(
            partial(next_grads_kernel, last),
            grid=(hidden // tile,),
            in_specs=tiles(tile) * 2 + [whole] * 2 + [FAR] * (1 + len(extra)),
            out_specs=tiles(tile) + [FAR] * (2 if last else 3),
            out_shape=shapes(BF16) + [slots] * 2 + ([] if last else [pair]),
            scratch_shapes=[turned] + sems + (
                [] if last else [
                    pltpu.VMEM(raws[0].shape, BF16), pltpu.VMEM(goals[0].shape, jnp.int32),
                    pltpu.VMEM(pair.shape, BF16), DMA((3,)),
                ]
            ),
            compiler_params=remote_params(7 if last else 6),
            name="expert_grads_2" if last else "expert_grads_1",
        )(up, down, grad_up, grad_down, rows, grads, sends, *extra)
        sends = more[0] if more else None
    return pl.pallas_call(
        last_grads_kernel,
        grid=(hidden // 768,),
        in_specs=tiles(768) * 2 + [whole] * 2,
        out_specs=tiles(768),
        out_shape=shapes(F32),
        scratch_shapes=[turned],
        compiler_params=pltpu.CompilerParams(vmem_limit_bytes=VMEM_LIMIT),
        name="expert_grads_3",
    )(up, down, grad_up, grad_down, rows, grads)


def finish_kernel(
    totals_ref, in_ref, out_ref, scanw_ref, stepw_ref, decay_ref, conv_ref, vectors_ref, norms_ref,
    router_ref,
):
    in_rows, part = in_ref.shape[0], out_ref.shape[0]
    cols, rank, state, taps = (
        scanw_ref.shape[1], stepw_ref.shape[0], decay_ref.shape[0], conv_ref.shape[0]
    )
    experts, slice_w = router_ref.shape
    in_ref[...] = totals_ref[0:in_rows, :].astype(F32)
    out_ref[...] = totals_ref[in_rows : in_rows + part, :].astype(F32)
    at = in_rows + part
    unfolded = []
    for quarter in ((rank + state + 8) // 4, (cols + 8) // 4):
        block = totals_ref[at : at + 32, :].astype(F32)[:quarter]
        unfolded.append(
            jnp.concatenate([block[:, k * part : (k + 1) * part] for k in range(4)], 0)
        )
        at += 32
    scan, back = unfolded
    stepw_ref[...] = scan[:rank]
    decay_ref[...] = scan[rank : rank + state]
    scanw_ref[...] = back[:cols].T
    conv_ref[...] = back[cols : cols + taps]
    vectors_ref[...] = jnp.concatenate(
        [back[cols + taps : cols + taps + 1], scan[rank + state : rank + state + 2]], 0
    )
    tail = totals_ref[at : at + 16, :].astype(F32)[:, :slice_w]
    router_ref[...] = tail[:experts]
    norms_ref[...] = tail[experts : experts + 2]


def finish(totals, in_rows, part, cols, rank, state, taps, experts, slice_w):
    here = pl.BlockSpec(memory_space=pltpu.VMEM)
    return pl.pallas_call(
        finish_kernel,
        in_specs=[here],
        out_specs=[here] * 9,
        out_shape=[
            jax.ShapeDtypeStruct(shape, F32)
            for shape in (
                (in_rows, totals.shape[1]), (part, totals.shape[1]), (part, cols), (rank, part),
                (state, part), (taps, part), (3, part), (2, slice_w), (experts, slice_w),
            )
        ],
        compiler_params=pltpu.CompilerParams(vmem_limit_bytes=VMEM_LIMIT),
        name="finish",
    )(totals)


def gather(value):
    return lax.all_gather(value, "expert", axis=0, tiled=True)


def exchange(value):
    return lax.all_to_all(value, "expert", split_axis=0, concat_axis=0, tiled=True)


def shards(
    tokens, lengths, routes, slot_index, mixer_norm, in_weight, conv_weight, conv_bias,
    scan_weight, step_weight, step_bias, decay_log, skip_gain, out_weight, moe_norm, router_weight,
    up_weight, down_weight, cotangent,
):
    devices = lax.axis_size("expert")
    rows, width = tokens.shape[1:]
    part = out_weight.shape[0]
    channels = part * devices
    cols = scan_weight.shape[1]
    rank, state, taps = step_weight.shape[0], decay_log.shape[1], conv_weight.shape[0]
    experts = router_weight.shape[1]
    split = devices // experts
    slice_w = width // devices
    tile = channels // 2

    on_plane = devices == 8 and split == 1 and lax.axis_size("dp") == 4
    vectors = jnp.stack([conv_bias, step_bias, skip_gain])
    norms = jnp.stack([mixer_norm, moe_norm])
    in_t, decay_t, router_t = in_weight.T, decay_log.T, router_weight.T
    up, down = up_weight[0], down_weight[0]
    hidden = up.shape[1]
    if on_plane:
        (
            normed_low, x_inner, u_act, gate_in, proj, step_size, mixed, gated, mid, step_full, vec,
            router_t, gains, scan_full, in_t, out_full, normed_all, hist,
        ) = forward_plane(
            tokens[0], in_t, scan_weight, step_weight, decay_t, conv_weight, vectors, norms,
            router_t, out_weight,
        )
        in_t = in_t.reshape(2 * channels, width)
        scan_full = scan_full.reshape(channels, cols)
        out_full = out_full.reshape(channels, width)
        layer_out, grad_mid, grad_mix, grad_widths, rows_0, grads_0, *line = expert_layer(
            lengths, mid, gains, router_t, routes, slot_index, cotangent[0], up, down
        )
        raws, goals, grad_up, grad_down = line[:4], line[4:8], line[8], line[9]
        (
            tokens_grad, totals, rows_1, grads_1, left_3, right_3, goal_l3, goal_r3, sends
        ) = backward_plane(
            proj, step_full, vec, u_act, gate_in, out_full, grad_mix, step_size, mixed, scan_full,
            x_inner, in_t, tokens[0], gains, grad_widths, grad_mid, gated, normed_all, hist, rows_0,
            grads_0, raws, goals,
        )
        totals = lax.psum(totals, "dp")
        grad_up, grad_down = expert_grads_plane(
            up, down, grad_up, grad_down, rows_1, grads_1,
            sends.reshape((2,) + rows_1.shape), (raws[2], left_3, raws[3], right_3), (goals[2], goal_l3, goals[3], goal_r3), 512,
        )
        in_total, out_total, scan_w_total, step_w_total, decay_total, conv_total, *rest = finish(
            totals, 2 * part, part, cols, rank, state, taps, experts, slice_w
        )
        vector_totals, norm_totals, router_total = rest
    else:
        spare = jnp.zeros((8 - taps - 3, part), BF16)
        columns = jnp.concatenate([step_weight, decay_t, conv_weight, vectors, spare], 0)
        across = jnp.concatenate([router_t, norms, jnp.zeros((6, slice_w), BF16)], 0)
        in_t, scan_full, columns, across = (
            lax.all_gather(value, "expert") for value in (in_t, scan_weight, columns, across)
        )
        columns = columns.transpose(1, 0, 2).reshape(columns.shape[1], channels)
        across = across.transpose(1, 0, 2).reshape(across.shape[1], width)
        step_full, rest = columns[:rank], columns[rank:].astype(F32)
        vec = jnp.concatenate([-jnp.exp(rest[:state]), rest[state:]], 0)
        router_t, gains = across[:experts], across[experts:].astype(F32)
        in_t = in_t.reshape(2 * channels, width)
        scan_full = scan_full.reshape(channels, cols)
        normed_low, x_inner, u_act, gate_in, proj = front(
            tokens[0], gains, in_t, vec, scan_full, tile
        )
        live = (jnp.arange(rows, dtype=jnp.int32) < lengths[0]).astype(F32)[:, None]
        routes_col, slots_col = routes[0][:, None], slot_index[0][:, None]
        router, gain_second = router_t.T, gains[1:2]
        out_full = gather(out_weight)
        step_size, mixed, gated, hist, mid = scan_forward(
            proj, step_full, vec, u_act, gate_in, out_full, tokens[0], tile
        )
        send_rows, send_grads, normed_two, probs = router_step(
            mid, gain_second, router, routes_col, routes, slot_index, live, cotangent[0]
        )

        def to_pieces(value):
            wide = jnp.broadcast_to(value[:, None], (experts, split) + value.shape[1:])
            return exchange(wide.reshape(devices, CAP, width))

        def from_pieces(value):
            value = exchange(value).reshape(experts, split, CAP, width)
            if split == 1:
                return value[:, 0]
            return jnp.sum(value.astype(F32), 1).astype(BF16)

        some = min(512, hidden // 3)
        rows_in = to_pieces(send_rows)
        grads_in = to_pieces(send_grads)
        partial_out, slope = expert_out(rows_in, up, down, some)
        back_rows = from_pieces(partial_out)
        back_grads = from_pieces(expert_back(grads_in, up, down, slope, some))
        all_rows = lax.all_gather(rows_in, "dp")
        layer_out, grad_mid, grad_mix, grad_widths = combine_step(
            mid, gain_second, router, routes_col, slots_col, live, cotangent[0], probs, normed_two,
            back_rows, back_grads,
        )
        grad_mix, all_rows = lax.optimization_barrier((grad_mix, all_rows))
        all_grads = lax.all_gather(grads_in, "dp")
        out_parts = contract_rows(gated, grad_mix).astype(BF16).reshape(devices, part, width)
        grad_out_w = jnp.sum(exchange(out_parts).astype(F32), 0).astype(BF16)
        grad_u, grad_gate, scan_parts, grad_proj = scan_backward(
            proj, step_full, vec, u_act, gate_in, out_full, grad_mix, step_size, mixed, hist, tile,
            devices,
        )
        scan_small = jnp.sum(exchange(scan_parts).astype(F32), 0).astype(BF16)
        grad_x, back_parts, width_parts, tokens_grad = mixer_back(
            grad_proj, scan_full, grad_u, x_inner, vec, grad_gate, in_t, u_act, tokens[0], gains,
            grad_mid, grad_widths, tile, devices,
        )
        back_small = jnp.sum(exchange(back_parts).astype(F32), 0).astype(BF16)
        width_small = jnp.sum(exchange(width_parts).astype(F32), 0).astype(BF16)
        normed_all = gather(normed_low)
        grad_in_parts = exchange(jnp.concatenate([grad_x, grad_gate], 0))
        grad_in_w = contract_rows(
            grad_in_parts.reshape(devices * rows, 2 * part), normed_all
        ).astype(BF16)
        totals = (grad_in_w, grad_out_w, scan_small, back_small, width_small)
        totals, all_grads = lax.optimization_barrier((totals, all_grads))
        totals = lax.psum(totals, "dp")
        in_total, out_total, scan_small, back_small, width_small = (
            t.astype(F32) for t in totals
        )
        grad_up, grad_down = expert_grads(all_rows, all_grads, up, down, min(256, hidden))
        scan_w_total, conv_total = back_small[:cols].T, back_small[cols : cols + taps]
        step_w_total, decay_total = scan_small[:rank], scan_small[rank : rank + state]
        vector_totals = (
            back_small[cols + taps], scan_small[rank + state], scan_small[rank + state + 1]
        )
        router_total = width_small[:experts]
        norm_totals = (width_small[experts], width_small[experts + 1])
    return (
        layer_out[None],
        tokens_grad[None],
        norm_totals[1],
        in_total.T,
        conv_total,
        vector_totals[0],
        scan_w_total,
        step_w_total,
        vector_totals[1],
        decay_total.T,
        vector_totals[2],
        out_total,
        norm_totals[0],
        router_total.T,
        grad_up[None],
        grad_down[None],
    )


def solution(mesh):
    in_specs = (
        P(("dp", "expert"), None, None),
        P(("dp", "expert")),
        P(("dp", "expert"), None),
        P(("dp", "expert"), None),
        P("expert"),
        P(None, "expert"),
        P(None, "expert"),
        P("expert"),
        P("expert", None),
        P(None, "expert"),
        P("expert"),
        P("expert", None),
        P("expert"),
        P("expert", None),
        P("expert"),
        P("expert", None),
        P("expert", None, None),
        P("expert", None, None),
        P(("dp", "expert"), None, None),
    )
    out_specs = (
        P(("dp", "expert"), None, None),
        P(("dp", "expert"), None, None),
        P("expert"),
        P(None, "expert"),
        P(None, "expert"),
        P("expert"),
        P("expert", None),
        P(None, "expert"),
        P("expert"),
        P("expert", None),
        P("expert"),
        P("expert", None),
        P("expert"),
        P("expert", None),
        P("expert", None, None),
        P("expert", None, None),
    )
    return jax.shard_map(shards, mesh=mesh, in_specs=in_specs, out_specs=out_specs, check_vma=False)
```

```python
from functools import partial

import jax
import jax.numpy as jnp
from jax import lax
from jax.experimental import pallas as pl
from jax.experimental.pallas import tpu as pltpu
from jax.sharding import PartitionSpec as P

CAP = 64
BLOCK = 16
LOG2E = 1.4426950408889634
F32 = jnp.float32
BF16 = jnp.bfloat16
VMEM_LIMIT = 56 * 1024 * 1024


def product(left, right):
    return jnp.dot(left, right, preferred_element_type=F32)


def contract_rows(left, right):
    return lax.dot_general(left, right, (((0,), (0,)), ((), ())), preferred_element_type=F32)


def times_transpose(left, right):
    return lax.dot_general(left, right, (((1,), (1,)), ((), ())), preferred_element_type=F32)


def exact_product(left, right):
    return jnp.dot(left, right, preferred_element_type=F32, precision=lax.Precision.HIGHEST)


def iota(shape, axis):
    return lax.broadcasted_iota(jnp.int32, shape, axis)


def sigmoid(values):
    return 1.0 / (1.0 + jnp.exp(-values))


def softplus(values):
    return jnp.maximum(values, 0.0) + jnp.log1p(jnp.exp(-jnp.abs(values)))


class Rows:
    def __init__(self, ref, first, count):
        self.ref, self.first = ref, first
        self.shape = (count, ref.shape[1])

    def __getitem__(self, index):
        low, high = (0, self.shape[0]) if index is Ellipsis else (index[0].start, index[0].stop)
        return self.ref[self.first + low : self.first + high, :]


def conv_rows(misc_ref):
    return Rows(misc_ref, 0, 4), Rows(misc_ref, 4, 1)


def scan_rows(misc_ref):
    return Rows(misc_ref, 5, 1), Rows(misc_ref, 6, 1)


def split_lanes(out_ref, value):
    parts, _, width = out_ref.shape
    for part in range(parts):
        out_ref[part] = value[:, part * width : (part + 1) * width]


def shift_rows(values, offset):
    rows = values.shape[0]
    if offset == 0:
        return values
    rolled = pltpu.roll(values, offset % rows, 0)
    row = iota(values.shape, 0)
    keep = row >= offset if offset > 0 else row < rows + offset
    return jnp.where(keep, rolled, 0.0)


def two_parts(values):
    high = values.astype(BF16)
    low = (values - high.astype(F32)).astype(BF16)
    return high, low


def spread_rows(proj_block, first, state):
    rows, width = proj_block.shape
    big = rows * state
    pick = (iota((big, rows), 0) // state == iota((big, rows), 1)).astype(F32)
    copied = exact_product(pick, proj_block)
    lane = iota((big, width), 1)
    own = lane == first + iota((big, width), 0) % state
    column = jnp.sum(jnp.where(own, copied, 0.0), axis=1, keepdims=True)
    return jnp.broadcast_to(column, (big, 128))


def diagonal_blocks(proj_block, first, state):
    rows, width = proj_block.shape
    big = rows * state
    place = (iota((width, big), 0) == first + iota((width, big), 1) % state).astype(BF16)
    own = iota((rows, big), 0) == iota((rows, big), 1) // state
    parts = [
        jnp.where(own, product(part, place), 0.0).astype(BF16) for part in two_parts(proj_block)
    ]
    return jnp.concatenate(parts, 0)


def front_kernel(
    tokens_ref, gain_ref, wx_ref, wg_ref, misc_ref, scanw_ref,
    normed_ref, xin_ref, u_ref, gate_ref, proj_ref,
):
    step = pl.program_id(0)
    conv_ref, bias_ref = conv_rows(misc_ref)

    @pl.when(step == 0)
    def _():
        values = tokens_ref[...].astype(F32)
        scale = lax.rsqrt(jnp.mean(values * values, -1, keepdims=True) + 1e-05)
        normed_ref[...] = (values * scale * gain_ref[0:1, :]).astype(BF16)
        proj_ref[...] = jnp.zeros_like(proj_ref)

    normed = normed_ref[...]
    x_inner = times_transpose(normed, wx_ref[...])
    gate_ref[...] = times_transpose(normed, wg_ref[...])
    xin_ref[...] = x_inner
    taps = conv_ref.shape[0]
    summed = bias_ref[...] + conv_ref[taps - 1 : taps, :] * x_inner
    for back in range(1, taps):
        tap = taps - 1 - back
        summed = summed + conv_ref[tap : tap + 1, :] * shift_rows(x_inner, back)
    u_act = summed * sigmoid(summed)
    u_ref[...] = u_act
    proj_ref[...] += product(u_act.astype(BF16), scanw_ref[...])


def front(tokens, gains, in_t, vec, scan_w, tile):
    rows, width = tokens.shape
    channels = scan_w.shape[0]
    cols = scan_w.shape[1]
    steps = channels // tile
    return pl.pallas_call(
        front_kernel,
        grid=(steps,),
        in_specs=[
            pl.BlockSpec((rows, width), lambda i: (0, 0)),
            pl.BlockSpec(gains.shape, lambda i: (0, 0)),
            pl.BlockSpec((tile, width), lambda i: (i, 0)),
            pl.BlockSpec((tile, width), lambda i: (i + steps, 0)),
            pl.BlockSpec((8, tile), lambda i: ((vec.shape[0] - 8) // 8, i)),
            pl.BlockSpec((tile, cols), lambda i: (i, 0)),
        ],
        out_specs=[
            pl.BlockSpec((rows, width), lambda i: (0, 0)),
            pl.BlockSpec((rows, tile), lambda i: (0, i)),
            pl.BlockSpec((rows, tile), lambda i: (0, i)),
            pl.BlockSpec((rows, tile), lambda i: (0, i)),
            pl.BlockSpec((rows, cols), lambda i: (0, 0)),
        ],
        out_shape=[
            jax.ShapeDtypeStruct((rows, width), BF16),
            jax.ShapeDtypeStruct((rows, channels), F32),
            jax.ShapeDtypeStruct((rows, channels), F32),
            jax.ShapeDtypeStruct((rows, channels), F32),
            jax.ShapeDtypeStruct((rows, cols), F32),
        ],
        compiler_params=pltpu.CompilerParams(vmem_limit_bytes=VMEM_LIMIT),
        name="mixer_front",
    )(tokens, gains, in_t, in_t, vec, scan_w)


def scan_prepare(proj_ref, b_wide, c_blocks, b_first, c_first, state):
    blocks = proj_ref.shape[0] // BLOCK
    big = BLOCK * state

    def build(block, carry):
        part = proj_ref[pl.ds(pl.multiple_of(block * BLOCK, BLOCK), BLOCK), :]
        b_wide[pl.ds(pl.multiple_of(block * big, big), big), :] = spread_rows(part, b_first, state)
        c_blocks[pl.ds(pl.multiple_of(block * 2 * BLOCK, 2 * BLOCK), 2 * BLOCK), :] = (
            diagonal_blocks(part, c_first, state)
        )
        return carry

    lax.fori_loop(0, blocks, build, 0)


def scan_tile(
    proj_ref, stepw_ref, decay_ref, misc_ref, u_ref, gate_ref, step_ref, mixed_ref, hist_ref,
    b_wide, c_blocks, du, scanned, between,
):
    rank, state = stepw_ref.shape[0], decay_ref.shape[0]
    rows, tile = u_ref.shape
    blocks = rows // BLOCK
    big = BLOCK * state
    dbias_ref, skip_ref = scan_rows(misc_ref)
    u_act = u_ref[...]
    step_size = softplus(
        product(proj_ref[:, :rank].astype(BF16), stepw_ref[...]) + dbias_ref[...]
    )
    step_ref[...] = step_size
    du[...] = step_size * u_act
    decay = decay_ref[...] * LOG2E
    hist_ref[0:state, :] = jnp.zeros((state, tile), BF16)

    def run_block(block, held):
        base = pl.multiple_of(block * BLOCK, BLOCK)
        steps_now = step_ref[pl.ds(base, BLOCK), :]
        du_now = du[pl.ds(base, BLOCK), :]
        wide_base = pl.multiple_of(block * big, big)
        for t in range(BLOCK):
            b_now = b_wide[pl.ds(wide_base + t * state, state), :]
            fade = jnp.exp2(steps_now[t : t + 1, :] * decay)
            fresh = du_now[t : t + 1, :] * jnp.concatenate([b_now] * (tile // 128), 1)
            held = fade * held + fresh
            hist_ref[pl.ds(wide_base + (t + 1) * state, state), :] = held.astype(BF16)
        weights = c_blocks[pl.ds(pl.multiple_of(block * 2 * BLOCK, 2 * BLOCK), 2 * BLOCK), :]
        both = product(weights, hist_ref[pl.ds(wide_base + state, big), :])
        scanned[pl.ds(base, BLOCK), :] = both[:BLOCK] + both[BLOCK:]
        return held

    held = jnp.zeros((state, tile), F32)
    held = lax.fori_loop(0, blocks // 2, run_block, held)
    between(0)
    lax.fori_loop(blocks // 2, blocks, run_block, held)
    between(1)
    mixed = scanned[...] + skip_ref[...] * u_act
    mixed_ref[...] = mixed
    gate_in = gate_ref[...]
    return (mixed * (gate_in * sigmoid(gate_in))).astype(BF16)


def scan_kernel(
    proj_ref, stepw_ref, decay_ref, misc_ref, u_ref, gate_ref, outw_ref, tokens_ref,
    step_ref, mixed_ref, gated_ref, hist_ref, mid_ref,
    b_wide, c_blocks, du, scanned,
):
    rank, state = stepw_ref.shape[0], decay_ref.shape[0]

    @pl.when(pl.program_id(0) == 0)
    def _():
        mid_ref[...] = tokens_ref[...].astype(F32)
        scan_prepare(proj_ref, b_wide, c_blocks, rank, rank + state, state)

    gated = scan_tile(
        proj_ref, stepw_ref, decay_ref, misc_ref, u_ref, gate_ref, step_ref, mixed_ref, hist_ref,
        b_wide, c_blocks, du, scanned, lambda half: None,
    )
    gated_ref[...] = gated
    mid_ref[...] += product(gated, outw_ref[...])


def scan_forward(proj, step_w, vec, u_act, gate_in, out_w, tokens, tile):
    rows, channels = u_act.shape
    width = tokens.shape[1]
    cols = proj.shape[1]
    rank, state = step_w.shape[0], vec.shape[0] - 8
    steps = channels // tile
    hist_rows = (rows + 1) * state
    column = lambda i: (0, i)
    fixed = lambda i: (0, 0)
    return pl.pallas_call(
        scan_kernel,
        grid=(steps,),
        in_specs=[
            pl.BlockSpec((rows, cols), fixed),
            pl.BlockSpec((rank, tile), column),
            pl.BlockSpec((state, tile), column),
            pl.BlockSpec((8, tile), lambda i: ((vec.shape[0] - 8) // 8, i)),
            pl.BlockSpec((rows, tile), column),
            pl.BlockSpec((rows, tile), column),
            pl.BlockSpec((tile, width), lambda i: (i, 0)),
            pl.BlockSpec((rows, width), fixed),
        ],
        out_specs=[
            pl.BlockSpec((rows, tile), column),
            pl.BlockSpec((rows, tile), column),
            pl.BlockSpec((rows, tile), column),
            pl.BlockSpec((hist_rows, tile), column),
            pl.BlockSpec((rows, width), fixed),
        ],
        out_shape=[
            jax.ShapeDtypeStruct((rows, channels), F32),
            jax.ShapeDtypeStruct((rows, channels), F32),
            jax.ShapeDtypeStruct((rows, channels), BF16),
            jax.ShapeDtypeStruct((hist_rows, channels), BF16),
            jax.ShapeDtypeStruct((rows, width), F32),
        ],
        scratch_shapes=[
            pltpu.VMEM((rows * state, 128), F32),
            pltpu.VMEM((rows * 2, BLOCK * state), BF16),
            pltpu.VMEM((rows, tile), F32),
            pltpu.VMEM((rows, tile), F32),
        ],
        compiler_params=pltpu.CompilerParams(vmem_limit_bytes=VMEM_LIMIT),
        name="scan_forward",
    )(proj, step_w, vec, vec, u_act, gate_in, out_w, tokens)


def scan_back_kernel(*refs):
    scan_back_tile(lambda half: None, split_lanes, *refs)


def scan_back_tile(
    between, put_gate, proj_ref, stepw_ref, decay_ref, misc_ref, u_ref, gate_ref, outw_ref, gradmix_ref,
    step_ref, mixed_ref, hist_ref,
    gradu_ref, gradgate_ref, pack_ref, gradproj_ref,
    c_wide, b_blocks, b_sums, c_sums, gy, du, g_hist, w_hist, grad_du, grad_step,
):
    tile_id = pl.program_id(0)
    cols, rank = proj_ref.shape[1], stepw_ref.shape[0]
    state = decay_ref.shape[0]
    rows, tile = u_ref.shape
    blocks = rows // BLOCK
    big = BLOCK * state

    @pl.when(tile_id == 0)
    def _():
        gradproj_ref[...] = jnp.zeros_like(gradproj_ref)
        b_sums[...] = jnp.zeros_like(b_sums)
        c_sums[...] = jnp.zeros_like(c_sums)
        scan_prepare(proj_ref, c_wide, b_blocks, rank + state, rank, state)

    skip_ref = scan_rows(misc_ref)[1]
    grad_gated = times_transpose(gradmix_ref[...], outw_ref[...])
    gate_in = gate_ref[...]
    gate_sig = sigmoid(gate_in)
    grad_mixed = grad_gated * (gate_in * gate_sig)
    put_gate(
        gradgate_ref,
        (grad_gated * mixed_ref[...] * (gate_sig * (1.0 + gate_in * (1.0 - gate_sig)))).astype(BF16),
    )
    u_act = u_ref[...]
    step_size = step_ref[...]
    gy[...] = grad_mixed
    du[...] = step_size * u_act
    grad_skip = jnp.sum(grad_mixed * u_act, 0, keepdims=True)
    rate = decay_ref[...]
    decay = rate * LOG2E
    sums = (iota((BLOCK, big), 0) == iota((BLOCK, big), 1) // state).astype(BF16)

    def run_block(turn, carry):
        carried, log_sum = carry
        block = blocks - 1 - turn
        base = pl.multiple_of(block * BLOCK, BLOCK)
        wide_base = pl.multiple_of(block * big, big)
        steps_now = step_ref[pl.ds(base, BLOCK), :]
        gy_now = gy[pl.ds(base, BLOCK), :]
        for t in range(BLOCK - 1, -1, -1):
            c_now = c_wide[pl.ds(wide_base + t * state, state), :]
            step_now = steps_now[t : t + 1, :]
            fade = jnp.exp2(step_now * decay)
            grad = gy_now[t : t + 1, :] * jnp.concatenate([c_now] * (tile // 128), 1) + carried
            g_hist[t * state : (t + 1) * state, :] = grad.astype(BF16)
            carried = fade * grad
            before = hist_ref[pl.ds(wide_base + t * state, state), :].astype(F32)
            weighted = carried * before * rate
            w_hist[t * state : (t + 1) * state, :] = weighted.astype(BF16)
            log_sum = log_sum + weighted * step_now
        grads = g_hist[...]
        both = product(
            b_blocks[pl.ds(pl.multiple_of(block * 2 * BLOCK, 2 * BLOCK), 2 * BLOCK), :], grads
        )
        grad_du[pl.ds(base, BLOCK), :] = both[:BLOCK] + both[BLOCK:]
        grad_step[pl.ds(base, BLOCK), :] = product(sums, w_hist[...])
        b_sums[pl.ds(base, BLOCK), :] += times_transpose(
            du[pl.ds(base, BLOCK), :].astype(BF16), grads
        )
        c_sums[pl.ds(base, BLOCK), :] += times_transpose(
            gy_now.astype(BF16), hist_ref[pl.ds(wide_base + state, big), :]
        )
        return carried, log_sum

    zeros = jnp.zeros((state, tile), F32)
    held = lax.fori_loop(0, blocks // 2, run_block, (zeros, zeros))
    between(0)
    _, log_sum = lax.fori_loop(blocks // 2, blocks, run_block, held)
    between(1)
    full_du = grad_du[...]
    gradu_ref[...] = full_du * step_size + skip_ref[...] * gy[...]
    grad_size = grad_step[...] + full_du * u_act
    grad_pre = grad_size * (1.0 - jnp.exp(-step_size))
    grad_low = grad_pre.astype(BF16)
    grad_step_w = contract_rows(proj_ref[:, :rank].astype(BF16), grad_low)
    packed = jnp.concatenate(
        [grad_step_w, log_sum, jnp.sum(grad_pre, 0, keepdims=True), grad_skip, zeros[:6]], 0
    )
    split_lanes(pack_ref, packed.astype(BF16))
    gradproj_ref[:, :rank] += times_transpose(grad_low, stepw_ref[...])

    @pl.when(tile_id == pl.num_programs(0) - 1)
    def _():
        own = iota((rows, big), 0) % BLOCK == iota((rows, big), 1) // state
        lane = iota((big, cols), 1)
        slot = iota((big, cols), 0) % state
        total = gradproj_ref[...]
        for sums_ref, first in ((b_sums, rank), (c_sums, rank + state)):
            place = (lane == first + slot).astype(F32)
            total = total + exact_product(jnp.where(own, sums_ref[...], 0.0), place)
        gradproj_ref[...] = total


def scan_backward(
    proj, step_w, vec, u_act, gate_in, out_w, grad_mix, step_size, mixed, hist, tile, devices
):
    rows, channels = u_act.shape
    gate_parts = tile * devices // (2 * channels)
    pack_parts = tile * devices // channels
    pack_rows = step_w.shape[0] + vec.shape[0]
    width = grad_mix.shape[1]
    cols = proj.shape[1]
    rank, state = step_w.shape[0], vec.shape[0] - 8
    steps = channels // tile
    big = BLOCK * state
    column = lambda i: (0, i)
    fixed = lambda i: (0, 0)
    return pl.pallas_call(
        scan_back_kernel,
        grid=(steps,),
        in_specs=[
            pl.BlockSpec((rows, cols), fixed),
            pl.BlockSpec((rank, tile), column),
            pl.BlockSpec((state, tile), column),
            pl.BlockSpec((8, tile), lambda i: ((vec.shape[0] - 8) // 8, i)),
            pl.BlockSpec((rows, tile), column),
            pl.BlockSpec((rows, tile), column),
            pl.BlockSpec((tile, width), lambda i: (i, 0)),
            pl.BlockSpec((rows, width), fixed),
            pl.BlockSpec((rows, tile), column),
            pl.BlockSpec((rows, tile), column),
            pl.BlockSpec((hist.shape[0], tile), column),
        ],
        out_specs=[
            pl.BlockSpec((rows, tile), column),
            pl.BlockSpec((gate_parts, rows, tile // gate_parts), lambda i: (i, 0, 0)),
            pl.BlockSpec((pack_parts, pack_rows, tile // pack_parts), lambda i: (i, 0, 0)),
            pl.BlockSpec((rows, cols), fixed),
        ],
        out_shape=[
            jax.ShapeDtypeStruct((rows, channels), F32),
            jax.ShapeDtypeStruct((devices // 2, rows, 2 * channels // devices), BF16),
            jax.ShapeDtypeStruct((devices, pack_rows, channels // devices), BF16),
            jax.ShapeDtypeStruct((rows, cols), F32),
        ],
        scratch_shapes=[
            pltpu.VMEM((rows * state, 128), F32),
            pltpu.VMEM((rows * 2, big), BF16),
            pltpu.VMEM((rows, big), F32),
            pltpu.VMEM((rows, big), F32),
            pltpu.VMEM((rows, tile), F32),
            pltpu.VMEM((rows, tile), F32),
            pltpu.VMEM((big, tile), BF16),
            pltpu.VMEM((big, tile), BF16),
            pltpu.VMEM((rows, tile), F32),
            pltpu.VMEM((rows, tile), F32),
        ],
        compiler_params=pltpu.CompilerParams(vmem_limit_bytes=VMEM_LIMIT),
        name="scan_backward",
    )(proj, step_w, vec, vec, u_act, gate_in, out_w, grad_mix, step_size, mixed, hist)


def back_kernel(
    gradproj_ref, scanw_ref, gradu_ref, xin_ref, misc_ref, gradgate_ref, wx_ref, wg_ref,
    u_ref, tokens_ref, gain_ref, gradmid_ref, widths_ref,
    gradx_ref, pack_ref, tail_ref, gradtok_ref,
    total,
):
    tile_id = pl.program_id(0)

    @pl.when(tile_id == 0)
    def _():
        total[...] = jnp.zeros_like(total)

    conv_ref, bias_ref = conv_rows(misc_ref)
    grad_proj = gradproj_ref[...].astype(BF16)
    grad_u = gradu_ref[...] + times_transpose(grad_proj, scanw_ref[...])
    pieces = [contract_rows(grad_proj, u_ref[...].astype(BF16))]
    x_inner = xin_ref[...]
    taps = conv_ref.shape[0]
    shifted = [shift_rows(x_inner, taps - 1 - tap) for tap in range(taps)]
    summed = bias_ref[...]
    for tap in range(taps):
        summed = summed + conv_ref[tap : tap + 1, :] * shifted[tap]
    sig = sigmoid(summed)
    grad_sum = grad_u * (sig * (1.0 + summed * (1.0 - sig)))
    grad_x = jnp.zeros_like(x_inner)
    for tap in range(taps):
        pieces.append(jnp.sum(grad_sum * shifted[tap], 0, keepdims=True))
        grad_x = grad_x + conv_ref[tap : tap + 1, :] * shift_rows(grad_sum, tap + 1 - taps)
    pieces.append(jnp.sum(grad_sum, 0, keepdims=True))
    pieces.append(jnp.zeros((pack_ref.shape[1] - grad_proj.shape[1] - taps - 1, x_inner.shape[1]), F32))
    split_lanes(pack_ref, jnp.concatenate(pieces, 0).astype(BF16))
    grad_x = grad_x.astype(BF16)
    split_lanes(gradx_ref, grad_x)
    grad_gate = jnp.concatenate([gradgate_ref[k] for k in range(gradgate_ref.shape[0])], 1)
    total[...] += product(grad_x, wx_ref[...]) + product(grad_gate, wg_ref[...])

    @pl.when(tile_id == pl.num_programs(0) - 1)
    def _():
        values = tokens_ref[...].astype(F32)
        scale = lax.rsqrt(jnp.mean(values * values, -1, keepdims=True) + 1e-05)
        unit = values * scale
        grad = total[...]
        widths = jnp.concatenate([widths_ref[...], jnp.sum(grad * unit, 0, keepdims=True)], 0)
        widths = jnp.concatenate(
            [widths, jnp.zeros((tail_ref.shape[1] - widths.shape[0], widths.shape[1]), F32)], 0
        )
        split_lanes(tail_ref, widths.astype(BF16))
        inner = grad * gain_ref[0:1, :]
        gradtok_ref[...] = gradmid_ref[...] + scale * (
            inner - unit * jnp.mean(inner * unit, -1, keepdims=True)
        )


def mixer_back(
    grad_proj, scan_w, grad_u, x_inner, vec, grad_gate, in_t, u_act, tokens, gains, grad_mid,
    grad_widths, tile, devices,
):
    rows, channels = u_act.shape
    gate_parts = tile * devices // (2 * channels)
    pack_parts = tile * devices // channels
    pack_rows = scan_w.shape[1] + 8
    tail_rows = grad_widths.shape[0] + 7
    width = tokens.shape[1]
    cols = scan_w.shape[1]
    steps = channels // tile
    column = lambda i: (0, i)
    fixed = lambda i: (0, 0)
    return pl.pallas_call(
        back_kernel,
        grid=(steps,),
        in_specs=[
            pl.BlockSpec((rows, cols), fixed),
            pl.BlockSpec((tile, cols), lambda i: (i, 0)),
            pl.BlockSpec((rows, tile), column),
            pl.BlockSpec((rows, tile), column),
            pl.BlockSpec((8, tile), lambda i: ((vec.shape[0] - 8) // 8, i)),
            pl.BlockSpec((gate_parts, rows, tile // gate_parts), lambda i: (i, 0, 0)),
            pl.BlockSpec((tile, width), lambda i: (i, 0)),
            pl.BlockSpec((tile, width), lambda i: (i + steps, 0)),
            pl.BlockSpec((rows, tile), column),
            pl.BlockSpec((rows, width), fixed),
            pl.BlockSpec(gains.shape, fixed),
            pl.BlockSpec((rows, width), fixed),
            pl.BlockSpec(grad_widths.shape, fixed),
        ],
        out_specs=[
            pl.BlockSpec((gate_parts, rows, tile // gate_parts), lambda i: (i, 0, 0)),
            pl.BlockSpec((pack_parts, pack_rows, tile // pack_parts), lambda i: (i, 0, 0)),
            pl.BlockSpec((devices, tail_rows, width // devices), lambda i: (0, 0, 0)),
            pl.BlockSpec((rows, width), fixed),
        ],
        out_shape=[
            jax.ShapeDtypeStruct((devices // 2, rows, 2 * channels // devices), BF16),
            jax.ShapeDtypeStruct((devices, pack_rows, channels // devices), BF16),
            jax.ShapeDtypeStruct((devices, tail_rows, width // devices), BF16),
            jax.ShapeDtypeStruct((rows, width), F32),
        ],
        scratch_shapes=[pltpu.VMEM((rows, width), F32)],
        compiler_params=pltpu.CompilerParams(vmem_limit_bytes=VMEM_LIMIT),
        name="mixer_back",
    )(
        grad_proj, scan_w, grad_u, x_inner, vec, grad_gate, in_t, in_t, u_act, tokens, gains,
        grad_mid, grad_widths,
    )


def gelu_parts(values):
    weight = jnp.exp(values * values * -0.5)
    scaled = jnp.abs(values) * 0.7071067811865476
    ratio = 1.0 / (1.0 + 0.3275911 * scaled)
    series = 1.061405429 * ratio - 1.453152027
    series = series * ratio + 1.421413741
    series = series * ratio - 0.284496736
    series = series * ratio + 0.254829592
    tail = (0.5 * ratio) * series * weight
    below = jnp.where(values >= 0.0, 1.0 - tail, tail)
    return values * below, below + values * weight * 0.3989422804014327


def router_kernel(
    mid_ref, gain_ref, router_ref, routes_col_ref, routes_row_ref, slots_row_ref, live_ref, cot_ref,
    sendr_ref, sendg_ref, normed_ref, probs_ref,
):
    mid = mid_ref[...]
    rows = mid.shape[0]
    experts = router_ref.shape[1]
    scale = lax.rsqrt(jnp.mean(mid * mid, -1, keepdims=True) + 1e-05)
    normed = (mid * scale * gain_ref[...]).astype(BF16)
    normed_ref[...] = normed
    logits = product(normed, router_ref[...])
    weights = jnp.exp(logits - jnp.max(logits, -1, keepdims=True))
    probs = weights / jnp.sum(weights, -1, keepdims=True)
    probs_ref[...] = probs
    chosen = (routes_col_ref[...] == iota((rows, experts), 1)).astype(F32)
    gate = jnp.sum(probs * chosen, 1, keepdims=True)
    grads = (gate * (cot_ref[...].astype(F32) * live_ref[...])).astype(BF16)
    slot = iota((experts * CAP, rows), 0)
    dispatch = (
        (routes_row_ref[...] == slot // CAP) & (slots_row_ref[...] == slot % CAP)
    ).astype(BF16)
    width = mid.shape[1]
    sendr_ref[...] = product(dispatch, normed).astype(BF16).reshape(experts, CAP, width)
    sendg_ref[...] = product(dispatch, grads).astype(BF16).reshape(experts, CAP, width)


def router_step(mid, gain, router, routes_col, routes_row, slots_row, live, cotangent):
    rows, width = mid.shape
    experts = router.shape[1]
    return pl.pallas_call(
        router_kernel,
        out_shape=[
            jax.ShapeDtypeStruct((experts, CAP, width), BF16),
            jax.ShapeDtypeStruct((experts, CAP, width), BF16),
            jax.ShapeDtypeStruct((rows, width), BF16),
            jax.ShapeDtypeStruct((rows, experts), F32),
        ],
        compiler_params=pltpu.CompilerParams(vmem_limit_bytes=VMEM_LIMIT),
        name="router_step",
    )(mid, gain, router, routes_col, routes_row, slots_row, live, cotangent)


def expert_out_kernel(rows_ref, up_ref, down_ref, out_ref, slope_ref, total):
    step = pl.program_id(0)
    pieces, cap, width = rows_ref.shape
    rows = rows_ref[...].reshape(pieces * cap, width)

    @pl.when(step == 0)
    def _():
        total[...] = jnp.zeros_like(total)

    activated, slope = gelu_parts(product(rows, up_ref[...]))
    slope_ref[...] = slope.astype(BF16)
    total[...] += product(activated.astype(BF16), down_ref[...])

    @pl.when(step == pl.num_programs(0) - 1)
    def _():
        out_ref[...] = total[...].astype(BF16).reshape(pieces, cap, width)


def expert_out(rows, up, down, tile):
    pieces, cap, width = rows.shape
    hidden = up.shape[1]
    fixed = lambda i: (0, 0, 0)
    return pl.pallas_call(
        expert_out_kernel,
        grid=(hidden // tile,),
        in_specs=[
            pl.BlockSpec(rows.shape, fixed),
            pl.BlockSpec((width, tile), lambda i: (0, i)),
            pl.BlockSpec((tile, width), lambda i: (i, 0)),
        ],
        out_specs=[
            pl.BlockSpec(rows.shape, fixed),
            pl.BlockSpec((pieces * cap, tile), lambda i: (0, i)),
        ],
        out_shape=[
            jax.ShapeDtypeStruct(rows.shape, BF16),
            jax.ShapeDtypeStruct((pieces * cap, hidden), BF16),
        ],
        scratch_shapes=[pltpu.VMEM((pieces * cap, width), F32)],
        compiler_params=pltpu.CompilerParams(vmem_limit_bytes=VMEM_LIMIT),
        name="expert_out",
    )(rows, up, down)


def expert_back_kernel(grads_ref, up_ref, down_ref, slope_ref, out_ref, total):
    step = pl.program_id(0)
    pieces, cap, width = grads_ref.shape
    grads = grads_ref[...].reshape(pieces * cap, width)

    @pl.when(step == 0)
    def _():
        total[...] = jnp.zeros_like(total)

    slope = slope_ref[...].astype(F32)
    grad_pre = (times_transpose(grads, down_ref[...]) * slope).astype(BF16)
    total[...] += times_transpose(grad_pre, up_ref[...])

    @pl.when(step == pl.num_programs(0) - 1)
    def _():
        out_ref[...] = total[...].astype(BF16).reshape(pieces, cap, width)


def expert_back(grads, up, down, slope, tile):
    pieces, cap, width = grads.shape
    hidden = up.shape[1]
    fixed = lambda i: (0, 0, 0)
    return pl.pallas_call(
        expert_back_kernel,
        grid=(hidden // tile,),
        in_specs=[
            pl.BlockSpec(grads.shape, fixed),
            pl.BlockSpec((width, tile), lambda i: (0, i)),
            pl.BlockSpec((tile, width), lambda i: (i, 0)),
            pl.BlockSpec((pieces * cap, tile), lambda i: (0, i)),
        ],
        out_specs=pl.BlockSpec(grads.shape, fixed),
        out_shape=jax.ShapeDtypeStruct(grads.shape, BF16),
        scratch_shapes=[pltpu.VMEM((pieces * cap, width), F32)],
        compiler_params=pltpu.CompilerParams(vmem_limit_bytes=VMEM_LIMIT),
        name="expert_back",
    )(grads, up, down, slope)


def expert_grads_kernel(chunks, rows_ref, grads_ref, up_ref, down_ref, gup_ref, gdown_ref, rows_t):
    chunk = pl.program_id(1)
    groups, pieces, cap, width = rows_ref.shape
    count = groups * pieces * cap
    rows = rows_ref[...].reshape(count, width)
    grads = grads_ref[...].reshape(count, width)

    @pl.when((pl.program_id(0) == 0) | (chunks > 1))
    def _():
        rows_t[...] = rows.T

    activated, slope = gelu_parts(product(rows, up_ref[...]))
    grad_pre = (times_transpose(grads, down_ref[...]) * slope).astype(BF16)
    grad_up = product(rows_t[...], grad_pre)
    grad_down = contract_rows(activated.astype(BF16), grads)

    @pl.when(chunk == 0)
    def _():
        gup_ref[...] = grad_up
        gdown_ref[...] = grad_down

    if chunks > 1:

        @pl.when(chunk > 0)
        def _():
            gup_ref[...] += grad_up
            gdown_ref[...] += grad_down


def expert_grads(rows, grads, up, down, tile):
    groups, pieces, cap, width = rows.shape
    hidden = up.shape[1]
    together = max(1, min(groups, 32 // pieces))
    chunks = groups // together
    some = pl.BlockSpec((together, pieces, cap, width), lambda i, j: (j, 0, 0, 0))
    return pl.pallas_call(
        partial(expert_grads_kernel, chunks),
        grid=(hidden // tile, chunks),
        in_specs=[
            some,
            some,
            pl.BlockSpec((width, tile), lambda i, j: (0, i)),
            pl.BlockSpec((tile, width), lambda i, j: (i, 0)),
        ],
        out_specs=[
            pl.BlockSpec((width, tile), lambda i, j: (0, i)),
            pl.BlockSpec((tile, width), lambda i, j: (i, 0)),
        ],
        out_shape=[
            jax.ShapeDtypeStruct((width, hidden), F32),
            jax.ShapeDtypeStruct((hidden, width), F32),
        ],
        scratch_shapes=[pltpu.VMEM((width, together * pieces * cap), BF16)],
        compiler_params=pltpu.CompilerParams(vmem_limit_bytes=VMEM_LIMIT),
        name="expert_grads",
    )(rows, grads, up, down)


def combine_kernel(
    mid_ref, gain_ref, router_ref, routes_ref, slots_ref, live_ref, cot_ref, probs_ref, normed_ref,
    backr_ref, backg_ref, out_ref, gradmid_ref, gradmix_ref, widths_ref,
):
    mid = mid_ref[...]
    rows, width = mid.shape
    experts = router_ref.shape[1]
    routes = routes_ref[...]
    chosen = (routes == iota((rows, experts), 1)).astype(F32)
    probs = probs_ref[...]
    gate = jnp.sum(probs * chosen, 1, keepdims=True)
    live = live_ref[...]
    slot = iota((rows, experts * CAP), 1)
    collect = ((routes == slot // CAP) & (slots_ref[...] == slot % CAP)).astype(BF16)
    expert_sum = product(collect, backr_ref[...].reshape(experts * CAP, width))
    out_ref[...] = (live * (mid + gate * expert_sum)).astype(BF16)
    grad_out = cot_ref[...].astype(F32) * live
    grad_gate = jnp.sum(grad_out * expert_sum, 1, keepdims=True)
    grad_logits = (probs * (chosen * grad_gate - gate * grad_gate)).astype(BF16)
    grad_router = contract_rows(grad_logits, normed_ref[...])
    grad = product(collect, backg_ref[...].reshape(experts * CAP, width))
    grad = grad + times_transpose(grad_logits, router_ref[...])
    scale = lax.rsqrt(jnp.mean(mid * mid, -1, keepdims=True) + 1e-05)
    unit = mid * scale
    widths_ref[...] = jnp.concatenate([grad_router, jnp.sum(grad * unit, 0, keepdims=True)], 0)
    inner = grad * gain_ref[...]
    grad_mid = grad_out + scale * (inner - unit * jnp.mean(inner * unit, -1, keepdims=True))
    gradmid_ref[...] = grad_mid
    gradmix_ref[...] = grad_mid.astype(BF16)


def combine_step(mid, gain, router, routes, slots, live, cotangent, probs, normed, backr, backg):
    rows, width = mid.shape
    return pl.pallas_call(
        combine_kernel,
        out_shape=[
            jax.ShapeDtypeStruct((rows, width), BF16),
            jax.ShapeDtypeStruct((rows, width), F32),
            jax.ShapeDtypeStruct((rows, width), BF16),
            jax.ShapeDtypeStruct((router.shape[1] + 1, width), F32),
        ],
        compiler_params=pltpu.CompilerParams(vmem_limit_bytes=VMEM_LIMIT),
        name="combine_step",
    )(mid, gain, router, routes, slots, live, cotangent, probs, normed, backr, backg)


MESH = pl.DeviceIdType.MESH


def neighbour(bit):
    me = lax.axis_index("expert")
    return me + (1 - 2 * ((me // bit) % 2)) * bit


def greet(line=True):
    devices, copies = lax.axis_size("expert"), lax.axis_size("dp")
    me, place = lax.axis_index("expert"), lax.axis_index("dp")
    barrier = pltpu.get_barrier_semaphore()
    for k in range(1, devices):
        pl.semaphore_signal(
            barrier, inc=1, device_id={"expert": (me + k) % devices}, device_id_type=MESH
        )
    if line:

        @pl.when(place < copies - 1)
        def _():
            pl.semaphore_signal(barrier, inc=1, device_id={"dp": place + 1}, device_id_type=MESH)

        @pl.when(place > 0)
        def _():
            pl.semaphore_signal(barrier, inc=1, device_id={"dp": place - 1}, device_id_type=MESH)

    ends = (place == 0) | (place == copies - 1)
    if line:
        pl.when(ends)(lambda: pl.semaphore_wait(barrier, devices))
        pl.when(jnp.logical_not(ends))(lambda: pl.semaphore_wait(barrier, devices + 1))
    else:
        pl.semaphore_wait(barrier, devices - 1)


class Exchange:
    def __init__(self, source, target, send_sems, recv_sems, local_sem):
        devices, me = lax.axis_size("expert"), lax.axis_index("expert")
        self.copies = []
        for k in range(1, devices):
            peer = (me + k) % devices
            self.copies.append(
                pltpu.make_async_remote_copy(
                    source.at[peer], target.at[me], send_sems.at[k], recv_sems.at[k],
                    device_id={"expert": peer}, device_id_type=MESH,
                )
            )
        self.local = pltpu.make_async_copy(source.at[me], target.at[me], local_sem)

    def start(self):
        for copy in self.copies:
            copy.start()
        self.local.start()

    def wait(self):
        self.local.wait()
        for copy in self.copies:
            copy.wait()


class Line:
    def __init__(self, stage, from_left, from_right, next_left, next_right, send_sems, recv_sems):
        place = lax.axis_index("dp")
        last = lax.axis_size("dp") - 1
        self.right = pltpu.make_async_remote_copy(
            from_left, next_left, send_sems.at[0], recv_sems.at[0],
            device_id={"dp": jnp.minimum(place + 1, last)}, device_id_type=MESH,
        )
        self.left = pltpu.make_async_remote_copy(
            from_right, next_right, send_sems.at[1], recv_sems.at[1],
            device_id={"dp": jnp.maximum(place - 1, 0)}, device_id_type=MESH,
        )
        self.send_right = (place >= stage - 1) & (place < last)
        self.send_left = (last - place >= stage - 1) & (place > 0)
        self.get_left = place >= stage
        self.get_right = last - place >= stage

    def start(self):
        pl.when(self.send_right)(lambda: self.right.start())
        pl.when(self.send_left)(lambda: self.left.start())

    def wait(self):
        pl.when(self.send_right)(lambda: self.right.wait_send())
        pl.when(self.send_left)(lambda: self.left.wait_send())
        pl.when(self.get_left)(lambda: self.right.wait_recv())
        pl.when(self.get_right)(lambda: self.left.wait_recv())


def as_column(row):
    return jnp.broadcast_to(row.astype(F32), (8, row.shape[1])).T[:, 0:1].astype(jnp.int32)


def dispatch_matrix(goal, experts):
    slot = iota((experts * CAP, goal.shape[1]), 0)
    return (goal[0:1, :] == slot).astype(BF16)


def expert_layer_kernel(
    length_ref, mid_ref, gains_ref, router_ref, routes_ref, slots_ref, cot_ref, up_hbm, down_hbm,
    out_ref, gradmid_ref, gradmix_ref, widths_ref, rows_out, grads_out,
    left_1, right_1, left_2, right_2, goal_l1, goal_r1, goal_l2, goal_r2, gup_hbm, gdown_hbm,
    raw, goal, up_ref, down_ref, send_r, send_g, got_r, got_g, slope_ref, total, give_r, give_g,
    back_r, back_g, probs_ref, act_ref, rows_t, gup_ref, gdown_ref,
    weight_sems, send_sems, recv_sems, local_sems, line_send, line_recv, out_sems, grad_sems,
):
    tile = 512
    rows, width = mid_ref.shape
    experts = router_ref.shape[0]
    hidden = up_ref.shape[1]
    load_up = pltpu.make_async_copy(up_hbm, up_ref, weight_sems.at[0])
    load_down = pltpu.make_async_copy(down_hbm, down_ref, weight_sems.at[1])
    load_up.start()
    load_down.start()
    greet()

    ways = [
        Exchange(source, target, send_sems.at[k], recv_sems.at[k], local_sems.at[k])
        for k, (source, target) in enumerate(
            [(send_r, got_r), (send_g, got_g), (give_r, back_r), (give_g, back_g)]
        )
    ]
    lines = [
        Line(stage, *buffers, line_send.at[k], line_recv.at[k])
        for k, (stage, buffers) in enumerate(
            [(1, (raw.at[part], raw.at[part], left_1.at[part], right_1.at[part])) for part in (0, 1)]
            + [(1, (goal, goal, goal_l1, goal_r1))]
            + [
                (2, (left_1.at[part], right_1.at[part], left_2.at[part], right_2.at[part]))
                for part in (0, 1)
            ]
            + [(2, (goal_l1, goal_r1, goal_l2, goal_r2))]
        )
    ]
    gain = gains_ref[1:2, :]
    live = (iota((rows, 1), 0) < length_ref[0]).astype(F32)
    routes, slots = as_column(routes_ref[...]), as_column(slots_ref[...])
    mid = mid_ref[...]
    scale = lax.rsqrt(jnp.mean(mid * mid, -1, keepdims=True) + 1e-05)
    normed = (mid * scale * gain).astype(BF16)
    raw[0] = normed
    slots_row = slots_ref[...]
    target = jnp.where(slots_row < CAP, routes_ref[...] * CAP + slots_row, -1)
    goal[...] = jnp.broadcast_to(target, goal.shape)
    dispatch = dispatch_matrix(goal, experts)
    send_r[...] = product(dispatch, normed).astype(BF16).reshape(experts, CAP, width)
    ways[0].start()
    for k in (0, 2):
        lines[k].start()
    logits = times_transpose(normed, router_ref[...])
    weights = jnp.exp(logits - jnp.max(logits, -1, keepdims=True))
    probs = weights / jnp.sum(weights, -1, keepdims=True)
    probs_ref[...] = probs
    chosen = (routes == iota((rows, experts), 1)).astype(F32)
    gate = jnp.sum(probs * chosen, 1, keepdims=True)
    grads = (gate * (cot_ref[...].astype(F32) * live)).astype(BF16)
    raw[1] = grads
    send_g[...] = product(dispatch, grads).astype(BF16).reshape(experts, CAP, width)
    ways[1].start()
    lines[1].start()

    load_up.wait()
    load_down.wait()
    ways[0].wait()
    for k in (0, 2):
        lines[k].wait()
        lines[k + 3].start()
    keep_rows = pltpu.make_async_copy(got_r, rows_out, out_sems.at[0])
    keep_rows.start()
    total[...] = jnp.zeros_like(total)

    def forward(step, carry):
        at = pl.ds(pl.multiple_of(step * tile, tile), tile)
        inputs = got_r[...].reshape(experts * CAP, width)
        activated, slope = gelu_parts(product(inputs, up_ref[:, at]))
        slope_ref[:, at] = slope.astype(BF16)
        activated = activated.astype(BF16)
        act_ref[:, at] = activated
        total[...] += product(activated, down_ref[at, :])
        return carry

    lax.fori_loop(0, hidden // tile, forward, 0)
    give_r[...] = total[...].astype(BF16).reshape(experts, CAP, width)
    ways[2].start()
    ways[1].wait()
    lines[1].wait()
    lines[4].start()
    keep_grads = pltpu.make_async_copy(got_g, grads_out, out_sems.at[1])
    keep_grads.start()
    total[...] = jnp.zeros_like(total)

    def backward(step, carry):
        at = pl.ds(pl.multiple_of(step * tile, tile), tile)
        outputs = got_g[...].reshape(experts * CAP, width)
        slope = slope_ref[:, at].astype(F32)
        grad_pre = (times_transpose(outputs, down_ref[at, :]) * slope).astype(BF16)
        slope_ref[:, at] = grad_pre
        total[...] += times_transpose(grad_pre, up_ref[:, at])
        return carry

    lax.fori_loop(0, hidden // tile, backward, 0)
    give_g[...] = total[...].astype(BF16).reshape(experts, CAP, width)
    ways[3].start()

    rows_t[...] = got_r[...].reshape(experts * CAP, width).T
    stores = []
    for step in range(hidden // tile):
        spot = step % 2
        at = pl.ds(step * tile, tile)
        if step >= 2:
            for store in stores[2 * (step - 2) : 2 * (step - 1)]:
                store.wait()
        gup_ref[spot] = product(rows_t[...], slope_ref[:, at]).astype(BF16)
        gdown_ref[spot] = contract_rows(
            act_ref[:, at], got_g[...].reshape(experts * CAP, width)
        ).astype(BF16)
        stores += [
            pltpu.make_async_copy(gup_ref.at[spot], gup_hbm.at[:, at], grad_sems.at[0, spot]),
            pltpu.make_async_copy(gdown_ref.at[spot], gdown_hbm.at[at], grad_sems.at[1, spot]),
        ]
        for store in stores[-2:]:
            store.start()

    chosen = (routes == iota((rows, experts), 1)).astype(F32)
    probs = probs_ref[...]
    gate = jnp.sum(probs * chosen, 1, keepdims=True)
    slot = iota((rows, experts * CAP), 1)
    collect = ((routes == slot // CAP) & (slots == slot % CAP)).astype(BF16)
    ways[2].wait()
    expert_sum = product(collect, back_r[...].reshape(experts * CAP, width))
    mid = mid_ref[...]
    out_ref[...] = (live * (mid + gate * expert_sum)).astype(BF16)
    grad_out = cot_ref[...].astype(F32) * live
    grad_gate = jnp.sum(grad_out * expert_sum, 1, keepdims=True)
    grad_logits = (probs * (chosen * grad_gate - gate * grad_gate)).astype(BF16)
    grad_router = contract_rows(grad_logits, raw[0])
    from_logits = product(grad_logits, router_ref[...])
    scale = lax.rsqrt(jnp.mean(mid * mid, -1, keepdims=True) + 1e-05)
    unit = mid * scale
    ways[3].wait()
    grad = product(collect, back_g[...].reshape(experts * CAP, width)) + from_logits
    widths_ref[...] = jnp.concatenate([grad_router, jnp.sum(grad * unit, 0, keepdims=True)], 0)
    inner = grad * gain
    grad_mid = grad_out + scale * (inner - unit * jnp.mean(inner * unit, -1, keepdims=True))
    gradmid_ref[...] = grad_mid
    gradmix_ref[...] = grad_mid.astype(BF16)
    for store in stores[-4:]:
        store.wait()
    keep_rows.wait()
    keep_grads.wait()
    for k in (3, 4, 5):
        lines[k].wait()


def expert_layer(lengths, mid, gains, router, routes, slots, cotangent, up, down):
    rows, width = mid.shape
    experts = router.shape[0]
    hidden = up.shape[1]
    buffer = (experts, CAP, width)
    here = pl.BlockSpec(memory_space=pltpu.VMEM)
    far = pl.BlockSpec(memory_space=pl.ANY)
    blocks = jax.ShapeDtypeStruct(buffer, BF16)
    raw = jax.ShapeDtypeStruct((2, rows, width), BF16)
    goal = jax.ShapeDtypeStruct((8, rows), jnp.int32)
    dma = pltpu.SemaphoreType.DMA
    return pl.pallas_call(
        expert_layer_kernel,
        in_specs=[pl.BlockSpec(memory_space=pltpu.SMEM)] + [here] * 6 + [far] * 2,
        out_specs=[here] * 4 + [far] * 12,
        out_shape=[
            jax.ShapeDtypeStruct((rows, width), BF16),
            jax.ShapeDtypeStruct((rows, width), F32),
            jax.ShapeDtypeStruct((rows, width), BF16),
            jax.ShapeDtypeStruct((experts + 1, width), F32),
        ] + [blocks] * 2 + [raw] * 4 + [goal] * 4 + [
            jax.ShapeDtypeStruct(up.shape, BF16),
            jax.ShapeDtypeStruct(down.shape, BF16),
        ],
        scratch_shapes=[
            pltpu.VMEM(raw.shape, BF16),
            pltpu.VMEM(goal.shape, jnp.int32),
            pltpu.VMEM(up.shape, BF16),
            pltpu.VMEM(down.shape, BF16),
        ] + [pltpu.VMEM(buffer, BF16)] * 4 + [
            pltpu.VMEM((experts * CAP, hidden), BF16),
            pltpu.VMEM((experts * CAP, width), F32),
        ] + [pltpu.VMEM(buffer, BF16)] * 4 + [
            pltpu.VMEM((rows, experts), F32),
            pltpu.VMEM((experts * CAP, hidden), BF16),
            pltpu.VMEM((width, experts * CAP), BF16),
            pltpu.VMEM((2, width, 512), BF16),
            pltpu.VMEM((2, 512, width), BF16),
            dma((2,)), dma((4, experts)), dma((4, experts)), dma((4,)), dma((6, 2)), dma((6, 2)),
            dma((2,)), dma((2, 2)),
        ],
        compiler_params=pltpu.CompilerParams(
            vmem_limit_bytes=VMEM_LIMIT, collective_id=1, has_side_effects=True
        ),
        name="expert_layer",
    )(lengths, mid, gains, router, routes, slots, cotangent, up, down)


class PlaneGather:
    def __init__(self, source, target, send_sems, recv_sems, local_sem):
        me = lax.axis_index("expert")
        core, side, above = neighbour(1), neighbour(2), neighbour(4)
        far = side + above - me
        rows = target.shape[1]
        first, second = pl.ds(0, rows // 2), pl.ds(rows // 2, rows - rows // 2)
        every = pl.ds(0, rows)

        def send(k, block, owner, part, device):
            return pltpu.make_async_remote_copy(
                block, target.at[owner, part], send_sems.at[k], recv_sems.at[k],
                device_id={"expert": device}, device_id_type=MESH,
            )

        self.copies = [
            send(0, source.at[first], me, first, side),
            send(1, source.at[second], me, second, side),
            send(2, source.at[first], me, first, above),
            send(3, source.at[second], me, second, above),
            send(4, target.at[side, first], side, first, above),
            send(5, target.at[above, second], above, second, side),
            send(6, source, me, every, core),
            send(7, target.at[side], side, every, core),
            send(8, target.at[above], above, every, core),
            send(9, target.at[far], far, every, core),
        ]
        self.local = pltpu.make_async_copy(source, target.at[me], local_sem)

    def step(self, number):
        copies = self.copies
        for k in ((), (0, 3), (1, 2), (4, 5), (6, 7, 8, 9))[number]:
            copies[k].wait_recv()
        for k in ((0, 3, 1, 2, 6), (4, 5), (7, 8), (9,), ())[number]:
            copies[k].start()
        if number == 0:
            self.local.start()
        if number == 4:
            self.local.wait()
            for copy in copies:
                copy.wait_send()


class WideGather:
    def __init__(self, source, target, send_sems, recv_sems, local_sem):
        me, place = lax.axis_index("expert"), lax.axis_index("dp")
        core, side, above = neighbour(1), neighbour(2), neighbour(4)
        far = side + above - me
        odd = place % 2
        partner = place + 1 - 2 * odd
        rows = target.shape[1]
        unit = rows // 6

        def part(start, count):
            return pl.ds(pl.multiple_of(start * unit, unit), count * unit)

        def send(k, block, owner, where, **device):
            return pltpu.make_async_remote_copy(
                block, target.at[owner, where], send_sems.at[k], recv_sems.at[k],
                device_id=device, device_id_type=MESH,
            )

        def forward(k, owner, where, **device):
            return send(k, target.at[owner, where], owner, where, **device)

        outer, inner = part(4 * odd, 2), part(4 * (1 - odd), 2)
        middle = part(2, 2)
        self.copies = [
            send(0, source.at[outer], me, outer, expert=side),
            send(1, source.at[middle], me, middle, expert=side),
            send(2, source.at[inner], me, inner, expert=above),
            send(3, source.at[middle], me, middle, expert=above),
            forward(4, side, outer, expert=above),
            forward(5, side, part(2 + odd, 1), expert=above),
            forward(6, above, inner, expert=side),
            forward(7, above, part(3 - odd, 1), expert=side),
            forward(8, side, outer, dp=partner),
            forward(9, above, inner, dp=partner),
            send(10, source, me, part(0, 6), expert=core),
            forward(11, side, part(2 * odd, 4), expert=core),
            forward(12, above, part(2 - 2 * odd, 4), expert=core),
            forward(13, side, inner, expert=core),
            forward(14, above, outer, expert=core),
            forward(15, far, part(0, 6), expert=core),
        ]
        self.local = pltpu.make_async_copy(source, target.at[me], local_sem)

    def step(self, number):
        copies = self.copies
        for k in ((), (0, 2), (1, 3), (8, 9), (4, 5, 6, 7), (10, 11, 12, 13, 14, 15))[number]:
            copies[k].wait_recv()
        for k in ((0, 2, 1, 3, 10), (4, 6, 8, 9), (5, 7, 11, 12), (13, 14), (15,), ())[number]:
            copies[k].start()
        if number == 0:
            self.local.start()
        if number == 5:
            self.local.wait()
            for copy in copies:
                copy.wait_send()


class Near:
    def __init__(self, own, target, send_sems, recv_sems):
        self.place = lax.axis_index("dp")
        self.last = lax.axis_size("dp") - 1
        self.right = pltpu.make_async_remote_copy(
            own, target, send_sems.at[0], recv_sems.at[0],
            device_id={"dp": jnp.minimum(self.place + 1, self.last)}, device_id_type=MESH,
        )
        self.left = pltpu.make_async_remote_copy(
            own, target, send_sems.at[1], recv_sems.at[1],
            device_id={"dp": jnp.maximum(self.place - 1, 0)}, device_id_type=MESH,
        )

    def start(self):
        pl.when(self.place < self.last)(lambda: self.right.start())
        pl.when(self.place == 1)(lambda: self.left.start())

    def wait(self):
        pl.when(self.place < self.last)(lambda: self.right.wait_send())
        pl.when(self.place == 1)(lambda: self.left.wait_send())
        pl.when(self.place > 0)(lambda: self.right.wait_recv())
        pl.when(self.place == 0)(lambda: self.left.wait_recv())


DMA = pltpu.SemaphoreType.DMA
FAR = pl.BlockSpec(memory_space=pl.ANY)


def remote_params(collective_id):
    return pltpu.CompilerParams(
        vmem_limit_bytes=VMEM_LIMIT, collective_id=collective_id, has_side_effects=True
    )


def columns_of(proj_ref, first, state, target):
    turned = proj_ref[...].T[first : first + state]
    for block in range(proj_ref.shape[0] // BLOCK):
        target[block * state : (block + 1) * state, 0:BLOCK] = turned[
            :, block * BLOCK : (block + 1) * BLOCK
        ]


def diagonals_of(proj_ref, first, state, high_ref, low_ref):
    rows, width = proj_ref.shape
    big = BLOCK * state
    place = (iota((width, big), 0) == first + iota((width, big), 1) % state).astype(BF16)
    own = iota((rows, big), 0) % BLOCK == iota((rows, big), 1) // state
    for part, target in zip(two_parts(proj_ref[...]), (high_ref, low_ref)):
        target[...] = jnp.where(own, product(part, place), 0.0).astype(BF16)


def block_of(ref, block, size):
    return ref[pl.ds(pl.multiple_of(block * size, size), size), :]


def forward_kernel(
    tokens_ref, in_ref, scan_ref, step_w_ref, decay_ref, conv_ref, bias_ref, dbias_ref, skip_ref,
    norm_ref, norm_two_ref, router_ref, outw_ref,
    normed_ref, xin_ref, u_out, gate_out, proj_ref, step_ref, mixed_ref, gated_ref, mid_ref,
    step_full, vec_ref, router_full, gains_ref, scan_full, in_full, outw_all, normed_all, hist_hbm,
    columns, widths, columns_all, widths_all, scan_here, in_here, u_all, gate_all, b_cols, c_high, c_low, du,
    scanned, gated_all, outw_here, ring,
    send_sems, recv_sems, local_sems, ring_sems,
):
    step = pl.program_id(0)
    devices, rank, part = columns_all.shape[0], step_w_ref.shape[0], step_w_ref.shape[1]
    state, taps, experts = decay_ref.shape[0], conv_ref.shape[0], router_ref.shape[0]
    slice_w = widths.shape[1]
    rows, tile = xin_ref.shape
    width = tokens_ref.shape[1]
    big = BLOCK * state
    turns = ring.shape[0]
    last = rows // BLOCK - 1
    small = [
        PlaneGather(source, target, send_sems.at[k], recv_sems.at[k], local_sems.at[k])
        for k, (source, target) in enumerate(
            [(columns, columns_all), (widths, widths_all), (scan_ref, scan_here)]
        )
    ]
    big_gather = WideGather(in_ref, in_here, send_sems.at[3], recv_sems.at[3], local_sems.at[3])
    gather = WideGather(outw_ref, outw_here, send_sems.at[4], recv_sems.at[4], local_sems.at[4])
    normed_gather = PlaneGather(
        normed_ref, normed_all, send_sems.at[5], recv_sems.at[5], local_sems.at[5]
    )
    keep = pltpu.make_async_copy(outw_here, outw_all, local_sems.at[6])
    keep_in = pltpu.make_async_copy(in_here, in_full, local_sems.at[7])
    half = step % 2
    lanes = pl.ds(pl.multiple_of(half * tile, tile), tile)

    @pl.when(step == 0)
    def _():
        spare = columns.shape[0] - rank - state - taps - 3
        columns[...] = jnp.concatenate(
            [
                step_w_ref[...].astype(F32), decay_ref[...].astype(F32), conv_ref[...].astype(F32),
                *(ref[...].astype(F32)[None] for ref in (bias_ref, dbias_ref, skip_ref)),
                jnp.zeros((spare, part), F32),
            ],
            0,
        ).astype(BF16)
        widths[...] = jnp.concatenate(
            [
                router_ref[...].astype(F32),
                *(ref[...].astype(F32)[None] for ref in (norm_ref, norm_two_ref)),
                jnp.zeros((widths.shape[0] - experts - 2, slice_w), F32),
            ],
            0,
        ).astype(BF16)
        greet()
        for number in range(3):
            for one in small:
                one.step(number)
            big_gather.step(number)
        for number in (3, 4):
            for one in small:
                one.step(number)
        big_gather.step(3)
        table = jnp.concatenate([columns_all[k].astype(F32) for k in range(devices)], 1)
        step_full[...] = table[:rank].astype(BF16)
        scan_full[...] = scan_here[...]
        rest = table[rank:]
        vec_ref[0:state, :] = -jnp.exp(rest[:state])
        vec_ref[state : state + 8, :] = rest[state : state + 8]
        across = jnp.concatenate([widths_all[k].astype(F32) for k in range(devices)], 1)
        router_full[...] = across[:experts].astype(BF16)
        gains_ref[...] = across[experts : experts + 8]
        values = tokens_ref[...].astype(F32)
        scale = lax.rsqrt(jnp.mean(values * values, -1, keepdims=True) + 1e-05)
        normed_ref[...] = (values * scale * gains_ref[0:1, :]).astype(BF16)
        proj_ref[...] = jnp.zeros_like(proj_ref)
        big_gather.step(4)
        gather.step(0)
        big_gather.step(5)
        keep_in.start()

    @pl.when(step < 2)
    def _():
        misc = vec_ref[state : state + 8, lanes]
        normed = normed_ref[...]
        own = devices // 4

        def weights(first):
            rows_here = in_here.shape[1]
            return in_here[pl.ds(first + half * own, own)].reshape(own * rows_here, width)

        x_inner = times_transpose(normed, weights(0))
        gate_in = times_transpose(normed, weights(devices // 2))
        gate_out[...] = gate_in
        gate_all[:, lanes] = gate_in
        xin_ref[...] = x_inner
        summed = misc[taps : taps + 1] + misc[taps - 1 : taps] * x_inner
        for back in range(1, taps):
            tap = taps - 1 - back
            summed = summed + misc[tap : tap + 1] * shift_rows(x_inner, back)
        u_act = summed * sigmoid(summed)
        u_out[...] = u_act
        u_all[:, lanes] = u_act
        parts = devices // 2
        scan_rows_here = scan_here[pl.ds(half * parts, parts)].reshape(tile, scan_here.shape[2])
        proj_ref[...] += product(u_act.astype(BF16), scan_rows_here)

    @pl.when(step == 1)
    def _():
        gather.step(1)
        gather.step(2)
        normed_gather.step(0)
        columns_of(proj_ref, rank, state, b_cols)
        diagonals_of(proj_ref, rank + state, state, c_high, c_low)

    def store(spot, block):
        start = pl.multiple_of((block * BLOCK + 1) * state, state)
        return pltpu.make_async_copy(
            ring.at[spot], hist_hbm.at[pl.ds(start, big), lanes], ring_sems.at[spot]
        )

    def sum_states(spot, block):
        high, low = block_of(c_high, block, BLOCK), block_of(c_low, block, BLOCK)
        both = product(jnp.concatenate([high, low], 0), ring[spot])
        return both[:BLOCK] + both[BLOCK:]

    def between(position):
        if position == 1:
            gather.step(3)
            gather.step(4)
        if position == 4:
            gather.step(5)
            keep.start()
            normed_gather.step(1)
            normed_gather.step(2)
        if position == 7:
            normed_gather.step(3)

    @pl.when(step >= 2)
    def _():
        misc = vec_ref[state : state + 8, lanes]
        u_act = u_all[:, lanes]
        step_size = softplus(
            product(proj_ref[:, :rank].astype(BF16), step_full[:, lanes])
            + misc[taps + 1 : taps + 2]
        )
        step_ref[...] = step_size
        du[...] = step_size * u_act
        decay = vec_ref[0:state, lanes] * LOG2E
        ring[turns - 1] = jnp.zeros((big, tile), BF16)
        zero_row = pltpu.make_async_copy(
            ring.at[turns - 1, pl.ds(0, state)], hist_hbm.at[pl.ds(0, state), lanes],
            ring_sems.at[turns],
        )
        zero_row.start()
        zero_row.wait()

        def run_blocks(quarter, held):
            for spot in range(turns):
                block = quarter * turns + spot
                pl.when(quarter > 0)(lambda: store(spot, block).wait())
                base = pl.multiple_of(block * BLOCK, BLOCK)
                before = (spot - 1) % turns
                scanned[pl.ds(base, BLOCK), :] = sum_states(before, jnp.maximum(block - 1, 0))
                steps_now, du_now = block_of(step_ref, block, BLOCK), block_of(du, block, BLOCK)
                b_now = block_of(b_cols, block, state)
                for t in range(BLOCK):
                    b_wide = jnp.broadcast_to(b_now[:, t : t + 1], (state, tile))
                    fade = jnp.exp2(steps_now[t : t + 1, :] * decay)
                    held = fade * held + du_now[t : t + 1, :] * b_wide
                    ring[spot, t * state : (t + 1) * state, :] = held.astype(BF16)
                store(spot, block).start()
            for turn in range(2):
                for count in range(rows // BLOCK // turns):

                    @pl.when((step == turn + 2) & (quarter == count))
                    def _():
                        between(turn * 4 + count)

            return held

        quarters = rows // BLOCK // turns
        lax.fori_loop(0, quarters, run_blocks, jnp.zeros((state, tile), F32))
        scanned[pl.ds(rows, BLOCK), :] = sum_states(turns - 1, last)
        mixed = scanned[pl.ds(BLOCK, rows), :] + misc[taps + 2 : taps + 3] * u_act
        mixed_ref[...] = mixed
        gate_in = gate_all[:, lanes]
        gated = (mixed * (gate_in * sigmoid(gate_in))).astype(BF16)
        gated_ref[...] = gated.T.reshape(gated_ref.shape)
        gated_all[:, lanes] = gated
        for spot in range(turns):
            store(spot, last - turns + 1 + spot).wait()

    @pl.when(step == 3)
    def _():
        weights = outw_here[...].reshape(devices * part, width)
        mid_ref[...] = tokens_ref[...].astype(F32) + product(gated_all[...], weights)
        keep.wait()
        keep_in.wait()
        normed_gather.step(4)


def forward_plane(
    tokens, in_t, scan_w, step_w, decay_t, conv, bias, dbias, skip, norm, norm_two, router_t, out_w
):
    rows, width = tokens.shape
    rank, part = step_w.shape
    cols = scan_w.shape[1]
    devices = lax.axis_size("expert")
    channels = devices * part
    state, experts, slice_w = decay_t.shape[0], router_t.shape[0], router_t.shape[1]
    tile = channels // 2
    hist_rows = (rows + 1) * state
    first = lambda i: jnp.minimum(i, 1)
    second = lambda i: jnp.maximum(i - 2, 0)

    def whole(shape):
        return pl.BlockSpec(shape, lambda i: (0,) * len(shape), pipeline_mode=pl.Buffered(1))

    def kept(shape):
        return pl.BlockSpec(shape, lambda i: (0,) * len(shape))

    def halves(index):
        return pl.BlockSpec((rows, tile), lambda i: (0, index(i)))

    inputs = (
        tokens, in_t, scan_w, step_w, decay_t, conv, bias, dbias, skip, norm, norm_two, router_t
    )
    fixed = [
        ((rank, channels), BF16), ((state + 8, channels), F32), ((experts, width), BF16),
        ((8, width), F32), ((devices, part, cols), BF16),
    ]
    return pl.pallas_call(
        forward_kernel,
        grid=(4,),
        in_specs=[whole(value.shape) for value in inputs] + [FAR],
        out_specs=[
            kept((rows, width)),
            halves(first),
            halves(first),
            halves(first),
            kept((rows, cols)),
            halves(second),
            halves(second),
            pl.BlockSpec((devices // 2, part, rows), lambda i: (second(i), 0, 0)),
            kept((rows, width)),
        ] + [kept(shape) for shape, _ in fixed] + [FAR] * 4,
        out_shape=[
            jax.ShapeDtypeStruct((rows, width), BF16),
            jax.ShapeDtypeStruct((rows, channels), F32),
            jax.ShapeDtypeStruct((rows, channels), F32),
            jax.ShapeDtypeStruct((rows, channels), F32),
            jax.ShapeDtypeStruct((rows, cols), F32),
            jax.ShapeDtypeStruct((rows, channels), F32),
            jax.ShapeDtypeStruct((rows, channels), F32),
            jax.ShapeDtypeStruct((devices, part, rows), BF16),
            jax.ShapeDtypeStruct((rows, width), F32),
        ] + [jax.ShapeDtypeStruct(shape, kind) for shape, kind in fixed] + [
            jax.ShapeDtypeStruct((devices,) + in_t.shape, BF16),
            jax.ShapeDtypeStruct((devices, part, width), BF16),
            jax.ShapeDtypeStruct((devices, rows, width), BF16),
            jax.ShapeDtypeStruct((hist_rows, channels), BF16),
        ],
        scratch_shapes=[
            pltpu.VMEM((rank + state + 8, part), BF16),
            pltpu.VMEM((32, slice_w), BF16),
            pltpu.VMEM((devices, rank + state + 8, part), BF16),
            pltpu.VMEM((devices, 32, slice_w), BF16),
            pltpu.VMEM((devices, part, cols), BF16),
            pltpu.VMEM((devices,) + in_t.shape, BF16),
            pltpu.VMEM((rows, channels), F32),
            pltpu.VMEM((rows, channels), F32),
            pltpu.VMEM((rows // BLOCK * state, 128), F32),
            pltpu.VMEM((rows, BLOCK * state), BF16),
            pltpu.VMEM((rows, BLOCK * state), BF16),
            pltpu.VMEM((rows, tile), F32),
            pltpu.VMEM((rows + BLOCK, tile), F32),
            pltpu.VMEM((rows, channels), BF16),
            pltpu.VMEM((devices, part, width), BF16),
            pltpu.VMEM((4, BLOCK * state, tile), BF16),
            DMA((6, 16)), DMA((6, 16)), DMA((8,)), DMA((5,)),
        ],
        compiler_params=remote_params(3),
        name="mixer_forward",
    )(*inputs, out_w)


def prepare_sends(raw, goal, sends):
    experts, cap, width = sends.shape[1:]
    matrix = dispatch_matrix(goal, experts)
    for part in range(2):
        values = product(matrix, raw[part]).astype(BF16)
        sends[part] = values.reshape(experts, cap, width)


def pick(choices, raw, goal, sems):
    place = lax.axis_index("dp")
    for where, (source, source_goal) in enumerate(choices):

        @pl.when(place == where)
        def _():
            copies = [
                pltpu.make_async_copy(source, raw, sems.at[0]),
                pltpu.make_async_copy(source_goal, goal, sems.at[1]),
            ]
            for copy in copies:
                copy.start()
            for copy in copies:
                copy.wait()


def fold_rows(got_ref, width):
    total = jnp.sum(got_ref[...].astype(F32), 0)
    quarter = total.shape[0] // 4
    folded = jnp.concatenate([total[k * quarter : (k + 1) * quarter] for k in range(4)], 1)
    return jnp.concatenate([folded, jnp.zeros((32 - quarter, width), F32)], 0).astype(BF16)


def backward_kernel(
    proj_ref, stepw_ref, decay_ref, misc_ref, u_ref, gate_ref, outw_ref, gradmix_ref, step_ref,
    mixed_ref, scanw_ref, xin_ref, misc_x_ref, wx_ref, wg_ref, u_x_ref, tokens_ref, gains_ref,
    widths_ref,
    gradmid_hbm, gated_hbm, normed_hbm, hist_hbm, rows_0, grads_0, left_2, right_2, right_1,
    goal_l2, goal_r2, goal_r1,
    gradtok_hbm, totals_hbm, rows_1, grads_1, left_3, right_3, goal_l3, goal_r3, sends_hbm,
    c_cols, b_high, b_low, b_sums, c_sums, gy, du, grad_du, grad_step, ring, g_ring, w_ring,
    gradproj, gradu_all, gate_all, send_in, got_in, everyone, gated_all, send_scan, got_scan,
    pack_back, send_back, got_back, send_tail, got_tail, totals, raw, goal,
    g_send, g_recv, x_send, x_recv, l_send, l_recv, local_sems, ring_sems, load_sems,
):
    step = pl.program_id(0)
    devices, me = lax.axis_size("expert"), lax.axis_index("expert")
    half = devices // 2
    rank, state = stepw_ref.shape[0], decay_ref.shape[0]
    rows, cols = proj_ref.shape
    tile, small_tile, width = u_ref.shape[1], xin_ref.shape[1], tokens_ref.shape[1]
    blocks, big = rows // BLOCK, BLOCK * state
    turns = ring.shape[0]
    quarters = blocks // turns
    in_part = send_in.shape[0] // devices
    channels = half * in_part
    steps_x = channels // small_tile
    mix = PlaneGather(gradmix_ref, everyone, g_send, g_recv, local_sems.at[0])
    ways = [
        Exchange(source, target, x_send.at[k], x_recv.at[k], local_sems.at[k + 1])
        for k, (source, target) in enumerate(
            [
                (gated_hbm, gated_all), (send_scan, got_scan), (send_back, got_back),
                (send_tail, got_tail),
            ]
        )
    ]

    def input_part(device):
        return send_in.at[pl.ds(pl.multiple_of(device * in_part, in_part), in_part)]

    input_copies = [
        pltpu.make_async_remote_copy(
            input_part((me + k) % devices), got_in.at[me], x_send.at[4, k], x_recv.at[4, k],
            device_id={"expert": (me + k) % devices}, device_id_type=MESH,
        )
        for k in range(1, devices)
    ]
    input_local = pltpu.make_async_copy(input_part(me), got_in.at[me], local_sems.at[5])

    def start_inputs(first, last):
        for k, copy in enumerate(input_copies):
            peer = (me + k + 1) % devices
            pl.when((peer >= first) & (peer < last))(lambda copy=copy: copy.start())
        pl.when((me >= first) & (me < last))(lambda: input_local.start())

    lines = [
        Line(3, left_2, right_2, left_3, right_3, l_send.at[0], l_recv.at[0]),
        Line(3, goal_l2, goal_r2, goal_l3, goal_r3, l_send.at[1], l_recv.at[1]),
        Near(rows_0, rows_1, l_send.at[2], l_recv.at[2]),
        Near(grads_0, grads_1, l_send.at[3], l_recv.at[3]),
    ]
    load_normed = pltpu.make_async_copy(normed_hbm, everyone, load_sems.at[0])
    load_mid = pltpu.make_async_copy(gradmid_hbm, gy, load_sems.at[1])
    store_sends = [
        pltpu.make_async_copy(source, sends_hbm.at[k], load_sems.at[6 + k])
        for k, source in enumerate((g_ring, w_ring))
    ]
    x_spot = (jnp.maximum(step - 2, 0) % steps_x) // (steps_x // 2)
    x_lanes = pl.ds(
        pl.multiple_of((jnp.maximum(step - 2, 0) % (steps_x // 2)) * small_tile, small_tile),
        small_tile,
    )
    lanes = pl.ds(pl.multiple_of(jnp.minimum(step, 1) * tile, tile), tile)

    def load(spot, block):
        start = pl.multiple_of(block * big, big)
        return pltpu.make_async_copy(
            hist_hbm.at[pl.ds(start, big + state), lanes], ring.at[spot], ring_sems.at[spot]
        )

    @pl.when(step < 2)
    def _():
        for spot in range(turns - 1):
            load(spot, blocks - 1 - spot).start()

    @pl.when(step == 0)
    def _():
        greet()
        mix.step(0)
        for line in lines:
            line.start()
        gradproj[...] = jnp.zeros_like(gradproj)
        b_sums[...] = jnp.zeros_like(b_sums)
        c_sums[...] = jnp.zeros_like(c_sums)
        columns_of(proj_ref, rank + state, state, c_cols)
        diagonals_of(proj_ref, rank, state, b_high, b_low)

    def between(position):
        if position == 2:
            mix.step(1)
            mix.step(2)
            ways[0].start()
        if position == 5:
            mix.step(3)
        if position == 7:
            mix.step(4)
            ways[0].wait()

    @pl.when(step < 2)
    def _():
        skip_ref = scan_rows(misc_ref)[1]
        grad_gated = times_transpose(gradmix_ref[...], outw_ref[...])
        gate_in = gate_ref[...]
        gate_sig = sigmoid(gate_in)
        grad_mixed = grad_gated * (gate_in * gate_sig)
        grad_gate = (
            grad_gated * mixed_ref[...] * (gate_sig * (1.0 + gate_in * (1.0 - gate_sig)))
        ).astype(BF16)
        gate_all[:, lanes] = grad_gate
        start = pl.multiple_of(channels + step * tile, tile)
        send_in[pl.ds(start, tile), :] = grad_gate.T
        u_act = u_ref[...]
        step_size = step_ref[...]
        gy[...] = grad_mixed
        du[0:rows, :] = step_size * u_act
        du[rows:, :] = jnp.zeros((BLOCK, tile), F32)
        grad_skip = jnp.sum(grad_mixed * u_act, 0, keepdims=True)
        rate = decay_ref[...]
        decay = rate * LOG2E
        sums = (iota((BLOCK, big), 0) == iota((BLOCK, big), 1) // state).astype(BF16)
        g_ring[1] = jnp.zeros((big, tile), BF16)
        w_ring[1] = jnp.zeros((big, tile), BF16)

        def reduce_block(spot, block):
            grads = g_ring[spot]
            source = jnp.minimum(block, blocks - 1)
            high, low = block_of(b_high, source, BLOCK), block_of(b_low, source, BLOCK)
            both = product(jnp.concatenate([high, low], 0), grads)
            base = pl.ds(pl.multiple_of(block * BLOCK, BLOCK), BLOCK)
            grad_du[base, :] = both[:BLOCK] + both[BLOCK:]
            grad_step[base, :] = product(sums, w_ring[spot])
            b_sums[base, :] += times_transpose(du[base, :].astype(BF16), grads)

        def run_blocks(quarter, carry):
            carried, log_sum = carry
            for spot in range(turns):
                turn = quarter * turns + spot
                block = blocks - 1 - turn
                later = (spot + turns - 1) % turns
                if spot == 0:
                    load(later, block - turns + 1).start()
                else:
                    pl.when(quarter < quarters - 1)(
                        lambda: load(later, block - turns + 1).start()
                    )
                load(spot, block).wait()
                here, before = spot % 2, (spot + 1) % 2
                reduce_block(before, block + 1)
                base = pl.ds(pl.multiple_of(block * BLOCK, BLOCK), BLOCK)
                steps_now, gy_now = step_ref[base, :], gy[base, :]
                c_now = block_of(c_cols, block, state)
                c_sums[base, :] += times_transpose(gy_now.astype(BF16), ring[spot, state:, :])
                for t in range(BLOCK - 1, -1, -1):
                    at = slice(t * state, (t + 1) * state)
                    c_wide = jnp.broadcast_to(c_now[:, t : t + 1], (state, tile))
                    step_now = steps_now[t : t + 1, :]
                    fade = jnp.exp2(step_now * decay)
                    grad = gy_now[t : t + 1, :] * c_wide + carried
                    g_ring[here, at, :] = grad.astype(BF16)
                    carried = fade * grad
                    weighted = carried * ring[spot, at, :].astype(F32) * rate
                    w_ring[here, at, :] = weighted.astype(BF16)
                    log_sum = log_sum + weighted * step_now
            for turn in range(2):
                for part in range(quarters):

                    @pl.when((step == turn) & (quarter == part))
                    def _():
                        between(turn * 4 + part)

            return carried, log_sum

        zeros = jnp.zeros((state, tile), F32)
        _, log_sum = lax.fori_loop(0, quarters, run_blocks, (zeros, zeros))
        reduce_block(1, 0)
        full_du = grad_du[0:rows, :]
        gradu_all[:, lanes] = full_du * step_size + skip_ref[...] * gy[...]
        grad_size = grad_step[0:rows, :] + full_du * u_act
        grad_pre = grad_size * (1.0 - jnp.exp(-step_size))
        grad_low = grad_pre.astype(BF16)
        grad_step_w = contract_rows(proj_ref[:, :rank].astype(BF16), grad_low)
        packed = jnp.concatenate(
            [grad_step_w, log_sum, jnp.sum(grad_pre, 0, keepdims=True), grad_skip, zeros[:6]], 0
        ).astype(BF16)
        for turn in range(2):

            @pl.when(step == turn)
            def _():
                split_lanes(send_scan.at[pl.ds(turn * half, half)], packed)
                start_inputs(half + turn * half // 2, half + (turn + 1) * half // 2)

        gradproj[:, :rank] += times_transpose(grad_low, stepw_ref[...])

    @pl.when(step == 1)
    def _():
        ways[1].start()
        own = iota((rows, big), 0) % BLOCK == iota((rows, big), 1) // state
        lane = iota((big, cols), 1)
        slot = iota((big, cols), 0) % state
        total = gradproj[...]
        for sums_here, first in ((b_sums[0:rows, :], rank), (c_sums[...], rank + state)):
            place = (lane == first + slot).astype(F32)
            total = total + exact_product(jnp.where(own, sums_here, 0.0), place)
        gradproj[...] = total

    @pl.when(step == 2)
    def _():
        load_mid.start()
        grad_du[...] = jnp.zeros_like(grad_du)

    @pl.when(step == steps_x + 2)
    def _():
        split_lanes(send_back, pack_back[...])
        ways[2].start()
        lhs = jnp.concatenate([gated_all[k] for k in range(devices)], 1)
        totals[2 * gated_all.shape[1] : 3 * gated_all.shape[1], :] = product(
            lhs, everyone[...].reshape(devices * rows, width)
        ).astype(BF16)
        load_normed.start()

    here = pl.ds(
        pl.multiple_of((jnp.maximum(step - 2, 0) % steps_x) * small_tile, small_tile), small_tile
    )

    @pl.when((step >= 2) & (step < steps_x + 2))
    def _():
        conv_ref, bias_ref = conv_rows(misc_x_ref)
        grad_proj = gradproj[...].astype(BF16)
        grad_u = gradu_all[:, here] + times_transpose(grad_proj, scanw_ref[...])
        pieces = [contract_rows(grad_proj, u_x_ref[...].astype(BF16))]
        x_inner = xin_ref[...]
        taps = conv_ref.shape[0]
        shifted = [shift_rows(x_inner, taps - 1 - tap) for tap in range(taps)]
        summed = bias_ref[...]
        for tap in range(taps):
            summed = summed + conv_ref[tap : tap + 1, :] * shifted[tap]
        sig = sigmoid(summed)
        grad_sum = grad_u * (sig * (1.0 + summed * (1.0 - sig)))
        grad_x = jnp.zeros_like(x_inner)
        for tap in range(taps):
            pieces.append(jnp.sum(grad_sum * shifted[tap], 0, keepdims=True))
            grad_x = grad_x + conv_ref[tap : tap + 1, :] * shift_rows(grad_sum, tap + 1 - taps)
        pieces.append(jnp.sum(grad_sum, 0, keepdims=True))
        pieces.append(jnp.zeros((pack_back.shape[0] - cols - taps - 1, small_tile), F32))
        pack_back[:, here] = jnp.concatenate(pieces, 0).astype(BF16)
        grad_x = grad_x.astype(BF16)
        send_in[here, :] = grad_x.T
        ring[x_spot, 0:rows, x_lanes] = grad_x
        for part in range(half):
            done = -(-(part + 1) * in_part // small_tile) + 1
            pl.when(step == done)(lambda: start_inputs(part, part + 1))

    @pl.when(step >= steps_x + 2)
    def _():
        grad_du[0:rows, :] += product(ring[x_spot, 0:rows, x_lanes], wx_ref[...]) + product(
            gate_all[:, here], wg_ref[...]
        )

    @pl.when(step == steps_x + 3)
    def _():
        next_to = [(left_2, goal_l2), (right_2, goal_r2), (right_1, goal_r1)]
        pick(
            (next_to[1], next_to[2], next_to[2], next_to[0]), raw, goal, load_sems.at[pl.ds(4, 2)]
        )
        matrix = dispatch_matrix(goal, devices)
        for part, (target, store) in enumerate(zip((g_ring, w_ring), store_sends)):
            target[...] = product(matrix, raw[part]).astype(BF16).reshape(target.shape)
            store.start()

    @pl.when(step == 2 * steps_x + 1)
    def _():
        values = tokens_ref[...].astype(F32)
        scale = lax.rsqrt(jnp.mean(values * values, -1, keepdims=True) + 1e-05)
        unit = values * scale
        grad = grad_du[0:rows, :]
        widths = jnp.concatenate([widths_ref[...], jnp.sum(grad * unit, 0, keepdims=True)], 0)
        widths = jnp.concatenate(
            [widths, jnp.zeros((send_tail.shape[1] - widths.shape[0], width), F32)], 0
        )
        split_lanes(send_tail, widths.astype(BF16))
        ways[3].start()
        inner = grad * gains_ref[0:1, :]
        load_mid.wait()
        gy[...] += scale * (inner - unit * jnp.mean(inner * unit, -1, keepdims=True))
        store_tokens = pltpu.make_async_copy(gy, gradtok_hbm, load_sems.at[2])
        store_tokens.start()
        at = 3 * gated_all.shape[1]
        for way, got in ((ways[1], got_scan), (ways[2], got_back)):
            way.wait()
            totals[at : at + 32, :] = fold_rows(got, width)
            at += 32
        ways[3].wait()
        tail = jnp.sum(got_tail[...].astype(F32), 0)
        tail = jnp.concatenate([tail, jnp.zeros((tail.shape[0], width - tail.shape[1]), F32)], 1)
        totals[at : at + 16, :] = tail.astype(BF16)
        load_normed.wait()
        input_local.wait()
        for copy in input_copies:
            copy.wait()
        lhs = jnp.concatenate([got_in[k] for k in range(devices)], 1)
        totals[0:in_part, :] = product(
            lhs, everyone[...].reshape(devices * rows, width)
        ).astype(BF16)
        store_totals = pltpu.make_async_copy(totals, totals_hbm, load_sems.at[3])
        store_totals.start()
        for line in lines:
            line.wait()
        store_tokens.wait()
        store_totals.wait()
        for store in store_sends:
            store.wait()


def backward_plane(
    proj, step_w, vec, u_act, gate_in, out_w, grad_mix, step_size, mixed, scan_w, x_inner, in_t,
    tokens, gains, grad_widths, grad_mid, gated, normed_all, hist, rows_0, grads_0, raws, goals,
):
    rows, channels = u_act.shape
    width = grad_mix.shape[1]
    cols = proj.shape[1]
    rank, state = step_w.shape[0], vec.shape[0] - 8
    devices = lax.axis_size("expert")
    part = channels // devices
    tile, small = channels // 2, channels // 6
    big = BLOCK * state
    pack_rows, tail_rows = cols + 8, grad_widths.shape[0] + 7
    fixed = lambda i: (0, 0)
    first = lambda i: jnp.minimum(i, 1)
    second = lambda i: jnp.clip(i - 2, 0, 5)
    once = pl.Buffered(1)
    slots = jax.ShapeDtypeStruct(rows_0.shape, BF16)
    raw = jax.ShapeDtypeStruct(raws[0].shape, BF16)
    goal = jax.ShapeDtypeStruct(goals[0].shape, jnp.int32)
    total_rows = 3 * part + 80
    pair = jax.ShapeDtypeStruct((2, 2, big, tile), BF16)
    third = lambda i: jnp.maximum(i - 8, 0)
    packs = [
        pltpu.VMEM((devices, count, lanes), BF16)
        for count, lanes in (
            (rank + state + 8, part), (pack_rows, part), (tail_rows, width // devices)
        )
        for _ in range(2)
    ]
    return pl.pallas_call(
        backward_kernel,
        grid=(14,),
        in_specs=[
            pl.BlockSpec((rows, cols), fixed),
            pl.BlockSpec((rank, tile), lambda i: (0, first(i))),
            pl.BlockSpec((state, tile), lambda i: (0, first(i))),
            pl.BlockSpec((8, tile), lambda i: (state // 8, first(i))),
            pl.BlockSpec((rows, tile), lambda i: (0, first(i))),
            pl.BlockSpec((rows, tile), lambda i: (0, first(i))),
            pl.BlockSpec((tile, width), lambda i: (first(i), 0), pipeline_mode=once),
            pl.BlockSpec((rows, width), fixed, pipeline_mode=once),
            pl.BlockSpec((rows, tile), lambda i: (0, first(i))),
            pl.BlockSpec((rows, tile), lambda i: (0, first(i))),
            pl.BlockSpec((small, cols), lambda i: (second(i), 0)),
            pl.BlockSpec((rows, small), lambda i: (0, second(i))),
            pl.BlockSpec((8, small), lambda i: (state // 8, second(i))),
            pl.BlockSpec((small, width), lambda i: (third(i), 0)),
            pl.BlockSpec((small, width), lambda i: (third(i) + 6, 0)),
            pl.BlockSpec((rows, small), lambda i: (0, second(i))),
            pl.BlockSpec((rows, width), fixed, pipeline_mode=once),
            pl.BlockSpec(gains.shape, fixed),
            pl.BlockSpec(grad_widths.shape, fixed),
        ] + [FAR] * 12,
        out_specs=[FAR] * 9,
        out_shape=[
            jax.ShapeDtypeStruct((rows, width), F32),
            jax.ShapeDtypeStruct((total_rows, width), BF16),
            slots, slots, raw, raw, goal, goal, pair,
        ],
        scratch_shapes=[
            pltpu.VMEM((rows // BLOCK * state, 128), F32),
            pltpu.VMEM((rows, big), BF16),
            pltpu.VMEM((rows, big), BF16),
            pltpu.VMEM((rows + BLOCK, big), F32),
            pltpu.VMEM((rows, big), F32),
            pltpu.VMEM((rows, tile), F32),
            pltpu.VMEM((rows + BLOCK, tile), F32),
            pltpu.VMEM((rows + BLOCK, tile), F32),
            pltpu.VMEM((rows + BLOCK, tile), F32),
            pltpu.VMEM((4, big + state, tile), BF16),
            pltpu.VMEM((2, big, tile), BF16),
            pltpu.VMEM((2, big, tile), BF16),
            pltpu.VMEM((rows, cols), F32),
            pltpu.VMEM((rows, channels), F32),
            pltpu.VMEM((rows, channels), BF16),
            pltpu.VMEM((2 * channels, rows), BF16),
            pltpu.VMEM((devices, 2 * part, rows), BF16),
            pltpu.VMEM((devices, rows, width), BF16),
            pltpu.VMEM(gated.shape, BF16),
            packs[0],
            packs[1],
            pltpu.VMEM((pack_rows, channels), BF16),
            *packs[2:],
            pltpu.VMEM((total_rows, width), BF16),
            pltpu.VMEM(raw.shape, BF16),
            pltpu.VMEM(goal.shape, jnp.int32),
            DMA((10,)), DMA((10,)), DMA((5, devices)), DMA((5, devices)), DMA((4, 2)), DMA((4, 2)),
            DMA((6,)), DMA((4,)), DMA((8,)),
        ],
        compiler_params=pltpu.CompilerParams(
            vmem_limit_bytes=VMEM_LIMIT, collective_id=4, has_side_effects=True
        ),
        name="mixer_backward",
    )(
        proj, step_w, vec, vec, u_act, gate_in, out_w, grad_mix, step_size, mixed, scan_w, x_inner,
        vec, in_t, in_t, u_act, tokens, gains, grad_widths, grad_mid, gated, normed_all, hist,
        rows_0, grads_0, raws[2], raws[3], raws[1], goals[2], goals[3], goals[1],
    )


def add_groups(rows, grads, rows_t, up_ref, down_ref):
    activated, slope = gelu_parts(product(rows, up_ref[...]))
    grad_pre = (times_transpose(grads, down_ref[...]) * slope).astype(BF16)
    return product(rows_t, grad_pre), contract_rows(activated.astype(BF16), grads)


def flat_rows(refs):
    experts, cap, width = refs[0].shape
    values = [ref[...].reshape(ref.shape[0] * cap, width) for ref in refs]
    return values[0] if len(values) == 1 else jnp.concatenate(values, 0)


def two_grads_kernel(
    up_ref, down_ref, gup_in, gdown_in, rows_1, grads_1, sends_2, left_2, left_3, right_2, right_3,
    goal_l2, goal_l3, goal_r2, goal_r3,
    gup_ref, gdown_ref, rows_3, grads_3,
    rows_t, gup_all, gdown_all, rows_2, grads_2, raw, goal, sends_3,
    x_send, x_recv, local_sems, load_sems,
):
    step = pl.program_id(0)
    tiles = gup_all.shape[0]
    spot = step % tiles
    seconds, thirds = (
        [
            Exchange(
                source.at[k], out, x_send.at[first + k], x_recv.at[first + k],
                local_sems.at[first + k],
            )
            for k, out in enumerate(targets)
        ]
        for first, source, targets in (
            (0, sends_2, (rows_2, grads_2)), (2, sends_3, (rows_3, grads_3))
        )
    )

    @pl.when(step == 0)
    def _():
        greet(line=False)
        for way in seconds:
            way.start()
        rows_t[...] = flat_rows((rows_1,)).T

    @pl.when(step == 1)
    def _():
        pick(
            ((right_3, goal_r3), (right_2, goal_r2), (left_2, goal_l2), (left_3, goal_l3)), raw,
            goal, load_sems,
        )
        prepare_sends(raw, goal, sends_3)

    @pl.when(step == tiles - 2)
    def _():
        for way in thirds:
            way.start()

    @pl.when(step < tiles)
    def _():
        grad_up, grad_down = add_groups(
            flat_rows((rows_1,)), flat_rows((grads_1,)), rows_t[...], up_ref, down_ref
        )
        gup_all[spot] = (gup_in[...].astype(F32) + grad_up).astype(BF16)
        gdown_all[spot] = (gdown_in[...].astype(F32) + grad_down).astype(BF16)

    @pl.when(step == tiles)
    def _():
        for way in seconds:
            way.wait()
        rows_t[...] = flat_rows((rows_2,)).T

    @pl.when(step >= tiles)
    def _():
        grad_up, grad_down = add_groups(
            flat_rows((rows_2,)), flat_rows((grads_2,)), rows_t[...], up_ref, down_ref
        )
        gup_ref[...] = (gup_all[spot].astype(F32) + grad_up).astype(BF16)
        gdown_ref[...] = (gdown_all[spot].astype(F32) + grad_down).astype(BF16)

    @pl.when(step == 2 * tiles - 1)
    def _():
        for way in thirds:
            way.wait()


def last_grads_kernel(
    up_ref, down_ref, gup_in, gdown_in, rows_ref, grads_ref, gup_ref, gdown_ref, rows_t
):
    rows, grads = flat_rows((rows_ref,)), flat_rows((grads_ref,))

    @pl.when(pl.program_id(0) == 0)
    def _():
        rows_t[...] = rows.T

    grad_up, grad_down = add_groups(rows, grads, rows_t[...], up_ref, down_ref)
    gup_ref[...] = gup_in[...].astype(F32) + grad_up
    gdown_ref[...] = gdown_in[...].astype(F32) + grad_down


def expert_grads_plane(up, down, grad_up, grad_down, rows, grads, sends, raws, goals, tile):
    width, hidden = up.shape
    devices, cap = grads.shape[:2]
    slots = jax.ShapeDtypeStruct(grads.shape, BF16)
    pair = jax.ShapeDtypeStruct(sends.shape, BF16)
    whole = pl.BlockSpec(grads.shape, lambda i: (0, 0, 0))

    def tiles(size):
        return [
            pl.BlockSpec((width, size), lambda i: (0, i)),
            pl.BlockSpec((size, width), lambda i: (i, 0)),
        ]

    def shapes(kind):
        return [
            jax.ShapeDtypeStruct((width, hidden), kind), jax.ShapeDtypeStruct((hidden, width), kind)
        ]

    turned = pltpu.VMEM((width, devices * cap), BF16)
    count = hidden // tile
    again = [
        pl.BlockSpec((width, tile), lambda i: (0, i % count)),
        pl.BlockSpec((tile, width), lambda i: (i % count, 0)),
    ]
    early = [
        pl.BlockSpec((width, tile), lambda i: (0, jnp.minimum(i, count - 1))),
        pl.BlockSpec((tile, width), lambda i: (jnp.minimum(i, count - 1), 0)),
    ]
    late = [
        pl.BlockSpec((width, tile), lambda i: (0, jnp.maximum(i - count, 0))),
        pl.BlockSpec((tile, width), lambda i: (jnp.maximum(i - count, 0), 0)),
    ]
    grad_up, grad_down, rows, grads = pl.pallas_call(
        two_grads_kernel,
        grid=(2 * count,),
        in_specs=again + early + [whole] * 2 + [FAR] * 9,
        out_specs=late + [FAR] * 2,
        out_shape=shapes(BF16) + [slots] * 2,
        scratch_shapes=[
            turned,
            pltpu.VMEM((count, width, tile), BF16),
            pltpu.VMEM((count, tile, width), BF16),
            pltpu.VMEM(slots.shape, BF16),
            pltpu.VMEM(slots.shape, BF16),
            pltpu.VMEM(raws[0].shape, BF16),
            pltpu.VMEM(goals[0].shape, jnp.int32),
            pltpu.VMEM(pair.shape, BF16),
            DMA((4, devices)), DMA((4, devices)), DMA((4,)), DMA((2,)),
        ],
        compiler_params=remote_params(6),
        name="expert_grads_12",
    )(up, down, grad_up, grad_down, rows, grads, sends, *raws, *goals)
    return pl.pallas_call(
        last_grads_kernel,
        grid=(hidden // 768,),
        in_specs=tiles(768) * 2 + [whole] * 2,
        out_specs=tiles(768),
        out_shape=shapes(F32),
        scratch_shapes=[turned],
        compiler_params=pltpu.CompilerParams(vmem_limit_bytes=VMEM_LIMIT),
        name="expert_grads_3",
    )(up, down, grad_up, grad_down, rows, grads)


def finish_kernel(
    totals_ref, in_ref, out_ref, scanw_ref, stepw_ref, decay_ref, conv_ref, router_ref, bias_ref,
    dbias_ref, skip_ref, norm_two_ref, norm_ref,
):
    in_rows, part = in_ref.shape[0], out_ref.shape[0]
    cols, rank, state, taps = (
        scanw_ref.shape[1], stepw_ref.shape[0], decay_ref.shape[0], conv_ref.shape[0]
    )
    experts, slice_w = router_ref.shape
    in_ref[...] = totals_ref[0:in_rows, :].astype(F32)
    out_ref[...] = totals_ref[in_rows : in_rows + part, :].astype(F32)
    at = in_rows + part
    unfolded = []
    for quarter in ((rank + state + 8) // 4, (cols + 8) // 4):
        block = totals_ref[at : at + 32, :].astype(F32)[:quarter]
        unfolded.append(
            jnp.concatenate([block[:, k * part : (k + 1) * part] for k in range(4)], 0)
        )
        at += 32
    scan, back = unfolded
    stepw_ref[...] = scan[:rank]
    decay_ref[...] = scan[rank : rank + state]
    scanw_ref[...] = back[:cols].T
    conv_ref[...] = back[cols : cols + taps]
    bias_ref[...] = back[cols + taps]
    dbias_ref[...] = scan[rank + state]
    skip_ref[...] = scan[rank + state + 1]
    tail = totals_ref[at : at + 16, :].astype(F32)[:, :slice_w]
    router_ref[...] = tail[:experts]
    norm_two_ref[...] = tail[experts]
    norm_ref[...] = tail[experts + 1]


def finish(totals, in_rows, part, cols, rank, state, taps, experts, slice_w):
    here = pl.BlockSpec(memory_space=pltpu.VMEM)
    return pl.pallas_call(
        finish_kernel,
        in_specs=[here],
        out_specs=[here] * 12,
        out_shape=[
            jax.ShapeDtypeStruct(shape, F32)
            for shape in (
                (in_rows, totals.shape[1]), (part, totals.shape[1]), (part, cols), (rank, part),
                (state, part), (taps, part), (experts, slice_w), (part,), (part,), (part,),
                (slice_w,), (slice_w,),
            )
        ],
        compiler_params=pltpu.CompilerParams(vmem_limit_bytes=VMEM_LIMIT),
        name="finish",
    )(totals)


def gather(value):
    return lax.all_gather(value, "expert", axis=0, tiled=True)


def exchange(value):
    return lax.all_to_all(value, "expert", split_axis=0, concat_axis=0, tiled=True)


def shards(
    tokens, lengths, routes, slot_index, mixer_norm, in_weight, conv_weight, conv_bias,
    scan_weight, step_weight, step_bias, decay_log, skip_gain, out_weight, moe_norm, router_weight,
    up_weight, down_weight, cotangent,
):
    devices = lax.axis_size("expert")
    rows, width = tokens.shape[1:]
    part = out_weight.shape[0]
    channels = part * devices
    cols = scan_weight.shape[1]
    rank, state, taps = step_weight.shape[0], decay_log.shape[1], conv_weight.shape[0]
    experts = router_weight.shape[1]
    split = devices // experts
    slice_w = width // devices
    tile = channels // 2

    on_plane = devices == 8 and split == 1 and lax.axis_size("dp") == 4
    in_t, decay_t, router_t = in_weight.T, decay_log.T, router_weight.T
    up, down = up_weight[0], down_weight[0]
    hidden = up.shape[1]
    if on_plane:
        (
            normed_low, x_inner, u_act, gate_in, proj, step_size, mixed, gated, mid, step_full, vec,
            router_t, gains, scan_full, in_t, out_full, normed_all, hist,
        ) = forward_plane(
            tokens[0], in_t, scan_weight, step_weight, decay_t, conv_weight, conv_bias, step_bias,
            skip_gain, mixer_norm, moe_norm, router_t, out_weight,
        )
        in_t = in_t.reshape(2 * channels, width)
        scan_full = scan_full.reshape(channels, cols)
        out_full = out_full.reshape(channels, width)
        layer_out, grad_mid, grad_mix, grad_widths, rows_0, grads_0, *line = expert_layer(
            lengths, mid, gains, router_t, routes, slot_index, cotangent[0], up, down
        )
        raws, goals, grad_up, grad_down = line[:4], line[4:8], line[8], line[9]
        (
            tokens_grad, totals, rows_1, grads_1, left_3, right_3, goal_l3, goal_r3, sends
        ) = backward_plane(
            proj, step_full, vec, u_act, gate_in, out_full, grad_mix, step_size, mixed, scan_full,
            x_inner, in_t, tokens[0], gains, grad_widths, grad_mid, gated, normed_all, hist, rows_0,
            grads_0, raws, goals,
        )
        totals = lax.psum(totals, "dp")
        grad_up, grad_down = expert_grads_plane(
            up, down, grad_up, grad_down, rows_1, grads_1,
            sends.reshape((2,) + rows_1.shape), (raws[2], left_3, raws[3], right_3), (goals[2], goal_l3, goals[3], goal_r3), 512,
        )
        in_total, out_total, scan_w_total, step_w_total, decay_total, conv_total, *rest = finish(
            totals, 2 * part, part, cols, rank, state, taps, experts, slice_w
        )
        router_total, vector_totals, norm_totals = rest[0], rest[1:4], rest[4:]
    else:
        vectors = jnp.stack([conv_bias, step_bias, skip_gain])
        norms = jnp.stack([mixer_norm, moe_norm])
        spare = jnp.zeros((8 - taps - 3, part), BF16)
        columns = jnp.concatenate([step_weight, decay_t, conv_weight, vectors, spare], 0)
        across = jnp.concatenate([router_t, norms, jnp.zeros((6, slice_w), BF16)], 0)
        in_t, scan_full, columns, across = (
            lax.all_gather(value, "expert") for value in (in_t, scan_weight, columns, across)
        )
        columns = columns.transpose(1, 0, 2).reshape(columns.shape[1], channels)
        across = across.transpose(1, 0, 2).reshape(across.shape[1], width)
        step_full, rest = columns[:rank], columns[rank:].astype(F32)
        vec = jnp.concatenate([-jnp.exp(rest[:state]), rest[state:]], 0)
        router_t, gains = across[:experts], across[experts:].astype(F32)
        in_t = in_t.reshape(2 * channels, width)
        scan_full = scan_full.reshape(channels, cols)
        normed_low, x_inner, u_act, gate_in, proj = front(
            tokens[0], gains, in_t, vec, scan_full, tile
        )
        live = (jnp.arange(rows, dtype=jnp.int32) < lengths[0]).astype(F32)[:, None]
        routes_col, slots_col = routes[0][:, None], slot_index[0][:, None]
        router, gain_second = router_t.T, gains[1:2]
        out_full = gather(out_weight)
        step_size, mixed, gated, hist, mid = scan_forward(
            proj, step_full, vec, u_act, gate_in, out_full, tokens[0], tile
        )
        send_rows, send_grads, normed_two, probs = router_step(
            mid, gain_second, router, routes_col, routes, slot_index, live, cotangent[0]
        )

        def to_pieces(value):
            wide = jnp.broadcast_to(value[:, None], (experts, split) + value.shape[1:])
            return exchange(wide.reshape(devices, CAP, width))

        def from_pieces(value):
            value = exchange(value).reshape(experts, split, CAP, width)
            if split == 1:
                return value[:, 0]
            return jnp.sum(value.astype(F32), 1).astype(BF16)

        some = min(512, hidden // 3)
        rows_in = to_pieces(send_rows)
        grads_in = to_pieces(send_grads)
        partial_out, slope = expert_out(rows_in, up, down, some)
        back_rows = from_pieces(partial_out)
        back_grads = from_pieces(expert_back(grads_in, up, down, slope, some))
        all_rows = lax.all_gather(rows_in, "dp")
        layer_out, grad_mid, grad_mix, grad_widths = combine_step(
            mid, gain_second, router, routes_col, slots_col, live, cotangent[0], probs, normed_two,
            back_rows, back_grads,
        )
        grad_mix, all_rows = lax.optimization_barrier((grad_mix, all_rows))
        all_grads = lax.all_gather(grads_in, "dp")
        out_parts = contract_rows(gated, grad_mix).astype(BF16).reshape(devices, part, width)
        grad_out_w = jnp.sum(exchange(out_parts).astype(F32), 0).astype(BF16)
        grad_u, grad_gate, scan_parts, grad_proj = scan_backward(
            proj, step_full, vec, u_act, gate_in, out_full, grad_mix, step_size, mixed, hist, tile,
            devices,
        )
        scan_small = jnp.sum(exchange(scan_parts).astype(F32), 0).astype(BF16)
        grad_x, back_parts, width_parts, tokens_grad = mixer_back(
            grad_proj, scan_full, grad_u, x_inner, vec, grad_gate, in_t, u_act, tokens[0], gains,
            grad_mid, grad_widths, tile, devices,
        )
        back_small = jnp.sum(exchange(back_parts).astype(F32), 0).astype(BF16)
        width_small = jnp.sum(exchange(width_parts).astype(F32), 0).astype(BF16)
        normed_all = gather(normed_low)
        grad_in_parts = exchange(jnp.concatenate([grad_x, grad_gate], 0))
        grad_in_w = contract_rows(
            grad_in_parts.reshape(devices * rows, 2 * part), normed_all
        ).astype(BF16)
        totals = (grad_in_w, grad_out_w, scan_small, back_small, width_small)
        totals, all_grads = lax.optimization_barrier((totals, all_grads))
        totals = lax.psum(totals, "dp")
        in_total, out_total, scan_small, back_small, width_small = (
            t.astype(F32) for t in totals
        )
        grad_up, grad_down = expert_grads(all_rows, all_grads, up, down, min(256, hidden))
        scan_w_total, conv_total = back_small[:cols].T, back_small[cols : cols + taps]
        step_w_total, decay_total = scan_small[:rank], scan_small[rank : rank + state]
        vector_totals = (
            back_small[cols + taps], scan_small[rank + state], scan_small[rank + state + 1]
        )
        router_total = width_small[:experts]
        norm_totals = (width_small[experts], width_small[experts + 1])
    return (
        layer_out[None],
        tokens_grad[None],
        norm_totals[1],
        in_total.T,
        conv_total,
        vector_totals[0],
        scan_w_total,
        step_w_total,
        vector_totals[1],
        decay_total.T,
        vector_totals[2],
        out_total,
        norm_totals[0],
        router_total.T,
        grad_up[None],
        grad_down[None],
    )


def solution(mesh):
    in_specs = (
        P(("dp", "expert"), None, None),
        P(("dp", "expert")),
        P(("dp", "expert"), None),
        P(("dp", "expert"), None),
        P("expert"),
        P(None, "expert"),
        P(None, "expert"),
        P("expert"),
        P("expert", None),
        P(None, "expert"),
        P("expert"),
        P("expert", None),
        P("expert"),
        P("expert", None),
        P("expert"),
        P("expert", None),
        P("expert", None, None),
        P("expert", None, None),
        P(("dp", "expert"), None, None),
    )
    out_specs = (
        P(("dp", "expert"), None, None),
        P(("dp", "expert"), None, None),
        P("expert"),
        P(None, "expert"),
        P(None, "expert"),
        P("expert"),
        P("expert", None),
        P(None, "expert"),
        P("expert"),
        P("expert", None),
        P("expert"),
        P("expert", None),
        P("expert"),
        P("expert", None),
        P("expert", None, None),
        P("expert", None, None),
    )
    return jax.shard_map(shards, mesh=mesh, in_specs=in_specs, out_specs=out_specs, check_vma=False)
```

```python
from functools import partial

import jax
import jax.numpy as jnp
from jax import lax
from jax.experimental import pallas as pl
from jax.experimental.pallas import tpu as pltpu
from jax.sharding import PartitionSpec as P

CAP = 64
BLOCK = 16
LOG2E = 1.4426950408889634
F32 = jnp.float32
BF16 = jnp.bfloat16
VMEM_LIMIT = 56 * 1024 * 1024


def product(left, right):
    return jnp.dot(left, right, preferred_element_type=F32)


def contract_rows(left, right):
    return lax.dot_general(left, right, (((0,), (0,)), ((), ())), preferred_element_type=F32)


def times_transpose(left, right):
    return lax.dot_general(left, right, (((1,), (1,)), ((), ())), preferred_element_type=F32)


def exact_product(left, right):
    return jnp.dot(left, right, preferred_element_type=F32, precision=lax.Precision.HIGHEST)


def iota(shape, axis):
    return lax.broadcasted_iota(jnp.int32, shape, axis)


def sigmoid(values):
    return 1.0 / (1.0 + jnp.exp(-values))


def softplus(values):
    return jnp.maximum(values, 0.0) + jnp.log1p(jnp.exp(-jnp.abs(values)))


class Rows:
    def __init__(self, ref, first, count):
        self.ref, self.first = ref, first
        self.shape = (count, ref.shape[1])

    def __getitem__(self, index):
        low, high = (0, self.shape[0]) if index is Ellipsis else (index[0].start, index[0].stop)
        return self.ref[self.first + low : self.first + high, :]


def conv_rows(misc_ref):
    return Rows(misc_ref, 0, 4), Rows(misc_ref, 4, 1)


def scan_rows(misc_ref):
    return Rows(misc_ref, 5, 1), Rows(misc_ref, 6, 1)


def split_lanes(out_ref, value):
    parts, _, width = out_ref.shape
    for part in range(parts):
        out_ref[part] = value[:, part * width : (part + 1) * width]


def shift_rows(values, offset):
    rows = values.shape[0]
    if offset == 0:
        return values
    rolled = pltpu.roll(values, offset % rows, 0)
    row = iota(values.shape, 0)
    keep = row >= offset if offset > 0 else row < rows + offset
    return jnp.where(keep, rolled, 0.0)


def two_parts(values):
    high = values.astype(BF16)
    low = (values - high.astype(F32)).astype(BF16)
    return high, low


def spread_rows(proj_block, first, state):
    rows, width = proj_block.shape
    big = rows * state
    pick = (iota((big, rows), 0) // state == iota((big, rows), 1)).astype(F32)
    copied = exact_product(pick, proj_block)
    lane = iota((big, width), 1)
    own = lane == first + iota((big, width), 0) % state
    column = jnp.sum(jnp.where(own, copied, 0.0), axis=1, keepdims=True)
    return jnp.broadcast_to(column, (big, 128))


def diagonal_blocks(proj_block, first, state):
    rows, width = proj_block.shape
    big = rows * state
    place = (iota((width, big), 0) == first + iota((width, big), 1) % state).astype(BF16)
    own = iota((rows, big), 0) == iota((rows, big), 1) // state
    parts = [
        jnp.where(own, product(part, place), 0.0).astype(BF16) for part in two_parts(proj_block)
    ]
    return jnp.concatenate(parts, 0)


def front_kernel(
    tokens_ref, gain_ref, wx_ref, wg_ref, misc_ref, scanw_ref,
    normed_ref, xin_ref, u_ref, gate_ref, proj_ref,
):
    step = pl.program_id(0)
    conv_ref, bias_ref = conv_rows(misc_ref)

    @pl.when(step == 0)
    def _():
        values = tokens_ref[...].astype(F32)
        scale = lax.rsqrt(jnp.mean(values * values, -1, keepdims=True) + 1e-05)
        normed_ref[...] = (values * scale * gain_ref[0:1, :]).astype(BF16)
        proj_ref[...] = jnp.zeros_like(proj_ref)

    normed = normed_ref[...]
    x_inner = times_transpose(normed, wx_ref[...])
    gate_ref[...] = times_transpose(normed, wg_ref[...])
    xin_ref[...] = x_inner
    taps = conv_ref.shape[0]
    summed = bias_ref[...] + conv_ref[taps - 1 : taps, :] * x_inner
    for back in range(1, taps):
        tap = taps - 1 - back
        summed = summed + conv_ref[tap : tap + 1, :] * shift_rows(x_inner, back)
    u_act = summed * sigmoid(summed)
    u_ref[...] = u_act
    proj_ref[...] += product(u_act.astype(BF16), scanw_ref[...])


def front(tokens, gains, in_t, vec, scan_w, tile):
    rows, width = tokens.shape
    channels = scan_w.shape[0]
    cols = scan_w.shape[1]
    steps = channels // tile
    return pl.pallas_call(
        front_kernel,
        grid=(steps,),
        in_specs=[
            pl.BlockSpec((rows, width), lambda i: (0, 0)),
            pl.BlockSpec(gains.shape, lambda i: (0, 0)),
            pl.BlockSpec((tile, width), lambda i: (i, 0)),
            pl.BlockSpec((tile, width), lambda i: (i + steps, 0)),
            pl.BlockSpec((8, tile), lambda i: ((vec.shape[0] - 8) // 8, i)),
            pl.BlockSpec((tile, cols), lambda i: (i, 0)),
        ],
        out_specs=[
            pl.BlockSpec((rows, width), lambda i: (0, 0)),
            pl.BlockSpec((rows, tile), lambda i: (0, i)),
            pl.BlockSpec((rows, tile), lambda i: (0, i)),
            pl.BlockSpec((rows, tile), lambda i: (0, i)),
            pl.BlockSpec((rows, cols), lambda i: (0, 0)),
        ],
        out_shape=[
            jax.ShapeDtypeStruct((rows, width), BF16),
            jax.ShapeDtypeStruct((rows, channels), F32),
            jax.ShapeDtypeStruct((rows, channels), F32),
            jax.ShapeDtypeStruct((rows, channels), F32),
            jax.ShapeDtypeStruct((rows, cols), F32),
        ],
        compiler_params=pltpu.CompilerParams(vmem_limit_bytes=VMEM_LIMIT),
        name="mixer_front",
    )(tokens, gains, in_t, in_t, vec, scan_w)


def scan_prepare(proj_ref, b_wide, c_blocks, b_first, c_first, state):
    blocks = proj_ref.shape[0] // BLOCK
    big = BLOCK * state

    def build(block, carry):
        part = proj_ref[pl.ds(pl.multiple_of(block * BLOCK, BLOCK), BLOCK), :]
        b_wide[pl.ds(pl.multiple_of(block * big, big), big), :] = spread_rows(part, b_first, state)
        c_blocks[pl.ds(pl.multiple_of(block * 2 * BLOCK, 2 * BLOCK), 2 * BLOCK), :] = (
            diagonal_blocks(part, c_first, state)
        )
        return carry

    lax.fori_loop(0, blocks, build, 0)


def scan_tile(
    proj_ref, stepw_ref, decay_ref, misc_ref, u_ref, gate_ref, step_ref, mixed_ref, hist_ref,
    b_wide, c_blocks, du, scanned, between,
):
    rank, state = stepw_ref.shape[0], decay_ref.shape[0]
    rows, tile = u_ref.shape
    blocks = rows // BLOCK
    big = BLOCK * state
    dbias_ref, skip_ref = scan_rows(misc_ref)
    u_act = u_ref[...]
    step_size = softplus(
        product(proj_ref[:, :rank].astype(BF16), stepw_ref[...]) + dbias_ref[...]
    )
    step_ref[...] = step_size
    du[...] = step_size * u_act
    decay = decay_ref[...] * LOG2E
    hist_ref[0:state, :] = jnp.zeros((state, tile), BF16)

    def run_block(block, held):
        base = pl.multiple_of(block * BLOCK, BLOCK)
        steps_now = step_ref[pl.ds(base, BLOCK), :]
        du_now = du[pl.ds(base, BLOCK), :]
        wide_base = pl.multiple_of(block * big, big)
        for t in range(BLOCK):
            b_now = b_wide[pl.ds(wide_base + t * state, state), :]
            fade = jnp.exp2(steps_now[t : t + 1, :] * decay)
            fresh = du_now[t : t + 1, :] * jnp.concatenate([b_now] * (tile // 128), 1)
            held = fade * held + fresh
            hist_ref[pl.ds(wide_base + (t + 1) * state, state), :] = held.astype(BF16)
        weights = c_blocks[pl.ds(pl.multiple_of(block * 2 * BLOCK, 2 * BLOCK), 2 * BLOCK), :]
        both = product(weights, hist_ref[pl.ds(wide_base + state, big), :])
        scanned[pl.ds(base, BLOCK), :] = both[:BLOCK] + both[BLOCK:]
        return held

    held = jnp.zeros((state, tile), F32)
    held = lax.fori_loop(0, blocks // 2, run_block, held)
    between(0)
    lax.fori_loop(blocks // 2, blocks, run_block, held)
    between(1)
    mixed = scanned[...] + skip_ref[...] * u_act
    mixed_ref[...] = mixed
    gate_in = gate_ref[...]
    return (mixed * (gate_in * sigmoid(gate_in))).astype(BF16)


def scan_kernel(
    proj_ref, stepw_ref, decay_ref, misc_ref, u_ref, gate_ref, outw_ref, tokens_ref,
    step_ref, mixed_ref, gated_ref, hist_ref, mid_ref,
    b_wide, c_blocks, du, scanned,
):
    rank, state = stepw_ref.shape[0], decay_ref.shape[0]

    @pl.when(pl.program_id(0) == 0)
    def _():
        mid_ref[...] = tokens_ref[...].astype(F32)
        scan_prepare(proj_ref, b_wide, c_blocks, rank, rank + state, state)

    gated = scan_tile(
        proj_ref, stepw_ref, decay_ref, misc_ref, u_ref, gate_ref, step_ref, mixed_ref, hist_ref,
        b_wide, c_blocks, du, scanned, lambda half: None,
    )
    gated_ref[...] = gated
    mid_ref[...] += product(gated, outw_ref[...])


def scan_forward(proj, step_w, vec, u_act, gate_in, out_w, tokens, tile):
    rows, channels = u_act.shape
    width = tokens.shape[1]
    cols = proj.shape[1]
    rank, state = step_w.shape[0], vec.shape[0] - 8
    steps = channels // tile
    hist_rows = (rows + 1) * state
    column = lambda i: (0, i)
    fixed = lambda i: (0, 0)
    return pl.pallas_call(
        scan_kernel,
        grid=(steps,),
        in_specs=[
            pl.BlockSpec((rows, cols), fixed),
            pl.BlockSpec((rank, tile), column),
            pl.BlockSpec((state, tile), column),
            pl.BlockSpec((8, tile), lambda i: ((vec.shape[0] - 8) // 8, i)),
            pl.BlockSpec((rows, tile), column),
            pl.BlockSpec((rows, tile), column),
            pl.BlockSpec((tile, width), lambda i: (i, 0)),
            pl.BlockSpec((rows, width), fixed),
        ],
        out_specs=[
            pl.BlockSpec((rows, tile), column),
            pl.BlockSpec((rows, tile), column),
            pl.BlockSpec((rows, tile), column),
            pl.BlockSpec((hist_rows, tile), column),
            pl.BlockSpec((rows, width), fixed),
        ],
        out_shape=[
            jax.ShapeDtypeStruct((rows, channels), F32),
            jax.ShapeDtypeStruct((rows, channels), F32),
            jax.ShapeDtypeStruct((rows, channels), BF16),
            jax.ShapeDtypeStruct((hist_rows, channels), BF16),
            jax.ShapeDtypeStruct((rows, width), F32),
        ],
        scratch_shapes=[
            pltpu.VMEM((rows * state, 128), F32),
            pltpu.VMEM((rows * 2, BLOCK * state), BF16),
            pltpu.VMEM((rows, tile), F32),
            pltpu.VMEM((rows, tile), F32),
        ],
        compiler_params=pltpu.CompilerParams(vmem_limit_bytes=VMEM_LIMIT),
        name="scan_forward",
    )(proj, step_w, vec, vec, u_act, gate_in, out_w, tokens)


def scan_back_kernel(*refs):
    scan_back_tile(lambda half: None, split_lanes, *refs)


def scan_back_tile(
    between, put_gate, proj_ref, stepw_ref, decay_ref, misc_ref, u_ref, gate_ref, outw_ref, gradmix_ref,
    step_ref, mixed_ref, hist_ref,
    gradu_ref, gradgate_ref, pack_ref, gradproj_ref,
    c_wide, b_blocks, b_sums, c_sums, gy, du, g_hist, w_hist, grad_du, grad_step,
):
    tile_id = pl.program_id(0)
    cols, rank = proj_ref.shape[1], stepw_ref.shape[0]
    state = decay_ref.shape[0]
    rows, tile = u_ref.shape
    blocks = rows // BLOCK
    big = BLOCK * state

    @pl.when(tile_id == 0)
    def _():
        gradproj_ref[...] = jnp.zeros_like(gradproj_ref)
        b_sums[...] = jnp.zeros_like(b_sums)
        c_sums[...] = jnp.zeros_like(c_sums)
        scan_prepare(proj_ref, c_wide, b_blocks, rank + state, rank, state)

    skip_ref = scan_rows(misc_ref)[1]
    grad_gated = times_transpose(gradmix_ref[...], outw_ref[...])
    gate_in = gate_ref[...]
    gate_sig = sigmoid(gate_in)
    grad_mixed = grad_gated * (gate_in * gate_sig)
    put_gate(
        gradgate_ref,
        (grad_gated * mixed_ref[...] * (gate_sig * (1.0 + gate_in * (1.0 - gate_sig)))).astype(BF16),
    )
    u_act = u_ref[...]
    step_size = step_ref[...]
    gy[...] = grad_mixed
    du[...] = step_size * u_act
    grad_skip = jnp.sum(grad_mixed * u_act, 0, keepdims=True)
    rate = decay_ref[...]
    decay = rate * LOG2E
    sums = (iota((BLOCK, big), 0) == iota((BLOCK, big), 1) // state).astype(BF16)

    def run_block(turn, carry):
        carried, log_sum = carry
        block = blocks - 1 - turn
        base = pl.multiple_of(block * BLOCK, BLOCK)
        wide_base = pl.multiple_of(block * big, big)
        steps_now = step_ref[pl.ds(base, BLOCK), :]
        gy_now = gy[pl.ds(base, BLOCK), :]
        for t in range(BLOCK - 1, -1, -1):
            c_now = c_wide[pl.ds(wide_base + t * state, state), :]
            step_now = steps_now[t : t + 1, :]
            fade = jnp.exp2(step_now * decay)
            grad = gy_now[t : t + 1, :] * jnp.concatenate([c_now] * (tile // 128), 1) + carried
            g_hist[t * state : (t + 1) * state, :] = grad.astype(BF16)
            carried = fade * grad
            before = hist_ref[pl.ds(wide_base + t * state, state), :].astype(F32)
            weighted = carried * before * rate
            w_hist[t * state : (t + 1) * state, :] = weighted.astype(BF16)
            log_sum = log_sum + weighted * step_now
        grads = g_hist[...]
        both = product(
            b_blocks[pl.ds(pl.multiple_of(block * 2 * BLOCK, 2 * BLOCK), 2 * BLOCK), :], grads
        )
        grad_du[pl.ds(base, BLOCK), :] = both[:BLOCK] + both[BLOCK:]
        grad_step[pl.ds(base, BLOCK), :] = product(sums, w_hist[...])
        b_sums[pl.ds(base, BLOCK), :] += times_transpose(
            du[pl.ds(base, BLOCK), :].astype(BF16), grads
        )
        c_sums[pl.ds(base, BLOCK), :] += times_transpose(
            gy_now.astype(BF16), hist_ref[pl.ds(wide_base + state, big), :]
        )
        return carried, log_sum

    zeros = jnp.zeros((state, tile), F32)
    held = lax.fori_loop(0, blocks // 2, run_block, (zeros, zeros))
    between(0)
    _, log_sum = lax.fori_loop(blocks // 2, blocks, run_block, held)
    between(1)
    full_du = grad_du[...]
    gradu_ref[...] = full_du * step_size + skip_ref[...] * gy[...]
    grad_size = grad_step[...] + full_du * u_act
    grad_pre = grad_size * (1.0 - jnp.exp(-step_size))
    grad_low = grad_pre.astype(BF16)
    grad_step_w = contract_rows(proj_ref[:, :rank].astype(BF16), grad_low)
    packed = jnp.concatenate(
        [grad_step_w, log_sum, jnp.sum(grad_pre, 0, keepdims=True), grad_skip, zeros[:6]], 0
    )
    split_lanes(pack_ref, packed.astype(BF16))
    gradproj_ref[:, :rank] += times_transpose(grad_low, stepw_ref[...])

    @pl.when(tile_id == pl.num_programs(0) - 1)
    def _():
        own = iota((rows, big), 0) % BLOCK == iota((rows, big), 1) // state
        lane = iota((big, cols), 1)
        slot = iota((big, cols), 0) % state
        total = gradproj_ref[...]
        for sums_ref, first in ((b_sums, rank), (c_sums, rank + state)):
            place = (lane == first + slot).astype(F32)
            total = total + exact_product(jnp.where(own, sums_ref[...], 0.0), place)
        gradproj_ref[...] = total


def scan_backward(
    proj, step_w, vec, u_act, gate_in, out_w, grad_mix, step_size, mixed, hist, tile, devices
):
    rows, channels = u_act.shape
    gate_parts = tile * devices // (2 * channels)
    pack_parts = tile * devices // channels
    pack_rows = step_w.shape[0] + vec.shape[0]
    width = grad_mix.shape[1]
    cols = proj.shape[1]
    rank, state = step_w.shape[0], vec.shape[0] - 8
    steps = channels // tile
    big = BLOCK * state
    column = lambda i: (0, i)
    fixed = lambda i: (0, 0)
    return pl.pallas_call(
        scan_back_kernel,
        grid=(steps,),
        in_specs=[
            pl.BlockSpec((rows, cols), fixed),
            pl.BlockSpec((rank, tile), column),
            pl.BlockSpec((state, tile), column),
            pl.BlockSpec((8, tile), lambda i: ((vec.shape[0] - 8) // 8, i)),
            pl.BlockSpec((rows, tile), column),
            pl.BlockSpec((rows, tile), column),
            pl.BlockSpec((tile, width), lambda i: (i, 0)),
            pl.BlockSpec((rows, width), fixed),
            pl.BlockSpec((rows, tile), column),
            pl.BlockSpec((rows, tile), column),
            pl.BlockSpec((hist.shape[0], tile), column),
        ],
        out_specs=[
            pl.BlockSpec((rows, tile), column),
            pl.BlockSpec((gate_parts, rows, tile // gate_parts), lambda i: (i, 0, 0)),
            pl.BlockSpec((pack_parts, pack_rows, tile // pack_parts), lambda i: (i, 0, 0)),
            pl.BlockSpec((rows, cols), fixed),
        ],
        out_shape=[
            jax.ShapeDtypeStruct((rows, channels), F32),
            jax.ShapeDtypeStruct((devices // 2, rows, 2 * channels // devices), BF16),
            jax.ShapeDtypeStruct((devices, pack_rows, channels // devices), BF16),
            jax.ShapeDtypeStruct((rows, cols), F32),
        ],
        scratch_shapes=[
            pltpu.VMEM((rows * state, 128), F32),
            pltpu.VMEM((rows * 2, big), BF16),
            pltpu.VMEM((rows, big), F32),
            pltpu.VMEM((rows, big), F32),
            pltpu.VMEM((rows, tile), F32),
            pltpu.VMEM((rows, tile), F32),
            pltpu.VMEM((big, tile), BF16),
            pltpu.VMEM((big, tile), BF16),
            pltpu.VMEM((rows, tile), F32),
            pltpu.VMEM((rows, tile), F32),
        ],
        compiler_params=pltpu.CompilerParams(vmem_limit_bytes=VMEM_LIMIT),
        name="scan_backward",
    )(proj, step_w, vec, vec, u_act, gate_in, out_w, grad_mix, step_size, mixed, hist)


def back_kernel(
    gradproj_ref, scanw_ref, gradu_ref, xin_ref, misc_ref, gradgate_ref, wx_ref, wg_ref,
    u_ref, tokens_ref, gain_ref, gradmid_ref, widths_ref,
    gradx_ref, pack_ref, tail_ref, gradtok_ref,
    total,
):
    tile_id = pl.program_id(0)

    @pl.when(tile_id == 0)
    def _():
        total[...] = jnp.zeros_like(total)

    conv_ref, bias_ref = conv_rows(misc_ref)
    grad_proj = gradproj_ref[...].astype(BF16)
    grad_u = gradu_ref[...] + times_transpose(grad_proj, scanw_ref[...])
    pieces = [contract_rows(grad_proj, u_ref[...].astype(BF16))]
    x_inner = xin_ref[...]
    taps = conv_ref.shape[0]
    shifted = [shift_rows(x_inner, taps - 1 - tap) for tap in range(taps)]
    summed = bias_ref[...]
    for tap in range(taps):
        summed = summed + conv_ref[tap : tap + 1, :] * shifted[tap]
    sig = sigmoid(summed)
    grad_sum = grad_u * (sig * (1.0 + summed * (1.0 - sig)))
    grad_x = jnp.zeros_like(x_inner)
    for tap in range(taps):
        pieces.append(jnp.sum(grad_sum * shifted[tap], 0, keepdims=True))
        grad_x = grad_x + conv_ref[tap : tap + 1, :] * shift_rows(grad_sum, tap + 1 - taps)
    pieces.append(jnp.sum(grad_sum, 0, keepdims=True))
    pieces.append(jnp.zeros((pack_ref.shape[1] - grad_proj.shape[1] - taps - 1, x_inner.shape[1]), F32))
    split_lanes(pack_ref, jnp.concatenate(pieces, 0).astype(BF16))
    grad_x = grad_x.astype(BF16)
    split_lanes(gradx_ref, grad_x)
    grad_gate = jnp.concatenate([gradgate_ref[k] for k in range(gradgate_ref.shape[0])], 1)
    total[...] += product(grad_x, wx_ref[...]) + product(grad_gate, wg_ref[...])

    @pl.when(tile_id == pl.num_programs(0) - 1)
    def _():
        values = tokens_ref[...].astype(F32)
        scale = lax.rsqrt(jnp.mean(values * values, -1, keepdims=True) + 1e-05)
        unit = values * scale
        grad = total[...]
        widths = jnp.concatenate([widths_ref[...], jnp.sum(grad * unit, 0, keepdims=True)], 0)
        widths = jnp.concatenate(
            [widths, jnp.zeros((tail_ref.shape[1] - widths.shape[0], widths.shape[1]), F32)], 0
        )
        split_lanes(tail_ref, widths.astype(BF16))
        inner = grad * gain_ref[0:1, :]
        gradtok_ref[...] = gradmid_ref[...] + scale * (
            inner - unit * jnp.mean(inner * unit, -1, keepdims=True)
        )


def mixer_back(
    grad_proj, scan_w, grad_u, x_inner, vec, grad_gate, in_t, u_act, tokens, gains, grad_mid,
    grad_widths, tile, devices,
):
    rows, channels = u_act.shape
    gate_parts = tile * devices // (2 * channels)
    pack_parts = tile * devices // channels
    pack_rows = scan_w.shape[1] + 8
    tail_rows = grad_widths.shape[0] + 7
    width = tokens.shape[1]
    cols = scan_w.shape[1]
    steps = channels // tile
    column = lambda i: (0, i)
    fixed = lambda i: (0, 0)
    return pl.pallas_call(
        back_kernel,
        grid=(steps,),
        in_specs=[
            pl.BlockSpec((rows, cols), fixed),
            pl.BlockSpec((tile, cols), lambda i: (i, 0)),
            pl.BlockSpec((rows, tile), column),
            pl.BlockSpec((rows, tile), column),
            pl.BlockSpec((8, tile), lambda i: ((vec.shape[0] - 8) // 8, i)),
            pl.BlockSpec((gate_parts, rows, tile // gate_parts), lambda i: (i, 0, 0)),
            pl.BlockSpec((tile, width), lambda i: (i, 0)),
            pl.BlockSpec((tile, width), lambda i: (i + steps, 0)),
            pl.BlockSpec((rows, tile), column),
            pl.BlockSpec((rows, width), fixed),
            pl.BlockSpec(gains.shape, fixed),
            pl.BlockSpec((rows, width), fixed),
            pl.BlockSpec(grad_widths.shape, fixed),
        ],
        out_specs=[
            pl.BlockSpec((gate_parts, rows, tile // gate_parts), lambda i: (i, 0, 0)),
            pl.BlockSpec((pack_parts, pack_rows, tile // pack_parts), lambda i: (i, 0, 0)),
            pl.BlockSpec((devices, tail_rows, width // devices), lambda i: (0, 0, 0)),
            pl.BlockSpec((rows, width), fixed),
        ],
        out_shape=[
            jax.ShapeDtypeStruct((devices // 2, rows, 2 * channels // devices), BF16),
            jax.ShapeDtypeStruct((devices, pack_rows, channels // devices), BF16),
            jax.ShapeDtypeStruct((devices, tail_rows, width // devices), BF16),
            jax.ShapeDtypeStruct((rows, width), F32),
        ],
        scratch_shapes=[pltpu.VMEM((rows, width), F32)],
        compiler_params=pltpu.CompilerParams(vmem_limit_bytes=VMEM_LIMIT),
        name="mixer_back",
    )(
        grad_proj, scan_w, grad_u, x_inner, vec, grad_gate, in_t, in_t, u_act, tokens, gains,
        grad_mid, grad_widths,
    )


def gelu_parts(values):
    weight = jnp.exp(values * values * -0.5)
    scaled = jnp.abs(values) * 0.7071067811865476
    ratio = 1.0 / (1.0 + 0.3275911 * scaled)
    series = 1.061405429 * ratio - 1.453152027
    series = series * ratio + 1.421413741
    series = series * ratio - 0.284496736
    series = series * ratio + 0.254829592
    tail = (0.5 * ratio) * series * weight
    below = jnp.where(values >= 0.0, 1.0 - tail, tail)
    return values * below, below + values * weight * 0.3989422804014327


def router_kernel(
    mid_ref, gain_ref, router_ref, routes_col_ref, routes_row_ref, slots_row_ref, live_ref, cot_ref,
    sendr_ref, sendg_ref, normed_ref, probs_ref,
):
    mid = mid_ref[...]
    rows = mid.shape[0]
    experts = router_ref.shape[1]
    scale = lax.rsqrt(jnp.mean(mid * mid, -1, keepdims=True) + 1e-05)
    normed = (mid * scale * gain_ref[...]).astype(BF16)
    normed_ref[...] = normed
    logits = product(normed, router_ref[...])
    weights = jnp.exp(logits - jnp.max(logits, -1, keepdims=True))
    probs = weights / jnp.sum(weights, -1, keepdims=True)
    probs_ref[...] = probs
    chosen = (routes_col_ref[...] == iota((rows, experts), 1)).astype(F32)
    gate = jnp.sum(probs * chosen, 1, keepdims=True)
    grads = (gate * (cot_ref[...].astype(F32) * live_ref[...])).astype(BF16)
    slot = iota((experts * CAP, rows), 0)
    dispatch = (
        (routes_row_ref[...] == slot // CAP) & (slots_row_ref[...] == slot % CAP)
    ).astype(BF16)
    width = mid.shape[1]
    sendr_ref[...] = product(dispatch, normed).astype(BF16).reshape(experts, CAP, width)
    sendg_ref[...] = product(dispatch, grads).astype(BF16).reshape(experts, CAP, width)


def router_step(mid, gain, router, routes_col, routes_row, slots_row, live, cotangent):
    rows, width = mid.shape
    experts = router.shape[1]
    return pl.pallas_call(
        router_kernel,
        out_shape=[
            jax.ShapeDtypeStruct((experts, CAP, width), BF16),
            jax.ShapeDtypeStruct((experts, CAP, width), BF16),
            jax.ShapeDtypeStruct((rows, width), BF16),
            jax.ShapeDtypeStruct((rows, experts), F32),
        ],
        compiler_params=pltpu.CompilerParams(vmem_limit_bytes=VMEM_LIMIT),
        name="router_step",
    )(mid, gain, router, routes_col, routes_row, slots_row, live, cotangent)


def expert_out_kernel(rows_ref, up_ref, down_ref, out_ref, slope_ref, total):
    step = pl.program_id(0)
    pieces, cap, width = rows_ref.shape
    rows = rows_ref[...].reshape(pieces * cap, width)

    @pl.when(step == 0)
    def _():
        total[...] = jnp.zeros_like(total)

    activated, slope = gelu_parts(product(rows, up_ref[...]))
    slope_ref[...] = slope.astype(BF16)
    total[...] += product(activated.astype(BF16), down_ref[...])

    @pl.when(step == pl.num_programs(0) - 1)
    def _():
        out_ref[...] = total[...].astype(BF16).reshape(pieces, cap, width)


def expert_out(rows, up, down, tile):
    pieces, cap, width = rows.shape
    hidden = up.shape[1]
    fixed = lambda i: (0, 0, 0)
    return pl.pallas_call(
        expert_out_kernel,
        grid=(hidden // tile,),
        in_specs=[
            pl.BlockSpec(rows.shape, fixed),
            pl.BlockSpec((width, tile), lambda i: (0, i)),
            pl.BlockSpec((tile, width), lambda i: (i, 0)),
        ],
        out_specs=[
            pl.BlockSpec(rows.shape, fixed),
            pl.BlockSpec((pieces * cap, tile), lambda i: (0, i)),
        ],
        out_shape=[
            jax.ShapeDtypeStruct(rows.shape, BF16),
            jax.ShapeDtypeStruct((pieces * cap, hidden), BF16),
        ],
        scratch_shapes=[pltpu.VMEM((pieces * cap, width), F32)],
        compiler_params=pltpu.CompilerParams(vmem_limit_bytes=VMEM_LIMIT),
        name="expert_out",
    )(rows, up, down)


def expert_back_kernel(grads_ref, up_ref, down_ref, slope_ref, out_ref, total):
    step = pl.program_id(0)
    pieces, cap, width = grads_ref.shape
    grads = grads_ref[...].reshape(pieces * cap, width)

    @pl.when(step == 0)
    def _():
        total[...] = jnp.zeros_like(total)

    slope = slope_ref[...].astype(F32)
    grad_pre = (times_transpose(grads, down_ref[...]) * slope).astype(BF16)
    total[...] += times_transpose(grad_pre, up_ref[...])

    @pl.when(step == pl.num_programs(0) - 1)
    def _():
        out_ref[...] = total[...].astype(BF16).reshape(pieces, cap, width)


def expert_back(grads, up, down, slope, tile):
    pieces, cap, width = grads.shape
    hidden = up.shape[1]
    fixed = lambda i: (0, 0, 0)
    return pl.pallas_call(
        expert_back_kernel,
        grid=(hidden // tile,),
        in_specs=[
            pl.BlockSpec(grads.shape, fixed),
            pl.BlockSpec((width, tile), lambda i: (0, i)),
            pl.BlockSpec((tile, width), lambda i: (i, 0)),
            pl.BlockSpec((pieces * cap, tile), lambda i: (0, i)),
        ],
        out_specs=pl.BlockSpec(grads.shape, fixed),
        out_shape=jax.ShapeDtypeStruct(grads.shape, BF16),
        scratch_shapes=[pltpu.VMEM((pieces * cap, width), F32)],
        compiler_params=pltpu.CompilerParams(vmem_limit_bytes=VMEM_LIMIT),
        name="expert_back",
    )(grads, up, down, slope)


def expert_grads_kernel(chunks, rows_ref, grads_ref, up_ref, down_ref, gup_ref, gdown_ref, rows_t):
    chunk = pl.program_id(1)
    groups, pieces, cap, width = rows_ref.shape
    count = groups * pieces * cap
    rows = rows_ref[...].reshape(count, width)
    grads = grads_ref[...].reshape(count, width)

    @pl.when((pl.program_id(0) == 0) | (chunks > 1))
    def _():
        rows_t[...] = rows.T

    activated, slope = gelu_parts(product(rows, up_ref[...]))
    grad_pre = (times_transpose(grads, down_ref[...]) * slope).astype(BF16)
    grad_up = product(rows_t[...], grad_pre)
    grad_down = contract_rows(activated.astype(BF16), grads)

    @pl.when(chunk == 0)
    def _():
        gup_ref[...] = grad_up
        gdown_ref[...] = grad_down

    if chunks > 1:

        @pl.when(chunk > 0)
        def _():
            gup_ref[...] += grad_up
            gdown_ref[...] += grad_down


def expert_grads(rows, grads, up, down, tile):
    groups, pieces, cap, width = rows.shape
    hidden = up.shape[1]
    together = max(1, min(groups, 32 // pieces))
    chunks = groups // together
    some = pl.BlockSpec((together, pieces, cap, width), lambda i, j: (j, 0, 0, 0))
    return pl.pallas_call(
        partial(expert_grads_kernel, chunks),
        grid=(hidden // tile, chunks),
        in_specs=[
            some,
            some,
            pl.BlockSpec((width, tile), lambda i, j: (0, i)),
            pl.BlockSpec((tile, width), lambda i, j: (i, 0)),
        ],
        out_specs=[
            pl.BlockSpec((width, tile), lambda i, j: (0, i)),
            pl.BlockSpec((tile, width), lambda i, j: (i, 0)),
        ],
        out_shape=[
            jax.ShapeDtypeStruct((width, hidden), F32),
            jax.ShapeDtypeStruct((hidden, width), F32),
        ],
        scratch_shapes=[pltpu.VMEM((width, together * pieces * cap), BF16)],
        compiler_params=pltpu.CompilerParams(vmem_limit_bytes=VMEM_LIMIT),
        name="expert_grads",
    )(rows, grads, up, down)


def combine_kernel(
    mid_ref, gain_ref, router_ref, routes_ref, slots_ref, live_ref, cot_ref, probs_ref, normed_ref,
    backr_ref, backg_ref, out_ref, gradmid_ref, gradmix_ref, widths_ref,
):
    mid = mid_ref[...]
    rows, width = mid.shape
    experts = router_ref.shape[1]
    routes = routes_ref[...]
    chosen = (routes == iota((rows, experts), 1)).astype(F32)
    probs = probs_ref[...]
    gate = jnp.sum(probs * chosen, 1, keepdims=True)
    live = live_ref[...]
    slot = iota((rows, experts * CAP), 1)
    collect = ((routes == slot // CAP) & (slots_ref[...] == slot % CAP)).astype(BF16)
    expert_sum = product(collect, backr_ref[...].reshape(experts * CAP, width))
    out_ref[...] = (live * (mid + gate * expert_sum)).astype(BF16)
    grad_out = cot_ref[...].astype(F32) * live
    grad_gate = jnp.sum(grad_out * expert_sum, 1, keepdims=True)
    grad_logits = (probs * (chosen * grad_gate - gate * grad_gate)).astype(BF16)
    grad_router = contract_rows(grad_logits, normed_ref[...])
    grad = product(collect, backg_ref[...].reshape(experts * CAP, width))
    grad = grad + times_transpose(grad_logits, router_ref[...])
    scale = lax.rsqrt(jnp.mean(mid * mid, -1, keepdims=True) + 1e-05)
    unit = mid * scale
    widths_ref[...] = jnp.concatenate([grad_router, jnp.sum(grad * unit, 0, keepdims=True)], 0)
    inner = grad * gain_ref[...]
    grad_mid = grad_out + scale * (inner - unit * jnp.mean(inner * unit, -1, keepdims=True))
    gradmid_ref[...] = grad_mid
    gradmix_ref[...] = grad_mid.astype(BF16)


def combine_step(mid, gain, router, routes, slots, live, cotangent, probs, normed, backr, backg):
    rows, width = mid.shape
    return pl.pallas_call(
        combine_kernel,
        out_shape=[
            jax.ShapeDtypeStruct((rows, width), BF16),
            jax.ShapeDtypeStruct((rows, width), F32),
            jax.ShapeDtypeStruct((rows, width), BF16),
            jax.ShapeDtypeStruct((router.shape[1] + 1, width), F32),
        ],
        compiler_params=pltpu.CompilerParams(vmem_limit_bytes=VMEM_LIMIT),
        name="combine_step",
    )(mid, gain, router, routes, slots, live, cotangent, probs, normed, backr, backg)


MESH = pl.DeviceIdType.MESH


def neighbour(bit):
    me = lax.axis_index("expert")
    return me + (1 - 2 * ((me // bit) % 2)) * bit


def greet_send(line=True):
    devices, copies = lax.axis_size("expert"), lax.axis_size("dp")
    me, place = lax.axis_index("expert"), lax.axis_index("dp")
    barrier = pltpu.get_barrier_semaphore()
    for k in range(1, devices):
        pl.semaphore_signal(
            barrier, inc=1, device_id={"expert": (me + k) % devices}, device_id_type=MESH
        )
    if line:

        @pl.when(place < copies - 1)
        def _():
            pl.semaphore_signal(barrier, inc=1, device_id={"dp": place + 1}, device_id_type=MESH)

        @pl.when(place > 0)
        def _():
            pl.semaphore_signal(barrier, inc=1, device_id={"dp": place - 1}, device_id_type=MESH)


def greet_wait(line=True):
    devices, copies = lax.axis_size("expert"), lax.axis_size("dp")
    place = lax.axis_index("dp")
    barrier = pltpu.get_barrier_semaphore()
    ends = (place == 0) | (place == copies - 1)
    if line:
        pl.when(ends)(lambda: pl.semaphore_wait(barrier, devices))
        pl.when(jnp.logical_not(ends))(lambda: pl.semaphore_wait(barrier, devices + 1))
    else:
        pl.semaphore_wait(barrier, devices - 1)


def greet(line=True):
    greet_send(line)
    greet_wait(line)


class Exchange:
    def __init__(self, source, target, send_sems, recv_sems, local_sem):
        devices, me = lax.axis_size("expert"), lax.axis_index("expert")
        self.copies = []
        for k in range(1, devices):
            peer = (me + k) % devices
            self.copies.append(
                pltpu.make_async_remote_copy(
                    source.at[peer], target.at[me], send_sems.at[k], recv_sems.at[k],
                    device_id={"expert": peer}, device_id_type=MESH,
                )
            )
        self.local = pltpu.make_async_copy(source.at[me], target.at[me], local_sem)

    def start(self):
        for copy in self.copies:
            copy.start()
        self.local.start()

    def wait(self):
        self.local.wait()
        for copy in self.copies:
            copy.wait()


class Line:
    def __init__(self, stage, from_left, from_right, next_left, next_right, send_sems, recv_sems):
        place = lax.axis_index("dp")
        last = lax.axis_size("dp") - 1
        self.right = pltpu.make_async_remote_copy(
            from_left, next_left, send_sems.at[0], recv_sems.at[0],
            device_id={"dp": jnp.minimum(place + 1, last)}, device_id_type=MESH,
        )
        self.left = pltpu.make_async_remote_copy(
            from_right, next_right, send_sems.at[1], recv_sems.at[1],
            device_id={"dp": jnp.maximum(place - 1, 0)}, device_id_type=MESH,
        )
        self.send_right = (place >= stage - 1) & (place < last)
        self.send_left = (last - place >= stage - 1) & (place > 0)
        self.get_left = place >= stage
        self.get_right = last - place >= stage

    def start(self):
        pl.when(self.send_right)(lambda: self.right.start())
        pl.when(self.send_left)(lambda: self.left.start())

    def wait(self):
        pl.when(self.send_right)(lambda: self.right.wait_send())
        pl.when(self.send_left)(lambda: self.left.wait_send())
        pl.when(self.get_left)(lambda: self.right.wait_recv())
        pl.when(self.get_right)(lambda: self.left.wait_recv())


def as_column(row):
    return jnp.broadcast_to(row.astype(F32), (8, row.shape[1])).T[:, 0:1].astype(jnp.int32)


def dispatch_matrix(goal, experts):
    slot = iota((experts * CAP, goal.shape[1]), 0)
    return (goal[0:1, :] == slot).astype(BF16)


def expert_layer_kernel(
    length_ref, mid_ref, gains_ref, router_ref, routes_ref, slots_ref, cot_ref, up_hbm, down_hbm,
    out_ref, gradmid_ref, gradmix_ref, widths_ref, rows_out, grads_out,
    left_1, right_1, left_2, right_2, goal_l1, goal_r1, goal_l2, goal_r2, gup_hbm, gdown_hbm,
    raw, goal, up_ref, down_ref, send_r, send_g, got_r, got_g, slope_ref, total, give_r, give_g,
    back_r, back_g, probs_ref, act_ref, rows_t, gup_ref, gdown_ref,
    weight_sems, send_sems, recv_sems, local_sems, line_send, line_recv, out_sems, grad_sems,
):
    tile = 512
    rows, width = mid_ref.shape
    experts = router_ref.shape[0]
    hidden = up_ref.shape[1]
    load_up = pltpu.make_async_copy(up_hbm, up_ref, weight_sems.at[0])
    load_down = pltpu.make_async_copy(down_hbm, down_ref, weight_sems.at[1])
    greet_send()
    load_up.start()
    load_down.start()

    ways = [
        Exchange(source, target, send_sems.at[k], recv_sems.at[k], local_sems.at[k])
        for k, (source, target) in enumerate(
            [(send_r, got_r), (send_g, got_g), (give_r, back_r), (give_g, back_g)]
        )
    ]
    lines = [
        Line(stage, *buffers, line_send.at[k], line_recv.at[k])
        for k, (stage, buffers) in enumerate(
            [(1, (raw.at[part], raw.at[part], left_1.at[part], right_1.at[part])) for part in (0, 1)]
            + [(1, (goal, goal, goal_l1, goal_r1))]
            + [
                (2, (left_1.at[part], right_1.at[part], left_2.at[part], right_2.at[part]))
                for part in (0, 1)
            ]
            + [(2, (goal_l1, goal_r1, goal_l2, goal_r2))]
        )
    ]
    gain = gains_ref[1:2, :]
    live = (iota((rows, 1), 0) < length_ref[0]).astype(F32)
    routes, slots = as_column(routes_ref[...]), as_column(slots_ref[...])
    mid = mid_ref[...]
    scale = lax.rsqrt(jnp.mean(mid * mid, -1, keepdims=True) + 1e-05)
    normed = (mid * scale * gain).astype(BF16)
    raw[0] = normed
    slots_row = slots_ref[...]
    target = jnp.where(slots_row < CAP, routes_ref[...] * CAP + slots_row, -1)
    goal[...] = jnp.broadcast_to(target, goal.shape)
    dispatch = dispatch_matrix(goal, experts)
    send_r[...] = product(dispatch, normed).astype(BF16).reshape(experts, CAP, width)
    greet_wait()
    ways[0].start()
    for k in (0, 2):
        lines[k].start()
    logits = times_transpose(normed, router_ref[...])
    weights = jnp.exp(logits - jnp.max(logits, -1, keepdims=True))
    probs = weights / jnp.sum(weights, -1, keepdims=True)
    probs_ref[...] = probs
    chosen = (routes == iota((rows, experts), 1)).astype(F32)
    gate = jnp.sum(probs * chosen, 1, keepdims=True)
    grads = (gate * (cot_ref[...].astype(F32) * live)).astype(BF16)
    raw[1] = grads
    send_g[...] = product(dispatch, grads).astype(BF16).reshape(experts, CAP, width)
    ways[1].start()
    lines[1].start()

    load_up.wait()
    load_down.wait()
    ways[0].wait()
    for k in (0, 2):
        lines[k].wait()
        lines[k + 3].start()
    keep_rows = pltpu.make_async_copy(got_r, rows_out, out_sems.at[0])
    keep_rows.start()
    total[...] = jnp.zeros_like(total)

    def forward(step, carry):
        at = pl.ds(pl.multiple_of(step * tile, tile), tile)
        inputs = got_r[...].reshape(experts * CAP, width)
        activated, slope = gelu_parts(product(inputs, up_ref[:, at]))
        slope_ref[:, at] = slope.astype(BF16)
        activated = activated.astype(BF16)
        act_ref[:, at] = activated
        total[...] += product(activated, down_ref[at, :])
        return carry

    lax.fori_loop(0, hidden // tile, forward, 0)
    give_r[...] = total[...].astype(BF16).reshape(experts, CAP, width)
    ways[2].start()
    ways[1].wait()
    lines[1].wait()
    lines[4].start()
    keep_grads = pltpu.make_async_copy(got_g, grads_out, out_sems.at[1])
    keep_grads.start()
    total[...] = jnp.zeros_like(total)

    def backward(step, carry):
        at = pl.ds(pl.multiple_of(step * tile, tile), tile)
        outputs = got_g[...].reshape(experts * CAP, width)
        slope = slope_ref[:, at].astype(F32)
        grad_pre = (times_transpose(outputs, down_ref[at, :]) * slope).astype(BF16)
        slope_ref[:, at] = grad_pre
        total[...] += times_transpose(grad_pre, up_ref[:, at])
        return carry

    lax.fori_loop(0, hidden // tile, backward, 0)
    give_g[...] = total[...].astype(BF16).reshape(experts, CAP, width)
    ways[3].start()

    rows_t[...] = got_r[...].reshape(experts * CAP, width).T
    stores = []
    for step in range(hidden // tile):
        spot = step % 2
        at = pl.ds(step * tile, tile)
        if step >= 2:
            for store in stores[2 * (step - 2) : 2 * (step - 1)]:
                store.wait()
        gup_ref[spot] = product(rows_t[...], slope_ref[:, at]).astype(BF16)
        gdown_ref[spot] = contract_rows(
            act_ref[:, at], got_g[...].reshape(experts * CAP, width)
        ).astype(BF16)
        stores += [
            pltpu.make_async_copy(gup_ref.at[spot], gup_hbm.at[:, at], grad_sems.at[0, spot]),
            pltpu.make_async_copy(gdown_ref.at[spot], gdown_hbm.at[at], grad_sems.at[1, spot]),
        ]
        for store in stores[-2:]:
            store.start()

    chosen = (routes == iota((rows, experts), 1)).astype(F32)
    probs = probs_ref[...]
    gate = jnp.sum(probs * chosen, 1, keepdims=True)
    slot = iota((rows, experts * CAP), 1)
    collect = ((routes == slot // CAP) & (slots == slot % CAP)).astype(BF16)
    ways[2].wait()
    expert_sum = product(collect, back_r[...].reshape(experts * CAP, width))
    mid = mid_ref[...]
    out_ref[...] = (live * (mid + gate * expert_sum)).astype(BF16)
    grad_out = cot_ref[...].astype(F32) * live
    grad_gate = jnp.sum(grad_out * expert_sum, 1, keepdims=True)
    grad_logits = (probs * (chosen * grad_gate - gate * grad_gate)).astype(BF16)
    grad_router = contract_rows(grad_logits, raw[0])
    from_logits = product(grad_logits, router_ref[...])
    scale = lax.rsqrt(jnp.mean(mid * mid, -1, keepdims=True) + 1e-05)
    unit = mid * scale
    ways[3].wait()
    grad = product(collect, back_g[...].reshape(experts * CAP, width)) + from_logits
    widths_ref[...] = jnp.concatenate([grad_router, jnp.sum(grad * unit, 0, keepdims=True)], 0)
    inner = grad * gain
    grad_mid = grad_out + scale * (inner - unit * jnp.mean(inner * unit, -1, keepdims=True))
    gradmid_ref[...] = grad_mid
    gradmix_ref[...] = grad_mid.astype(BF16)
    for store in stores[-4:]:
        store.wait()
    keep_rows.wait()
    keep_grads.wait()
    for k in (3, 4, 5):
        lines[k].wait()


def expert_layer(lengths, mid, gains, router, routes, slots, cotangent, up, down):
    rows, width = mid.shape
    experts = router.shape[0]
    hidden = up.shape[1]
    buffer = (experts, CAP, width)
    here = pl.BlockSpec(memory_space=pltpu.VMEM)
    far = pl.BlockSpec(memory_space=pl.ANY)
    blocks = jax.ShapeDtypeStruct(buffer, BF16)
    raw = jax.ShapeDtypeStruct((2, rows, width), BF16)
    goal = jax.ShapeDtypeStruct((8, rows), jnp.int32)
    dma = pltpu.SemaphoreType.DMA
    return pl.pallas_call(
        expert_layer_kernel,
        in_specs=[pl.BlockSpec(memory_space=pltpu.SMEM)] + [here] * 6 + [far] * 2,
        out_specs=[here] * 4 + [far] * 12,
        out_shape=[
            jax.ShapeDtypeStruct((rows, width), BF16),
            jax.ShapeDtypeStruct((rows, width), F32),
            jax.ShapeDtypeStruct((rows, width), BF16),
            jax.ShapeDtypeStruct((experts + 1, width), F32),
        ] + [blocks] * 2 + [raw] * 4 + [goal] * 4 + [
            jax.ShapeDtypeStruct(up.shape, BF16),
            jax.ShapeDtypeStruct(down.shape, BF16),
        ],
        scratch_shapes=[
            pltpu.VMEM(raw.shape, BF16),
            pltpu.VMEM(goal.shape, jnp.int32),
            pltpu.VMEM(up.shape, BF16),
            pltpu.VMEM(down.shape, BF16),
        ] + [pltpu.VMEM(buffer, BF16)] * 4 + [
            pltpu.VMEM((experts * CAP, hidden), BF16),
            pltpu.VMEM((experts * CAP, width), F32),
        ] + [pltpu.VMEM(buffer, BF16)] * 4 + [
            pltpu.VMEM((rows, experts), F32),
            pltpu.VMEM((experts * CAP, hidden), BF16),
            pltpu.VMEM((width, experts * CAP), BF16),
            pltpu.VMEM((2, width, 512), BF16),
            pltpu.VMEM((2, 512, width), BF16),
            dma((2,)), dma((4, experts)), dma((4, experts)), dma((4,)), dma((6, 2)), dma((6, 2)),
            dma((2,)), dma((2, 2)),
        ],
        compiler_params=pltpu.CompilerParams(
            vmem_limit_bytes=VMEM_LIMIT, collective_id=1, has_side_effects=True
        ),
        name="expert_layer",
    )(lengths, mid, gains, router, routes, slots, cotangent, up, down)


class PlaneGather:
    def __init__(self, source, target, send_sems, recv_sems, local_sem):
        me = lax.axis_index("expert")
        core, side, above = neighbour(1), neighbour(2), neighbour(4)
        far = side + above - me
        rows = target.shape[1]
        first, second = pl.ds(0, rows // 2), pl.ds(rows // 2, rows - rows // 2)
        every = pl.ds(0, rows)

        def send(k, block, owner, part, device):
            return pltpu.make_async_remote_copy(
                block, target.at[owner, part], send_sems.at[k], recv_sems.at[k],
                device_id={"expert": device}, device_id_type=MESH,
            )

        self.copies = [
            send(0, source.at[first], me, first, side),
            send(1, source.at[second], me, second, side),
            send(2, source.at[first], me, first, above),
            send(3, source.at[second], me, second, above),
            send(4, target.at[side, first], side, first, above),
            send(5, target.at[above, second], above, second, side),
            send(6, source, me, every, core),
            send(7, target.at[side], side, every, core),
            send(8, target.at[above], above, every, core),
            send(9, target.at[far], far, every, core),
        ]
        self.local = pltpu.make_async_copy(source, target.at[me], local_sem)

    def step(self, number):
        copies = self.copies
        for k in ((), (0, 3), (1, 2), (4, 5), (6, 7, 8, 9))[number]:
            copies[k].wait_recv()
        for k in ((0, 3, 1, 2, 6), (4, 5), (7, 8), (9,), ())[number]:
            copies[k].start()
        if number == 0:
            self.local.start()
        if number == 4:
            self.local.wait()
            for copy in copies:
                copy.wait_send()


def greet_all():
    devices, copies = lax.axis_size("expert"), lax.axis_size("dp")
    me, place = lax.axis_index("expert"), lax.axis_index("dp")
    barrier = pltpu.get_barrier_semaphore()
    for k in range(1, devices):
        pl.semaphore_signal(
            barrier, inc=1, device_id={"expert": (me + k) % devices}, device_id_type=MESH
        )
    for k in range(1, copies):
        pl.semaphore_signal(
            barrier, inc=1, device_id={"dp": (place + k) % copies}, device_id_type=MESH
        )
    pl.semaphore_wait(barrier, devices + copies - 2)


class WideGather:
    def __init__(self, source, target, send_sems, recv_sems, local_sem):
        me, place = lax.axis_index("expert"), lax.axis_index("dp")
        core, side, above = neighbour(1), neighbour(2), neighbour(4)
        far = side + above - me
        odd = place % 2
        partner = place + 1 - 2 * odd
        rows = target.shape[1]
        unit = rows // 6

        def part(start, count):
            return pl.ds(pl.multiple_of(start * unit, unit), count * unit)

        def send(k, block, owner, where, **device):
            return pltpu.make_async_remote_copy(
                block, target.at[owner, where], send_sems.at[k], recv_sems.at[k],
                device_id=device, device_id_type=MESH,
            )

        def forward(k, owner, where, **device):
            return send(k, target.at[owner, where], owner, where, **device)

        outer, inner = part(4 * odd, 2), part(4 * (1 - odd), 2)
        middle = part(2, 2)
        self.copies = [
            send(0, source.at[outer], me, outer, expert=side),
            send(1, source.at[middle], me, middle, expert=side),
            send(2, source.at[inner], me, inner, expert=above),
            send(3, source.at[middle], me, middle, expert=above),
            forward(4, side, outer, expert=above),
            forward(5, side, part(2 + odd, 1), expert=above),
            forward(6, above, inner, expert=side),
            forward(7, above, part(3 - odd, 1), expert=side),
            forward(8, side, outer, dp=partner),
            forward(9, above, inner, dp=partner),
            send(10, source, me, part(0, 6), expert=core),
            forward(11, side, part(2 * odd, 4), expert=core),
            forward(12, above, part(2 - 2 * odd, 4), expert=core),
            forward(13, side, inner, expert=core),
            forward(14, above, outer, expert=core),
            forward(15, far, part(0, 6), expert=core),
        ]
        self.local = pltpu.make_async_copy(source, target.at[me], local_sem)

    def step(self, number):
        copies = self.copies
        for k in ((), (0, 2), (1, 3), (8, 9), (4, 5, 6, 7), (10, 11, 12, 13, 14, 15))[number]:
            copies[k].wait_recv()
        for k in ((0, 2, 1, 3, 10), (4, 6, 8, 9), (5, 7, 11, 12), (13, 14), (15,), ())[number]:
            copies[k].start()
        if number == 0:
            self.local.start()
        if number == 5:
            self.local.wait()
            for copy in copies:
                copy.wait_send()


class Near:
    def __init__(self, own, target, send_sems, recv_sems):
        self.place = lax.axis_index("dp")
        self.last = lax.axis_size("dp") - 1
        self.right = pltpu.make_async_remote_copy(
            own, target, send_sems.at[0], recv_sems.at[0],
            device_id={"dp": jnp.minimum(self.place + 1, self.last)}, device_id_type=MESH,
        )
        self.left = pltpu.make_async_remote_copy(
            own, target, send_sems.at[1], recv_sems.at[1],
            device_id={"dp": jnp.maximum(self.place - 1, 0)}, device_id_type=MESH,
        )

    def start(self):
        pl.when(self.place < self.last)(lambda: self.right.start())
        pl.when(self.place == 1)(lambda: self.left.start())

    def wait(self):
        pl.when(self.place < self.last)(lambda: self.right.wait_send())
        pl.when(self.place == 1)(lambda: self.left.wait_send())
        pl.when(self.place > 0)(lambda: self.right.wait_recv())
        pl.when(self.place == 0)(lambda: self.left.wait_recv())


DMA = pltpu.SemaphoreType.DMA
FAR = pl.BlockSpec(memory_space=pl.ANY)


def remote_params(collective_id):
    return pltpu.CompilerParams(
        vmem_limit_bytes=VMEM_LIMIT, collective_id=collective_id, has_side_effects=True
    )


def columns_of(proj_ref, first, state, target):
    turned = proj_ref[...].T[first : first + state]
    for block in range(proj_ref.shape[0] // BLOCK):
        target[block * state : (block + 1) * state, 0:BLOCK] = turned[
            :, block * BLOCK : (block + 1) * BLOCK
        ]


def diagonals_of(proj_ref, first, state, high_ref, low_ref):
    rows, width = proj_ref.shape
    big = BLOCK * state
    place = (iota((width, big), 0) == first + iota((width, big), 1) % state).astype(BF16)
    own = iota((rows, big), 0) % BLOCK == iota((rows, big), 1) // state
    for part, target in zip(two_parts(proj_ref[...]), (high_ref, low_ref)):
        target[...] = jnp.where(own, product(part, place), 0.0).astype(BF16)


def block_of(ref, block, size):
    return ref[pl.ds(pl.multiple_of(block * size, size), size), :]


def forward_kernel(
    tokens_ref, in_ref, scan_ref, step_w_ref, decay_ref, conv_ref, bias_ref, dbias_ref, skip_ref,
    norm_ref, norm_two_ref, router_ref, outw_ref,
    normed_ref, xin_ref, u_out, gate_out, proj_ref, step_ref, mixed_ref, gated_ref, mid_ref,
    step_full, vec_ref, router_full, gains_ref, scan_full, in_full, outw_all, normed_all, hist_hbm,
    columns, widths, columns_all, widths_all, scan_here, in_here, u_all, gate_all, b_cols, c_high, c_low, du,
    scanned, gated_all, outw_here, ring,
    send_sems, recv_sems, local_sems, ring_sems,
):
    step = pl.program_id(0)
    devices, rank, part = columns_all.shape[0], step_w_ref.shape[0], step_w_ref.shape[1]
    state, taps, experts = decay_ref.shape[0], conv_ref.shape[0], router_ref.shape[0]
    slice_w = widths.shape[1]
    rows, tile = xin_ref.shape
    width = tokens_ref.shape[1]
    big = BLOCK * state
    turns = ring.shape[0]
    last = rows // BLOCK - 1
    small = [
        PlaneGather(source, target, send_sems.at[k], recv_sems.at[k], local_sems.at[k])
        for k, (source, target) in enumerate(
            [(columns, columns_all), (widths, widths_all), (scan_ref, scan_here)]
        )
    ]
    big_gather = WideGather(in_ref, in_here, send_sems.at[3], recv_sems.at[3], local_sems.at[3])
    gather = WideGather(outw_ref, outw_here, send_sems.at[4], recv_sems.at[4], local_sems.at[4])
    normed_gather = PlaneGather(
        normed_ref, normed_all, send_sems.at[5], recv_sems.at[5], local_sems.at[5]
    )
    keep = pltpu.make_async_copy(outw_here, outw_all, local_sems.at[6])
    keep_in = pltpu.make_async_copy(in_here, in_full, local_sems.at[7])
    half = step % 2
    lanes = pl.ds(pl.multiple_of(half * tile, tile), tile)

    @pl.when(step == 0)
    def _():
        spare = columns.shape[0] - rank - state - taps - 3
        columns[...] = jnp.concatenate(
            [
                step_w_ref[...].astype(F32), decay_ref[...].astype(F32), conv_ref[...].astype(F32),
                *(ref[...].astype(F32)[None] for ref in (bias_ref, dbias_ref, skip_ref)),
                jnp.zeros((spare, part), F32),
            ],
            0,
        ).astype(BF16)
        widths[...] = jnp.concatenate(
            [
                router_ref[...].astype(F32),
                *(ref[...].astype(F32)[None] for ref in (norm_ref, norm_two_ref)),
                jnp.zeros((widths.shape[0] - experts - 2, slice_w), F32),
            ],
            0,
        ).astype(BF16)
        greet()
        for number in range(3):
            for one in small:
                one.step(number)
            big_gather.step(number)
        for number in (3, 4):
            for one in small:
                one.step(number)
        big_gather.step(3)
        gather.step(0)
        table = jnp.concatenate([columns_all[k].astype(F32) for k in range(devices)], 1)
        step_full[...] = table[:rank].astype(BF16)
        scan_full[...] = scan_here[...]
        rest = table[rank:]
        vec_ref[0:state, :] = -jnp.exp(rest[:state])
        vec_ref[state : state + 8, :] = rest[state : state + 8]
        across = jnp.concatenate([widths_all[k].astype(F32) for k in range(devices)], 1)
        router_full[...] = across[:experts].astype(BF16)
        gains_ref[...] = across[experts : experts + 8]
        values = tokens_ref[...].astype(F32)
        scale = lax.rsqrt(jnp.mean(values * values, -1, keepdims=True) + 1e-05)
        normed_ref[...] = (values * scale * gains_ref[0:1, :]).astype(BF16)
        proj_ref[...] = jnp.zeros_like(proj_ref)
        big_gather.step(4)
        big_gather.step(5)
        keep_in.start()
        gather.step(1)

    @pl.when(step < 2)
    def _():
        misc = vec_ref[state : state + 8, lanes]
        normed = normed_ref[...]
        own = devices // 4

        def weights(first):
            rows_here = in_here.shape[1]
            return in_here[pl.ds(first + half * own, own)].reshape(own * rows_here, width)

        x_inner = times_transpose(normed, weights(0))
        gate_in = times_transpose(normed, weights(devices // 2))
        gate_out[...] = gate_in
        gate_all[:, lanes] = gate_in
        xin_ref[...] = x_inner
        summed = misc[taps : taps + 1] + misc[taps - 1 : taps] * x_inner
        for back in range(1, taps):
            tap = taps - 1 - back
            summed = summed + misc[tap : tap + 1] * shift_rows(x_inner, back)
        u_act = summed * sigmoid(summed)
        u_out[...] = u_act
        u_all[:, lanes] = u_act
        parts = devices // 2
        scan_rows_here = scan_here[pl.ds(half * parts, parts)].reshape(tile, scan_here.shape[2])
        proj_ref[...] += product(u_act.astype(BF16), scan_rows_here)

    @pl.when(step == 1)
    def _():
        gather.step(2)
        normed_gather.step(0)
        columns_of(proj_ref, rank, state, b_cols)
        diagonals_of(proj_ref, rank + state, state, c_high, c_low)

    def store(spot, block):
        start = pl.multiple_of((block * BLOCK + 1) * state, state)
        return pltpu.make_async_copy(
            ring.at[spot], hist_hbm.at[pl.ds(start, big), lanes], ring_sems.at[spot]
        )

    def sum_states(spot, block):
        high, low = block_of(c_high, block, BLOCK), block_of(c_low, block, BLOCK)
        both = product(jnp.concatenate([high, low], 0), ring[spot])
        return both[:BLOCK] + both[BLOCK:]

    def between(position):
        if position == 1:
            gather.step(3)
            gather.step(4)
        if position == 4:
            gather.step(5)
            keep.start()
            normed_gather.step(1)
            normed_gather.step(2)
        if position == 7:
            normed_gather.step(3)

    @pl.when(step >= 2)
    def _():
        misc = vec_ref[state : state + 8, lanes]
        u_act = u_all[:, lanes]
        step_size = softplus(
            product(proj_ref[:, :rank].astype(BF16), step_full[:, lanes])
            + misc[taps + 1 : taps + 2]
        )
        step_ref[...] = step_size
        du[...] = step_size * u_act
        decay = vec_ref[0:state, lanes] * LOG2E
        ring[turns - 1] = jnp.zeros((big, tile), BF16)
        zero_row = pltpu.make_async_copy(
            ring.at[turns - 1, pl.ds(0, state)], hist_hbm.at[pl.ds(0, state), lanes],
            ring_sems.at[turns],
        )
        zero_row.start()
        zero_row.wait()

        def run_blocks(quarter, held):
            for spot in range(turns):
                block = quarter * turns + spot
                pl.when(quarter > 0)(lambda: store(spot, block).wait())
                base = pl.multiple_of(block * BLOCK, BLOCK)
                before = (spot - 1) % turns
                scanned[pl.ds(base, BLOCK), :] = sum_states(before, jnp.maximum(block - 1, 0))
                steps_now, du_now = block_of(step_ref, block, BLOCK), block_of(du, block, BLOCK)
                b_now = block_of(b_cols, block, state)
                for t in range(BLOCK):
                    b_wide = jnp.broadcast_to(b_now[:, t : t + 1], (state, tile))
                    fade = jnp.exp2(steps_now[t : t + 1, :] * decay)
                    held = fade * held + du_now[t : t + 1, :] * b_wide
                    ring[spot, t * state : (t + 1) * state, :] = held.astype(BF16)
                store(spot, block).start()
            for turn in range(2):
                for count in range(rows // BLOCK // turns):

                    @pl.when((step == turn + 2) & (quarter == count))
                    def _():
                        between(turn * 4 + count)

            return held

        quarters = rows // BLOCK // turns
        lax.fori_loop(0, quarters, run_blocks, jnp.zeros((state, tile), F32))
        scanned[pl.ds(rows, BLOCK), :] = sum_states(turns - 1, last)
        mixed = scanned[pl.ds(BLOCK, rows), :] + misc[taps + 2 : taps + 3] * u_act
        mixed_ref[...] = mixed
        gate_in = gate_all[:, lanes]
        gated = (mixed * (gate_in * sigmoid(gate_in))).astype(BF16)
        gated_ref[...] = gated.T.reshape(gated_ref.shape)
        gated_all[:, lanes] = gated
        for spot in range(turns):
            store(spot, last - turns + 1 + spot).wait()

    @pl.when(step == 3)
    def _():
        weights = outw_here[...].reshape(devices * part, width)
        mid_ref[...] = tokens_ref[...].astype(F32) + product(gated_all[...], weights)
        keep.wait()
        keep_in.wait()
        normed_gather.step(4)


def forward_plane(
    tokens, in_t, scan_w, step_w, decay_t, conv, bias, dbias, skip, norm, norm_two, router_t, out_w
):
    rows, width = tokens.shape
    rank, part = step_w.shape
    cols = scan_w.shape[1]
    devices = lax.axis_size("expert")
    channels = devices * part
    state, experts, slice_w = decay_t.shape[0], router_t.shape[0], router_t.shape[1]
    tile = channels // 2
    hist_rows = (rows + 1) * state
    first = lambda i: jnp.minimum(i, 1)
    second = lambda i: jnp.maximum(i - 2, 0)

    def whole(shape):
        return pl.BlockSpec(shape, lambda i: (0,) * len(shape), pipeline_mode=pl.Buffered(1))

    def kept(shape):
        return pl.BlockSpec(shape, lambda i: (0,) * len(shape))

    def halves(index):
        return pl.BlockSpec((rows, tile), lambda i: (0, index(i)))

    inputs = (
        tokens, in_t, scan_w, step_w, decay_t, conv, bias, dbias, skip, norm, norm_two, router_t
    )
    fixed = [
        ((rank, channels), BF16), ((state + 8, channels), F32), ((experts, width), BF16),
        ((8, width), F32), ((devices, part, cols), BF16),
    ]
    return pl.pallas_call(
        forward_kernel,
        grid=(4,),
        in_specs=[whole(value.shape) for value in inputs] + [FAR],
        out_specs=[
            kept((rows, width)),
            halves(first),
            halves(first),
            halves(first),
            kept((rows, cols)),
            halves(second),
            halves(second),
            pl.BlockSpec((devices // 2, part, rows), lambda i: (second(i), 0, 0)),
            kept((rows, width)),
        ] + [kept(shape) for shape, _ in fixed] + [FAR] * 4,
        out_shape=[
            jax.ShapeDtypeStruct((rows, width), BF16),
            jax.ShapeDtypeStruct((rows, channels), F32),
            jax.ShapeDtypeStruct((rows, channels), F32),
            jax.ShapeDtypeStruct((rows, channels), F32),
            jax.ShapeDtypeStruct((rows, cols), F32),
            jax.ShapeDtypeStruct((rows, channels), F32),
            jax.ShapeDtypeStruct((rows, channels), F32),
            jax.ShapeDtypeStruct((devices, part, rows), BF16),
            jax.ShapeDtypeStruct((rows, width), F32),
        ] + [jax.ShapeDtypeStruct(shape, kind) for shape, kind in fixed] + [
            jax.ShapeDtypeStruct((devices,) + in_t.shape, BF16),
            jax.ShapeDtypeStruct((devices, part, width), BF16),
            jax.ShapeDtypeStruct((devices, rows, width), BF16),
            jax.ShapeDtypeStruct((hist_rows, channels), BF16),
        ],
        scratch_shapes=[
            pltpu.VMEM((rank + state + 8, part), BF16),
            pltpu.VMEM((32, slice_w), BF16),
            pltpu.VMEM((devices, rank + state + 8, part), BF16),
            pltpu.VMEM((devices, 32, slice_w), BF16),
            pltpu.VMEM((devices, part, cols), BF16),
            pltpu.VMEM((devices,) + in_t.shape, BF16),
            pltpu.VMEM((rows, channels), F32),
            pltpu.VMEM((rows, channels), F32),
            pltpu.VMEM((rows // BLOCK * state, 128), F32),
            pltpu.VMEM((rows, BLOCK * state), BF16),
            pltpu.VMEM((rows, BLOCK * state), BF16),
            pltpu.VMEM((rows, tile), F32),
            pltpu.VMEM((rows + BLOCK, tile), F32),
            pltpu.VMEM((rows, channels), BF16),
            pltpu.VMEM((devices, part, width), BF16),
            pltpu.VMEM((4, BLOCK * state, tile), BF16),
            DMA((6, 16)), DMA((6, 16)), DMA((8,)), DMA((5,)),
        ],
        compiler_params=remote_params(3),
        name="mixer_forward",
    )(*inputs, out_w)


def prepare_sends(raw, goal, sends):
    experts, cap, width = sends.shape[1:]
    matrix = dispatch_matrix(goal, experts)
    for part in range(2):
        values = product(matrix, raw[part]).astype(BF16)
        sends[part] = values.reshape(experts, cap, width)


def pick(choices, raw, goal, sems):
    place = lax.axis_index("dp")
    for where, (source, source_goal) in enumerate(choices):

        @pl.when(place == where)
        def _():
            copies = [
                pltpu.make_async_copy(source, raw, sems.at[0]),
                pltpu.make_async_copy(source_goal, goal, sems.at[1]),
            ]
            for copy in copies:
                copy.start()
            for copy in copies:
                copy.wait()


def fold_rows(got_ref, width):
    return fold_value(jnp.sum(got_ref[...].astype(F32), 0), width)


def fold_value(total, width):
    quarter = total.shape[0] // 4
    folded = jnp.concatenate([total[k * quarter : (k + 1) * quarter] for k in range(4)], 1)
    return jnp.concatenate([folded, jnp.zeros((32 - quarter, width), F32)], 0).astype(BF16)


def backward_kernel(
    proj_ref, stepw_ref, decay_ref, misc_ref, u_ref, gate_ref, outw_ref, gradmix_ref, step_ref,
    mixed_ref, scanw_ref, xin_ref, misc_x_ref, wx_ref, wg_ref, u_x_ref, tokens_ref, gains_ref,
    widths_ref,
    gradmid_hbm, gated_hbm, normed_hbm, hist_hbm, rows_0, grads_0, left_1, right_1, left_2, right_2, goal_l1,
    goal_r1, goal_l2, goal_r2,
    gradtok_hbm, totals_hbm, back_hbm, tail_hbm, rows_1, grads_1, left_3, right_3, goal_l3, goal_r3, sends_hbm,
    c_cols, b_high, b_low, b_sums, c_sums, gy, du, grad_du, grad_step, ring, g_ring, w_ring,
    gradproj, gradu_all, gate_all, send_in, got_in, everyone, gated_all, send_scan, got_scan,
    pack_back, send_back, send_tail, totals, raw, goal, send_grads,
    g_send, g_recv, x_send, x_recv, l_send, l_recv, local_sems, ring_sems, load_sems,
):
    step = pl.program_id(0)
    devices, me = lax.axis_size("expert"), lax.axis_index("expert")
    half = devices // 2
    rank, state = stepw_ref.shape[0], decay_ref.shape[0]
    rows, cols = proj_ref.shape
    tile, small_tile, width = u_ref.shape[1], xin_ref.shape[1], tokens_ref.shape[1]
    blocks, big = rows // BLOCK, BLOCK * state
    turns = ring.shape[0]
    quarters = blocks // turns
    in_part = send_in.shape[0] // devices
    channels = half * in_part
    steps_x = channels // small_tile
    mix = PlaneGather(gradmix_ref, everyone, g_send, g_recv, local_sems.at[0])
    gated = Exchange(gated_hbm, gated_all, x_send.at[0], x_recv.at[0], local_sems.at[1])
    scan = Exchange(send_scan, got_scan, x_send.at[1], x_recv.at[1], local_sems.at[2])
    near_grads = Exchange(send_grads, grads_1, x_send.at[2], x_recv.at[2], local_sems.at[3])

    def input_part(device):
        return send_in.at[pl.ds(pl.multiple_of(device * in_part, in_part), in_part)]

    input_copies = [
        pltpu.make_async_remote_copy(
            input_part((me + k) % devices), got_in.at[me], x_send.at[3, k], x_recv.at[3, k],
            device_id={"expert": (me + k) % devices}, device_id_type=MESH,
        )
        for k in range(1, devices)
    ]
    input_local = pltpu.make_async_copy(input_part(me), got_in.at[me], local_sems.at[4])

    def start_some(copies, local, first, last):
        for k, copy in enumerate(copies):
            peer = (me + k + 1) % devices
            pl.when((peer >= first) & (peer < last))(lambda copy=copy: copy.start())
        pl.when((me >= first) & (me < last))(lambda: local.start())

    def start_inputs(first, last):
        start_some(input_copies, input_local, first, last)

    lines = [
        Line(3, left_2, right_2, left_3, right_3, l_send.at[0], l_recv.at[0]),
        Line(3, goal_l2, goal_r2, goal_l3, goal_r3, l_send.at[1], l_recv.at[1]),
        Near(rows_0, rows_1, l_send.at[2], l_recv.at[2]),
        *(
            Near(grads_0.at[k], grads_1.at[k], l_send.at[3 + k // 2], l_recv.at[3 + k // 2])
            for k in range(1, devices, 2)
        ),
    ]
    load_normed = pltpu.make_async_copy(normed_hbm, everyone, load_sems.at[0])
    load_mid = pltpu.make_async_copy(gradmid_hbm, gy, load_sems.at[1])
    store_back = pltpu.make_async_copy(send_back, back_hbm, load_sems.at[8])
    store_tail = pltpu.make_async_copy(send_tail, tail_hbm, load_sems.at[9])
    store_sends = [
        pltpu.make_async_copy(source, sends_hbm.at[k], load_sems.at[6 + k])
        for k, source in enumerate((g_ring, w_ring))
    ]
    x_spot = (jnp.maximum(step - 2, 0) % steps_x) // (steps_x // 2)
    x_lanes = pl.ds(
        pl.multiple_of((jnp.maximum(step - 2, 0) % (steps_x // 2)) * small_tile, small_tile),
        small_tile,
    )
    lanes = pl.ds(pl.multiple_of(jnp.minimum(step, 1) * tile, tile), tile)

    def load(spot, block):
        start = pl.multiple_of(block * big, big)
        return pltpu.make_async_copy(
            hist_hbm.at[pl.ds(start, big + state), lanes], ring.at[spot], ring_sems.at[spot]
        )

    @pl.when(step < 2)
    def _():
        for spot in range(turns - 1):
            load(spot, blocks - 1 - spot).start()

    @pl.when(step == 0)
    def _():
        greet()
        mix.step(0)
        for line in lines:
            line.start()
        near_l, near_r = (left_1, goal_l1), (right_1, goal_r1)
        pick((near_r, near_l, near_l, near_l), raw, goal, load_sems.at[pl.ds(4, 2)])
        matrix = dispatch_matrix(goal, devices)
        send_grads[...] = product(matrix, raw[1]).astype(BF16).reshape(send_grads.shape)
        gradproj[...] = jnp.zeros_like(gradproj)
        b_sums[...] = jnp.zeros_like(b_sums)
        c_sums[...] = jnp.zeros_like(c_sums)
        columns_of(proj_ref, rank + state, state, c_cols)
        diagonals_of(proj_ref, rank, state, b_high, b_low)

    def between(position):
        if position == 1:
            pl.when(me % 2 == 0)(lambda: near_grads.start())
        if position == 2:
            mix.step(1)
            mix.step(2)
            gated.start()
        if position == 5:
            mix.step(3)
        if position == 7:
            mix.step(4)
            gated.wait()

    @pl.when(step < 2)
    def _():
        skip_ref = scan_rows(misc_ref)[1]
        grad_gated = times_transpose(gradmix_ref[...], outw_ref[...])
        gate_in = gate_ref[...]
        gate_sig = sigmoid(gate_in)
        grad_mixed = grad_gated * (gate_in * gate_sig)
        grad_gate = (
            grad_gated * mixed_ref[...] * (gate_sig * (1.0 + gate_in * (1.0 - gate_sig)))
        ).astype(BF16)
        gate_all[:, lanes] = grad_gate
        start = pl.multiple_of(channels + step * tile, tile)
        send_in[pl.ds(start, tile), :] = grad_gate.T
        u_act = u_ref[...]
        step_size = step_ref[...]
        gy[...] = grad_mixed
        du[0:rows, :] = step_size * u_act
        du[rows:, :] = jnp.zeros((BLOCK, tile), F32)
        grad_skip = jnp.sum(grad_mixed * u_act, 0, keepdims=True)
        rate = decay_ref[...]
        decay = rate * LOG2E
        sums = (iota((BLOCK, big), 0) == iota((BLOCK, big), 1) // state).astype(BF16)
        g_ring[1] = jnp.zeros((big, tile), BF16)
        w_ring[1] = jnp.zeros((big, tile), BF16)

        def reduce_block(spot, block):
            grads = g_ring[spot]
            source = jnp.minimum(block, blocks - 1)
            high, low = block_of(b_high, source, BLOCK), block_of(b_low, source, BLOCK)
            both = product(jnp.concatenate([high, low], 0), grads)
            base = pl.ds(pl.multiple_of(block * BLOCK, BLOCK), BLOCK)
            grad_du[base, :] = both[:BLOCK] + both[BLOCK:]
            grad_step[base, :] = product(sums, w_ring[spot])
            b_sums[base, :] += times_transpose(du[base, :].astype(BF16), grads)

        def run_blocks(quarter, carry):
            carried, log_sum = carry
            for spot in range(turns):
                turn = quarter * turns + spot
                block = blocks - 1 - turn
                later = (spot + turns - 1) % turns
                if spot == 0:
                    load(later, block - turns + 1).start()
                else:
                    pl.when(quarter < quarters - 1)(
                        lambda: load(later, block - turns + 1).start()
                    )
                load(spot, block).wait()
                here, before = spot % 2, (spot + 1) % 2
                reduce_block(before, block + 1)
                base = pl.ds(pl.multiple_of(block * BLOCK, BLOCK), BLOCK)
                steps_now, gy_now = step_ref[base, :], gy[base, :]
                c_now = block_of(c_cols, block, state)
                c_sums[base, :] += times_transpose(gy_now.astype(BF16), ring[spot, state:, :])
                for t in range(BLOCK - 1, -1, -1):
                    at = slice(t * state, (t + 1) * state)
                    c_wide = jnp.broadcast_to(c_now[:, t : t + 1], (state, tile))
                    step_now = steps_now[t : t + 1, :]
                    fade = jnp.exp2(step_now * decay)
                    grad = gy_now[t : t + 1, :] * c_wide + carried
                    g_ring[here, at, :] = grad.astype(BF16)
                    carried = fade * grad
                    weighted = carried * ring[spot, at, :].astype(F32) * rate
                    w_ring[here, at, :] = weighted.astype(BF16)
                    log_sum = log_sum + weighted * step_now
            for turn in range(2):
                for part in range(quarters):

                    @pl.when((step == turn) & (quarter == part))
                    def _():
                        between(turn * 4 + part)

            return carried, log_sum

        zeros = jnp.zeros((state, tile), F32)
        _, log_sum = lax.fori_loop(0, quarters, run_blocks, (zeros, zeros))
        reduce_block(1, 0)
        full_du = grad_du[0:rows, :]
        gradu_all[:, lanes] = full_du * step_size + skip_ref[...] * gy[...]
        grad_size = grad_step[0:rows, :] + full_du * u_act
        grad_pre = grad_size * (1.0 - jnp.exp(-step_size))
        grad_low = grad_pre.astype(BF16)
        grad_step_w = contract_rows(proj_ref[:, :rank].astype(BF16), grad_low)
        packed = jnp.concatenate(
            [grad_step_w, log_sum, jnp.sum(grad_pre, 0, keepdims=True), grad_skip, zeros[:6]], 0
        ).astype(BF16)
        for turn in range(2):

            @pl.when(step == turn)
            def _():
                split_lanes(send_scan.at[pl.ds(turn * half, half)], packed)
                start_some(scan.copies, scan.local, turn * half, (turn + 1) * half)
                start_inputs(half + turn * half // 2, half + (turn + 1) * half // 2)

        gradproj[:, :rank] += times_transpose(grad_low, stepw_ref[...])

    @pl.when(step == 1)
    def _():
        own = iota((rows, big), 0) % BLOCK == iota((rows, big), 1) // state
        lane = iota((big, cols), 1)
        slot = iota((big, cols), 0) % state
        total = gradproj[...]
        for sums_here, first in ((b_sums[0:rows, :], rank), (c_sums[...], rank + state)):
            place = (lane == first + slot).astype(F32)
            total = total + exact_product(jnp.where(own, sums_here, 0.0), place)
        gradproj[...] = total

    @pl.when(step == 2)
    def _():
        load_mid.start()
        grad_du[...] = jnp.zeros_like(grad_du)

    @pl.when(step == steps_x + 2)
    def _():
        split_lanes(send_back, pack_back[...])
        store_back.start()
        lhs = jnp.concatenate([gated_all[k] for k in range(devices)], 1)
        totals[2 * gated_all.shape[1] : 3 * gated_all.shape[1], :] = product(
            lhs, everyone[...].reshape(devices * rows, width)
        ).astype(BF16)
        load_normed.start()

    here = pl.ds(
        pl.multiple_of((jnp.maximum(step - 2, 0) % steps_x) * small_tile, small_tile), small_tile
    )

    @pl.when((step >= 2) & (step < steps_x + 2))
    def _():
        conv_ref, bias_ref = conv_rows(misc_x_ref)
        grad_proj = gradproj[...].astype(BF16)
        grad_u = gradu_all[:, here] + times_transpose(grad_proj, scanw_ref[...])
        pieces = [contract_rows(grad_proj, u_x_ref[...].astype(BF16))]
        x_inner = xin_ref[...]
        taps = conv_ref.shape[0]
        shifted = [shift_rows(x_inner, taps - 1 - tap) for tap in range(taps)]
        summed = bias_ref[...]
        for tap in range(taps):
            summed = summed + conv_ref[tap : tap + 1, :] * shifted[tap]
        sig = sigmoid(summed)
        grad_sum = grad_u * (sig * (1.0 + summed * (1.0 - sig)))
        grad_x = jnp.zeros_like(x_inner)
        for tap in range(taps):
            pieces.append(jnp.sum(grad_sum * shifted[tap], 0, keepdims=True))
            grad_x = grad_x + conv_ref[tap : tap + 1, :] * shift_rows(grad_sum, tap + 1 - taps)
        pieces.append(jnp.sum(grad_sum, 0, keepdims=True))
        pieces.append(jnp.zeros((pack_back.shape[0] - cols - taps - 1, small_tile), F32))
        pack_back[:, here] = jnp.concatenate(pieces, 0).astype(BF16)
        grad_x = grad_x.astype(BF16)
        send_in[here, :] = grad_x.T
        ring[x_spot, 0:rows, x_lanes] = grad_x
        for part in range(half):
            done = -(-(part + 1) * in_part // small_tile) + 1
            pl.when(step == done)(lambda: start_inputs(part, part + 1))

    @pl.when(step >= steps_x + 2)
    def _():
        grad_du[0:rows, :] += product(ring[x_spot, 0:rows, x_lanes], wx_ref[...]) + product(
            gate_all[:, here], wg_ref[...]
        )

    @pl.when(step == steps_x + 3)
    def _():
        next_to = [(left_2, goal_l2), (right_2, goal_r2), (right_1, goal_r1)]
        pick(
            (next_to[1], next_to[2], next_to[2], next_to[0]), raw, goal, load_sems.at[pl.ds(4, 2)]
        )
        matrix = dispatch_matrix(goal, devices)
        for part, (target, store) in enumerate(zip((g_ring, w_ring), store_sends)):
            target[...] = product(matrix, raw[part]).astype(BF16).reshape(target.shape)
            store.start()

    @pl.when(step == 2 * steps_x + 1)
    def _():
        values = tokens_ref[...].astype(F32)
        scale = lax.rsqrt(jnp.mean(values * values, -1, keepdims=True) + 1e-05)
        unit = values * scale
        grad = grad_du[0:rows, :]
        widths = jnp.concatenate([widths_ref[...], jnp.sum(grad * unit, 0, keepdims=True)], 0)
        widths = jnp.concatenate(
            [widths, jnp.zeros((send_tail.shape[1] - widths.shape[0], width), F32)], 0
        )
        split_lanes(send_tail, widths.astype(BF16))
        store_tail.start()
        inner = grad * gains_ref[0:1, :]
        load_mid.wait()
        gy[...] += scale * (inner - unit * jnp.mean(inner * unit, -1, keepdims=True))
        store_tokens = pltpu.make_async_copy(gy, gradtok_hbm, load_sems.at[2])
        store_tokens.start()
        at = 3 * gated_all.shape[1]
        scan.wait()
        totals[at : at + 32, :] = fold_rows(got_scan, width)
        load_normed.wait()
        input_local.wait()
        for copy in input_copies:
            copy.wait()
        lhs = jnp.concatenate([got_in[k] for k in range(devices)], 1)
        totals[0:in_part, :] = product(
            lhs, everyone[...].reshape(devices * rows, width)
        ).astype(BF16)
        store_totals = pltpu.make_async_copy(totals, totals_hbm, load_sems.at[3])
        store_totals.start()
        for line in lines:
            line.wait()
        for k, copy in enumerate(near_grads.copies):
            pl.when(me % 2 == 0)(lambda copy=copy: copy.wait_send())
            source = (me + devices - k - 1) % devices
            pl.when(source % 2 == 0)(lambda copy=copy: copy.wait_recv())
        pl.when(me % 2 == 0)(lambda: near_grads.local.wait())
        store_back.wait()
        store_tail.wait()
        store_tokens.wait()
        store_totals.wait()
        for store in store_sends:
            store.wait()


def backward_plane(
    proj, step_w, vec, u_act, gate_in, out_w, grad_mix, step_size, mixed, scan_w, x_inner, in_t,
    tokens, gains, grad_widths, grad_mid, gated, normed_all, hist, rows_0, grads_0, raws,
    goals,
):
    rows, channels = u_act.shape
    width = grad_mix.shape[1]
    cols = proj.shape[1]
    rank, state = step_w.shape[0], vec.shape[0] - 8
    devices = lax.axis_size("expert")
    part = channels // devices
    tile, small = channels // 2, channels // 6
    big = BLOCK * state
    pack_rows, tail_rows = cols + 8, grad_widths.shape[0] + 7
    fixed = lambda i: (0, 0)
    first = lambda i: jnp.minimum(i, 1)
    second = lambda i: jnp.clip(i - 2, 0, 5)
    once = pl.Buffered(1)
    slots = jax.ShapeDtypeStruct(rows_0.shape, BF16)
    raw = jax.ShapeDtypeStruct(raws[0].shape, BF16)
    goal = jax.ShapeDtypeStruct(goals[0].shape, jnp.int32)
    total_rows = 3 * part + 32
    pair = jax.ShapeDtypeStruct((2, 2, big, tile), BF16)
    third = lambda i: jnp.maximum(i - 8, 0)
    scan_pack = (devices, rank + state + 8, part)
    back_pack = (devices, pack_rows, part)
    tail_pack = (devices, tail_rows, width // devices)
    return pl.pallas_call(
        backward_kernel,
        grid=(14,),
        in_specs=[
            pl.BlockSpec((rows, cols), fixed),
            pl.BlockSpec((rank, tile), lambda i: (0, first(i))),
            pl.BlockSpec((state, tile), lambda i: (0, first(i))),
            pl.BlockSpec((8, tile), lambda i: (state // 8, first(i))),
            pl.BlockSpec((rows, tile), lambda i: (0, first(i))),
            pl.BlockSpec((rows, tile), lambda i: (0, first(i))),
            pl.BlockSpec((tile, width), lambda i: (first(i), 0), pipeline_mode=once),
            pl.BlockSpec((rows, width), fixed, pipeline_mode=once),
            pl.BlockSpec((rows, tile), lambda i: (0, first(i))),
            pl.BlockSpec((rows, tile), lambda i: (0, first(i))),
            pl.BlockSpec((small, cols), lambda i: (second(i), 0)),
            pl.BlockSpec((rows, small), lambda i: (0, second(i))),
            pl.BlockSpec((8, small), lambda i: (state // 8, second(i))),
            pl.BlockSpec((small, width), lambda i: (third(i), 0)),
            pl.BlockSpec((small, width), lambda i: (third(i) + 6, 0)),
            pl.BlockSpec((rows, small), lambda i: (0, second(i))),
            pl.BlockSpec((rows, width), fixed, pipeline_mode=once),
            pl.BlockSpec(gains.shape, fixed),
            pl.BlockSpec(grad_widths.shape, fixed),
        ] + [FAR] * 14,
        out_specs=[FAR] * 11,
        out_shape=[
            jax.ShapeDtypeStruct((rows, width), F32),
            jax.ShapeDtypeStruct((total_rows, width), BF16),
            jax.ShapeDtypeStruct(back_pack, BF16),
            jax.ShapeDtypeStruct(tail_pack, BF16),
            slots, slots, raw, raw, goal, goal, pair,
        ],
        scratch_shapes=[
            pltpu.VMEM((rows // BLOCK * state, 128), F32),
            pltpu.VMEM((rows, big), BF16),
            pltpu.VMEM((rows, big), BF16),
            pltpu.VMEM((rows + BLOCK, big), F32),
            pltpu.VMEM((rows, big), F32),
            pltpu.VMEM((rows, tile), F32),
            pltpu.VMEM((rows + BLOCK, tile), F32),
            pltpu.VMEM((rows + BLOCK, tile), F32),
            pltpu.VMEM((rows + BLOCK, tile), F32),
            pltpu.VMEM((4, big + state, tile), BF16),
            pltpu.VMEM((2, big, tile), BF16),
            pltpu.VMEM((2, big, tile), BF16),
            pltpu.VMEM((rows, cols), F32),
            pltpu.VMEM((rows, channels), F32),
            pltpu.VMEM((rows, channels), BF16),
            pltpu.VMEM((2 * channels, rows), BF16),
            pltpu.VMEM((devices, 2 * part, rows), BF16),
            pltpu.VMEM((devices, rows, width), BF16),
            pltpu.VMEM(gated.shape, BF16),
            pltpu.VMEM(scan_pack, BF16),
            pltpu.VMEM(scan_pack, BF16),
            pltpu.VMEM((pack_rows, channels), BF16),
            pltpu.VMEM(back_pack, BF16),
            pltpu.VMEM(tail_pack, BF16),
            pltpu.VMEM((total_rows, width), BF16),
            pltpu.VMEM(raw.shape, BF16),
            pltpu.VMEM(goal.shape, jnp.int32),
            pltpu.VMEM(slots.shape, BF16),
            DMA((10,)), DMA((10,)), DMA((4, devices)), DMA((4, devices)), DMA((7, 2)), DMA((7, 2)),
            DMA((5,)), DMA((4,)), DMA((10,)),
        ],
        compiler_params=pltpu.CompilerParams(
            vmem_limit_bytes=VMEM_LIMIT, collective_id=4, has_side_effects=True
        ),
        name="mixer_backward",
    )(
        proj, step_w, vec, vec, u_act, gate_in, out_w, grad_mix, step_size, mixed, scan_w, x_inner,
        vec, in_t, in_t, u_act, tokens, gains, grad_widths, grad_mid, gated, normed_all, hist,
        rows_0, grads_0, *raws, *goals,
    )


def add_groups(rows, grads, rows_t, up_ref, down_ref):
    activated, slope = gelu_parts(product(rows, up_ref[...]))
    grad_pre = (times_transpose(grads, down_ref[...]) * slope).astype(BF16)
    return product(rows_t, grad_pre), contract_rows(activated.astype(BF16), grads)


def flat_rows(refs):
    experts, cap, width = refs[0].shape
    values = [ref[...].reshape(ref.shape[0] * cap, width) for ref in refs]
    return values[0] if len(values) == 1 else jnp.concatenate(values, 0)


def two_grads_kernel(
    up_ref, down_ref, gup_in, gdown_in, rows_1, grads_1, sends_2, left_2, left_3, right_2, right_3,
    goal_l2, goal_l3, goal_r2, goal_r3, back_hbm, tail_hbm,
    gup_ref, gdown_ref, rows_3, grads_3, small_ref,
    rows_t, gup_all, gdown_all, rows_2, grads_2, raw, goal, sends_3, own_back, pair_back, pair_sum,
    far_back, got_tail, small_here, small_all, z_send, z_recv, b_send, b_recv, x_send, x_recv,
    local_sems, load_sems, back_sems,
):
    step = pl.program_id(0)
    tiles = gup_all.shape[0]
    spot = step % tiles
    seconds, thirds = (
        [
            Exchange(
                source.at[k], out, x_send.at[first + k], x_recv.at[first + k],
                local_sems.at[first + k],
            )
            for k, out in enumerate(targets)
        ]
        for first, source, targets in (
            (0, sends_2, (rows_2, grads_2)), (2, sends_3, (rows_3, grads_3))
        )
    )

    small_tail = Exchange(
        tail_hbm, got_tail, x_send.at[4], x_recv.at[4], local_sems.at[4]
    )
    me = lax.axis_index("expert")
    core, chip = me % 2, me // 2
    chips = pair_sum.shape[0]
    to_core = [
        pltpu.make_async_remote_copy(
            back_hbm.at[2 * k + 1 - core], pair_back.at[k], b_send.at[k], b_recv.at[k],
            device_id={"expert": neighbour(1)}, device_id_type=MESH,
        )
        for k in range(chips)
    ]
    own_loads = [
        pltpu.make_async_copy(back_hbm.at[2 * k + core], own_back.at[k], back_sems.at[k])
        for k in range(chips)
    ]
    to_chips = [
        pltpu.make_async_remote_copy(
            pair_sum.at[(chip + k) % chips], far_back.at[k - 1], b_send.at[chips + k - 1],
            b_recv.at[chips + k - 1], device_id={"expert": 2 * ((chip + k) % chips) + core},
            device_id_type=MESH,
        )
        for k in range(1, chips)
    ]
    place, copies = lax.axis_index("dp"), lax.axis_size("dp")
    to_copies = [
        pltpu.make_async_remote_copy(
            small_here, small_all.at[k - 1], z_send.at[k - 1], z_recv.at[k - 1],
            device_id={"dp": (place + k) % copies}, device_id_type=MESH,
        )
        for k in range(1, copies)
    ]

    @pl.when(step == 0)
    def _():
        greet_all()
        for way in seconds:
            way.start()
        for copy in to_core + own_loads:
            copy.start()
        rows_t[...] = flat_rows((rows_1,)).T

    @pl.when(step == 1)
    def _():
        pick(
            ((right_3, goal_r3), (right_2, goal_r2), (left_2, goal_l2), (left_3, goal_l3)), raw,
            goal, load_sems,
        )
        prepare_sends(raw, goal, sends_3)

    @pl.when(step == tiles - 2)
    def _():
        for copy in to_core + own_loads:
            copy.wait()
        pair_sum[...] = (own_back[...].astype(F32) + pair_back[...].astype(F32)).astype(BF16)
        for copy in to_chips:
            copy.start()
        small_tail.start()
        for way in thirds:
            way.start()

    @pl.when(step == 2 * tiles - 3)
    def _():
        small_tail.wait()
        for copy in to_chips:
            copy.wait()
        width = small_here.shape[1]
        back = pair_sum[chip].astype(F32) + jnp.sum(far_back[...].astype(F32), 0)
        small_here[0:32, :] = fold_value(back, width)
        tail = jnp.sum(got_tail[...].astype(F32), 0)
        tail = jnp.concatenate([tail, jnp.zeros((tail.shape[0], width - tail.shape[1]), F32)], 1)
        small_here[32:48, :] = tail.astype(BF16)
        for copy in to_copies:
            copy.start()

    @pl.when(step < tiles)
    def _():
        grad_up, grad_down = add_groups(
            flat_rows((rows_1,)), flat_rows((grads_1,)), rows_t[...], up_ref, down_ref
        )
        gup_all[spot] = (gup_in[...].astype(F32) + grad_up).astype(BF16)
        gdown_all[spot] = (gdown_in[...].astype(F32) + grad_down).astype(BF16)

    @pl.when(step == tiles)
    def _():
        for way in seconds:
            way.wait()
        rows_t[...] = flat_rows((rows_2,)).T

    @pl.when(step >= tiles)
    def _():
        grad_up, grad_down = add_groups(
            flat_rows((rows_2,)), flat_rows((grads_2,)), rows_t[...], up_ref, down_ref
        )
        gup_ref[...] = (gup_all[spot].astype(F32) + grad_up).astype(BF16)
        gdown_ref[...] = (gdown_all[spot].astype(F32) + grad_down).astype(BF16)

    @pl.when(step == 2 * tiles - 1)
    def _():
        for copy in to_copies:
            copy.wait()
        small_ref[...] = small_here[...].astype(F32) + jnp.sum(small_all[...].astype(F32), 0)
        for way in thirds:
            way.wait()


def last_grads_kernel(
    up_ref, down_ref, gup_in, gdown_in, rows_ref, grads_ref, gup_ref, gdown_ref, rows_t
):
    rows, grads = flat_rows((rows_ref,)), flat_rows((grads_ref,))

    @pl.when(pl.program_id(0) == 0)
    def _():
        rows_t[...] = rows.T

    grad_up, grad_down = add_groups(rows, grads, rows_t[...], up_ref, down_ref)
    gup_ref[...] = gup_in[...].astype(F32) + grad_up
    gdown_ref[...] = gdown_in[...].astype(F32) + grad_down


def expert_grads_plane(
    up, down, grad_up, grad_down, rows, grads, sends, raws, goals, back, tail, tile
):
    width, hidden = up.shape
    devices, cap = grads.shape[:2]
    slots = jax.ShapeDtypeStruct(grads.shape, BF16)
    pair = jax.ShapeDtypeStruct(sends.shape, BF16)
    whole = pl.BlockSpec(grads.shape, lambda i: (0, 0, 0))

    def tiles(size):
        return [
            pl.BlockSpec((width, size), lambda i: (0, i)),
            pl.BlockSpec((size, width), lambda i: (i, 0)),
        ]

    def shapes(kind):
        return [
            jax.ShapeDtypeStruct((width, hidden), kind), jax.ShapeDtypeStruct((hidden, width), kind)
        ]

    turned = pltpu.VMEM((width, devices * cap), BF16)
    count = hidden // tile
    again = [
        pl.BlockSpec((width, tile), lambda i: (0, i % count)),
        pl.BlockSpec((tile, width), lambda i: (i % count, 0)),
    ]
    early = [
        pl.BlockSpec((width, tile), lambda i: (0, jnp.minimum(i, count - 1))),
        pl.BlockSpec((tile, width), lambda i: (jnp.minimum(i, count - 1), 0)),
    ]
    late = [
        pl.BlockSpec((width, tile), lambda i: (0, jnp.maximum(i - count, 0))),
        pl.BlockSpec((tile, width), lambda i: (jnp.maximum(i - count, 0), 0)),
    ]
    small = (48, width)
    grad_up, grad_down, rows, grads, small_total = pl.pallas_call(
        two_grads_kernel,
        grid=(2 * count,),
        in_specs=again + early + [whole] * 2 + [FAR] * 11,
        out_specs=late + [FAR] * 2 + [pl.BlockSpec(small, lambda i: (0, 0))],
        out_shape=shapes(BF16) + [slots] * 2 + [jax.ShapeDtypeStruct(small, F32)],
        scratch_shapes=[
            turned,
            pltpu.VMEM((count, width, tile), BF16),
            pltpu.VMEM((count, tile, width), BF16),
            pltpu.VMEM(slots.shape, BF16),
            pltpu.VMEM(slots.shape, BF16),
            pltpu.VMEM(raws[0].shape, BF16),
            pltpu.VMEM(goals[0].shape, jnp.int32),
            pltpu.VMEM(pair.shape, BF16),
            pltpu.VMEM((devices // 2,) + back.shape[1:], BF16),
            pltpu.VMEM((devices // 2,) + back.shape[1:], BF16),
            pltpu.VMEM((devices // 2,) + back.shape[1:], BF16),
            pltpu.VMEM((devices // 2 - 1,) + back.shape[1:], BF16),
            pltpu.VMEM(tail.shape, BF16),
            pltpu.VMEM(small, BF16),
            pltpu.VMEM((3,) + small, BF16),
            DMA((3,)), DMA((3,)), DMA((devices - 1,)), DMA((devices - 1,)), DMA((5, devices)),
            DMA((5, devices)), DMA((5,)), DMA((2,)), DMA((devices // 2,)),
        ],
        compiler_params=remote_params(6),
        name="expert_grads_12",
    )(up, down, grad_up, grad_down, rows, grads, sends, *raws, *goals, back, tail)
    grad_up, grad_down = pl.pallas_call(
        last_grads_kernel,
        grid=(hidden // 768,),
        in_specs=tiles(768) * 2 + [whole] * 2,
        out_specs=tiles(768),
        out_shape=shapes(F32),
        scratch_shapes=[turned],
        compiler_params=pltpu.CompilerParams(vmem_limit_bytes=VMEM_LIMIT),
        name="expert_grads_3",
    )(up, down, grad_up, grad_down, rows, grads)
    return grad_up, grad_down, small_total


def finish_kernel(
    totals_ref, small_ref, in_ref, out_ref, scanw_ref, stepw_ref, decay_ref, conv_ref, router_ref, bias_ref,
    dbias_ref, skip_ref, norm_two_ref, norm_ref,
):
    in_rows, part = in_ref.shape[0], out_ref.shape[0]
    cols, rank, state, taps = (
        scanw_ref.shape[1], stepw_ref.shape[0], decay_ref.shape[0], conv_ref.shape[0]
    )
    experts, slice_w = router_ref.shape
    in_ref[...] = totals_ref[0:in_rows, :].astype(F32)
    out_ref[...] = totals_ref[in_rows : in_rows + part, :].astype(F32)
    at = in_rows + part
    unfolded = []
    for block, quarter in (
        (totals_ref[at : at + 32, :].astype(F32), (rank + state + 8) // 4),
        (small_ref[0:32, :], (cols + 8) // 4),
    ):
        unfolded.append(
            jnp.concatenate(
                [block[:quarter, k * part : (k + 1) * part] for k in range(4)], 0
            )
        )
    scan, back = unfolded
    stepw_ref[...] = scan[:rank]
    decay_ref[...] = scan[rank : rank + state]
    scanw_ref[...] = back[:cols].T
    conv_ref[...] = back[cols : cols + taps]
    bias_ref[...] = back[cols + taps]
    dbias_ref[...] = scan[rank + state]
    skip_ref[...] = scan[rank + state + 1]
    tail = small_ref[32:48, :][:, :slice_w]
    router_ref[...] = tail[:experts]
    norm_two_ref[...] = tail[experts]
    norm_ref[...] = tail[experts + 1]


def finish(totals, small, in_rows, part, cols, rank, state, taps, experts, slice_w):
    here = pl.BlockSpec(memory_space=pltpu.VMEM)
    return pl.pallas_call(
        finish_kernel,
        in_specs=[here] * 2,
        out_specs=[here] * 12,
        out_shape=[
            jax.ShapeDtypeStruct(shape, F32)
            for shape in (
                (in_rows, totals.shape[1]), (part, totals.shape[1]), (part, cols), (rank, part),
                (state, part), (taps, part), (experts, slice_w), (part,), (part,), (part,),
                (slice_w,), (slice_w,),
            )
        ],
        compiler_params=pltpu.CompilerParams(vmem_limit_bytes=VMEM_LIMIT),
        name="finish",
    )(totals, small)


def gather(value):
    return lax.all_gather(value, "expert", axis=0, tiled=True)


def exchange(value):
    return lax.all_to_all(value, "expert", split_axis=0, concat_axis=0, tiled=True)


def shards(
    tokens, lengths, routes, slot_index, mixer_norm, in_weight, conv_weight, conv_bias,
    scan_weight, step_weight, step_bias, decay_log, skip_gain, out_weight, moe_norm, router_weight,
    up_weight, down_weight, cotangent,
):
    devices = lax.axis_size("expert")
    rows, width = tokens.shape[1:]
    part = out_weight.shape[0]
    channels = part * devices
    cols = scan_weight.shape[1]
    rank, state, taps = step_weight.shape[0], decay_log.shape[1], conv_weight.shape[0]
    experts = router_weight.shape[1]
    split = devices // experts
    slice_w = width // devices
    tile = channels // 2

    on_plane = devices == 8 and split == 1 and lax.axis_size("dp") == 4
    in_t, decay_t, router_t = in_weight.T, decay_log.T, router_weight.T
    up, down = up_weight[0], down_weight[0]
    hidden = up.shape[1]
    if on_plane:
        (
            normed_low, x_inner, u_act, gate_in, proj, step_size, mixed, gated, mid, step_full, vec,
            router_t, gains, scan_full, in_t, out_full, normed_all, hist,
        ) = forward_plane(
            tokens[0], in_t, scan_weight, step_weight, decay_t, conv_weight, conv_bias, step_bias,
            skip_gain, mixer_norm, moe_norm, router_t, out_weight,
        )
        in_t = in_t.reshape(2 * channels, width)
        scan_full = scan_full.reshape(channels, cols)
        out_full = out_full.reshape(channels, width)
        layer_out, grad_mid, grad_mix, grad_widths, rows_0, grads_0, *line = expert_layer(
            lengths, mid, gains, router_t, routes, slot_index, cotangent[0], up, down
        )
        raws, goals, grad_up, grad_down = line[:4], line[4:8], line[8], line[9]
        (
            tokens_grad, totals, back_parts, tail_parts, rows_1, grads_1, left_3, right_3, goal_l3,
            goal_r3, sends,
        ) = backward_plane(
            proj, step_full, vec, u_act, gate_in, out_full, grad_mix, step_size, mixed, scan_full,
            x_inner, in_t, tokens[0], gains, grad_widths, grad_mid, gated, normed_all, hist, rows_0,
            grads_0, raws, goals,
        )
        totals = lax.psum(totals, "dp")
        grad_up, grad_down, small_total = expert_grads_plane(
            up, down, grad_up, grad_down, rows_1, grads_1,
            sends.reshape((2,) + rows_1.shape), (raws[2], left_3, raws[3], right_3),
            (goals[2], goal_l3, goals[3], goal_r3), back_parts, tail_parts, 512,
        )
        in_total, out_total, scan_w_total, step_w_total, decay_total, conv_total, *rest = finish(
            totals, small_total, 2 * part, part, cols, rank, state, taps, experts, slice_w
        )
        router_total, vector_totals, norm_totals = rest[0], rest[1:4], rest[4:]
    else:
        vectors = jnp.stack([conv_bias, step_bias, skip_gain])
        norms = jnp.stack([mixer_norm, moe_norm])
        spare = jnp.zeros((8 - taps - 3, part), BF16)
        columns = jnp.concatenate([step_weight, decay_t, conv_weight, vectors, spare], 0)
        across = jnp.concatenate([router_t, norms, jnp.zeros((6, slice_w), BF16)], 0)
        in_t, scan_full, columns, across = (
            lax.all_gather(value, "expert") for value in (in_t, scan_weight, columns, across)
        )
        columns = columns.transpose(1, 0, 2).reshape(columns.shape[1], channels)
        across = across.transpose(1, 0, 2).reshape(across.shape[1], width)
        step_full, rest = columns[:rank], columns[rank:].astype(F32)
        vec = jnp.concatenate([-jnp.exp(rest[:state]), rest[state:]], 0)
        router_t, gains = across[:experts], across[experts:].astype(F32)
        in_t = in_t.reshape(2 * channels, width)
        scan_full = scan_full.reshape(channels, cols)
        normed_low, x_inner, u_act, gate_in, proj = front(
            tokens[0], gains, in_t, vec, scan_full, tile
        )
        live = (jnp.arange(rows, dtype=jnp.int32) < lengths[0]).astype(F32)[:, None]
        routes_col, slots_col = routes[0][:, None], slot_index[0][:, None]
        router, gain_second = router_t.T, gains[1:2]
        out_full = gather(out_weight)
        step_size, mixed, gated, hist, mid = scan_forward(
            proj, step_full, vec, u_act, gate_in, out_full, tokens[0], tile
        )
        send_rows, send_grads, normed_two, probs = router_step(
            mid, gain_second, router, routes_col, routes, slot_index, live, cotangent[0]
        )

        def to_pieces(value):
            wide = jnp.broadcast_to(value[:, None], (experts, split) + value.shape[1:])
            return exchange(wide.reshape(devices, CAP, width))

        def from_pieces(value):
            value = exchange(value).reshape(experts, split, CAP, width)
            if split == 1:
                return value[:, 0]
            return jnp.sum(value.astype(F32), 1).astype(BF16)

        some = min(512, hidden // 3)
        rows_in = to_pieces(send_rows)
        grads_in = to_pieces(send_grads)
        partial_out, slope = expert_out(rows_in, up, down, some)
        back_rows = from_pieces(partial_out)
        back_grads = from_pieces(expert_back(grads_in, up, down, slope, some))
        all_rows = lax.all_gather(rows_in, "dp")
        layer_out, grad_mid, grad_mix, grad_widths = combine_step(
            mid, gain_second, router, routes_col, slots_col, live, cotangent[0], probs, normed_two,
            back_rows, back_grads,
        )
        grad_mix, all_rows = lax.optimization_barrier((grad_mix, all_rows))
        all_grads = lax.all_gather(grads_in, "dp")
        out_parts = contract_rows(gated, grad_mix).astype(BF16).reshape(devices, part, width)
        grad_out_w = jnp.sum(exchange(out_parts).astype(F32), 0).astype(BF16)
        grad_u, grad_gate, scan_parts, grad_proj = scan_backward(
            proj, step_full, vec, u_act, gate_in, out_full, grad_mix, step_size, mixed, hist, tile,
            devices,
        )
        scan_small = jnp.sum(exchange(scan_parts).astype(F32), 0).astype(BF16)
        grad_x, back_parts, width_parts, tokens_grad = mixer_back(
            grad_proj, scan_full, grad_u, x_inner, vec, grad_gate, in_t, u_act, tokens[0], gains,
            grad_mid, grad_widths, tile, devices,
        )
        back_small = jnp.sum(exchange(back_parts).astype(F32), 0).astype(BF16)
        width_small = jnp.sum(exchange(width_parts).astype(F32), 0).astype(BF16)
        normed_all = gather(normed_low)
        grad_in_parts = exchange(jnp.concatenate([grad_x, grad_gate], 0))
        grad_in_w = contract_rows(
            grad_in_parts.reshape(devices * rows, 2 * part), normed_all
        ).astype(BF16)
        totals = (grad_in_w, grad_out_w, scan_small, back_small, width_small)
        totals, all_grads = lax.optimization_barrier((totals, all_grads))
        totals = lax.psum(totals, "dp")
        in_total, out_total, scan_small, back_small, width_small = (
            t.astype(F32) for t in totals
        )
        grad_up, grad_down = expert_grads(all_rows, all_grads, up, down, min(256, hidden))
        scan_w_total, conv_total = back_small[:cols].T, back_small[cols : cols + taps]
        step_w_total, decay_total = scan_small[:rank], scan_small[rank : rank + state]
        vector_totals = (
            back_small[cols + taps], scan_small[rank + state], scan_small[rank + state + 1]
        )
        router_total = width_small[:experts]
        norm_totals = (width_small[experts], width_small[experts + 1])
    return (
        layer_out[None],
        tokens_grad[None],
        norm_totals[1],
        in_total.T,
        conv_total,
        vector_totals[0],
        scan_w_total,
        step_w_total,
        vector_totals[1],
        decay_total.T,
        vector_totals[2],
        out_total,
        norm_totals[0],
        router_total.T,
        grad_up[None],
        grad_down[None],
    )


def solution(mesh):
    in_specs = (
        P(("dp", "expert"), None, None),
        P(("dp", "expert")),
        P(("dp", "expert"), None),
        P(("dp", "expert"), None),
        P("expert"),
        P(None, "expert"),
        P(None, "expert"),
        P("expert"),
        P("expert", None),
        P(None, "expert"),
        P("expert"),
        P("expert", None),
        P("expert"),
        P("expert", None),
        P("expert"),
        P("expert", None),
        P("expert", None, None),
        P("expert", None, None),
        P(("dp", "expert"), None, None),
    )
    out_specs = (
        P(("dp", "expert"), None, None),
        P(("dp", "expert"), None, None),
        P("expert"),
        P(None, "expert"),
        P(None, "expert"),
        P("expert"),
        P("expert", None),
        P(None, "expert"),
        P("expert"),
        P("expert", None),
        P("expert"),
        P("expert", None),
        P("expert"),
        P("expert", None),
        P("expert", None, None),
        P("expert", None, None),
    )
    return jax.shard_map(shards, mesh=mesh, in_specs=in_specs, out_specs=out_specs, check_vma=False)
```

```python
from functools import partial

import jax
import jax.numpy as jnp
from jax import lax
from jax.experimental import pallas as pl
from jax.experimental.pallas import tpu as pltpu
from jax.sharding import PartitionSpec as P

CAP = 64
BLOCK = 16
LOG2E = 1.4426950408889634
F32 = jnp.float32
BF16 = jnp.bfloat16
VMEM_LIMIT = 56 * 1024 * 1024


def product(left, right):
    return jnp.dot(left, right, preferred_element_type=F32)


def contract_rows(left, right):
    return lax.dot_general(left, right, (((0,), (0,)), ((), ())), preferred_element_type=F32)


def times_transpose(left, right):
    return lax.dot_general(left, right, (((1,), (1,)), ((), ())), preferred_element_type=F32)


def exact_product(left, right):
    return jnp.dot(left, right, preferred_element_type=F32, precision=lax.Precision.HIGHEST)


def iota(shape, axis):
    return lax.broadcasted_iota(jnp.int32, shape, axis)


def sigmoid(values):
    return 1.0 / (1.0 + jnp.exp(-values))


def softplus(values):
    return jnp.maximum(values, 0.0) + jnp.log1p(jnp.exp(-jnp.abs(values)))


class Rows:
    def __init__(self, ref, first, count):
        self.ref, self.first = ref, first
        self.shape = (count, ref.shape[1])

    def __getitem__(self, index):
        low, high = (0, self.shape[0]) if index is Ellipsis else (index[0].start, index[0].stop)
        return self.ref[self.first + low : self.first + high, :]


def conv_rows(misc_ref):
    return Rows(misc_ref, 0, 4), Rows(misc_ref, 4, 1)


def scan_rows(misc_ref):
    return Rows(misc_ref, 5, 1), Rows(misc_ref, 6, 1)


def split_lanes(out_ref, value):
    parts, _, width = out_ref.shape
    for part in range(parts):
        out_ref[part] = value[:, part * width : (part + 1) * width]


def shift_rows(values, offset):
    rows = values.shape[0]
    if offset == 0:
        return values
    rolled = pltpu.roll(values, offset % rows, 0)
    row = iota(values.shape, 0)
    keep = row >= offset if offset > 0 else row < rows + offset
    return jnp.where(keep, rolled, 0.0)


def two_parts(values):
    high = values.astype(BF16)
    low = (values - high.astype(F32)).astype(BF16)
    return high, low


def spread_rows(proj_block, first, state):
    rows, width = proj_block.shape
    big = rows * state
    pick = (iota((big, rows), 0) // state == iota((big, rows), 1)).astype(F32)
    copied = exact_product(pick, proj_block)
    lane = iota((big, width), 1)
    own = lane == first + iota((big, width), 0) % state
    column = jnp.sum(jnp.where(own, copied, 0.0), axis=1, keepdims=True)
    return jnp.broadcast_to(column, (big, 128))


def diagonal_blocks(proj_block, first, state):
    rows, width = proj_block.shape
    big = rows * state
    place = (iota((width, big), 0) == first + iota((width, big), 1) % state).astype(BF16)
    own = iota((rows, big), 0) == iota((rows, big), 1) // state
    parts = [
        jnp.where(own, product(part, place), 0.0).astype(BF16) for part in two_parts(proj_block)
    ]
    return jnp.concatenate(parts, 0)


def front_kernel(
    tokens_ref, gain_ref, wx_ref, wg_ref, misc_ref, scanw_ref,
    normed_ref, xin_ref, u_ref, gate_ref, proj_ref,
):
    step = pl.program_id(0)
    conv_ref, bias_ref = conv_rows(misc_ref)

    @pl.when(step == 0)
    def _():
        values = tokens_ref[...].astype(F32)
        scale = lax.rsqrt(jnp.mean(values * values, -1, keepdims=True) + 1e-05)
        normed_ref[...] = (values * scale * gain_ref[0:1, :]).astype(BF16)
        proj_ref[...] = jnp.zeros_like(proj_ref)

    normed = normed_ref[...]
    x_inner = times_transpose(normed, wx_ref[...])
    gate_ref[...] = times_transpose(normed, wg_ref[...])
    xin_ref[...] = x_inner
    taps = conv_ref.shape[0]
    summed = bias_ref[...] + conv_ref[taps - 1 : taps, :] * x_inner
    for back in range(1, taps):
        tap = taps - 1 - back
        summed = summed + conv_ref[tap : tap + 1, :] * shift_rows(x_inner, back)
    u_act = summed * sigmoid(summed)
    u_ref[...] = u_act
    proj_ref[...] += product(u_act.astype(BF16), scanw_ref[...])


def front(tokens, gains, in_t, vec, scan_w, tile):
    rows, width = tokens.shape
    channels = scan_w.shape[0]
    cols = scan_w.shape[1]
    steps = channels // tile
    return pl.pallas_call(
        front_kernel,
        grid=(steps,),
        in_specs=[
            pl.BlockSpec((rows, width), lambda i: (0, 0)),
            pl.BlockSpec(gains.shape, lambda i: (0, 0)),
            pl.BlockSpec((tile, width), lambda i: (i, 0)),
            pl.BlockSpec((tile, width), lambda i: (i + steps, 0)),
            pl.BlockSpec((8, tile), lambda i: ((vec.shape[0] - 8) // 8, i)),
            pl.BlockSpec((tile, cols), lambda i: (i, 0)),
        ],
        out_specs=[
            pl.BlockSpec((rows, width), lambda i: (0, 0)),
            pl.BlockSpec((rows, tile), lambda i: (0, i)),
            pl.BlockSpec((rows, tile), lambda i: (0, i)),
            pl.BlockSpec((rows, tile), lambda i: (0, i)),
            pl.BlockSpec((rows, cols), lambda i: (0, 0)),
        ],
        out_shape=[
            jax.ShapeDtypeStruct((rows, width), BF16),
            jax.ShapeDtypeStruct((rows, channels), F32),
            jax.ShapeDtypeStruct((rows, channels), F32),
            jax.ShapeDtypeStruct((rows, channels), F32),
            jax.ShapeDtypeStruct((rows, cols), F32),
        ],
        compiler_params=pltpu.CompilerParams(vmem_limit_bytes=VMEM_LIMIT),
        name="mixer_front",
    )(tokens, gains, in_t, in_t, vec, scan_w)


def scan_prepare(proj_ref, b_wide, c_blocks, b_first, c_first, state):
    blocks = proj_ref.shape[0] // BLOCK
    big = BLOCK * state

    def build(block, carry):
        part = proj_ref[pl.ds(pl.multiple_of(block * BLOCK, BLOCK), BLOCK), :]
        b_wide[pl.ds(pl.multiple_of(block * big, big), big), :] = spread_rows(part, b_first, state)
        c_blocks[pl.ds(pl.multiple_of(block * 2 * BLOCK, 2 * BLOCK), 2 * BLOCK), :] = (
            diagonal_blocks(part, c_first, state)
        )
        return carry

    lax.fori_loop(0, blocks, build, 0)


def scan_tile(
    proj_ref, stepw_ref, decay_ref, misc_ref, u_ref, gate_ref, step_ref, mixed_ref, hist_ref,
    b_wide, c_blocks, du, scanned, between,
):
    rank, state = stepw_ref.shape[0], decay_ref.shape[0]
    rows, tile = u_ref.shape
    blocks = rows // BLOCK
    big = BLOCK * state
    dbias_ref, skip_ref = scan_rows(misc_ref)
    u_act = u_ref[...]
    step_size = softplus(
        product(proj_ref[:, :rank].astype(BF16), stepw_ref[...]) + dbias_ref[...]
    )
    step_ref[...] = step_size
    du[...] = step_size * u_act
    decay = decay_ref[...] * LOG2E
    hist_ref[0:state, :] = jnp.zeros((state, tile), BF16)

    def run_block(block, held):
        base = pl.multiple_of(block * BLOCK, BLOCK)
        steps_now = step_ref[pl.ds(base, BLOCK), :]
        du_now = du[pl.ds(base, BLOCK), :]
        wide_base = pl.multiple_of(block * big, big)
        for t in range(BLOCK):
            b_now = b_wide[pl.ds(wide_base + t * state, state), :]
            fade = jnp.exp2(steps_now[t : t + 1, :] * decay)
            fresh = du_now[t : t + 1, :] * jnp.concatenate([b_now] * (tile // 128), 1)
            held = fade * held + fresh
            hist_ref[pl.ds(wide_base + (t + 1) * state, state), :] = held.astype(BF16)
        weights = c_blocks[pl.ds(pl.multiple_of(block * 2 * BLOCK, 2 * BLOCK), 2 * BLOCK), :]
        both = product(weights, hist_ref[pl.ds(wide_base + state, big), :])
        scanned[pl.ds(base, BLOCK), :] = both[:BLOCK] + both[BLOCK:]
        return held

    held = jnp.zeros((state, tile), F32)
    held = lax.fori_loop(0, blocks // 2, run_block, held)
    between(0)
    lax.fori_loop(blocks // 2, blocks, run_block, held)
    between(1)
    mixed = scanned[...] + skip_ref[...] * u_act
    mixed_ref[...] = mixed
    gate_in = gate_ref[...]
    return (mixed * (gate_in * sigmoid(gate_in))).astype(BF16)


def scan_kernel(
    proj_ref, stepw_ref, decay_ref, misc_ref, u_ref, gate_ref, outw_ref, tokens_ref,
    step_ref, mixed_ref, gated_ref, hist_ref, mid_ref,
    b_wide, c_blocks, du, scanned,
):
    rank, state = stepw_ref.shape[0], decay_ref.shape[0]

    @pl.when(pl.program_id(0) == 0)
    def _():
        mid_ref[...] = tokens_ref[...].astype(F32)
        scan_prepare(proj_ref, b_wide, c_blocks, rank, rank + state, state)

    gated = scan_tile(
        proj_ref, stepw_ref, decay_ref, misc_ref, u_ref, gate_ref, step_ref, mixed_ref, hist_ref,
        b_wide, c_blocks, du, scanned, lambda half: None,
    )
    gated_ref[...] = gated
    mid_ref[...] += product(gated, outw_ref[...])


def scan_forward(proj, step_w, vec, u_act, gate_in, out_w, tokens, tile):
    rows, channels = u_act.shape
    width = tokens.shape[1]
    cols = proj.shape[1]
    rank, state = step_w.shape[0], vec.shape[0] - 8
    steps = channels // tile
    hist_rows = (rows + 1) * state
    column = lambda i: (0, i)
    fixed = lambda i: (0, 0)
    return pl.pallas_call(
        scan_kernel,
        grid=(steps,),
        in_specs=[
            pl.BlockSpec((rows, cols), fixed),
            pl.BlockSpec((rank, tile), column),
            pl.BlockSpec((state, tile), column),
            pl.BlockSpec((8, tile), lambda i: ((vec.shape[0] - 8) // 8, i)),
            pl.BlockSpec((rows, tile), column),
            pl.BlockSpec((rows, tile), column),
            pl.BlockSpec((tile, width), lambda i: (i, 0)),
            pl.BlockSpec((rows, width), fixed),
        ],
        out_specs=[
            pl.BlockSpec((rows, tile), column),
            pl.BlockSpec((rows, tile), column),
            pl.BlockSpec((rows, tile), column),
            pl.BlockSpec((hist_rows, tile), column),
            pl.BlockSpec((rows, width), fixed),
        ],
        out_shape=[
            jax.ShapeDtypeStruct((rows, channels), F32),
            jax.ShapeDtypeStruct((rows, channels), F32),
            jax.ShapeDtypeStruct((rows, channels), BF16),
            jax.ShapeDtypeStruct((hist_rows, channels), BF16),
            jax.ShapeDtypeStruct((rows, width), F32),
        ],
        scratch_shapes=[
            pltpu.VMEM((rows * state, 128), F32),
            pltpu.VMEM((rows * 2, BLOCK * state), BF16),
            pltpu.VMEM((rows, tile), F32),
            pltpu.VMEM((rows, tile), F32),
        ],
        compiler_params=pltpu.CompilerParams(vmem_limit_bytes=VMEM_LIMIT),
        name="scan_forward",
    )(proj, step_w, vec, vec, u_act, gate_in, out_w, tokens)


def scan_back_kernel(*refs):
    scan_back_tile(lambda half: None, split_lanes, *refs)


def scan_back_tile(
    between, put_gate, proj_ref, stepw_ref, decay_ref, misc_ref, u_ref, gate_ref, outw_ref, gradmix_ref,
    step_ref, mixed_ref, hist_ref,
    gradu_ref, gradgate_ref, pack_ref, gradproj_ref,
    c_wide, b_blocks, b_sums, c_sums, gy, du, g_hist, w_hist, grad_du, grad_step,
):
    tile_id = pl.program_id(0)
    cols, rank = proj_ref.shape[1], stepw_ref.shape[0]
    state = decay_ref.shape[0]
    rows, tile = u_ref.shape
    blocks = rows // BLOCK
    big = BLOCK * state

    @pl.when(tile_id == 0)
    def _():
        gradproj_ref[...] = jnp.zeros_like(gradproj_ref)
        b_sums[...] = jnp.zeros_like(b_sums)
        c_sums[...] = jnp.zeros_like(c_sums)
        scan_prepare(proj_ref, c_wide, b_blocks, rank + state, rank, state)

    skip_ref = scan_rows(misc_ref)[1]
    grad_gated = times_transpose(gradmix_ref[...], outw_ref[...])
    gate_in = gate_ref[...]
    gate_sig = sigmoid(gate_in)
    grad_mixed = grad_gated * (gate_in * gate_sig)
    put_gate(
        gradgate_ref,
        (grad_gated * mixed_ref[...] * (gate_sig * (1.0 + gate_in * (1.0 - gate_sig)))).astype(BF16),
    )
    u_act = u_ref[...]
    step_size = step_ref[...]
    gy[...] = grad_mixed
    du[...] = step_size * u_act
    grad_skip = jnp.sum(grad_mixed * u_act, 0, keepdims=True)
    rate = decay_ref[...]
    decay = rate * LOG2E
    sums = (iota((BLOCK, big), 0) == iota((BLOCK, big), 1) // state).astype(BF16)

    def run_block(turn, carry):
        carried, log_sum = carry
        block = blocks - 1 - turn
        base = pl.multiple_of(block * BLOCK, BLOCK)
        wide_base = pl.multiple_of(block * big, big)
        steps_now = step_ref[pl.ds(base, BLOCK), :]
        gy_now = gy[pl.ds(base, BLOCK), :]
        for t in range(BLOCK - 1, -1, -1):
            c_now = c_wide[pl.ds(wide_base + t * state, state), :]
            step_now = steps_now[t : t + 1, :]
            fade = jnp.exp2(step_now * decay)
            grad = gy_now[t : t + 1, :] * jnp.concatenate([c_now] * (tile // 128), 1) + carried
            g_hist[t * state : (t + 1) * state, :] = grad.astype(BF16)
            carried = fade * grad
            before = hist_ref[pl.ds(wide_base + t * state, state), :].astype(F32)
            weighted = carried * before * rate
            w_hist[t * state : (t + 1) * state, :] = weighted.astype(BF16)
            log_sum = log_sum + weighted * step_now
        grads = g_hist[...]
        both = product(
            b_blocks[pl.ds(pl.multiple_of(block * 2 * BLOCK, 2 * BLOCK), 2 * BLOCK), :], grads
        )
        grad_du[pl.ds(base, BLOCK), :] = both[:BLOCK] + both[BLOCK:]
        grad_step[pl.ds(base, BLOCK), :] = product(sums, w_hist[...])
        b_sums[pl.ds(base, BLOCK), :] += times_transpose(
            du[pl.ds(base, BLOCK), :].astype(BF16), grads
        )
        c_sums[pl.ds(base, BLOCK), :] += times_transpose(
            gy_now.astype(BF16), hist_ref[pl.ds(wide_base + state, big), :]
        )
        return carried, log_sum

    zeros = jnp.zeros((state, tile), F32)
    held = lax.fori_loop(0, blocks // 2, run_block, (zeros, zeros))
    between(0)
    _, log_sum = lax.fori_loop(blocks // 2, blocks, run_block, held)
    between(1)
    full_du = grad_du[...]
    gradu_ref[...] = full_du * step_size + skip_ref[...] * gy[...]
    grad_size = grad_step[...] + full_du * u_act
    grad_pre = grad_size * (1.0 - jnp.exp(-step_size))
    grad_low = grad_pre.astype(BF16)
    grad_step_w = contract_rows(proj_ref[:, :rank].astype(BF16), grad_low)
    packed = jnp.concatenate(
        [grad_step_w, log_sum, jnp.sum(grad_pre, 0, keepdims=True), grad_skip, zeros[:6]], 0
    )
    split_lanes(pack_ref, packed.astype(BF16))
    gradproj_ref[:, :rank] += times_transpose(grad_low, stepw_ref[...])

    @pl.when(tile_id == pl.num_programs(0) - 1)
    def _():
        own = iota((rows, big), 0) % BLOCK == iota((rows, big), 1) // state
        lane = iota((big, cols), 1)
        slot = iota((big, cols), 0) % state
        total = gradproj_ref[...]
        for sums_ref, first in ((b_sums, rank), (c_sums, rank + state)):
            place = (lane == first + slot).astype(F32)
            total = total + exact_product(jnp.where(own, sums_ref[...], 0.0), place)
        gradproj_ref[...] = total


def scan_backward(
    proj, step_w, vec, u_act, gate_in, out_w, grad_mix, step_size, mixed, hist, tile, devices
):
    rows, channels = u_act.shape
    gate_parts = tile * devices // (2 * channels)
    pack_parts = tile * devices // channels
    pack_rows = step_w.shape[0] + vec.shape[0]
    width = grad_mix.shape[1]
    cols = proj.shape[1]
    rank, state = step_w.shape[0], vec.shape[0] - 8
    steps = channels // tile
    big = BLOCK * state
    column = lambda i: (0, i)
    fixed = lambda i: (0, 0)
    return pl.pallas_call(
        scan_back_kernel,
        grid=(steps,),
        in_specs=[
            pl.BlockSpec((rows, cols), fixed),
            pl.BlockSpec((rank, tile), column),
            pl.BlockSpec((state, tile), column),
            pl.BlockSpec((8, tile), lambda i: ((vec.shape[0] - 8) // 8, i)),
            pl.BlockSpec((rows, tile), column),
            pl.BlockSpec((rows, tile), column),
            pl.BlockSpec((tile, width), lambda i: (i, 0)),
            pl.BlockSpec((rows, width), fixed),
            pl.BlockSpec((rows, tile), column),
            pl.BlockSpec((rows, tile), column),
            pl.BlockSpec((hist.shape[0], tile), column),
        ],
        out_specs=[
            pl.BlockSpec((rows, tile), column),
            pl.BlockSpec((gate_parts, rows, tile // gate_parts), lambda i: (i, 0, 0)),
            pl.BlockSpec((pack_parts, pack_rows, tile // pack_parts), lambda i: (i, 0, 0)),
            pl.BlockSpec((rows, cols), fixed),
        ],
        out_shape=[
            jax.ShapeDtypeStruct((rows, channels), F32),
            jax.ShapeDtypeStruct((devices // 2, rows, 2 * channels // devices), BF16),
            jax.ShapeDtypeStruct((devices, pack_rows, channels // devices), BF16),
            jax.ShapeDtypeStruct((rows, cols), F32),
        ],
        scratch_shapes=[
            pltpu.VMEM((rows * state, 128), F32),
            pltpu.VMEM((rows * 2, big), BF16),
            pltpu.VMEM((rows, big), F32),
            pltpu.VMEM((rows, big), F32),
            pltpu.VMEM((rows, tile), F32),
            pltpu.VMEM((rows, tile), F32),
            pltpu.VMEM((big, tile), BF16),
            pltpu.VMEM((big, tile), BF16),
            pltpu.VMEM((rows, tile), F32),
            pltpu.VMEM((rows, tile), F32),
        ],
        compiler_params=pltpu.CompilerParams(vmem_limit_bytes=VMEM_LIMIT),
        name="scan_backward",
    )(proj, step_w, vec, vec, u_act, gate_in, out_w, grad_mix, step_size, mixed, hist)


def back_kernel(
    gradproj_ref, scanw_ref, gradu_ref, xin_ref, misc_ref, gradgate_ref, wx_ref, wg_ref,
    u_ref, tokens_ref, gain_ref, gradmid_ref, widths_ref,
    gradx_ref, pack_ref, tail_ref, gradtok_ref,
    total,
):
    tile_id = pl.program_id(0)

    @pl.when(tile_id == 0)
    def _():
        total[...] = jnp.zeros_like(total)

    conv_ref, bias_ref = conv_rows(misc_ref)
    grad_proj = gradproj_ref[...].astype(BF16)
    grad_u = gradu_ref[...] + times_transpose(grad_proj, scanw_ref[...])
    pieces = [contract_rows(grad_proj, u_ref[...].astype(BF16))]
    x_inner = xin_ref[...]
    taps = conv_ref.shape[0]
    shifted = [shift_rows(x_inner, taps - 1 - tap) for tap in range(taps)]
    summed = bias_ref[...]
    for tap in range(taps):
        summed = summed + conv_ref[tap : tap + 1, :] * shifted[tap]
    sig = sigmoid(summed)
    grad_sum = grad_u * (sig * (1.0 + summed * (1.0 - sig)))
    grad_x = jnp.zeros_like(x_inner)
    for tap in range(taps):
        pieces.append(jnp.sum(grad_sum * shifted[tap], 0, keepdims=True))
        grad_x = grad_x + conv_ref[tap : tap + 1, :] * shift_rows(grad_sum, tap + 1 - taps)
    pieces.append(jnp.sum(grad_sum, 0, keepdims=True))
    pieces.append(jnp.zeros((pack_ref.shape[1] - grad_proj.shape[1] - taps - 1, x_inner.shape[1]), F32))
    split_lanes(pack_ref, jnp.concatenate(pieces, 0).astype(BF16))
    grad_x = grad_x.astype(BF16)
    split_lanes(gradx_ref, grad_x)
    grad_gate = jnp.concatenate([gradgate_ref[k] for k in range(gradgate_ref.shape[0])], 1)
    total[...] += product(grad_x, wx_ref[...]) + product(grad_gate, wg_ref[...])

    @pl.when(tile_id == pl.num_programs(0) - 1)
    def _():
        values = tokens_ref[...].astype(F32)
        scale = lax.rsqrt(jnp.mean(values * values, -1, keepdims=True) + 1e-05)
        unit = values * scale
        grad = total[...]
        widths = jnp.concatenate([widths_ref[...], jnp.sum(grad * unit, 0, keepdims=True)], 0)
        widths = jnp.concatenate(
            [widths, jnp.zeros((tail_ref.shape[1] - widths.shape[0], widths.shape[1]), F32)], 0
        )
        split_lanes(tail_ref, widths.astype(BF16))
        inner = grad * gain_ref[0:1, :]
        gradtok_ref[...] = gradmid_ref[...] + scale * (
            inner - unit * jnp.mean(inner * unit, -1, keepdims=True)
        )


def mixer_back(
    grad_proj, scan_w, grad_u, x_inner, vec, grad_gate, in_t, u_act, tokens, gains, grad_mid,
    grad_widths, tile, devices,
):
    rows, channels = u_act.shape
    gate_parts = tile * devices // (2 * channels)
    pack_parts = tile * devices // channels
    pack_rows = scan_w.shape[1] + 8
    tail_rows = grad_widths.shape[0] + 7
    width = tokens.shape[1]
    cols = scan_w.shape[1]
    steps = channels // tile
    column = lambda i: (0, i)
    fixed = lambda i: (0, 0)
    return pl.pallas_call(
        back_kernel,
        grid=(steps,),
        in_specs=[
            pl.BlockSpec((rows, cols), fixed),
            pl.BlockSpec((tile, cols), lambda i: (i, 0)),
            pl.BlockSpec((rows, tile), column),
            pl.BlockSpec((rows, tile), column),
            pl.BlockSpec((8, tile), lambda i: ((vec.shape[0] - 8) // 8, i)),
            pl.BlockSpec((gate_parts, rows, tile // gate_parts), lambda i: (i, 0, 0)),
            pl.BlockSpec((tile, width), lambda i: (i, 0)),
            pl.BlockSpec((tile, width), lambda i: (i + steps, 0)),
            pl.BlockSpec((rows, tile), column),
            pl.BlockSpec((rows, width), fixed),
            pl.BlockSpec(gains.shape, fixed),
            pl.BlockSpec((rows, width), fixed),
            pl.BlockSpec(grad_widths.shape, fixed),
        ],
        out_specs=[
            pl.BlockSpec((gate_parts, rows, tile // gate_parts), lambda i: (i, 0, 0)),
            pl.BlockSpec((pack_parts, pack_rows, tile // pack_parts), lambda i: (i, 0, 0)),
            pl.BlockSpec((devices, tail_rows, width // devices), lambda i: (0, 0, 0)),
            pl.BlockSpec((rows, width), fixed),
        ],
        out_shape=[
            jax.ShapeDtypeStruct((devices // 2, rows, 2 * channels // devices), BF16),
            jax.ShapeDtypeStruct((devices, pack_rows, channels // devices), BF16),
            jax.ShapeDtypeStruct((devices, tail_rows, width // devices), BF16),
            jax.ShapeDtypeStruct((rows, width), F32),
        ],
        scratch_shapes=[pltpu.VMEM((rows, width), F32)],
        compiler_params=pltpu.CompilerParams(vmem_limit_bytes=VMEM_LIMIT),
        name="mixer_back",
    )(
        grad_proj, scan_w, grad_u, x_inner, vec, grad_gate, in_t, in_t, u_act, tokens, gains,
        grad_mid, grad_widths,
    )


def gelu_parts(values):
    weight = jnp.exp(values * values * -0.5)
    scaled = jnp.abs(values) * 0.7071067811865476
    ratio = 1.0 / (1.0 + 0.3275911 * scaled)
    series = 1.061405429 * ratio - 1.453152027
    series = series * ratio + 1.421413741
    series = series * ratio - 0.284496736
    series = series * ratio + 0.254829592
    tail = (0.5 * ratio) * series * weight
    below = jnp.where(values >= 0.0, 1.0 - tail, tail)
    return values * below, below + values * weight * 0.3989422804014327


def router_kernel(
    mid_ref, gain_ref, router_ref, routes_col_ref, routes_row_ref, slots_row_ref, live_ref, cot_ref,
    sendr_ref, sendg_ref, normed_ref, probs_ref,
):
    mid = mid_ref[...]
    rows = mid.shape[0]
    experts = router_ref.shape[1]
    scale = lax.rsqrt(jnp.mean(mid * mid, -1, keepdims=True) + 1e-05)
    normed = (mid * scale * gain_ref[...]).astype(BF16)
    normed_ref[...] = normed
    logits = product(normed, router_ref[...])
    weights = jnp.exp(logits - jnp.max(logits, -1, keepdims=True))
    probs = weights / jnp.sum(weights, -1, keepdims=True)
    probs_ref[...] = probs
    chosen = (routes_col_ref[...] == iota((rows, experts), 1)).astype(F32)
    gate = jnp.sum(probs * chosen, 1, keepdims=True)
    grads = (gate * (cot_ref[...].astype(F32) * live_ref[...])).astype(BF16)
    slot = iota((experts * CAP, rows), 0)
    dispatch = (
        (routes_row_ref[...] == slot // CAP) & (slots_row_ref[...] == slot % CAP)
    ).astype(BF16)
    width = mid.shape[1]
    sendr_ref[...] = product(dispatch, normed).astype(BF16).reshape(experts, CAP, width)
    sendg_ref[...] = product(dispatch, grads).astype(BF16).reshape(experts, CAP, width)


def router_step(mid, gain, router, routes_col, routes_row, slots_row, live, cotangent):
    rows, width = mid.shape
    experts = router.shape[1]
    return pl.pallas_call(
        router_kernel,
        out_shape=[
            jax.ShapeDtypeStruct((experts, CAP, width), BF16),
            jax.ShapeDtypeStruct((experts, CAP, width), BF16),
            jax.ShapeDtypeStruct((rows, width), BF16),
            jax.ShapeDtypeStruct((rows, experts), F32),
        ],
        compiler_params=pltpu.CompilerParams(vmem_limit_bytes=VMEM_LIMIT),
        name="router_step",
    )(mid, gain, router, routes_col, routes_row, slots_row, live, cotangent)


def expert_out_kernel(rows_ref, up_ref, down_ref, out_ref, slope_ref, total):
    step = pl.program_id(0)
    pieces, cap, width = rows_ref.shape
    rows = rows_ref[...].reshape(pieces * cap, width)

    @pl.when(step == 0)
    def _():
        total[...] = jnp.zeros_like(total)

    activated, slope = gelu_parts(product(rows, up_ref[...]))
    slope_ref[...] = slope.astype(BF16)
    total[...] += product(activated.astype(BF16), down_ref[...])

    @pl.when(step == pl.num_programs(0) - 1)
    def _():
        out_ref[...] = total[...].astype(BF16).reshape(pieces, cap, width)


def expert_out(rows, up, down, tile):
    pieces, cap, width = rows.shape
    hidden = up.shape[1]
    fixed = lambda i: (0, 0, 0)
    return pl.pallas_call(
        expert_out_kernel,
        grid=(hidden // tile,),
        in_specs=[
            pl.BlockSpec(rows.shape, fixed),
            pl.BlockSpec((width, tile), lambda i: (0, i)),
            pl.BlockSpec((tile, width), lambda i: (i, 0)),
        ],
        out_specs=[
            pl.BlockSpec(rows.shape, fixed),
            pl.BlockSpec((pieces * cap, tile), lambda i: (0, i)),
        ],
        out_shape=[
            jax.ShapeDtypeStruct(rows.shape, BF16),
            jax.ShapeDtypeStruct((pieces * cap, hidden), BF16),
        ],
        scratch_shapes=[pltpu.VMEM((pieces * cap, width), F32)],
        compiler_params=pltpu.CompilerParams(vmem_limit_bytes=VMEM_LIMIT),
        name="expert_out",
    )(rows, up, down)


def expert_back_kernel(grads_ref, up_ref, down_ref, slope_ref, out_ref, total):
    step = pl.program_id(0)
    pieces, cap, width = grads_ref.shape
    grads = grads_ref[...].reshape(pieces * cap, width)

    @pl.when(step == 0)
    def _():
        total[...] = jnp.zeros_like(total)

    slope = slope_ref[...].astype(F32)
    grad_pre = (times_transpose(grads, down_ref[...]) * slope).astype(BF16)
    total[...] += times_transpose(grad_pre, up_ref[...])

    @pl.when(step == pl.num_programs(0) - 1)
    def _():
        out_ref[...] = total[...].astype(BF16).reshape(pieces, cap, width)


def expert_back(grads, up, down, slope, tile):
    pieces, cap, width = grads.shape
    hidden = up.shape[1]
    fixed = lambda i: (0, 0, 0)
    return pl.pallas_call(
        expert_back_kernel,
        grid=(hidden // tile,),
        in_specs=[
            pl.BlockSpec(grads.shape, fixed),
            pl.BlockSpec((width, tile), lambda i: (0, i)),
            pl.BlockSpec((tile, width), lambda i: (i, 0)),
            pl.BlockSpec((pieces * cap, tile), lambda i: (0, i)),
        ],
        out_specs=pl.BlockSpec(grads.shape, fixed),
        out_shape=jax.ShapeDtypeStruct(grads.shape, BF16),
        scratch_shapes=[pltpu.VMEM((pieces * cap, width), F32)],
        compiler_params=pltpu.CompilerParams(vmem_limit_bytes=VMEM_LIMIT),
        name="expert_back",
    )(grads, up, down, slope)


def expert_grads_kernel(chunks, rows_ref, grads_ref, up_ref, down_ref, gup_ref, gdown_ref, rows_t):
    chunk = pl.program_id(1)
    groups, pieces, cap, width = rows_ref.shape
    count = groups * pieces * cap
    rows = rows_ref[...].reshape(count, width)
    grads = grads_ref[...].reshape(count, width)

    @pl.when((pl.program_id(0) == 0) | (chunks > 1))
    def _():
        rows_t[...] = rows.T

    activated, slope = gelu_parts(product(rows, up_ref[...]))
    grad_pre = (times_transpose(grads, down_ref[...]) * slope).astype(BF16)
    grad_up = product(rows_t[...], grad_pre)
    grad_down = contract_rows(activated.astype(BF16), grads)

    @pl.when(chunk == 0)
    def _():
        gup_ref[...] = grad_up
        gdown_ref[...] = grad_down

    if chunks > 1:

        @pl.when(chunk > 0)
        def _():
            gup_ref[...] += grad_up
            gdown_ref[...] += grad_down


def expert_grads(rows, grads, up, down, tile):
    groups, pieces, cap, width = rows.shape
    hidden = up.shape[1]
    together = max(1, min(groups, 32 // pieces))
    chunks = groups // together
    some = pl.BlockSpec((together, pieces, cap, width), lambda i, j: (j, 0, 0, 0))
    return pl.pallas_call(
        partial(expert_grads_kernel, chunks),
        grid=(hidden // tile, chunks),
        in_specs=[
            some,
            some,
            pl.BlockSpec((width, tile), lambda i, j: (0, i)),
            pl.BlockSpec((tile, width), lambda i, j: (i, 0)),
        ],
        out_specs=[
            pl.BlockSpec((width, tile), lambda i, j: (0, i)),
            pl.BlockSpec((tile, width), lambda i, j: (i, 0)),
        ],
        out_shape=[
            jax.ShapeDtypeStruct((width, hidden), F32),
            jax.ShapeDtypeStruct((hidden, width), F32),
        ],
        scratch_shapes=[pltpu.VMEM((width, together * pieces * cap), BF16)],
        compiler_params=pltpu.CompilerParams(vmem_limit_bytes=VMEM_LIMIT),
        name="expert_grads",
    )(rows, grads, up, down)


def combine_kernel(
    mid_ref, gain_ref, router_ref, routes_ref, slots_ref, live_ref, cot_ref, probs_ref, normed_ref,
    backr_ref, backg_ref, out_ref, gradmid_ref, gradmix_ref, widths_ref,
):
    mid = mid_ref[...]
    rows, width = mid.shape
    experts = router_ref.shape[1]
    routes = routes_ref[...]
    chosen = (routes == iota((rows, experts), 1)).astype(F32)
    probs = probs_ref[...]
    gate = jnp.sum(probs * chosen, 1, keepdims=True)
    live = live_ref[...]
    slot = iota((rows, experts * CAP), 1)
    collect = ((routes == slot // CAP) & (slots_ref[...] == slot % CAP)).astype(BF16)
    expert_sum = product(collect, backr_ref[...].reshape(experts * CAP, width))
    out_ref[...] = (live * (mid + gate * expert_sum)).astype(BF16)
    grad_out = cot_ref[...].astype(F32) * live
    grad_gate = jnp.sum(grad_out * expert_sum, 1, keepdims=True)
    grad_logits = (probs * (chosen * grad_gate - gate * grad_gate)).astype(BF16)
    grad_router = contract_rows(grad_logits, normed_ref[...])
    grad = product(collect, backg_ref[...].reshape(experts * CAP, width))
    grad = grad + times_transpose(grad_logits, router_ref[...])
    scale = lax.rsqrt(jnp.mean(mid * mid, -1, keepdims=True) + 1e-05)
    unit = mid * scale
    widths_ref[...] = jnp.concatenate([grad_router, jnp.sum(grad * unit, 0, keepdims=True)], 0)
    inner = grad * gain_ref[...]
    grad_mid = grad_out + scale * (inner - unit * jnp.mean(inner * unit, -1, keepdims=True))
    gradmid_ref[...] = grad_mid
    gradmix_ref[...] = grad_mid.astype(BF16)


def combine_step(mid, gain, router, routes, slots, live, cotangent, probs, normed, backr, backg):
    rows, width = mid.shape
    return pl.pallas_call(
        combine_kernel,
        out_shape=[
            jax.ShapeDtypeStruct((rows, width), BF16),
            jax.ShapeDtypeStruct((rows, width), F32),
            jax.ShapeDtypeStruct((rows, width), BF16),
            jax.ShapeDtypeStruct((router.shape[1] + 1, width), F32),
        ],
        compiler_params=pltpu.CompilerParams(vmem_limit_bytes=VMEM_LIMIT),
        name="combine_step",
    )(mid, gain, router, routes, slots, live, cotangent, probs, normed, backr, backg)


MESH = pl.DeviceIdType.MESH


def neighbour(bit):
    me = lax.axis_index("expert")
    return me + (1 - 2 * ((me // bit) % 2)) * bit


def greet_send(line=True):
    devices, copies = lax.axis_size("expert"), lax.axis_size("dp")
    me, place = lax.axis_index("expert"), lax.axis_index("dp")
    barrier = pltpu.get_barrier_semaphore()
    for k in range(1, devices):
        pl.semaphore_signal(
            barrier, inc=1, device_id={"expert": (me + k) % devices}, device_id_type=MESH
        )
    if line:

        @pl.when(place < copies - 1)
        def _():
            pl.semaphore_signal(barrier, inc=1, device_id={"dp": place + 1}, device_id_type=MESH)

        @pl.when(place > 0)
        def _():
            pl.semaphore_signal(barrier, inc=1, device_id={"dp": place - 1}, device_id_type=MESH)


def greet_wait(line=True):
    devices, copies = lax.axis_size("expert"), lax.axis_size("dp")
    place = lax.axis_index("dp")
    barrier = pltpu.get_barrier_semaphore()
    ends = (place == 0) | (place == copies - 1)
    if line:
        pl.when(ends)(lambda: pl.semaphore_wait(barrier, devices))
        pl.when(jnp.logical_not(ends))(lambda: pl.semaphore_wait(barrier, devices + 1))
    else:
        pl.semaphore_wait(barrier, devices - 1)


def greet(line=True):
    greet_send(line)
    greet_wait(line)


class Exchange:
    def __init__(self, source, target, send_sems, recv_sems, local_sem):
        devices, me = lax.axis_size("expert"), lax.axis_index("expert")
        self.copies = []
        for k in range(1, devices):
            peer = (me + k) % devices
            self.copies.append(
                pltpu.make_async_remote_copy(
                    source.at[peer], target.at[me], send_sems.at[k], recv_sems.at[k],
                    device_id={"expert": peer}, device_id_type=MESH,
                )
            )
        self.local = pltpu.make_async_copy(source.at[me], target.at[me], local_sem)

    def start(self):
        for copy in self.copies:
            copy.start()
        self.local.start()

    def wait(self):
        self.local.wait()
        for copy in self.copies:
            copy.wait()


class Line:
    def __init__(self, stage, from_left, from_right, next_left, next_right, send_sems, recv_sems):
        place = lax.axis_index("dp")
        last = lax.axis_size("dp") - 1
        self.right = pltpu.make_async_remote_copy(
            from_left, next_left, send_sems.at[0], recv_sems.at[0],
            device_id={"dp": jnp.minimum(place + 1, last)}, device_id_type=MESH,
        )
        self.left = pltpu.make_async_remote_copy(
            from_right, next_right, send_sems.at[1], recv_sems.at[1],
            device_id={"dp": jnp.maximum(place - 1, 0)}, device_id_type=MESH,
        )
        self.send_right = (place >= stage - 1) & (place < last)
        self.send_left = (last - place >= stage - 1) & (place > 0)
        self.get_left = place >= stage
        self.get_right = last - place >= stage

    def start(self):
        pl.when(self.send_right)(lambda: self.right.start())
        pl.when(self.send_left)(lambda: self.left.start())

    def wait(self):
        pl.when(self.send_right)(lambda: self.right.wait_send())
        pl.when(self.send_left)(lambda: self.left.wait_send())
        pl.when(self.get_left)(lambda: self.right.wait_recv())
        pl.when(self.get_right)(lambda: self.left.wait_recv())


def as_column(row):
    return jnp.broadcast_to(row.astype(F32), (8, row.shape[1])).T[:, 0:1].astype(jnp.int32)


def dispatch_matrix(goal, experts):
    slot = iota((experts * CAP, goal.shape[1]), 0)
    return (goal[0:1, :] == slot).astype(BF16)


def expert_layer_kernel(
    length_ref, mid_ref, gains_ref, router_ref, routes_ref, slots_ref, cot_ref, up_hbm, down_hbm,
    out_ref, gradmid_ref, gradmix_ref, widths_ref, rows_out, grads_out,
    left_1, right_1, left_2, right_2, goal_l1, goal_r1, goal_l2, goal_r2, gup_hbm, gdown_hbm,
    raw, goal, up_ref, down_ref, send_r, send_g, got_r, got_g, slope_ref, total, give_r, give_g,
    back_r, back_g, probs_ref, act_ref, rows_t, gup_ref, gdown_ref,
    weight_sems, send_sems, recv_sems, local_sems, line_send, line_recv, out_sems, grad_sems,
):
    tile = 512
    rows, width = mid_ref.shape
    experts = router_ref.shape[0]
    hidden = up_ref.shape[1]
    load_up = pltpu.make_async_copy(up_hbm, up_ref, weight_sems.at[0])
    load_down = pltpu.make_async_copy(down_hbm, down_ref, weight_sems.at[1])
    greet_send()
    load_up.start()
    load_down.start()

    ways = [
        Exchange(source, target, send_sems.at[k], recv_sems.at[k], local_sems.at[k])
        for k, (source, target) in enumerate(
            [(send_r, got_r), (send_g, got_g), (give_r, back_r), (give_g, back_g)]
        )
    ]
    lines = [
        Line(stage, *buffers, line_send.at[k], line_recv.at[k])
        for k, (stage, buffers) in enumerate(
            [(1, (raw.at[part], raw.at[part], left_1.at[part], right_1.at[part])) for part in (0, 1)]
            + [(1, (goal, goal, goal_l1, goal_r1))]
            + [
                (2, (left_1.at[part], right_1.at[part], left_2.at[part], right_2.at[part]))
                for part in (0, 1)
            ]
            + [(2, (goal_l1, goal_r1, goal_l2, goal_r2))]
        )
    ]
    gain = gains_ref[1:2, :]
    live = (iota((rows, 1), 0) < length_ref[0]).astype(F32)
    routes, slots = as_column(routes_ref[...]), as_column(slots_ref[...])
    mid = mid_ref[...]
    scale = lax.rsqrt(jnp.mean(mid * mid, -1, keepdims=True) + 1e-05)
    normed = (mid * scale * gain).astype(BF16)
    raw[0] = normed
    slots_row = slots_ref[...]
    target = jnp.where(slots_row < CAP, routes_ref[...] * CAP + slots_row, -1)
    goal[...] = jnp.broadcast_to(target, goal.shape)
    dispatch = dispatch_matrix(goal, experts)
    send_r[...] = product(dispatch, normed).astype(BF16).reshape(experts, CAP, width)
    greet_wait()
    ways[0].start()
    for k in (0, 2):
        lines[k].start()
    logits = times_transpose(normed, router_ref[...])
    weights = jnp.exp(logits - jnp.max(logits, -1, keepdims=True))
    probs = weights / jnp.sum(weights, -1, keepdims=True)
    probs_ref[...] = probs
    chosen = (routes == iota((rows, experts), 1)).astype(F32)
    gate = jnp.sum(probs * chosen, 1, keepdims=True)
    grads = (gate * (cot_ref[...].astype(F32) * live)).astype(BF16)
    raw[1] = grads
    send_g[...] = product(dispatch, grads).astype(BF16).reshape(experts, CAP, width)
    ways[1].start()
    lines[1].start()

    load_up.wait()
    load_down.wait()
    ways[0].wait()
    for k in (0, 2):
        lines[k].wait()
        lines[k + 3].start()
    keep_rows = pltpu.make_async_copy(got_r, rows_out, out_sems.at[0])
    keep_rows.start()
    total[...] = jnp.zeros_like(total)

    def forward(step, carry):
        at = pl.ds(pl.multiple_of(step * tile, tile), tile)
        inputs = got_r[...].reshape(experts * CAP, width)
        activated, slope = gelu_parts(product(inputs, up_ref[:, at]))
        slope_ref[:, at] = slope.astype(BF16)
        activated = activated.astype(BF16)
        act_ref[:, at] = activated
        total[...] += product(activated, down_ref[at, :])
        return carry

    lax.fori_loop(0, hidden // tile, forward, 0)
    give_r[...] = total[...].astype(BF16).reshape(experts, CAP, width)
    ways[2].start()
    ways[1].wait()
    lines[1].wait()
    lines[4].start()
    keep_grads = pltpu.make_async_copy(got_g, grads_out, out_sems.at[1])
    keep_grads.start()
    total[...] = jnp.zeros_like(total)

    def backward(step, carry):
        at = pl.ds(pl.multiple_of(step * tile, tile), tile)
        outputs = got_g[...].reshape(experts * CAP, width)
        slope = slope_ref[:, at].astype(F32)
        grad_pre = (times_transpose(outputs, down_ref[at, :]) * slope).astype(BF16)
        slope_ref[:, at] = grad_pre
        total[...] += times_transpose(grad_pre, up_ref[:, at])
        return carry

    lax.fori_loop(0, hidden // tile, backward, 0)
    give_g[...] = total[...].astype(BF16).reshape(experts, CAP, width)
    ways[3].start()

    rows_t[...] = got_r[...].reshape(experts * CAP, width).T
    stores = []
    for step in range(hidden // tile):
        spot = step % 2
        at = pl.ds(step * tile, tile)
        if step >= 2:
            for store in stores[2 * (step - 2) : 2 * (step - 1)]:
                store.wait()
        gup_ref[spot] = product(rows_t[...], slope_ref[:, at]).astype(BF16)
        gdown_ref[spot] = contract_rows(
            act_ref[:, at], got_g[...].reshape(experts * CAP, width)
        ).astype(BF16)
        stores += [
            pltpu.make_async_copy(gup_ref.at[spot], gup_hbm.at[:, at], grad_sems.at[0, spot]),
            pltpu.make_async_copy(gdown_ref.at[spot], gdown_hbm.at[at], grad_sems.at[1, spot]),
        ]
        for store in stores[-2:]:
            store.start()

    chosen = (routes == iota((rows, experts), 1)).astype(F32)
    probs = probs_ref[...]
    gate = jnp.sum(probs * chosen, 1, keepdims=True)
    slot = iota((rows, experts * CAP), 1)
    collect = ((routes == slot // CAP) & (slots == slot % CAP)).astype(BF16)
    ways[2].wait()
    expert_sum = product(collect, back_r[...].reshape(experts * CAP, width))
    mid = mid_ref[...]
    out_ref[...] = (live * (mid + gate * expert_sum)).astype(BF16)
    grad_out = cot_ref[...].astype(F32) * live
    grad_gate = jnp.sum(grad_out * expert_sum, 1, keepdims=True)
    grad_logits = (probs * (chosen * grad_gate - gate * grad_gate)).astype(BF16)
    grad_router = contract_rows(grad_logits, raw[0])
    from_logits = product(grad_logits, router_ref[...])
    scale = lax.rsqrt(jnp.mean(mid * mid, -1, keepdims=True) + 1e-05)
    unit = mid * scale
    ways[3].wait()
    grad = product(collect, back_g[...].reshape(experts * CAP, width)) + from_logits
    widths_ref[...] = jnp.concatenate([grad_router, jnp.sum(grad * unit, 0, keepdims=True)], 0)
    inner = grad * gain
    grad_mid = grad_out + scale * (inner - unit * jnp.mean(inner * unit, -1, keepdims=True))
    gradmid_ref[...] = grad_mid
    gradmix_ref[...] = grad_mid.astype(BF16)
    for store in stores[-4:]:
        store.wait()
    keep_rows.wait()
    keep_grads.wait()
    for k in (3, 4, 5):
        lines[k].wait()


def expert_layer(lengths, mid, gains, router, routes, slots, cotangent, up, down):
    rows, width = mid.shape
    experts = router.shape[0]
    hidden = up.shape[1]
    buffer = (experts, CAP, width)
    here = pl.BlockSpec(memory_space=pltpu.VMEM)
    far = pl.BlockSpec(memory_space=pl.ANY)
    blocks = jax.ShapeDtypeStruct(buffer, BF16)
    raw = jax.ShapeDtypeStruct((2, rows, width), BF16)
    goal = jax.ShapeDtypeStruct((8, rows), jnp.int32)
    dma = pltpu.SemaphoreType.DMA
    return pl.pallas_call(
        expert_layer_kernel,
        in_specs=[pl.BlockSpec(memory_space=pltpu.SMEM)] + [here] * 6 + [far] * 2,
        out_specs=[here] * 4 + [far] * 12,
        out_shape=[
            jax.ShapeDtypeStruct((rows, width), BF16),
            jax.ShapeDtypeStruct((rows, width), F32),
            jax.ShapeDtypeStruct((rows, width), BF16),
            jax.ShapeDtypeStruct((experts + 1, width), F32),
        ] + [blocks] * 2 + [raw] * 4 + [goal] * 4 + [
            jax.ShapeDtypeStruct(up.shape, BF16),
            jax.ShapeDtypeStruct(down.shape, BF16),
        ],
        scratch_shapes=[
            pltpu.VMEM(raw.shape, BF16),
            pltpu.VMEM(goal.shape, jnp.int32),
            pltpu.VMEM(up.shape, BF16),
            pltpu.VMEM(down.shape, BF16),
        ] + [pltpu.VMEM(buffer, BF16)] * 4 + [
            pltpu.VMEM((experts * CAP, hidden), BF16),
            pltpu.VMEM((experts * CAP, width), F32),
        ] + [pltpu.VMEM(buffer, BF16)] * 4 + [
            pltpu.VMEM((rows, experts), F32),
            pltpu.VMEM((experts * CAP, hidden), BF16),
            pltpu.VMEM((width, experts * CAP), BF16),
            pltpu.VMEM((2, width, 512), BF16),
            pltpu.VMEM((2, 512, width), BF16),
            dma((2,)), dma((4, experts)), dma((4, experts)), dma((4,)), dma((6, 2)), dma((6, 2)),
            dma((2,)), dma((2, 2)),
        ],
        compiler_params=pltpu.CompilerParams(
            vmem_limit_bytes=VMEM_LIMIT, collective_id=1, has_side_effects=True
        ),
        name="expert_layer",
    )(lengths, mid, gains, router, routes, slots, cotangent, up, down)


class PlaneGather:
    def __init__(self, source, target, send_sems, recv_sems, local_sem):
        me = lax.axis_index("expert")
        core, side, above = neighbour(1), neighbour(2), neighbour(4)
        far = side + above - me
        rows = target.shape[1]
        first, second = pl.ds(0, rows // 2), pl.ds(rows // 2, rows - rows // 2)
        every = pl.ds(0, rows)

        def send(k, block, owner, part, device):
            return pltpu.make_async_remote_copy(
                block, target.at[owner, part], send_sems.at[k], recv_sems.at[k],
                device_id={"expert": device}, device_id_type=MESH,
            )

        self.copies = [
            send(0, source.at[first], me, first, side),
            send(1, source.at[second], me, second, side),
            send(2, source.at[first], me, first, above),
            send(3, source.at[second], me, second, above),
            send(4, target.at[side, first], side, first, above),
            send(5, target.at[above, second], above, second, side),
            send(6, source, me, every, core),
            send(7, target.at[side], side, every, core),
            send(8, target.at[above], above, every, core),
            send(9, target.at[far], far, every, core),
        ]
        self.local = pltpu.make_async_copy(source, target.at[me], local_sem)

    def step(self, number):
        copies = self.copies
        for k in ((), (0, 3), (1, 2), (4, 5), (6, 7, 8, 9))[number]:
            copies[k].wait_recv()
        for k in ((0, 3, 1, 2, 6), (4, 5), (7, 8), (9,), ())[number]:
            copies[k].start()
        if number == 0:
            self.local.start()
        if number == 4:
            self.local.wait()
            for copy in copies:
                copy.wait_send()


def greet_all():
    devices, copies = lax.axis_size("expert"), lax.axis_size("dp")
    me, place = lax.axis_index("expert"), lax.axis_index("dp")
    barrier = pltpu.get_barrier_semaphore()
    for k in range(1, devices):
        pl.semaphore_signal(
            barrier, inc=1, device_id={"expert": (me + k) % devices}, device_id_type=MESH
        )
    for k in range(1, copies):
        pl.semaphore_signal(
            barrier, inc=1, device_id={"dp": (place + k) % copies}, device_id_type=MESH
        )
    pl.semaphore_wait(barrier, devices + copies - 2)


class WideGather:
    def __init__(self, source, target, send_sems, recv_sems, local_sem):
        me, place = lax.axis_index("expert"), lax.axis_index("dp")
        core, side, above = neighbour(1), neighbour(2), neighbour(4)
        far = side + above - me
        odd = place % 2
        partner = place + 1 - 2 * odd
        rows = target.shape[1]
        unit = rows // 6

        def part(start, count):
            return pl.ds(pl.multiple_of(start * unit, unit), count * unit)

        def send(k, block, owner, where, **device):
            return pltpu.make_async_remote_copy(
                block, target.at[owner, where], send_sems.at[k], recv_sems.at[k],
                device_id=device, device_id_type=MESH,
            )

        def forward(k, owner, where, **device):
            return send(k, target.at[owner, where], owner, where, **device)

        outer, inner = part(4 * odd, 2), part(4 * (1 - odd), 2)
        middle = part(2, 2)
        self.copies = [
            send(0, source.at[outer], me, outer, expert=side),
            send(1, source.at[middle], me, middle, expert=side),
            send(2, source.at[inner], me, inner, expert=above),
            send(3, source.at[middle], me, middle, expert=above),
            forward(4, side, outer, expert=above),
            forward(5, side, part(2 + odd, 1), expert=above),
            forward(6, above, inner, expert=side),
            forward(7, above, part(3 - odd, 1), expert=side),
            forward(8, side, outer, dp=partner),
            forward(9, above, inner, dp=partner),
            send(10, source, me, part(0, 6), expert=core),
            forward(11, side, part(2 * odd, 4), expert=core),
            forward(12, above, part(2 - 2 * odd, 4), expert=core),
            forward(13, side, inner, expert=core),
            forward(14, above, outer, expert=core),
            forward(15, far, part(0, 6), expert=core),
        ]
        self.local = pltpu.make_async_copy(source, target.at[me], local_sem)

    def step(self, number):
        copies = self.copies
        for k in ((), (0, 2), (1, 3), (8, 9), (4, 5, 6, 7), (10, 11, 12, 13, 14, 15))[number]:
            copies[k].wait_recv()
        for k in ((0, 2, 1, 3, 10), (4, 6, 8, 9), (5, 7, 11, 12), (13, 14), (15,), ())[number]:
            copies[k].start()
        if number == 0:
            self.local.start()
        if number == 5:
            self.local.wait()
            for copy in copies:
                copy.wait_send()


class Near:
    def __init__(self, own, target, send_sems, recv_sems):
        self.place = lax.axis_index("dp")
        self.last = lax.axis_size("dp") - 1
        self.right = pltpu.make_async_remote_copy(
            own, target, send_sems.at[0], recv_sems.at[0],
            device_id={"dp": jnp.minimum(self.place + 1, self.last)}, device_id_type=MESH,
        )
        self.left = pltpu.make_async_remote_copy(
            own, target, send_sems.at[1], recv_sems.at[1],
            device_id={"dp": jnp.maximum(self.place - 1, 0)}, device_id_type=MESH,
        )

    def start(self):
        pl.when(self.place < self.last)(lambda: self.right.start())
        pl.when(self.place == 1)(lambda: self.left.start())

    def wait(self):
        pl.when(self.place < self.last)(lambda: self.right.wait_send())
        pl.when(self.place == 1)(lambda: self.left.wait_send())
        pl.when(self.place > 0)(lambda: self.right.wait_recv())
        pl.when(self.place == 0)(lambda: self.left.wait_recv())


DMA = pltpu.SemaphoreType.DMA
FAR = pl.BlockSpec(memory_space=pl.ANY)


def remote_params(collective_id):
    return pltpu.CompilerParams(
        vmem_limit_bytes=VMEM_LIMIT, collective_id=collective_id, has_side_effects=True
    )


def columns_of(proj_ref, first, state, target):
    turned = proj_ref[...].T[first : first + state]
    for block in range(proj_ref.shape[0] // BLOCK):
        target[block * state : (block + 1) * state, 0:BLOCK] = turned[
            :, block * BLOCK : (block + 1) * BLOCK
        ]


def diagonals_of(proj_ref, first, state, high_ref, low_ref):
    rows, width = proj_ref.shape
    big = BLOCK * state
    place = (iota((width, big), 0) == first + iota((width, big), 1) % state).astype(BF16)
    own = iota((rows, big), 0) % BLOCK == iota((rows, big), 1) // state
    for part, target in zip(two_parts(proj_ref[...]), (high_ref, low_ref)):
        target[...] = jnp.where(own, product(part, place), 0.0).astype(BF16)


def block_of(ref, block, size):
    return ref[pl.ds(pl.multiple_of(block * size, size), size), :]


def forward_kernel(
    tokens_ref, in_ref, scan_ref, step_w_ref, decay_ref, conv_ref, bias_ref, dbias_ref, skip_ref,
    norm_ref, norm_two_ref, router_ref, outw_ref,
    normed_ref, xin_ref, u_out, gate_out, proj_ref, step_ref, mixed_ref, gated_ref, mid_ref,
    step_full, vec_ref, router_full, gains_ref, scan_full, in_full, outw_all, normed_all, hist_hbm,
    columns, widths, columns_all, widths_all, scan_here, in_here, u_all, gate_all, b_cols, c_high, c_low, du,
    scanned, gated_all, outw_here, ring,
    send_sems, recv_sems, local_sems, ring_sems,
):
    step = pl.program_id(0)
    devices, rank, part = columns_all.shape[0], step_w_ref.shape[0], step_w_ref.shape[1]
    state, taps, experts = decay_ref.shape[0], conv_ref.shape[0], router_ref.shape[0]
    slice_w = widths.shape[1]
    rows, tile = xin_ref.shape
    width = tokens_ref.shape[1]
    big = BLOCK * state
    turns = ring.shape[0]
    last = rows // BLOCK - 1
    small = [
        PlaneGather(source, target, send_sems.at[k], recv_sems.at[k], local_sems.at[k])
        for k, (source, target) in enumerate(
            [(columns, columns_all), (widths, widths_all), (scan_ref, scan_here)]
        )
    ]
    big_gather = WideGather(in_ref, in_here, send_sems.at[3], recv_sems.at[3], local_sems.at[3])
    gather = WideGather(outw_ref, outw_here, send_sems.at[4], recv_sems.at[4], local_sems.at[4])
    normed_gather = PlaneGather(
        normed_ref, normed_all, send_sems.at[5], recv_sems.at[5], local_sems.at[5]
    )
    keep = pltpu.make_async_copy(outw_here, outw_all, local_sems.at[6])
    keep_in = pltpu.make_async_copy(in_here, in_full, local_sems.at[7])
    half = step % 2
    lanes = pl.ds(pl.multiple_of(half * tile, tile), tile)

    @pl.when(step == 0)
    def _():
        spare = columns.shape[0] - rank - state - taps - 3
        columns[...] = jnp.concatenate(
            [
                step_w_ref[...].astype(F32), decay_ref[...].astype(F32), conv_ref[...].astype(F32),
                *(ref[...].astype(F32)[None] for ref in (bias_ref, dbias_ref, skip_ref)),
                jnp.zeros((spare, part), F32),
            ],
            0,
        ).astype(BF16)
        widths[...] = jnp.concatenate(
            [
                router_ref[...].astype(F32),
                *(ref[...].astype(F32)[None] for ref in (norm_ref, norm_two_ref)),
                jnp.zeros((widths.shape[0] - experts - 2, slice_w), F32),
            ],
            0,
        ).astype(BF16)
        greet()
        for number in range(3):
            for one in small:
                one.step(number)
            big_gather.step(number)
        for number in (3, 4):
            for one in small:
                one.step(number)
        big_gather.step(3)
        gather.step(0)
        table = jnp.concatenate([columns_all[k].astype(F32) for k in range(devices)], 1)
        step_full[...] = table[:rank].astype(BF16)
        scan_full[...] = scan_here[...]
        rest = table[rank:]
        vec_ref[0:state, :] = -jnp.exp(rest[:state])
        vec_ref[state : state + 8, :] = rest[state : state + 8]
        across = jnp.concatenate([widths_all[k].astype(F32) for k in range(devices)], 1)
        router_full[...] = across[:experts].astype(BF16)
        gains_ref[...] = across[experts : experts + 8]
        values = tokens_ref[...].astype(F32)
        scale = lax.rsqrt(jnp.mean(values * values, -1, keepdims=True) + 1e-05)
        normed_ref[...] = (values * scale * gains_ref[0:1, :]).astype(BF16)
        proj_ref[...] = jnp.zeros_like(proj_ref)
        big_gather.step(4)
        big_gather.step(5)
        keep_in.start()
        gather.step(1)

    @pl.when(step < 2)
    def _():
        misc = vec_ref[state : state + 8, lanes]
        normed = normed_ref[...]
        own = devices // 4

        def weights(first):
            rows_here = in_here.shape[1]
            return in_here[pl.ds(first + half * own, own)].reshape(own * rows_here, width)

        x_inner = times_transpose(normed, weights(0))
        gate_in = times_transpose(normed, weights(devices // 2))
        gate_out[...] = gate_in
        gate_all[:, lanes] = gate_in
        xin_ref[...] = x_inner
        summed = misc[taps : taps + 1] + misc[taps - 1 : taps] * x_inner
        for back in range(1, taps):
            tap = taps - 1 - back
            summed = summed + misc[tap : tap + 1] * shift_rows(x_inner, back)
        u_act = summed * sigmoid(summed)
        u_out[...] = u_act
        u_all[:, lanes] = u_act
        parts = devices // 2
        scan_rows_here = scan_here[pl.ds(half * parts, parts)].reshape(tile, scan_here.shape[2])
        proj_ref[...] += product(u_act.astype(BF16), scan_rows_here)

    @pl.when(step == 1)
    def _():
        gather.step(2)
        normed_gather.step(0)
        columns_of(proj_ref, rank, state, b_cols)
        diagonals_of(proj_ref, rank + state, state, c_high, c_low)

    def store(spot, block):
        start = pl.multiple_of((block * BLOCK + 1) * state, state)
        return pltpu.make_async_copy(
            ring.at[spot], hist_hbm.at[pl.ds(start, big), lanes], ring_sems.at[spot]
        )

    def sum_states(spot, block):
        high, low = block_of(c_high, block, BLOCK), block_of(c_low, block, BLOCK)
        both = product(jnp.concatenate([high, low], 0), ring[spot])
        return both[:BLOCK] + both[BLOCK:]

    def between(position):
        if position == 1:
            gather.step(3)
            gather.step(4)
        if position == 4:
            gather.step(5)
            keep.start()
            normed_gather.step(1)
            normed_gather.step(2)
        if position == 7:
            normed_gather.step(3)

    @pl.when(step >= 2)
    def _():
        misc = vec_ref[state : state + 8, lanes]
        u_act = u_all[:, lanes]
        step_size = softplus(
            product(proj_ref[:, :rank].astype(BF16), step_full[:, lanes])
            + misc[taps + 1 : taps + 2]
        )
        step_ref[...] = step_size
        du[...] = step_size * u_act
        decay = vec_ref[0:state, lanes] * LOG2E
        ring[turns - 1] = jnp.zeros((big, tile), BF16)
        zero_row = pltpu.make_async_copy(
            ring.at[turns - 1, pl.ds(0, state)], hist_hbm.at[pl.ds(0, state), lanes],
            ring_sems.at[turns],
        )
        zero_row.start()
        zero_row.wait()

        def run_blocks(quarter, held):
            for spot in range(turns):
                block = quarter * turns + spot
                pl.when(quarter > 0)(lambda: store(spot, block).wait())
                base = pl.multiple_of(block * BLOCK, BLOCK)
                before = (spot - 1) % turns
                scanned[pl.ds(base, BLOCK), :] = sum_states(before, jnp.maximum(block - 1, 0))
                steps_now, du_now = block_of(step_ref, block, BLOCK), block_of(du, block, BLOCK)
                b_now = block_of(b_cols, block, state)
                for t in range(BLOCK):
                    b_wide = jnp.broadcast_to(b_now[:, t : t + 1], (state, tile))
                    fade = jnp.exp2(steps_now[t : t + 1, :] * decay)
                    held = fade * held + du_now[t : t + 1, :] * b_wide
                    ring[spot, t * state : (t + 1) * state, :] = held.astype(BF16)
                store(spot, block).start()
            for turn in range(2):
                for count in range(rows // BLOCK // turns):

                    @pl.when((step == turn + 2) & (quarter == count))
                    def _():
                        between(turn * 4 + count)

            return held

        quarters = rows // BLOCK // turns
        lax.fori_loop(0, quarters, run_blocks, jnp.zeros((state, tile), F32))
        scanned[pl.ds(rows, BLOCK), :] = sum_states(turns - 1, last)
        mixed = scanned[pl.ds(BLOCK, rows), :] + misc[taps + 2 : taps + 3] * u_act
        mixed_ref[...] = mixed
        gate_in = gate_all[:, lanes]
        gated = (mixed * (gate_in * sigmoid(gate_in))).astype(BF16)
        gated_ref[...] = gated.T.reshape(gated_ref.shape)
        gated_all[:, lanes] = gated
        for spot in range(turns):
            store(spot, last - turns + 1 + spot).wait()

    @pl.when(step == 3)
    def _():
        weights = outw_here[...].reshape(devices * part, width)
        mid_ref[...] = tokens_ref[...].astype(F32) + product(gated_all[...], weights)
        keep.wait()
        keep_in.wait()
        normed_gather.step(4)


def forward_plane(
    tokens, in_t, scan_w, step_w, decay_t, conv, bias, dbias, skip, norm, norm_two, router_t, out_w
):
    rows, width = tokens.shape
    rank, part = step_w.shape
    cols = scan_w.shape[1]
    devices = lax.axis_size("expert")
    channels = devices * part
    state, experts, slice_w = decay_t.shape[0], router_t.shape[0], router_t.shape[1]
    tile = channels // 2
    hist_rows = (rows + 1) * state
    first = lambda i: jnp.minimum(i, 1)
    second = lambda i: jnp.maximum(i - 2, 0)

    def whole(shape):
        return pl.BlockSpec(shape, lambda i: (0,) * len(shape), pipeline_mode=pl.Buffered(1))

    def kept(shape):
        return pl.BlockSpec(shape, lambda i: (0,) * len(shape))

    def halves(index):
        return pl.BlockSpec((rows, tile), lambda i: (0, index(i)))

    inputs = (
        tokens, in_t, scan_w, step_w, decay_t, conv, bias, dbias, skip, norm, norm_two, router_t
    )
    fixed = [
        ((rank, channels), BF16), ((state + 8, channels), F32), ((experts, width), BF16),
        ((8, width), F32), ((devices, part, cols), BF16),
    ]
    return pl.pallas_call(
        forward_kernel,
        grid=(4,),
        in_specs=[whole(value.shape) for value in inputs] + [FAR],
        out_specs=[
            kept((rows, width)),
            halves(first),
            halves(first),
            halves(first),
            kept((rows, cols)),
            halves(second),
            halves(second),
            pl.BlockSpec((devices // 2, part, rows), lambda i: (second(i), 0, 0)),
            kept((rows, width)),
        ] + [kept(shape) for shape, _ in fixed] + [FAR] * 4,
        out_shape=[
            jax.ShapeDtypeStruct((rows, width), BF16),
            jax.ShapeDtypeStruct((rows, channels), F32),
            jax.ShapeDtypeStruct((rows, channels), F32),
            jax.ShapeDtypeStruct((rows, channels), F32),
            jax.ShapeDtypeStruct((rows, cols), F32),
            jax.ShapeDtypeStruct((rows, channels), F32),
            jax.ShapeDtypeStruct((rows, channels), F32),
            jax.ShapeDtypeStruct((devices, part, rows), BF16),
            jax.ShapeDtypeStruct((rows, width), F32),
        ] + [jax.ShapeDtypeStruct(shape, kind) for shape, kind in fixed] + [
            jax.ShapeDtypeStruct((devices,) + in_t.shape, BF16),
            jax.ShapeDtypeStruct((devices, part, width), BF16),
            jax.ShapeDtypeStruct((devices, rows, width), BF16),
            jax.ShapeDtypeStruct((hist_rows, channels), BF16),
        ],
        scratch_shapes=[
            pltpu.VMEM((rank + state + 8, part), BF16),
            pltpu.VMEM((32, slice_w), BF16),
            pltpu.VMEM((devices, rank + state + 8, part), BF16),
            pltpu.VMEM((devices, 32, slice_w), BF16),
            pltpu.VMEM((devices, part, cols), BF16),
            pltpu.VMEM((devices,) + in_t.shape, BF16),
            pltpu.VMEM((rows, channels), F32),
            pltpu.VMEM((rows, channels), F32),
            pltpu.VMEM((rows // BLOCK * state, 128), F32),
            pltpu.VMEM((rows, BLOCK * state), BF16),
            pltpu.VMEM((rows, BLOCK * state), BF16),
            pltpu.VMEM((rows, tile), F32),
            pltpu.VMEM((rows + BLOCK, tile), F32),
            pltpu.VMEM((rows, channels), BF16),
            pltpu.VMEM((devices, part, width), BF16),
            pltpu.VMEM((4, BLOCK * state, tile), BF16),
            DMA((6, 16)), DMA((6, 16)), DMA((8,)), DMA((5,)),
        ],
        compiler_params=remote_params(3),
        name="mixer_forward",
    )(*inputs, out_w)


def prepare_sends(raw, goal, sends):
    experts, cap, width = sends.shape[1:]
    matrix = dispatch_matrix(goal, experts)
    for part in range(2):
        values = product(matrix, raw[part]).astype(BF16)
        sends[part] = values.reshape(experts, cap, width)


def pick(choices, raw, goal, sems):
    place = lax.axis_index("dp")
    for where, (source, source_goal) in enumerate(choices):

        @pl.when(place == where)
        def _():
            copies = [
                pltpu.make_async_copy(source, raw, sems.at[0]),
                pltpu.make_async_copy(source_goal, goal, sems.at[1]),
            ]
            for copy in copies:
                copy.start()
            for copy in copies:
                copy.wait()


def fold_rows(got_ref, width):
    return fold_value(jnp.sum(got_ref[...].astype(F32), 0), width)


def fold_value(total, width):
    quarter = total.shape[0] // 4
    folded = jnp.concatenate([total[k * quarter : (k + 1) * quarter] for k in range(4)], 1)
    return jnp.concatenate([folded, jnp.zeros((32 - quarter, width), F32)], 0).astype(BF16)


def backward_kernel(
    proj_ref, stepw_ref, decay_ref, misc_ref, u_ref, gate_ref, outw_ref, gradmix_ref, step_ref,
    mixed_ref, scanw_ref, xin_ref, misc_x_ref, wx_ref, wg_ref, u_x_ref, tokens_ref, gains_ref,
    widths_ref,
    gradmid_hbm, gated_hbm, normed_hbm, hist_hbm, rows_0, grads_0, left_1, right_1, left_2, right_2, goal_l1,
    goal_r1, goal_l2, goal_r2,
    gradtok_hbm, totals_hbm, back_hbm, tail_hbm, rows_1, grads_1, left_3, right_3, goal_l3, goal_r3, sends_hbm,
    c_cols, b_high, b_low, b_sums, c_sums, gy, du, grad_du, grad_step, ring, g_ring, w_ring,
    gradproj, gradu_all, gate_all, send_in, got_in, everyone, gated_all, send_scan, got_scan,
    pack_back, send_back, send_tail, totals, raw, goal, send_grads,
    g_send, g_recv, x_send, x_recv, l_send, l_recv, local_sems, ring_sems, load_sems,
):
    step = pl.program_id(0)
    devices, me = lax.axis_size("expert"), lax.axis_index("expert")
    half = devices // 2
    rank, state = stepw_ref.shape[0], decay_ref.shape[0]
    rows, cols = proj_ref.shape
    tile, small_tile, width = u_ref.shape[1], xin_ref.shape[1], tokens_ref.shape[1]
    blocks, big = rows // BLOCK, BLOCK * state
    turns = ring.shape[0]
    quarters = blocks // turns
    in_part = send_in.shape[0] // devices
    channels = half * in_part
    steps_x = channels // small_tile
    mix = PlaneGather(gradmix_ref, everyone, g_send, g_recv, local_sems.at[0])
    gated = Exchange(gated_hbm, gated_all, x_send.at[0], x_recv.at[0], local_sems.at[1])
    scan = Exchange(send_scan, got_scan, x_send.at[1], x_recv.at[1], local_sems.at[2])
    near_grads = Exchange(send_grads, grads_1, x_send.at[2], x_recv.at[2], local_sems.at[3])

    def input_part(device):
        return send_in.at[pl.ds(pl.multiple_of(device * in_part, in_part), in_part)]

    input_copies = [
        pltpu.make_async_remote_copy(
            input_part((me + k) % devices), got_in.at[me], x_send.at[3, k], x_recv.at[3, k],
            device_id={"expert": (me + k) % devices}, device_id_type=MESH,
        )
        for k in range(1, devices)
    ]
    input_local = pltpu.make_async_copy(input_part(me), got_in.at[me], local_sems.at[4])

    def start_some(copies, local, first, last):
        for k, copy in enumerate(copies):
            peer = (me + k + 1) % devices
            pl.when((peer >= first) & (peer < last))(lambda copy=copy: copy.start())
        pl.when((me >= first) & (me < last))(lambda: local.start())

    def start_inputs(first, last):
        start_some(input_copies, input_local, first, last)

    lines = [
        Line(3, left_2, right_2, left_3, right_3, l_send.at[0], l_recv.at[0]),
        Line(3, goal_l2, goal_r2, goal_l3, goal_r3, l_send.at[1], l_recv.at[1]),
        Near(rows_0, rows_1, l_send.at[2], l_recv.at[2]),
        Near(
            grads_0.at[pl.ds(half, half)], grads_1.at[pl.ds(half, half)], l_send.at[3], l_recv.at[3]
        ),
    ]
    load_normed = pltpu.make_async_copy(normed_hbm, everyone, load_sems.at[0])
    load_mid = pltpu.make_async_copy(gradmid_hbm, gy, load_sems.at[1])
    store_back = pltpu.make_async_copy(send_back, back_hbm, load_sems.at[8])
    store_tail = pltpu.make_async_copy(send_tail, tail_hbm, load_sems.at[9])
    store_sends = [
        pltpu.make_async_copy(source, sends_hbm.at[k], load_sems.at[6 + k])
        for k, source in enumerate((g_ring, w_ring))
    ]
    x_spot = (jnp.maximum(step - 2, 0) % steps_x) // (steps_x // 2)
    x_lanes = pl.ds(
        pl.multiple_of((jnp.maximum(step - 2, 0) % (steps_x // 2)) * small_tile, small_tile),
        small_tile,
    )
    lanes = pl.ds(pl.multiple_of(jnp.minimum(step, 1) * tile, tile), tile)

    def load(spot, block):
        start = pl.multiple_of(block * big, big)
        return pltpu.make_async_copy(
            hist_hbm.at[pl.ds(start, big + state), lanes], ring.at[spot], ring_sems.at[spot]
        )

    @pl.when(step < 2)
    def _():
        for spot in range(turns - 1):
            load(spot, blocks - 1 - spot).start()

    @pl.when(step == 0)
    def _():
        greet()
        mix.step(0)
        for line in lines:
            line.start()
        near_l, near_r = (left_1, goal_l1), (right_1, goal_r1)
        pick((near_r, near_l, near_l, near_l), raw, goal, load_sems.at[pl.ds(4, 2)])
        matrix = dispatch_matrix(goal, devices)
        send_grads[...] = product(matrix, raw[1]).astype(BF16).reshape(send_grads.shape)
        gradproj[...] = jnp.zeros_like(gradproj)
        b_sums[...] = jnp.zeros_like(b_sums)
        c_sums[...] = jnp.zeros_like(c_sums)
        columns_of(proj_ref, rank + state, state, c_cols)
        diagonals_of(proj_ref, rank, state, b_high, b_low)

    def between(position):
        if position == 1:
            pl.when(me < half)(lambda: near_grads.start())
        if position == 2:
            mix.step(1)
            mix.step(2)
            gated.start()
        if position == 5:
            mix.step(3)
        if position == 7:
            mix.step(4)
            gated.wait()

    @pl.when(step < 2)
    def _():
        skip_ref = scan_rows(misc_ref)[1]
        grad_gated = times_transpose(gradmix_ref[...], outw_ref[...])
        gate_in = gate_ref[...]
        gate_sig = sigmoid(gate_in)
        grad_mixed = grad_gated * (gate_in * gate_sig)
        grad_gate = (
            grad_gated * mixed_ref[...] * (gate_sig * (1.0 + gate_in * (1.0 - gate_sig)))
        ).astype(BF16)
        gate_all[:, lanes] = grad_gate
        start = pl.multiple_of(channels + step * tile, tile)
        send_in[pl.ds(start, tile), :] = grad_gate.T
        u_act = u_ref[...]
        step_size = step_ref[...]
        gy[...] = grad_mixed
        du[0:rows, :] = step_size * u_act
        du[rows:, :] = jnp.zeros((BLOCK, tile), F32)
        grad_skip = jnp.sum(grad_mixed * u_act, 0, keepdims=True)
        rate = decay_ref[...]
        decay = rate * LOG2E
        sums = (iota((BLOCK, big), 0) == iota((BLOCK, big), 1) // state).astype(BF16)
        g_ring[1] = jnp.zeros((big, tile), BF16)
        w_ring[1] = jnp.zeros((big, tile), BF16)

        def reduce_block(spot, block):
            grads = g_ring[spot]
            source = jnp.minimum(block, blocks - 1)
            high, low = block_of(b_high, source, BLOCK), block_of(b_low, source, BLOCK)
            both = product(jnp.concatenate([high, low], 0), grads)
            base = pl.ds(pl.multiple_of(block * BLOCK, BLOCK), BLOCK)
            grad_du[base, :] = both[:BLOCK] + both[BLOCK:]
            grad_step[base, :] = product(sums, w_ring[spot])
            b_sums[base, :] += times_transpose(du[base, :].astype(BF16), grads)

        def run_blocks(quarter, carry):
            carried, log_sum = carry
            for spot in range(turns):
                turn = quarter * turns + spot
                block = blocks - 1 - turn
                later = (spot + turns - 1) % turns
                if spot == 0:
                    load(later, block - turns + 1).start()
                else:
                    pl.when(quarter < quarters - 1)(
                        lambda: load(later, block - turns + 1).start()
                    )
                load(spot, block).wait()
                here, before = spot % 2, (spot + 1) % 2
                reduce_block(before, block + 1)
                base = pl.ds(pl.multiple_of(block * BLOCK, BLOCK), BLOCK)
                steps_now, gy_now = step_ref[base, :], gy[base, :]
                c_now = block_of(c_cols, block, state)
                c_sums[base, :] += times_transpose(gy_now.astype(BF16), ring[spot, state:, :])
                for t in range(BLOCK - 1, -1, -1):
                    at = slice(t * state, (t + 1) * state)
                    c_wide = jnp.broadcast_to(c_now[:, t : t + 1], (state, tile))
                    step_now = steps_now[t : t + 1, :]
                    fade = jnp.exp2(step_now * decay)
                    grad = gy_now[t : t + 1, :] * c_wide + carried
                    g_ring[here, at, :] = grad.astype(BF16)
                    carried = fade * grad
                    weighted = carried * ring[spot, at, :].astype(F32) * rate
                    w_ring[here, at, :] = weighted.astype(BF16)
                    log_sum = log_sum + weighted * step_now
            for turn in range(2):
                for part in range(quarters):

                    @pl.when((step == turn) & (quarter == part))
                    def _():
                        between(turn * 4 + part)

            return carried, log_sum

        zeros = jnp.zeros((state, tile), F32)
        _, log_sum = lax.fori_loop(0, quarters, run_blocks, (zeros, zeros))
        reduce_block(1, 0)
        full_du = grad_du[0:rows, :]
        gradu_all[:, lanes] = full_du * step_size + skip_ref[...] * gy[...]
        grad_size = grad_step[0:rows, :] + full_du * u_act
        grad_pre = grad_size * (1.0 - jnp.exp(-step_size))
        grad_low = grad_pre.astype(BF16)
        grad_step_w = contract_rows(proj_ref[:, :rank].astype(BF16), grad_low)
        packed = jnp.concatenate(
            [grad_step_w, log_sum, jnp.sum(grad_pre, 0, keepdims=True), grad_skip, zeros[:6]], 0
        ).astype(BF16)
        for turn in range(2):

            @pl.when(step == turn)
            def _():
                split_lanes(send_scan.at[pl.ds(turn * half, half)], packed)
                start_some(scan.copies, scan.local, turn * half, (turn + 1) * half)
                start_inputs(half + turn * half // 2, half + (turn + 1) * half // 2)

        gradproj[:, :rank] += times_transpose(grad_low, stepw_ref[...])

    @pl.when(step == 1)
    def _():
        own = iota((rows, big), 0) % BLOCK == iota((rows, big), 1) // state
        lane = iota((big, cols), 1)
        slot = iota((big, cols), 0) % state
        total = gradproj[...]
        for sums_here, first in ((b_sums[0:rows, :], rank), (c_sums[...], rank + state)):
            place = (lane == first + slot).astype(F32)
            total = total + exact_product(jnp.where(own, sums_here, 0.0), place)
        gradproj[...] = total

    @pl.when(step == 2)
    def _():
        load_mid.start()
        grad_du[...] = jnp.zeros_like(grad_du)

    @pl.when(step == steps_x + 2)
    def _():
        split_lanes(send_back, pack_back[...])
        store_back.start()
        lhs = jnp.concatenate([gated_all[k] for k in range(devices)], 1)
        totals[2 * gated_all.shape[1] : 3 * gated_all.shape[1], :] = product(
            lhs, everyone[...].reshape(devices * rows, width)
        ).astype(BF16)
        load_normed.start()

    here = pl.ds(
        pl.multiple_of((jnp.maximum(step - 2, 0) % steps_x) * small_tile, small_tile), small_tile
    )

    @pl.when((step >= 2) & (step < steps_x + 2))
    def _():
        conv_ref, bias_ref = conv_rows(misc_x_ref)
        grad_proj = gradproj[...].astype(BF16)
        grad_u = gradu_all[:, here] + times_transpose(grad_proj, scanw_ref[...])
        pieces = [contract_rows(grad_proj, u_x_ref[...].astype(BF16))]
        x_inner = xin_ref[...]
        taps = conv_ref.shape[0]
        shifted = [shift_rows(x_inner, taps - 1 - tap) for tap in range(taps)]
        summed = bias_ref[...]
        for tap in range(taps):
            summed = summed + conv_ref[tap : tap + 1, :] * shifted[tap]
        sig = sigmoid(summed)
        grad_sum = grad_u * (sig * (1.0 + summed * (1.0 - sig)))
        grad_x = jnp.zeros_like(x_inner)
        for tap in range(taps):
            pieces.append(jnp.sum(grad_sum * shifted[tap], 0, keepdims=True))
            grad_x = grad_x + conv_ref[tap : tap + 1, :] * shift_rows(grad_sum, tap + 1 - taps)
        pieces.append(jnp.sum(grad_sum, 0, keepdims=True))
        pieces.append(jnp.zeros((pack_back.shape[0] - cols - taps - 1, small_tile), F32))
        pack_back[:, here] = jnp.concatenate(pieces, 0).astype(BF16)
        grad_x = grad_x.astype(BF16)
        send_in[here, :] = grad_x.T
        ring[x_spot, 0:rows, x_lanes] = grad_x
        for part in range(half):
            done = -(-(part + 1) * in_part // small_tile) + 1
            pl.when(step == done)(lambda: start_inputs(part, part + 1))

    @pl.when(step >= steps_x + 2)
    def _():
        grad_du[0:rows, :] += product(ring[x_spot, 0:rows, x_lanes], wx_ref[...]) + product(
            gate_all[:, here], wg_ref[...]
        )

    @pl.when(step == steps_x + 3)
    def _():
        next_to = [(left_2, goal_l2), (right_2, goal_r2), (right_1, goal_r1)]
        pick(
            (next_to[1], next_to[2], next_to[2], next_to[0]), raw, goal, load_sems.at[pl.ds(4, 2)]
        )
        matrix = dispatch_matrix(goal, devices)
        for part, (target, store) in enumerate(zip((g_ring, w_ring), store_sends)):
            target[...] = product(matrix, raw[part]).astype(BF16).reshape(target.shape)
            store.start()

    @pl.when(step == 2 * steps_x + 1)
    def _():
        values = tokens_ref[...].astype(F32)
        scale = lax.rsqrt(jnp.mean(values * values, -1, keepdims=True) + 1e-05)
        unit = values * scale
        grad = grad_du[0:rows, :]
        widths = jnp.concatenate([widths_ref[...], jnp.sum(grad * unit, 0, keepdims=True)], 0)
        widths = jnp.concatenate(
            [widths, jnp.zeros((send_tail.shape[1] - widths.shape[0], width), F32)], 0
        )
        split_lanes(send_tail, widths.astype(BF16))
        store_tail.start()
        inner = grad * gains_ref[0:1, :]
        load_mid.wait()
        gy[...] += scale * (inner - unit * jnp.mean(inner * unit, -1, keepdims=True))
        store_tokens = pltpu.make_async_copy(gy, gradtok_hbm, load_sems.at[2])
        store_tokens.start()
        at = 3 * gated_all.shape[1]
        scan.wait()
        totals[at : at + 32, :] = fold_rows(got_scan, width)
        load_normed.wait()
        input_local.wait()
        for copy in input_copies:
            copy.wait()
        lhs = jnp.concatenate([got_in[k] for k in range(devices)], 1)
        totals[0:in_part, :] = product(
            lhs, everyone[...].reshape(devices * rows, width)
        ).astype(BF16)
        store_totals = pltpu.make_async_copy(totals, totals_hbm, load_sems.at[3])
        store_totals.start()
        for line in lines:
            line.wait()
        for k, copy in enumerate(near_grads.copies):
            pl.when(me < half)(lambda copy=copy: copy.wait_send())
            source = (me + devices - k - 1) % devices
            pl.when(source < half)(lambda copy=copy: copy.wait_recv())
        pl.when(me < half)(lambda: near_grads.local.wait())
        store_back.wait()
        store_tail.wait()
        store_tokens.wait()
        store_totals.wait()
        for store in store_sends:
            store.wait()


def backward_plane(
    proj, step_w, vec, u_act, gate_in, out_w, grad_mix, step_size, mixed, scan_w, x_inner, in_t,
    tokens, gains, grad_widths, grad_mid, gated, normed_all, hist, rows_0, grads_0, raws,
    goals,
):
    rows, channels = u_act.shape
    width = grad_mix.shape[1]
    cols = proj.shape[1]
    rank, state = step_w.shape[0], vec.shape[0] - 8
    devices = lax.axis_size("expert")
    part = channels // devices
    tile, small = channels // 2, channels // 6
    big = BLOCK * state
    pack_rows, tail_rows = cols + 8, grad_widths.shape[0] + 7
    fixed = lambda i: (0, 0)
    first = lambda i: jnp.minimum(i, 1)
    second = lambda i: jnp.clip(i - 2, 0, 5)
    once = pl.Buffered(1)
    slots = jax.ShapeDtypeStruct(rows_0.shape, BF16)
    raw = jax.ShapeDtypeStruct(raws[0].shape, BF16)
    goal = jax.ShapeDtypeStruct(goals[0].shape, jnp.int32)
    total_rows = 3 * part + 32
    pair = jax.ShapeDtypeStruct((2, 2, big, tile), BF16)
    third = lambda i: jnp.maximum(i - 8, 0)
    scan_pack = (devices, rank + state + 8, part)
    back_pack = (devices, pack_rows, part)
    tail_pack = (devices, tail_rows, width // devices)
    return pl.pallas_call(
        backward_kernel,
        grid=(14,),
        in_specs=[
            pl.BlockSpec((rows, cols), fixed),
            pl.BlockSpec((rank, tile), lambda i: (0, first(i))),
            pl.BlockSpec((state, tile), lambda i: (0, first(i))),
            pl.BlockSpec((8, tile), lambda i: (state // 8, first(i))),
            pl.BlockSpec((rows, tile), lambda i: (0, first(i))),
            pl.BlockSpec((rows, tile), lambda i: (0, first(i))),
            pl.BlockSpec((tile, width), lambda i: (first(i), 0), pipeline_mode=once),
            pl.BlockSpec((rows, width), fixed, pipeline_mode=once),
            pl.BlockSpec((rows, tile), lambda i: (0, first(i))),
            pl.BlockSpec((rows, tile), lambda i: (0, first(i))),
            pl.BlockSpec((small, cols), lambda i: (second(i), 0)),
            pl.BlockSpec((rows, small), lambda i: (0, second(i))),
            pl.BlockSpec((8, small), lambda i: (state // 8, second(i))),
            pl.BlockSpec((small, width), lambda i: (third(i), 0)),
            pl.BlockSpec((small, width), lambda i: (third(i) + 6, 0)),
            pl.BlockSpec((rows, small), lambda i: (0, second(i))),
            pl.BlockSpec((rows, width), fixed, pipeline_mode=once),
            pl.BlockSpec(gains.shape, fixed),
            pl.BlockSpec(grad_widths.shape, fixed),
        ] + [FAR] * 14,
        out_specs=[FAR] * 11,
        out_shape=[
            jax.ShapeDtypeStruct((rows, width), F32),
            jax.ShapeDtypeStruct((total_rows, width), BF16),
            jax.ShapeDtypeStruct(back_pack, BF16),
            jax.ShapeDtypeStruct(tail_pack, BF16),
            slots, slots, raw, raw, goal, goal, pair,
        ],
        scratch_shapes=[
            pltpu.VMEM((rows // BLOCK * state, 128), F32),
            pltpu.VMEM((rows, big), BF16),
            pltpu.VMEM((rows, big), BF16),
            pltpu.VMEM((rows + BLOCK, big), F32),
            pltpu.VMEM((rows, big), F32),
            pltpu.VMEM((rows, tile), F32),
            pltpu.VMEM((rows + BLOCK, tile), F32),
            pltpu.VMEM((rows + BLOCK, tile), F32),
            pltpu.VMEM((rows + BLOCK, tile), F32),
            pltpu.VMEM((4, big + state, tile), BF16),
            pltpu.VMEM((2, big, tile), BF16),
            pltpu.VMEM((2, big, tile), BF16),
            pltpu.VMEM((rows, cols), F32),
            pltpu.VMEM((rows, channels), F32),
            pltpu.VMEM((rows, channels), BF16),
            pltpu.VMEM((2 * channels, rows), BF16),
            pltpu.VMEM((devices, 2 * part, rows), BF16),
            pltpu.VMEM((devices, rows, width), BF16),
            pltpu.VMEM(gated.shape, BF16),
            pltpu.VMEM(scan_pack, BF16),
            pltpu.VMEM(scan_pack, BF16),
            pltpu.VMEM((pack_rows, channels), BF16),
            pltpu.VMEM(back_pack, BF16),
            pltpu.VMEM(tail_pack, BF16),
            pltpu.VMEM((total_rows, width), BF16),
            pltpu.VMEM(raw.shape, BF16),
            pltpu.VMEM(goal.shape, jnp.int32),
            pltpu.VMEM(slots.shape, BF16),
            DMA((10,)), DMA((10,)), DMA((4, devices)), DMA((4, devices)), DMA((4, 2)), DMA((4, 2)),
            DMA((5,)), DMA((4,)), DMA((10,)),
        ],
        compiler_params=pltpu.CompilerParams(
            vmem_limit_bytes=VMEM_LIMIT, collective_id=4, has_side_effects=True
        ),
        name="mixer_backward",
    )(
        proj, step_w, vec, vec, u_act, gate_in, out_w, grad_mix, step_size, mixed, scan_w, x_inner,
        vec, in_t, in_t, u_act, tokens, gains, grad_widths, grad_mid, gated, normed_all, hist,
        rows_0, grads_0, *raws, *goals,
    )


def add_groups(rows, grads, rows_t, up_ref, down_ref):
    activated, slope = gelu_parts(product(rows, up_ref[...]))
    grad_pre = (times_transpose(grads, down_ref[...]) * slope).astype(BF16)
    return product(rows_t, grad_pre), contract_rows(activated.astype(BF16), grads)


def flat_rows(refs):
    experts, cap, width = refs[0].shape
    values = [ref[...].reshape(ref.shape[0] * cap, width) for ref in refs]
    return values[0] if len(values) == 1 else jnp.concatenate(values, 0)


def two_grads_kernel(
    up_ref, down_ref, gup_in, gdown_in, rows_1, grads_1, sends_2, left_2, left_3, right_2, right_3,
    goal_l2, goal_l3, goal_r2, goal_r3, back_hbm, tail_hbm,
    gup_ref, gdown_ref, rows_3, grads_3, small_ref,
    rows_t, gup_all, gdown_all, rows_2, grads_2, raw, goal, sends_3, own_back, pair_back, pair_sum,
    far_back, got_tail, small_here, small_all, z_send, z_recv, b_send, b_recv, x_send, x_recv,
    local_sems, load_sems, back_sems,
):
    step = pl.program_id(0)
    tiles = gup_all.shape[0]
    spot = step % tiles
    seconds, thirds = (
        [
            Exchange(
                source.at[k], out, x_send.at[first + k], x_recv.at[first + k],
                local_sems.at[first + k],
            )
            for k, out in enumerate(targets)
        ]
        for first, source, targets in (
            (0, sends_2, (rows_2, grads_2)), (2, sends_3, (rows_3, grads_3))
        )
    )

    small_tail = Exchange(
        tail_hbm, got_tail, x_send.at[4], x_recv.at[4], local_sems.at[4]
    )
    me = lax.axis_index("expert")
    core, chip = me % 2, me // 2
    chips = pair_sum.shape[0]
    to_core = [
        pltpu.make_async_remote_copy(
            back_hbm.at[2 * k + 1 - core], pair_back.at[k], b_send.at[k], b_recv.at[k],
            device_id={"expert": neighbour(1)}, device_id_type=MESH,
        )
        for k in range(chips)
    ]
    own_loads = [
        pltpu.make_async_copy(back_hbm.at[2 * k + core], own_back.at[k], back_sems.at[k])
        for k in range(chips)
    ]
    to_chips = [
        pltpu.make_async_remote_copy(
            pair_sum.at[(chip + k) % chips], far_back.at[k - 1], b_send.at[chips + k - 1],
            b_recv.at[chips + k - 1], device_id={"expert": 2 * ((chip + k) % chips) + core},
            device_id_type=MESH,
        )
        for k in range(1, chips)
    ]
    place, copies = lax.axis_index("dp"), lax.axis_size("dp")
    to_copies = [
        pltpu.make_async_remote_copy(
            small_here, small_all.at[k - 1], z_send.at[k - 1], z_recv.at[k - 1],
            device_id={"dp": (place + k) % copies}, device_id_type=MESH,
        )
        for k in range(1, copies)
    ]

    @pl.when(step == 0)
    def _():
        greet_all()
        for way in seconds:
            way.start()
        for copy in to_core + own_loads:
            copy.start()
        rows_t[...] = flat_rows((rows_1,)).T

    @pl.when(step == 1)
    def _():
        pick(
            ((right_3, goal_r3), (right_2, goal_r2), (left_2, goal_l2), (left_3, goal_l3)), raw,
            goal, load_sems,
        )
        prepare_sends(raw, goal, sends_3)

    @pl.when(step == tiles - 2)
    def _():
        for copy in to_core + own_loads:
            copy.wait()
        pair_sum[...] = (own_back[...].astype(F32) + pair_back[...].astype(F32)).astype(BF16)
        for copy in to_chips:
            copy.start()
        small_tail.start()
        for way in thirds:
            way.start()

    @pl.when(step == 2 * tiles - 3)
    def _():
        small_tail.wait()
        for copy in to_chips:
            copy.wait()
        width = small_here.shape[1]
        back = pair_sum[chip].astype(F32) + jnp.sum(far_back[...].astype(F32), 0)
        small_here[0:32, :] = fold_value(back, width)
        tail = jnp.sum(got_tail[...].astype(F32), 0)
        tail = jnp.concatenate([tail, jnp.zeros((tail.shape[0], width - tail.shape[1]), F32)], 1)
        small_here[32:48, :] = tail.astype(BF16)
        for copy in to_copies:
            copy.start()

    @pl.when(step < tiles)
    def _():
        grad_up, grad_down = add_groups(
            flat_rows((rows_1,)), flat_rows((grads_1,)), rows_t[...], up_ref, down_ref
        )
        gup_all[spot] = (gup_in[...].astype(F32) + grad_up).astype(BF16)
        gdown_all[spot] = (gdown_in[...].astype(F32) + grad_down).astype(BF16)

    @pl.when(step == tiles)
    def _():
        for way in seconds:
            way.wait()
        rows_t[...] = flat_rows((rows_2,)).T

    @pl.when(step >= tiles)
    def _():
        grad_up, grad_down = add_groups(
            flat_rows((rows_2,)), flat_rows((grads_2,)), rows_t[...], up_ref, down_ref
        )
        gup_ref[...] = (gup_all[spot].astype(F32) + grad_up).astype(BF16)
        gdown_ref[...] = (gdown_all[spot].astype(F32) + grad_down).astype(BF16)

    @pl.when(step == 2 * tiles - 1)
    def _():
        for copy in to_copies:
            copy.wait()
        small_ref[...] = small_here[...].astype(F32) + jnp.sum(small_all[...].astype(F32), 0)
        for way in thirds:
            way.wait()


def last_grads_kernel(
    up_ref, down_ref, gup_in, gdown_in, rows_ref, grads_ref, gup_ref, gdown_ref, rows_t
):
    rows, grads = flat_rows((rows_ref,)), flat_rows((grads_ref,))

    @pl.when(pl.program_id(0) == 0)
    def _():
        rows_t[...] = rows.T

    grad_up, grad_down = add_groups(rows, grads, rows_t[...], up_ref, down_ref)
    gup_ref[...] = gup_in[...].astype(F32) + grad_up
    gdown_ref[...] = gdown_in[...].astype(F32) + grad_down


def expert_grads_plane(
    up, down, grad_up, grad_down, rows, grads, sends, raws, goals, back, tail, tile
):
    width, hidden = up.shape
    devices, cap = grads.shape[:2]
    slots = jax.ShapeDtypeStruct(grads.shape, BF16)
    pair = jax.ShapeDtypeStruct(sends.shape, BF16)
    whole = pl.BlockSpec(grads.shape, lambda i: (0, 0, 0))

    def tiles(size):
        return [
            pl.BlockSpec((width, size), lambda i: (0, i)),
            pl.BlockSpec((size, width), lambda i: (i, 0)),
        ]

    def shapes(kind):
        return [
            jax.ShapeDtypeStruct((width, hidden), kind), jax.ShapeDtypeStruct((hidden, width), kind)
        ]

    turned = pltpu.VMEM((width, devices * cap), BF16)
    count = hidden // tile
    again = [
        pl.BlockSpec((width, tile), lambda i: (0, i % count)),
        pl.BlockSpec((tile, width), lambda i: (i % count, 0)),
    ]
    early = [
        pl.BlockSpec((width, tile), lambda i: (0, jnp.minimum(i, count - 1))),
        pl.BlockSpec((tile, width), lambda i: (jnp.minimum(i, count - 1), 0)),
    ]
    late = [
        pl.BlockSpec((width, tile), lambda i: (0, jnp.maximum(i - count, 0))),
        pl.BlockSpec((tile, width), lambda i: (jnp.maximum(i - count, 0), 0)),
    ]
    small = (48, width)
    grad_up, grad_down, rows, grads, small_total = pl.pallas_call(
        two_grads_kernel,
        grid=(2 * count,),
        in_specs=again + early + [whole] * 2 + [FAR] * 11,
        out_specs=late + [FAR] * 2 + [pl.BlockSpec(small, lambda i: (0, 0))],
        out_shape=shapes(BF16) + [slots] * 2 + [jax.ShapeDtypeStruct(small, F32)],
        scratch_shapes=[
            turned,
            pltpu.VMEM((count, width, tile), BF16),
            pltpu.VMEM((count, tile, width), BF16),
            pltpu.VMEM(slots.shape, BF16),
            pltpu.VMEM(slots.shape, BF16),
            pltpu.VMEM(raws[0].shape, BF16),
            pltpu.VMEM(goals[0].shape, jnp.int32),
            pltpu.VMEM(pair.shape, BF16),
            pltpu.VMEM((devices // 2,) + back.shape[1:], BF16),
            pltpu.VMEM((devices // 2,) + back.shape[1:], BF16),
            pltpu.VMEM((devices // 2,) + back.shape[1:], BF16),
            pltpu.VMEM((devices // 2 - 1,) + back.shape[1:], BF16),
            pltpu.VMEM(tail.shape, BF16),
            pltpu.VMEM(small, BF16),
            pltpu.VMEM((3,) + small, BF16),
            DMA((3,)), DMA((3,)), DMA((devices - 1,)), DMA((devices - 1,)), DMA((5, devices)),
            DMA((5, devices)), DMA((5,)), DMA((2,)), DMA((devices // 2,)),
        ],
        compiler_params=remote_params(6),
        name="expert_grads_12",
    )(up, down, grad_up, grad_down, rows, grads, sends, *raws, *goals, back, tail)
    grad_up, grad_down = pl.pallas_call(
        last_grads_kernel,
        grid=(hidden // 768,),
        in_specs=tiles(768) * 2 + [whole] * 2,
        out_specs=tiles(768),
        out_shape=shapes(F32),
        scratch_shapes=[turned],
        compiler_params=pltpu.CompilerParams(vmem_limit_bytes=VMEM_LIMIT),
        name="expert_grads_3",
    )(up, down, grad_up, grad_down, rows, grads)
    return grad_up, grad_down, small_total


def finish_kernel(
    totals_ref, small_ref, in_ref, out_ref, scanw_ref, stepw_ref, decay_ref, conv_ref, router_ref, bias_ref,
    dbias_ref, skip_ref, norm_two_ref, norm_ref,
):
    in_rows, part = in_ref.shape[0], out_ref.shape[0]
    cols, rank, state, taps = (
        scanw_ref.shape[1], stepw_ref.shape[0], decay_ref.shape[0], conv_ref.shape[0]
    )
    experts, slice_w = router_ref.shape
    in_ref[...] = totals_ref[0:in_rows, :].astype(F32)
    out_ref[...] = totals_ref[in_rows : in_rows + part, :].astype(F32)
    at = in_rows + part
    unfolded = []
    for block, quarter in (
        (totals_ref[at : at + 32, :].astype(F32), (rank + state + 8) // 4),
        (small_ref[0:32, :], (cols + 8) // 4),
    ):
        unfolded.append(
            jnp.concatenate(
                [block[:quarter, k * part : (k + 1) * part] for k in range(4)], 0
            )
        )
    scan, back = unfolded
    stepw_ref[...] = scan[:rank]
    decay_ref[...] = scan[rank : rank + state]
    scanw_ref[...] = back[:cols].T
    conv_ref[...] = back[cols : cols + taps]
    bias_ref[...] = back[cols + taps]
    dbias_ref[...] = scan[rank + state]
    skip_ref[...] = scan[rank + state + 1]
    tail = small_ref[32:48, :][:, :slice_w]
    router_ref[...] = tail[:experts]
    norm_two_ref[...] = tail[experts]
    norm_ref[...] = tail[experts + 1]


def finish(totals, small, in_rows, part, cols, rank, state, taps, experts, slice_w):
    here = pl.BlockSpec(memory_space=pltpu.VMEM)
    return pl.pallas_call(
        finish_kernel,
        in_specs=[here] * 2,
        out_specs=[here] * 12,
        out_shape=[
            jax.ShapeDtypeStruct(shape, F32)
            for shape in (
                (in_rows, totals.shape[1]), (part, totals.shape[1]), (part, cols), (rank, part),
                (state, part), (taps, part), (experts, slice_w), (part,), (part,), (part,),
                (slice_w,), (slice_w,),
            )
        ],
        compiler_params=pltpu.CompilerParams(vmem_limit_bytes=VMEM_LIMIT),
        name="finish",
    )(totals, small)


def gather(value):
    return lax.all_gather(value, "expert", axis=0, tiled=True)


def exchange(value):
    return lax.all_to_all(value, "expert", split_axis=0, concat_axis=0, tiled=True)


def shards(
    tokens, lengths, routes, slot_index, mixer_norm, in_weight, conv_weight, conv_bias,
    scan_weight, step_weight, step_bias, decay_log, skip_gain, out_weight, moe_norm, router_weight,
    up_weight, down_weight, cotangent,
):
    devices = lax.axis_size("expert")
    rows, width = tokens.shape[1:]
    part = out_weight.shape[0]
    channels = part * devices
    cols = scan_weight.shape[1]
    rank, state, taps = step_weight.shape[0], decay_log.shape[1], conv_weight.shape[0]
    experts = router_weight.shape[1]
    split = devices // experts
    slice_w = width // devices
    tile = channels // 2

    on_plane = devices == 8 and split == 1 and lax.axis_size("dp") == 4
    in_t, decay_t, router_t = in_weight.T, decay_log.T, router_weight.T
    up, down = up_weight[0], down_weight[0]
    hidden = up.shape[1]
    if on_plane:
        (
            normed_low, x_inner, u_act, gate_in, proj, step_size, mixed, gated, mid, step_full, vec,
            router_t, gains, scan_full, in_t, out_full, normed_all, hist,
        ) = forward_plane(
            tokens[0], in_t, scan_weight, step_weight, decay_t, conv_weight, conv_bias, step_bias,
            skip_gain, mixer_norm, moe_norm, router_t, out_weight,
        )
        in_t = in_t.reshape(2 * channels, width)
        scan_full = scan_full.reshape(channels, cols)
        out_full = out_full.reshape(channels, width)
        layer_out, grad_mid, grad_mix, grad_widths, rows_0, grads_0, *line = expert_layer(
            lengths, mid, gains, router_t, routes, slot_index, cotangent[0], up, down
        )
        raws, goals, grad_up, grad_down = line[:4], line[4:8], line[8], line[9]
        (
            tokens_grad, totals, back_parts, tail_parts, rows_1, grads_1, left_3, right_3, goal_l3,
            goal_r3, sends,
        ) = backward_plane(
            proj, step_full, vec, u_act, gate_in, out_full, grad_mix, step_size, mixed, scan_full,
            x_inner, in_t, tokens[0], gains, grad_widths, grad_mid, gated, normed_all, hist, rows_0,
            grads_0, raws, goals,
        )
        totals = lax.psum(totals, "dp")
        grad_up, grad_down, small_total = expert_grads_plane(
            up, down, grad_up, grad_down, rows_1, grads_1,
            sends.reshape((2,) + rows_1.shape), (raws[2], left_3, raws[3], right_3),
            (goals[2], goal_l3, goals[3], goal_r3), back_parts, tail_parts, 512,
        )
        in_total, out_total, scan_w_total, step_w_total, decay_total, conv_total, *rest = finish(
            totals, small_total, 2 * part, part, cols, rank, state, taps, experts, slice_w
        )
        router_total, vector_totals, norm_totals = rest[0], rest[1:4], rest[4:]
    else:
        vectors = jnp.stack([conv_bias, step_bias, skip_gain])
        norms = jnp.stack([mixer_norm, moe_norm])
        spare = jnp.zeros((8 - taps - 3, part), BF16)
        columns = jnp.concatenate([step_weight, decay_t, conv_weight, vectors, spare], 0)
        across = jnp.concatenate([router_t, norms, jnp.zeros((6, slice_w), BF16)], 0)
        in_t, scan_full, columns, across = (
            lax.all_gather(value, "expert") for value in (in_t, scan_weight, columns, across)
        )
        columns = columns.transpose(1, 0, 2).reshape(columns.shape[1], channels)
        across = across.transpose(1, 0, 2).reshape(across.shape[1], width)
        step_full, rest = columns[:rank], columns[rank:].astype(F32)
        vec = jnp.concatenate([-jnp.exp(rest[:state]), rest[state:]], 0)
        router_t, gains = across[:experts], across[experts:].astype(F32)
        in_t = in_t.reshape(2 * channels, width)
        scan_full = scan_full.reshape(channels, cols)
        normed_low, x_inner, u_act, gate_in, proj = front(
            tokens[0], gains, in_t, vec, scan_full, tile
        )
        live = (jnp.arange(rows, dtype=jnp.int32) < lengths[0]).astype(F32)[:, None]
        routes_col, slots_col = routes[0][:, None], slot_index[0][:, None]
        router, gain_second = router_t.T, gains[1:2]
        out_full = gather(out_weight)
        step_size, mixed, gated, hist, mid = scan_forward(
            proj, step_full, vec, u_act, gate_in, out_full, tokens[0], tile
        )
        send_rows, send_grads, normed_two, probs = router_step(
            mid, gain_second, router, routes_col, routes, slot_index, live, cotangent[0]
        )

        def to_pieces(value):
            wide = jnp.broadcast_to(value[:, None], (experts, split) + value.shape[1:])
            return exchange(wide.reshape(devices, CAP, width))

        def from_pieces(value):
            value = exchange(value).reshape(experts, split, CAP, width)
            if split == 1:
                return value[:, 0]
            return jnp.sum(value.astype(F32), 1).astype(BF16)

        some = min(512, hidden // 3)
        rows_in = to_pieces(send_rows)
        grads_in = to_pieces(send_grads)
        partial_out, slope = expert_out(rows_in, up, down, some)
        back_rows = from_pieces(partial_out)
        back_grads = from_pieces(expert_back(grads_in, up, down, slope, some))
        all_rows = lax.all_gather(rows_in, "dp")
        layer_out, grad_mid, grad_mix, grad_widths = combine_step(
            mid, gain_second, router, routes_col, slots_col, live, cotangent[0], probs, normed_two,
            back_rows, back_grads,
        )
        grad_mix, all_rows = lax.optimization_barrier((grad_mix, all_rows))
        all_grads = lax.all_gather(grads_in, "dp")
        out_parts = contract_rows(gated, grad_mix).astype(BF16).reshape(devices, part, width)
        grad_out_w = jnp.sum(exchange(out_parts).astype(F32), 0).astype(BF16)
        grad_u, grad_gate, scan_parts, grad_proj = scan_backward(
            proj, step_full, vec, u_act, gate_in, out_full, grad_mix, step_size, mixed, hist, tile,
            devices,
        )
        scan_small = jnp.sum(exchange(scan_parts).astype(F32), 0).astype(BF16)
        grad_x, back_parts, width_parts, tokens_grad = mixer_back(
            grad_proj, scan_full, grad_u, x_inner, vec, grad_gate, in_t, u_act, tokens[0], gains,
            grad_mid, grad_widths, tile, devices,
        )
        back_small = jnp.sum(exchange(back_parts).astype(F32), 0).astype(BF16)
        width_small = jnp.sum(exchange(width_parts).astype(F32), 0).astype(BF16)
        normed_all = gather(normed_low)
        grad_in_parts = exchange(jnp.concatenate([grad_x, grad_gate], 0))
        grad_in_w = contract_rows(
            grad_in_parts.reshape(devices * rows, 2 * part), normed_all
        ).astype(BF16)
        totals = (grad_in_w, grad_out_w, scan_small, back_small, width_small)
        totals, all_grads = lax.optimization_barrier((totals, all_grads))
        totals = lax.psum(totals, "dp")
        in_total, out_total, scan_small, back_small, width_small = (
            t.astype(F32) for t in totals
        )
        grad_up, grad_down = expert_grads(all_rows, all_grads, up, down, min(256, hidden))
        scan_w_total, conv_total = back_small[:cols].T, back_small[cols : cols + taps]
        step_w_total, decay_total = scan_small[:rank], scan_small[rank : rank + state]
        vector_totals = (
            back_small[cols + taps], scan_small[rank + state], scan_small[rank + state + 1]
        )
        router_total = width_small[:experts]
        norm_totals = (width_small[experts], width_small[experts + 1])
    return (
        layer_out[None],
        tokens_grad[None],
        norm_totals[1],
        in_total.T,
        conv_total,
        vector_totals[0],
        scan_w_total,
        step_w_total,
        vector_totals[1],
        decay_total.T,
        vector_totals[2],
        out_total,
        norm_totals[0],
        router_total.T,
        grad_up[None],
        grad_down[None],
    )


def solution(mesh):
    in_specs = (
        P(("dp", "expert"), None, None),
        P(("dp", "expert")),
        P(("dp", "expert"), None),
        P(("dp", "expert"), None),
        P("expert"),
        P(None, "expert"),
        P(None, "expert"),
        P("expert"),
        P("expert", None),
        P(None, "expert"),
        P("expert"),
        P("expert", None),
        P("expert"),
        P("expert", None),
        P("expert"),
        P("expert", None),
        P("expert", None, None),
        P("expert", None, None),
        P(("dp", "expert"), None, None),
    )
    out_specs = (
        P(("dp", "expert"), None, None),
        P(("dp", "expert"), None, None),
        P("expert"),
        P(None, "expert"),
        P(None, "expert"),
        P("expert"),
        P("expert", None),
        P(None, "expert"),
        P("expert"),
        P("expert", None),
        P("expert"),
        P("expert", None),
        P("expert"),
        P("expert", None),
        P("expert", None, None),
        P("expert", None, None),
    )
    return jax.shard_map(shards, mesh=mesh, in_specs=in_specs, out_specs=out_specs, check_vma=False)
```

```python
from functools import partial

import jax
import jax.numpy as jnp
from jax import lax
from jax.experimental import pallas as pl
from jax.experimental.pallas import tpu as pltpu
from jax.sharding import PartitionSpec as P

CAP = 64
BLOCK = 16
LOG2E = 1.4426950408889634
F32 = jnp.float32
BF16 = jnp.bfloat16
VMEM_LIMIT = 56 * 1024 * 1024


def product(left, right):
    return jnp.dot(left, right, preferred_element_type=F32)


def contract_rows(left, right):
    return lax.dot_general(left, right, (((0,), (0,)), ((), ())), preferred_element_type=F32)


def times_transpose(left, right):
    return lax.dot_general(left, right, (((1,), (1,)), ((), ())), preferred_element_type=F32)


def exact_product(left, right):
    return jnp.dot(left, right, preferred_element_type=F32, precision=lax.Precision.HIGHEST)


def iota(shape, axis):
    return lax.broadcasted_iota(jnp.int32, shape, axis)


def sigmoid(values):
    return 1.0 / (1.0 + jnp.exp(-values))


def softplus(values):
    return jnp.maximum(values, 0.0) + jnp.log1p(jnp.exp(-jnp.abs(values)))


class Rows:
    def __init__(self, ref, first, count):
        self.ref, self.first = ref, first
        self.shape = (count, ref.shape[1])

    def __getitem__(self, index):
        low, high = (0, self.shape[0]) if index is Ellipsis else (index[0].start, index[0].stop)
        return self.ref[self.first + low : self.first + high, :]


def conv_rows(misc_ref):
    return Rows(misc_ref, 0, 4), Rows(misc_ref, 4, 1)


def scan_rows(misc_ref):
    return Rows(misc_ref, 5, 1), Rows(misc_ref, 6, 1)


def split_lanes(out_ref, value):
    parts, _, width = out_ref.shape
    for part in range(parts):
        out_ref[part] = value[:, part * width : (part + 1) * width]


def shift_rows(values, offset):
    rows = values.shape[0]
    if offset == 0:
        return values
    rolled = pltpu.roll(values, offset % rows, 0)
    row = iota(values.shape, 0)
    keep = row >= offset if offset > 0 else row < rows + offset
    return jnp.where(keep, rolled, 0.0)


def two_parts(values):
    high = values.astype(BF16)
    low = (values - high.astype(F32)).astype(BF16)
    return high, low


def spread_rows(proj_block, first, state):
    rows, width = proj_block.shape
    big = rows * state
    pick = (iota((big, rows), 0) // state == iota((big, rows), 1)).astype(F32)
    copied = exact_product(pick, proj_block)
    lane = iota((big, width), 1)
    own = lane == first + iota((big, width), 0) % state
    column = jnp.sum(jnp.where(own, copied, 0.0), axis=1, keepdims=True)
    return jnp.broadcast_to(column, (big, 128))


def diagonal_blocks(proj_block, first, state):
    rows, width = proj_block.shape
    big = rows * state
    place = (iota((width, big), 0) == first + iota((width, big), 1) % state).astype(BF16)
    own = iota((rows, big), 0) == iota((rows, big), 1) // state
    parts = [
        jnp.where(own, product(part, place), 0.0).astype(BF16) for part in two_parts(proj_block)
    ]
    return jnp.concatenate(parts, 0)


def front_kernel(
    tokens_ref, gain_ref, wx_ref, wg_ref, misc_ref, scanw_ref,
    normed_ref, xin_ref, u_ref, gate_ref, proj_ref,
):
    step = pl.program_id(0)
    conv_ref, bias_ref = conv_rows(misc_ref)

    @pl.when(step == 0)
    def _():
        values = tokens_ref[...].astype(F32)
        scale = lax.rsqrt(jnp.mean(values * values, -1, keepdims=True) + 1e-05)
        normed_ref[...] = (values * scale * gain_ref[0:1, :]).astype(BF16)
        proj_ref[...] = jnp.zeros_like(proj_ref)

    normed = normed_ref[...]
    x_inner = times_transpose(normed, wx_ref[...])
    gate_ref[...] = times_transpose(normed, wg_ref[...])
    xin_ref[...] = x_inner
    taps = conv_ref.shape[0]
    summed = bias_ref[...] + conv_ref[taps - 1 : taps, :] * x_inner
    for back in range(1, taps):
        tap = taps - 1 - back
        summed = summed + conv_ref[tap : tap + 1, :] * shift_rows(x_inner, back)
    u_act = summed * sigmoid(summed)
    u_ref[...] = u_act
    proj_ref[...] += product(u_act.astype(BF16), scanw_ref[...])


def front(tokens, gains, in_t, vec, scan_w, tile):
    rows, width = tokens.shape
    channels = scan_w.shape[0]
    cols = scan_w.shape[1]
    steps = channels // tile
    return pl.pallas_call(
        front_kernel,
        grid=(steps,),
        in_specs=[
            pl.BlockSpec((rows, width), lambda i: (0, 0)),
            pl.BlockSpec(gains.shape, lambda i: (0, 0)),
            pl.BlockSpec((tile, width), lambda i: (i, 0)),
            pl.BlockSpec((tile, width), lambda i: (i + steps, 0)),
            pl.BlockSpec((8, tile), lambda i: ((vec.shape[0] - 8) // 8, i)),
            pl.BlockSpec((tile, cols), lambda i: (i, 0)),
        ],
        out_specs=[
            pl.BlockSpec((rows, width), lambda i: (0, 0)),
            pl.BlockSpec((rows, tile), lambda i: (0, i)),
            pl.BlockSpec((rows, tile), lambda i: (0, i)),
            pl.BlockSpec((rows, tile), lambda i: (0, i)),
            pl.BlockSpec((rows, cols), lambda i: (0, 0)),
        ],
        out_shape=[
            jax.ShapeDtypeStruct((rows, width), BF16),
            jax.ShapeDtypeStruct((rows, channels), F32),
            jax.ShapeDtypeStruct((rows, channels), F32),
            jax.ShapeDtypeStruct((rows, channels), F32),
            jax.ShapeDtypeStruct((rows, cols), F32),
        ],
        compiler_params=pltpu.CompilerParams(vmem_limit_bytes=VMEM_LIMIT),
        name="mixer_front",
    )(tokens, gains, in_t, in_t, vec, scan_w)


def scan_prepare(proj_ref, b_wide, c_blocks, b_first, c_first, state):
    blocks = proj_ref.shape[0] // BLOCK
    big = BLOCK * state

    def build(block, carry):
        part = proj_ref[pl.ds(pl.multiple_of(block * BLOCK, BLOCK), BLOCK), :]
        b_wide[pl.ds(pl.multiple_of(block * big, big), big), :] = spread_rows(part, b_first, state)
        c_blocks[pl.ds(pl.multiple_of(block * 2 * BLOCK, 2 * BLOCK), 2 * BLOCK), :] = (
            diagonal_blocks(part, c_first, state)
        )
        return carry

    lax.fori_loop(0, blocks, build, 0)


def scan_tile(
    proj_ref, stepw_ref, decay_ref, misc_ref, u_ref, gate_ref, step_ref, mixed_ref, hist_ref,
    b_wide, c_blocks, du, scanned, between,
):
    rank, state = stepw_ref.shape[0], decay_ref.shape[0]
    rows, tile = u_ref.shape
    blocks = rows // BLOCK
    big = BLOCK * state
    dbias_ref, skip_ref = scan_rows(misc_ref)
    u_act = u_ref[...]
    step_size = softplus(
        product(proj_ref[:, :rank].astype(BF16), stepw_ref[...]) + dbias_ref[...]
    )
    step_ref[...] = step_size
    du[...] = step_size * u_act
    decay = decay_ref[...] * LOG2E
    hist_ref[0:state, :] = jnp.zeros((state, tile), BF16)

    def run_block(block, held):
        base = pl.multiple_of(block * BLOCK, BLOCK)
        steps_now = step_ref[pl.ds(base, BLOCK), :]
        du_now = du[pl.ds(base, BLOCK), :]
        wide_base = pl.multiple_of(block * big, big)
        for t in range(BLOCK):
            b_now = b_wide[pl.ds(wide_base + t * state, state), :]
            fade = jnp.exp2(steps_now[t : t + 1, :] * decay)
            fresh = du_now[t : t + 1, :] * jnp.concatenate([b_now] * (tile // 128), 1)
            held = fade * held + fresh
            hist_ref[pl.ds(wide_base + (t + 1) * state, state), :] = held.astype(BF16)
        weights = c_blocks[pl.ds(pl.multiple_of(block * 2 * BLOCK, 2 * BLOCK), 2 * BLOCK), :]
        both = product(weights, hist_ref[pl.ds(wide_base + state, big), :])
        scanned[pl.ds(base, BLOCK), :] = both[:BLOCK] + both[BLOCK:]
        return held

    held = jnp.zeros((state, tile), F32)
    held = lax.fori_loop(0, blocks // 2, run_block, held)
    between(0)
    lax.fori_loop(blocks // 2, blocks, run_block, held)
    between(1)
    mixed = scanned[...] + skip_ref[...] * u_act
    mixed_ref[...] = mixed
    gate_in = gate_ref[...]
    return (mixed * (gate_in * sigmoid(gate_in))).astype(BF16)


def scan_kernel(
    proj_ref, stepw_ref, decay_ref, misc_ref, u_ref, gate_ref, outw_ref, tokens_ref,
    step_ref, mixed_ref, gated_ref, hist_ref, mid_ref,
    b_wide, c_blocks, du, scanned,
):
    rank, state = stepw_ref.shape[0], decay_ref.shape[0]

    @pl.when(pl.program_id(0) == 0)
    def _():
        mid_ref[...] = tokens_ref[...].astype(F32)
        scan_prepare(proj_ref, b_wide, c_blocks, rank, rank + state, state)

    gated = scan_tile(
        proj_ref, stepw_ref, decay_ref, misc_ref, u_ref, gate_ref, step_ref, mixed_ref, hist_ref,
        b_wide, c_blocks, du, scanned, lambda half: None,
    )
    gated_ref[...] = gated
    mid_ref[...] += product(gated, outw_ref[...])


def scan_forward(proj, step_w, vec, u_act, gate_in, out_w, tokens, tile):
    rows, channels = u_act.shape
    width = tokens.shape[1]
    cols = proj.shape[1]
    rank, state = step_w.shape[0], vec.shape[0] - 8
    steps = channels // tile
    hist_rows = (rows + 1) * state
    column = lambda i: (0, i)
    fixed = lambda i: (0, 0)
    return pl.pallas_call(
        scan_kernel,
        grid=(steps,),
        in_specs=[
            pl.BlockSpec((rows, cols), fixed),
            pl.BlockSpec((rank, tile), column),
            pl.BlockSpec((state, tile), column),
            pl.BlockSpec((8, tile), lambda i: ((vec.shape[0] - 8) // 8, i)),
            pl.BlockSpec((rows, tile), column),
            pl.BlockSpec((rows, tile), column),
            pl.BlockSpec((tile, width), lambda i: (i, 0)),
            pl.BlockSpec((rows, width), fixed),
        ],
        out_specs=[
            pl.BlockSpec((rows, tile), column),
            pl.BlockSpec((rows, tile), column),
            pl.BlockSpec((rows, tile), column),
            pl.BlockSpec((hist_rows, tile), column),
            pl.BlockSpec((rows, width), fixed),
        ],
        out_shape=[
            jax.ShapeDtypeStruct((rows, channels), F32),
            jax.ShapeDtypeStruct((rows, channels), F32),
            jax.ShapeDtypeStruct((rows, channels), BF16),
            jax.ShapeDtypeStruct((hist_rows, channels), BF16),
            jax.ShapeDtypeStruct((rows, width), F32),
        ],
        scratch_shapes=[
            pltpu.VMEM((rows * state, 128), F32),
            pltpu.VMEM((rows * 2, BLOCK * state), BF16),
            pltpu.VMEM((rows, tile), F32),
            pltpu.VMEM((rows, tile), F32),
        ],
        compiler_params=pltpu.CompilerParams(vmem_limit_bytes=VMEM_LIMIT),
        name="scan_forward",
    )(proj, step_w, vec, vec, u_act, gate_in, out_w, tokens)


def scan_back_kernel(*refs):
    scan_back_tile(lambda half: None, split_lanes, *refs)


def scan_back_tile(
    between, put_gate, proj_ref, stepw_ref, decay_ref, misc_ref, u_ref, gate_ref, outw_ref, gradmix_ref,
    step_ref, mixed_ref, hist_ref,
    gradu_ref, gradgate_ref, pack_ref, gradproj_ref,
    c_wide, b_blocks, b_sums, c_sums, gy, du, g_hist, w_hist, grad_du, grad_step,
):
    tile_id = pl.program_id(0)
    cols, rank = proj_ref.shape[1], stepw_ref.shape[0]
    state = decay_ref.shape[0]
    rows, tile = u_ref.shape
    blocks = rows // BLOCK
    big = BLOCK * state

    @pl.when(tile_id == 0)
    def _():
        gradproj_ref[...] = jnp.zeros_like(gradproj_ref)
        b_sums[...] = jnp.zeros_like(b_sums)
        c_sums[...] = jnp.zeros_like(c_sums)
        scan_prepare(proj_ref, c_wide, b_blocks, rank + state, rank, state)

    skip_ref = scan_rows(misc_ref)[1]
    grad_gated = times_transpose(gradmix_ref[...], outw_ref[...])
    gate_in = gate_ref[...]
    gate_sig = sigmoid(gate_in)
    grad_mixed = grad_gated * (gate_in * gate_sig)
    put_gate(
        gradgate_ref,
        (grad_gated * mixed_ref[...] * (gate_sig * (1.0 + gate_in * (1.0 - gate_sig)))).astype(BF16),
    )
    u_act = u_ref[...]
    step_size = step_ref[...]
    gy[...] = grad_mixed
    du[...] = step_size * u_act
    grad_skip = jnp.sum(grad_mixed * u_act, 0, keepdims=True)
    rate = decay_ref[...]
    decay = rate * LOG2E
    sums = (iota((BLOCK, big), 0) == iota((BLOCK, big), 1) // state).astype(BF16)

    def run_block(turn, carry):
        carried, log_sum = carry
        block = blocks - 1 - turn
        base = pl.multiple_of(block * BLOCK, BLOCK)
        wide_base = pl.multiple_of(block * big, big)
        steps_now = step_ref[pl.ds(base, BLOCK), :]
        gy_now = gy[pl.ds(base, BLOCK), :]
        for t in range(BLOCK - 1, -1, -1):
            c_now = c_wide[pl.ds(wide_base + t * state, state), :]
            step_now = steps_now[t : t + 1, :]
            fade = jnp.exp2(step_now * decay)
            grad = gy_now[t : t + 1, :] * jnp.concatenate([c_now] * (tile // 128), 1) + carried
            g_hist[t * state : (t + 1) * state, :] = grad.astype(BF16)
            carried = fade * grad
            before = hist_ref[pl.ds(wide_base + t * state, state), :].astype(F32)
            weighted = carried * before * rate
            w_hist[t * state : (t + 1) * state, :] = weighted.astype(BF16)
            log_sum = log_sum + weighted * step_now
        grads = g_hist[...]
        both = product(
            b_blocks[pl.ds(pl.multiple_of(block * 2 * BLOCK, 2 * BLOCK), 2 * BLOCK), :], grads
        )
        grad_du[pl.ds(base, BLOCK), :] = both[:BLOCK] + both[BLOCK:]
        grad_step[pl.ds(base, BLOCK), :] = product(sums, w_hist[...])
        b_sums[pl.ds(base, BLOCK), :] += times_transpose(
            du[pl.ds(base, BLOCK), :].astype(BF16), grads
        )
        c_sums[pl.ds(base, BLOCK), :] += times_transpose(
            gy_now.astype(BF16), hist_ref[pl.ds(wide_base + state, big), :]
        )
        return carried, log_sum

    zeros = jnp.zeros((state, tile), F32)
    held = lax.fori_loop(0, blocks // 2, run_block, (zeros, zeros))
    between(0)
    _, log_sum = lax.fori_loop(blocks // 2, blocks, run_block, held)
    between(1)
    full_du = grad_du[...]
    gradu_ref[...] = full_du * step_size + skip_ref[...] * gy[...]
    grad_size = grad_step[...] + full_du * u_act
    grad_pre = grad_size * (1.0 - jnp.exp(-step_size))
    grad_low = grad_pre.astype(BF16)
    grad_step_w = contract_rows(proj_ref[:, :rank].astype(BF16), grad_low)
    packed = jnp.concatenate(
        [grad_step_w, log_sum, jnp.sum(grad_pre, 0, keepdims=True), grad_skip, zeros[:6]], 0
    )
    split_lanes(pack_ref, packed.astype(BF16))
    gradproj_ref[:, :rank] += times_transpose(grad_low, stepw_ref[...])

    @pl.when(tile_id == pl.num_programs(0) - 1)
    def _():
        own = iota((rows, big), 0) % BLOCK == iota((rows, big), 1) // state
        lane = iota((big, cols), 1)
        slot = iota((big, cols), 0) % state
        total = gradproj_ref[...]
        for sums_ref, first in ((b_sums, rank), (c_sums, rank + state)):
            place = (lane == first + slot).astype(F32)
            total = total + exact_product(jnp.where(own, sums_ref[...], 0.0), place)
        gradproj_ref[...] = total


def scan_backward(
    proj, step_w, vec, u_act, gate_in, out_w, grad_mix, step_size, mixed, hist, tile, devices
):
    rows, channels = u_act.shape
    gate_parts = tile * devices // (2 * channels)
    pack_parts = tile * devices // channels
    pack_rows = step_w.shape[0] + vec.shape[0]
    width = grad_mix.shape[1]
    cols = proj.shape[1]
    rank, state = step_w.shape[0], vec.shape[0] - 8
    steps = channels // tile
    big = BLOCK * state
    column = lambda i: (0, i)
    fixed = lambda i: (0, 0)
    return pl.pallas_call(
        scan_back_kernel,
        grid=(steps,),
        in_specs=[
            pl.BlockSpec((rows, cols), fixed),
            pl.BlockSpec((rank, tile), column),
            pl.BlockSpec((state, tile), column),
            pl.BlockSpec((8, tile), lambda i: ((vec.shape[0] - 8) // 8, i)),
            pl.BlockSpec((rows, tile), column),
            pl.BlockSpec((rows, tile), column),
            pl.BlockSpec((tile, width), lambda i: (i, 0)),
            pl.BlockSpec((rows, width), fixed),
            pl.BlockSpec((rows, tile), column),
            pl.BlockSpec((rows, tile), column),
            pl.BlockSpec((hist.shape[0], tile), column),
        ],
        out_specs=[
            pl.BlockSpec((rows, tile), column),
            pl.BlockSpec((gate_parts, rows, tile // gate_parts), lambda i: (i, 0, 0)),
            pl.BlockSpec((pack_parts, pack_rows, tile // pack_parts), lambda i: (i, 0, 0)),
            pl.BlockSpec((rows, cols), fixed),
        ],
        out_shape=[
            jax.ShapeDtypeStruct((rows, channels), F32),
            jax.ShapeDtypeStruct((devices // 2, rows, 2 * channels // devices), BF16),
            jax.ShapeDtypeStruct((devices, pack_rows, channels // devices), BF16),
            jax.ShapeDtypeStruct((rows, cols), F32),
        ],
        scratch_shapes=[
            pltpu.VMEM((rows * state, 128), F32),
            pltpu.VMEM((rows * 2, big), BF16),
            pltpu.VMEM((rows, big), F32),
            pltpu.VMEM((rows, big), F32),
            pltpu.VMEM((rows, tile), F32),
            pltpu.VMEM((rows, tile), F32),
            pltpu.VMEM((big, tile), BF16),
            pltpu.VMEM((big, tile), BF16),
            pltpu.VMEM((rows, tile), F32),
            pltpu.VMEM((rows, tile), F32),
        ],
        compiler_params=pltpu.CompilerParams(vmem_limit_bytes=VMEM_LIMIT),
        name="scan_backward",
    )(proj, step_w, vec, vec, u_act, gate_in, out_w, grad_mix, step_size, mixed, hist)


def back_kernel(
    gradproj_ref, scanw_ref, gradu_ref, xin_ref, misc_ref, gradgate_ref, wx_ref, wg_ref,
    u_ref, tokens_ref, gain_ref, gradmid_ref, widths_ref,
    gradx_ref, pack_ref, tail_ref, gradtok_ref,
    total,
):
    tile_id = pl.program_id(0)

    @pl.when(tile_id == 0)
    def _():
        total[...] = jnp.zeros_like(total)

    conv_ref, bias_ref = conv_rows(misc_ref)
    grad_proj = gradproj_ref[...].astype(BF16)
    grad_u = gradu_ref[...] + times_transpose(grad_proj, scanw_ref[...])
    pieces = [contract_rows(grad_proj, u_ref[...].astype(BF16))]
    x_inner = xin_ref[...]
    taps = conv_ref.shape[0]
    shifted = [shift_rows(x_inner, taps - 1 - tap) for tap in range(taps)]
    summed = bias_ref[...]
    for tap in range(taps):
        summed = summed + conv_ref[tap : tap + 1, :] * shifted[tap]
    sig = sigmoid(summed)
    grad_sum = grad_u * (sig * (1.0 + summed * (1.0 - sig)))
    grad_x = jnp.zeros_like(x_inner)
    for tap in range(taps):
        pieces.append(jnp.sum(grad_sum * shifted[tap], 0, keepdims=True))
        grad_x = grad_x + conv_ref[tap : tap + 1, :] * shift_rows(grad_sum, tap + 1 - taps)
    pieces.append(jnp.sum(grad_sum, 0, keepdims=True))
    pieces.append(jnp.zeros((pack_ref.shape[1] - grad_proj.shape[1] - taps - 1, x_inner.shape[1]), F32))
    split_lanes(pack_ref, jnp.concatenate(pieces, 0).astype(BF16))
    grad_x = grad_x.astype(BF16)
    split_lanes(gradx_ref, grad_x)
    grad_gate = jnp.concatenate([gradgate_ref[k] for k in range(gradgate_ref.shape[0])], 1)
    total[...] += product(grad_x, wx_ref[...]) + product(grad_gate, wg_ref[...])

    @pl.when(tile_id == pl.num_programs(0) - 1)
    def _():
        values = tokens_ref[...].astype(F32)
        scale = lax.rsqrt(jnp.mean(values * values, -1, keepdims=True) + 1e-05)
        unit = values * scale
        grad = total[...]
        widths = jnp.concatenate([widths_ref[...], jnp.sum(grad * unit, 0, keepdims=True)], 0)
        widths = jnp.concatenate(
            [widths, jnp.zeros((tail_ref.shape[1] - widths.shape[0], widths.shape[1]), F32)], 0
        )
        split_lanes(tail_ref, widths.astype(BF16))
        inner = grad * gain_ref[0:1, :]
        gradtok_ref[...] = gradmid_ref[...] + scale * (
            inner - unit * jnp.mean(inner * unit, -1, keepdims=True)
        )


def mixer_back(
    grad_proj, scan_w, grad_u, x_inner, vec, grad_gate, in_t, u_act, tokens, gains, grad_mid,
    grad_widths, tile, devices,
):
    rows, channels = u_act.shape
    gate_parts = tile * devices // (2 * channels)
    pack_parts = tile * devices // channels
    pack_rows = scan_w.shape[1] + 8
    tail_rows = grad_widths.shape[0] + 7
    width = tokens.shape[1]
    cols = scan_w.shape[1]
    steps = channels // tile
    column = lambda i: (0, i)
    fixed = lambda i: (0, 0)
    return pl.pallas_call(
        back_kernel,
        grid=(steps,),
        in_specs=[
            pl.BlockSpec((rows, cols), fixed),
            pl.BlockSpec((tile, cols), lambda i: (i, 0)),
            pl.BlockSpec((rows, tile), column),
            pl.BlockSpec((rows, tile), column),
            pl.BlockSpec((8, tile), lambda i: ((vec.shape[0] - 8) // 8, i)),
            pl.BlockSpec((gate_parts, rows, tile // gate_parts), lambda i: (i, 0, 0)),
            pl.BlockSpec((tile, width), lambda i: (i, 0)),
            pl.BlockSpec((tile, width), lambda i: (i + steps, 0)),
            pl.BlockSpec((rows, tile), column),
            pl.BlockSpec((rows, width), fixed),
            pl.BlockSpec(gains.shape, fixed),
            pl.BlockSpec((rows, width), fixed),
            pl.BlockSpec(grad_widths.shape, fixed),
        ],
        out_specs=[
            pl.BlockSpec((gate_parts, rows, tile // gate_parts), lambda i: (i, 0, 0)),
            pl.BlockSpec((pack_parts, pack_rows, tile // pack_parts), lambda i: (i, 0, 0)),
            pl.BlockSpec((devices, tail_rows, width // devices), lambda i: (0, 0, 0)),
            pl.BlockSpec((rows, width), fixed),
        ],
        out_shape=[
            jax.ShapeDtypeStruct((devices // 2, rows, 2 * channels // devices), BF16),
            jax.ShapeDtypeStruct((devices, pack_rows, channels // devices), BF16),
            jax.ShapeDtypeStruct((devices, tail_rows, width // devices), BF16),
            jax.ShapeDtypeStruct((rows, width), F32),
        ],
        scratch_shapes=[pltpu.VMEM((rows, width), F32)],
        compiler_params=pltpu.CompilerParams(vmem_limit_bytes=VMEM_LIMIT),
        name="mixer_back",
    )(
        grad_proj, scan_w, grad_u, x_inner, vec, grad_gate, in_t, in_t, u_act, tokens, gains,
        grad_mid, grad_widths,
    )


def gelu_parts(values):
    weight = jnp.exp(values * values * -0.5)
    scaled = jnp.abs(values) * 0.7071067811865476
    ratio = 1.0 / (1.0 + 0.3275911 * scaled)
    series = 1.061405429 * ratio - 1.453152027
    series = series * ratio + 1.421413741
    series = series * ratio - 0.284496736
    series = series * ratio + 0.254829592
    tail = (0.5 * ratio) * series * weight
    below = jnp.where(values >= 0.0, 1.0 - tail, tail)
    return values * below, below + values * weight * 0.3989422804014327


def router_kernel(
    mid_ref, gain_ref, router_ref, routes_col_ref, routes_row_ref, slots_row_ref, live_ref, cot_ref,
    sendr_ref, sendg_ref, normed_ref, probs_ref,
):
    mid = mid_ref[...]
    rows = mid.shape[0]
    experts = router_ref.shape[1]
    scale = lax.rsqrt(jnp.mean(mid * mid, -1, keepdims=True) + 1e-05)
    normed = (mid * scale * gain_ref[...]).astype(BF16)
    normed_ref[...] = normed
    logits = product(normed, router_ref[...])
    weights = jnp.exp(logits - jnp.max(logits, -1, keepdims=True))
    probs = weights / jnp.sum(weights, -1, keepdims=True)
    probs_ref[...] = probs
    chosen = (routes_col_ref[...] == iota((rows, experts), 1)).astype(F32)
    gate = jnp.sum(probs * chosen, 1, keepdims=True)
    grads = (gate * (cot_ref[...].astype(F32) * live_ref[...])).astype(BF16)
    slot = iota((experts * CAP, rows), 0)
    dispatch = (
        (routes_row_ref[...] == slot // CAP) & (slots_row_ref[...] == slot % CAP)
    ).astype(BF16)
    width = mid.shape[1]
    sendr_ref[...] = product(dispatch, normed).astype(BF16).reshape(experts, CAP, width)
    sendg_ref[...] = product(dispatch, grads).astype(BF16).reshape(experts, CAP, width)


def router_step(mid, gain, router, routes_col, routes_row, slots_row, live, cotangent):
    rows, width = mid.shape
    experts = router.shape[1]
    return pl.pallas_call(
        router_kernel,
        out_shape=[
            jax.ShapeDtypeStruct((experts, CAP, width), BF16),
            jax.ShapeDtypeStruct((experts, CAP, width), BF16),
            jax.ShapeDtypeStruct((rows, width), BF16),
            jax.ShapeDtypeStruct((rows, experts), F32),
        ],
        compiler_params=pltpu.CompilerParams(vmem_limit_bytes=VMEM_LIMIT),
        name="router_step",
    )(mid, gain, router, routes_col, routes_row, slots_row, live, cotangent)


def expert_out_kernel(rows_ref, up_ref, down_ref, out_ref, slope_ref, total):
    step = pl.program_id(0)
    pieces, cap, width = rows_ref.shape
    rows = rows_ref[...].reshape(pieces * cap, width)

    @pl.when(step == 0)
    def _():
        total[...] = jnp.zeros_like(total)

    activated, slope = gelu_parts(product(rows, up_ref[...]))
    slope_ref[...] = slope.astype(BF16)
    total[...] += product(activated.astype(BF16), down_ref[...])

    @pl.when(step == pl.num_programs(0) - 1)
    def _():
        out_ref[...] = total[...].astype(BF16).reshape(pieces, cap, width)


def expert_out(rows, up, down, tile):
    pieces, cap, width = rows.shape
    hidden = up.shape[1]
    fixed = lambda i: (0, 0, 0)
    return pl.pallas_call(
        expert_out_kernel,
        grid=(hidden // tile,),
        in_specs=[
            pl.BlockSpec(rows.shape, fixed),
            pl.BlockSpec((width, tile), lambda i: (0, i)),
            pl.BlockSpec((tile, width), lambda i: (i, 0)),
        ],
        out_specs=[
            pl.BlockSpec(rows.shape, fixed),
            pl.BlockSpec((pieces * cap, tile), lambda i: (0, i)),
        ],
        out_shape=[
            jax.ShapeDtypeStruct(rows.shape, BF16),
            jax.ShapeDtypeStruct((pieces * cap, hidden), BF16),
        ],
        scratch_shapes=[pltpu.VMEM((pieces * cap, width), F32)],
        compiler_params=pltpu.CompilerParams(vmem_limit_bytes=VMEM_LIMIT),
        name="expert_out",
    )(rows, up, down)


def expert_back_kernel(grads_ref, up_ref, down_ref, slope_ref, out_ref, total):
    step = pl.program_id(0)
    pieces, cap, width = grads_ref.shape
    grads = grads_ref[...].reshape(pieces * cap, width)

    @pl.when(step == 0)
    def _():
        total[...] = jnp.zeros_like(total)

    slope = slope_ref[...].astype(F32)
    grad_pre = (times_transpose(grads, down_ref[...]) * slope).astype(BF16)
    total[...] += times_transpose(grad_pre, up_ref[...])

    @pl.when(step == pl.num_programs(0) - 1)
    def _():
        out_ref[...] = total[...].astype(BF16).reshape(pieces, cap, width)


def expert_back(grads, up, down, slope, tile):
    pieces, cap, width = grads.shape
    hidden = up.shape[1]
    fixed = lambda i: (0, 0, 0)
    return pl.pallas_call(
        expert_back_kernel,
        grid=(hidden // tile,),
        in_specs=[
            pl.BlockSpec(grads.shape, fixed),
            pl.BlockSpec((width, tile), lambda i: (0, i)),
            pl.BlockSpec((tile, width), lambda i: (i, 0)),
            pl.BlockSpec((pieces * cap, tile), lambda i: (0, i)),
        ],
        out_specs=pl.BlockSpec(grads.shape, fixed),
        out_shape=jax.ShapeDtypeStruct(grads.shape, BF16),
        scratch_shapes=[pltpu.VMEM((pieces * cap, width), F32)],
        compiler_params=pltpu.CompilerParams(vmem_limit_bytes=VMEM_LIMIT),
        name="expert_back",
    )(grads, up, down, slope)


def expert_grads_kernel(chunks, rows_ref, grads_ref, up_ref, down_ref, gup_ref, gdown_ref, rows_t):
    chunk = pl.program_id(1)
    groups, pieces, cap, width = rows_ref.shape
    count = groups * pieces * cap
    rows = rows_ref[...].reshape(count, width)
    grads = grads_ref[...].reshape(count, width)

    @pl.when((pl.program_id(0) == 0) | (chunks > 1))
    def _():
        rows_t[...] = rows.T

    activated, slope = gelu_parts(product(rows, up_ref[...]))
    grad_pre = (times_transpose(grads, down_ref[...]) * slope).astype(BF16)
    grad_up = product(rows_t[...], grad_pre)
    grad_down = contract_rows(activated.astype(BF16), grads)

    @pl.when(chunk == 0)
    def _():
        gup_ref[...] = grad_up
        gdown_ref[...] = grad_down

    if chunks > 1:

        @pl.when(chunk > 0)
        def _():
            gup_ref[...] += grad_up
            gdown_ref[...] += grad_down


def expert_grads(rows, grads, up, down, tile):
    groups, pieces, cap, width = rows.shape
    hidden = up.shape[1]
    together = max(1, min(groups, 32 // pieces))
    chunks = groups // together
    some = pl.BlockSpec((together, pieces, cap, width), lambda i, j: (j, 0, 0, 0))
    return pl.pallas_call(
        partial(expert_grads_kernel, chunks),
        grid=(hidden // tile, chunks),
        in_specs=[
            some,
            some,
            pl.BlockSpec((width, tile), lambda i, j: (0, i)),
            pl.BlockSpec((tile, width), lambda i, j: (i, 0)),
        ],
        out_specs=[
            pl.BlockSpec((width, tile), lambda i, j: (0, i)),
            pl.BlockSpec((tile, width), lambda i, j: (i, 0)),
        ],
        out_shape=[
            jax.ShapeDtypeStruct((width, hidden), F32),
            jax.ShapeDtypeStruct((hidden, width), F32),
        ],
        scratch_shapes=[pltpu.VMEM((width, together * pieces * cap), BF16)],
        compiler_params=pltpu.CompilerParams(vmem_limit_bytes=VMEM_LIMIT),
        name="expert_grads",
    )(rows, grads, up, down)


def combine_kernel(
    mid_ref, gain_ref, router_ref, routes_ref, slots_ref, live_ref, cot_ref, probs_ref, normed_ref,
    backr_ref, backg_ref, out_ref, gradmid_ref, gradmix_ref, widths_ref,
):
    mid = mid_ref[...]
    rows, width = mid.shape
    experts = router_ref.shape[1]
    routes = routes_ref[...]
    chosen = (routes == iota((rows, experts), 1)).astype(F32)
    probs = probs_ref[...]
    gate = jnp.sum(probs * chosen, 1, keepdims=True)
    live = live_ref[...]
    slot = iota((rows, experts * CAP), 1)
    collect = ((routes == slot // CAP) & (slots_ref[...] == slot % CAP)).astype(BF16)
    expert_sum = product(collect, backr_ref[...].reshape(experts * CAP, width))
    out_ref[...] = (live * (mid + gate * expert_sum)).astype(BF16)
    grad_out = cot_ref[...].astype(F32) * live
    grad_gate = jnp.sum(grad_out * expert_sum, 1, keepdims=True)
    grad_logits = (probs * (chosen * grad_gate - gate * grad_gate)).astype(BF16)
    grad_router = contract_rows(grad_logits, normed_ref[...])
    grad = product(collect, backg_ref[...].reshape(experts * CAP, width))
    grad = grad + times_transpose(grad_logits, router_ref[...])
    scale = lax.rsqrt(jnp.mean(mid * mid, -1, keepdims=True) + 1e-05)
    unit = mid * scale
    widths_ref[...] = jnp.concatenate([grad_router, jnp.sum(grad * unit, 0, keepdims=True)], 0)
    inner = grad * gain_ref[...]
    grad_mid = grad_out + scale * (inner - unit * jnp.mean(inner * unit, -1, keepdims=True))
    gradmid_ref[...] = grad_mid
    gradmix_ref[...] = grad_mid.astype(BF16)


def combine_step(mid, gain, router, routes, slots, live, cotangent, probs, normed, backr, backg):
    rows, width = mid.shape
    return pl.pallas_call(
        combine_kernel,
        out_shape=[
            jax.ShapeDtypeStruct((rows, width), BF16),
            jax.ShapeDtypeStruct((rows, width), F32),
            jax.ShapeDtypeStruct((rows, width), BF16),
            jax.ShapeDtypeStruct((router.shape[1] + 1, width), F32),
        ],
        compiler_params=pltpu.CompilerParams(vmem_limit_bytes=VMEM_LIMIT),
        name="combine_step",
    )(mid, gain, router, routes, slots, live, cotangent, probs, normed, backr, backg)


MESH = pl.DeviceIdType.MESH


def neighbour(bit):
    me = lax.axis_index("expert")
    return me + (1 - 2 * ((me // bit) % 2)) * bit


def greet_send(line=True):
    devices, copies = lax.axis_size("expert"), lax.axis_size("dp")
    me, place = lax.axis_index("expert"), lax.axis_index("dp")
    barrier = pltpu.get_barrier_semaphore()
    for k in range(1, devices):
        pl.semaphore_signal(
            barrier, inc=1, device_id={"expert": (me + k) % devices}, device_id_type=MESH
        )
    if line:

        @pl.when(place < copies - 1)
        def _():
            pl.semaphore_signal(barrier, inc=1, device_id={"dp": place + 1}, device_id_type=MESH)

        @pl.when(place > 0)
        def _():
            pl.semaphore_signal(barrier, inc=1, device_id={"dp": place - 1}, device_id_type=MESH)


def greet_wait(line=True):
    devices, copies = lax.axis_size("expert"), lax.axis_size("dp")
    place = lax.axis_index("dp")
    barrier = pltpu.get_barrier_semaphore()
    ends = (place == 0) | (place == copies - 1)
    if line:
        pl.when(ends)(lambda: pl.semaphore_wait(barrier, devices))
        pl.when(jnp.logical_not(ends))(lambda: pl.semaphore_wait(barrier, devices + 1))
    else:
        pl.semaphore_wait(barrier, devices - 1)


def greet(line=True):
    greet_send(line)
    greet_wait(line)


class Exchange:
    def __init__(self, source, target, send_sems, recv_sems, local_sem):
        devices, me = lax.axis_size("expert"), lax.axis_index("expert")
        self.copies = []
        for k in range(1, devices):
            peer = (me + k) % devices
            self.copies.append(
                pltpu.make_async_remote_copy(
                    source.at[peer], target.at[me], send_sems.at[k], recv_sems.at[k],
                    device_id={"expert": peer}, device_id_type=MESH,
                )
            )
        self.local = pltpu.make_async_copy(source.at[me], target.at[me], local_sem)

    def start(self):
        for copy in self.copies:
            copy.start()
        self.local.start()

    def wait(self):
        self.local.wait()
        for copy in self.copies:
            copy.wait()


class Line:
    def __init__(self, stage, from_left, from_right, next_left, next_right, send_sems, recv_sems):
        place = lax.axis_index("dp")
        last = lax.axis_size("dp") - 1
        self.right = pltpu.make_async_remote_copy(
            from_left, next_left, send_sems.at[0], recv_sems.at[0],
            device_id={"dp": jnp.minimum(place + 1, last)}, device_id_type=MESH,
        )
        self.left = pltpu.make_async_remote_copy(
            from_right, next_right, send_sems.at[1], recv_sems.at[1],
            device_id={"dp": jnp.maximum(place - 1, 0)}, device_id_type=MESH,
        )
        self.send_right = (place >= stage - 1) & (place < last)
        self.send_left = (last - place >= stage - 1) & (place > 0)
        self.get_left = place >= stage
        self.get_right = last - place >= stage

    def start(self):
        pl.when(self.send_right)(lambda: self.right.start())
        pl.when(self.send_left)(lambda: self.left.start())

    def wait(self):
        pl.when(self.send_right)(lambda: self.right.wait_send())
        pl.when(self.send_left)(lambda: self.left.wait_send())
        pl.when(self.get_left)(lambda: self.right.wait_recv())
        pl.when(self.get_right)(lambda: self.left.wait_recv())


def as_column(row):
    return jnp.broadcast_to(row.astype(F32), (8, row.shape[1])).T[:, 0:1].astype(jnp.int32)


def dispatch_matrix(goal, experts):
    slot = iota((experts * CAP, goal.shape[1]), 0)
    return (goal[0:1, :] == slot).astype(BF16)


def expert_layer_kernel(
    length_ref, mid_ref, gains_ref, router_ref, routes_ref, slots_ref, cot_ref, up_hbm, down_hbm,
    out_ref, gradmid_ref, gradmix_ref, widths_ref, rows_out, grads_out,
    left_1, right_1, left_2, right_2, goal_l1, goal_r1, goal_l2, goal_r2, gup_hbm, gdown_hbm,
    raw, goal, up_ref, down_ref, send_r, send_g, got_r, got_g, slope_ref, total, give_r, give_g,
    back_r, back_g, probs_ref, act_ref, rows_t, gup_ref, gdown_ref,
    weight_sems, send_sems, recv_sems, local_sems, line_send, line_recv, out_sems, grad_sems,
):
    tile = 512
    rows, width = mid_ref.shape
    experts = router_ref.shape[0]
    hidden = up_ref.shape[1]
    load_up = pltpu.make_async_copy(up_hbm, up_ref, weight_sems.at[0])
    load_down = pltpu.make_async_copy(down_hbm, down_ref, weight_sems.at[1])
    greet_send()
    load_up.start()
    load_down.start()

    ways = [
        Exchange(source, target, send_sems.at[k], recv_sems.at[k], local_sems.at[k])
        for k, (source, target) in enumerate(
            [(send_r, got_r), (send_g, got_g), (give_r, back_r), (give_g, back_g)]
        )
    ]
    lines = [
        Line(stage, *buffers, line_send.at[k], line_recv.at[k])
        for k, (stage, buffers) in enumerate(
            [(1, (raw.at[part], raw.at[part], left_1.at[part], right_1.at[part])) for part in (0, 1)]
            + [(1, (goal, goal, goal_l1, goal_r1))]
            + [
                (2, (left_1.at[part], right_1.at[part], left_2.at[part], right_2.at[part]))
                for part in (0, 1)
            ]
            + [(2, (goal_l1, goal_r1, goal_l2, goal_r2))]
        )
    ]
    gain = gains_ref[1:2, :]
    live = (iota((rows, 1), 0) < length_ref[0]).astype(F32)
    routes, slots = as_column(routes_ref[...]), as_column(slots_ref[...])
    mid = mid_ref[...]
    scale = lax.rsqrt(jnp.mean(mid * mid, -1, keepdims=True) + 1e-05)
    normed = (mid * scale * gain).astype(BF16)
    raw[0] = normed
    slots_row = slots_ref[...]
    target = jnp.where(slots_row < CAP, routes_ref[...] * CAP + slots_row, -1)
    goal[...] = jnp.broadcast_to(target, goal.shape)
    dispatch = dispatch_matrix(goal, experts)
    send_r[...] = product(dispatch, normed).astype(BF16).reshape(experts, CAP, width)
    greet_wait()
    ways[0].start()
    for k in (0, 2):
        lines[k].start()
    logits = times_transpose(normed, router_ref[...])
    weights = jnp.exp(logits - jnp.max(logits, -1, keepdims=True))
    probs = weights / jnp.sum(weights, -1, keepdims=True)
    probs_ref[...] = probs
    chosen = (routes == iota((rows, experts), 1)).astype(F32)
    gate = jnp.sum(probs * chosen, 1, keepdims=True)
    grads = (gate * (cot_ref[...].astype(F32) * live)).astype(BF16)
    raw[1] = grads
    send_g[...] = product(dispatch, grads).astype(BF16).reshape(experts, CAP, width)
    ways[1].start()
    lines[1].start()

    load_up.wait()
    load_down.wait()
    ways[0].wait()
    for k in (0, 2):
        lines[k].wait()
        lines[k + 3].start()
    keep_rows = pltpu.make_async_copy(got_r, rows_out, out_sems.at[0])
    keep_rows.start()
    total[...] = jnp.zeros_like(total)

    def forward(step, carry):
        at = pl.ds(pl.multiple_of(step * tile, tile), tile)
        inputs = got_r[...].reshape(experts * CAP, width)
        activated, slope = gelu_parts(product(inputs, up_ref[:, at]))
        slope_ref[:, at] = slope.astype(BF16)
        activated = activated.astype(BF16)
        act_ref[:, at] = activated
        total[...] += product(activated, down_ref[at, :])
        return carry

    lax.fori_loop(0, hidden // tile, forward, 0)
    give_r[...] = total[...].astype(BF16).reshape(experts, CAP, width)
    ways[2].start()
    ways[1].wait()
    lines[1].wait()
    lines[4].start()
    keep_grads = pltpu.make_async_copy(got_g, grads_out, out_sems.at[1])
    keep_grads.start()
    total[...] = jnp.zeros_like(total)

    def backward(step, carry):
        at = pl.ds(pl.multiple_of(step * tile, tile), tile)
        outputs = got_g[...].reshape(experts * CAP, width)
        slope = slope_ref[:, at].astype(F32)
        grad_pre = (times_transpose(outputs, down_ref[at, :]) * slope).astype(BF16)
        slope_ref[:, at] = grad_pre
        total[...] += times_transpose(grad_pre, up_ref[:, at])
        return carry

    lax.fori_loop(0, hidden // tile, backward, 0)
    give_g[...] = total[...].astype(BF16).reshape(experts, CAP, width)
    ways[3].start()

    rows_t[...] = got_r[...].reshape(experts * CAP, width).T
    stores = []
    for step in range(hidden // tile):
        spot = step % 2
        at = pl.ds(step * tile, tile)
        if step >= 2:
            for store in stores[2 * (step - 2) : 2 * (step - 1)]:
                store.wait()
        gup_ref[spot] = product(rows_t[...], slope_ref[:, at]).astype(BF16)
        gdown_ref[spot] = contract_rows(
            act_ref[:, at], got_g[...].reshape(experts * CAP, width)
        ).astype(BF16)
        stores += [
            pltpu.make_async_copy(gup_ref.at[spot], gup_hbm.at[:, at], grad_sems.at[0, spot]),
            pltpu.make_async_copy(gdown_ref.at[spot], gdown_hbm.at[at], grad_sems.at[1, spot]),
        ]
        for store in stores[-2:]:
            store.start()

    chosen = (routes == iota((rows, experts), 1)).astype(F32)
    probs = probs_ref[...]
    gate = jnp.sum(probs * chosen, 1, keepdims=True)
    slot = iota((rows, experts * CAP), 1)
    collect = ((routes == slot // CAP) & (slots == slot % CAP)).astype(BF16)
    ways[2].wait()
    expert_sum = product(collect, back_r[...].reshape(experts * CAP, width))
    mid = mid_ref[...]
    out_ref[...] = (live * (mid + gate * expert_sum)).astype(BF16)
    grad_out = cot_ref[...].astype(F32) * live
    grad_gate = jnp.sum(grad_out * expert_sum, 1, keepdims=True)
    grad_logits = (probs * (chosen * grad_gate - gate * grad_gate)).astype(BF16)
    grad_router = contract_rows(grad_logits, raw[0])
    from_logits = product(grad_logits, router_ref[...])
    scale = lax.rsqrt(jnp.mean(mid * mid, -1, keepdims=True) + 1e-05)
    unit = mid * scale
    ways[3].wait()
    grad = product(collect, back_g[...].reshape(experts * CAP, width)) + from_logits
    widths_ref[...] = jnp.concatenate([grad_router, jnp.sum(grad * unit, 0, keepdims=True)], 0)
    inner = grad * gain
    grad_mid = grad_out + scale * (inner - unit * jnp.mean(inner * unit, -1, keepdims=True))
    gradmid_ref[...] = grad_mid
    gradmix_ref[...] = grad_mid.astype(BF16)
    for store in stores[-4:]:
        store.wait()
    keep_rows.wait()
    keep_grads.wait()
    for k in (3, 4, 5):
        lines[k].wait()


def expert_layer(lengths, mid, gains, router, routes, slots, cotangent, up, down):
    rows, width = mid.shape
    experts = router.shape[0]
    hidden = up.shape[1]
    buffer = (experts, CAP, width)
    here = pl.BlockSpec(memory_space=pltpu.VMEM)
    far = pl.BlockSpec(memory_space=pl.ANY)
    blocks = jax.ShapeDtypeStruct(buffer, BF16)
    raw = jax.ShapeDtypeStruct((2, rows, width), BF16)
    goal = jax.ShapeDtypeStruct((8, rows), jnp.int32)
    dma = pltpu.SemaphoreType.DMA
    return pl.pallas_call(
        expert_layer_kernel,
        in_specs=[pl.BlockSpec(memory_space=pltpu.SMEM)] + [here] * 6 + [far] * 2,
        out_specs=[here] * 4 + [far] * 12,
        out_shape=[
            jax.ShapeDtypeStruct((rows, width), BF16),
            jax.ShapeDtypeStruct((rows, width), F32),
            jax.ShapeDtypeStruct((rows, width), BF16),
            jax.ShapeDtypeStruct((experts + 1, width), F32),
        ] + [blocks] * 2 + [raw] * 4 + [goal] * 4 + [
            jax.ShapeDtypeStruct(up.shape, BF16),
            jax.ShapeDtypeStruct(down.shape, BF16),
        ],
        scratch_shapes=[
            pltpu.VMEM(raw.shape, BF16),
            pltpu.VMEM(goal.shape, jnp.int32),
            pltpu.VMEM(up.shape, BF16),
            pltpu.VMEM(down.shape, BF16),
        ] + [pltpu.VMEM(buffer, BF16)] * 4 + [
            pltpu.VMEM((experts * CAP, hidden), BF16),
            pltpu.VMEM((experts * CAP, width), F32),
        ] + [pltpu.VMEM(buffer, BF16)] * 4 + [
            pltpu.VMEM((rows, experts), F32),
            pltpu.VMEM((experts * CAP, hidden), BF16),
            pltpu.VMEM((width, experts * CAP), BF16),
            pltpu.VMEM((2, width, 512), BF16),
            pltpu.VMEM((2, 512, width), BF16),
            dma((2,)), dma((4, experts)), dma((4, experts)), dma((4,)), dma((6, 2)), dma((6, 2)),
            dma((2,)), dma((2, 2)),
        ],
        compiler_params=pltpu.CompilerParams(
            vmem_limit_bytes=VMEM_LIMIT, collective_id=1, has_side_effects=True
        ),
        name="expert_layer",
    )(lengths, mid, gains, router, routes, slots, cotangent, up, down)


class PlaneGather:
    def __init__(self, source, target, send_sems, recv_sems, local_sem):
        me = lax.axis_index("expert")
        core, side, above = neighbour(1), neighbour(2), neighbour(4)
        far = side + above - me
        rows = target.shape[1]
        first, second = pl.ds(0, rows // 2), pl.ds(rows // 2, rows - rows // 2)
        every = pl.ds(0, rows)

        def send(k, block, owner, part, device):
            return pltpu.make_async_remote_copy(
                block, target.at[owner, part], send_sems.at[k], recv_sems.at[k],
                device_id={"expert": device}, device_id_type=MESH,
            )

        self.copies = [
            send(0, source.at[first], me, first, side),
            send(1, source.at[second], me, second, side),
            send(2, source.at[first], me, first, above),
            send(3, source.at[second], me, second, above),
            send(4, target.at[side, first], side, first, above),
            send(5, target.at[above, second], above, second, side),
            send(6, source, me, every, core),
            send(7, target.at[side], side, every, core),
            send(8, target.at[above], above, every, core),
            send(9, target.at[far], far, every, core),
        ]
        self.local = pltpu.make_async_copy(source, target.at[me], local_sem)

    def step(self, number):
        copies = self.copies
        for k in ((), (0, 3), (1, 2), (4, 5), (6, 7, 8, 9))[number]:
            copies[k].wait_recv()
        for k in ((0, 3, 1, 2, 6), (4, 5), (7, 8), (9,), ())[number]:
            copies[k].start()
        if number == 0:
            self.local.start()
        if number == 4:
            self.local.wait()
            for copy in copies:
                copy.wait_send()


def greet_all():
    devices, copies = lax.axis_size("expert"), lax.axis_size("dp")
    me, place = lax.axis_index("expert"), lax.axis_index("dp")
    barrier = pltpu.get_barrier_semaphore()
    for k in range(1, devices):
        pl.semaphore_signal(
            barrier, inc=1, device_id={"expert": (me + k) % devices}, device_id_type=MESH
        )
    for k in range(1, copies):
        pl.semaphore_signal(
            barrier, inc=1, device_id={"dp": (place + k) % copies}, device_id_type=MESH
        )
    pl.semaphore_wait(barrier, devices + copies - 2)


class WideGather:
    def __init__(self, source, target, send_sems, recv_sems, local_sem):
        me, place = lax.axis_index("expert"), lax.axis_index("dp")
        core, side, above = neighbour(1), neighbour(2), neighbour(4)
        far = side + above - me
        odd = place % 2
        partner = place + 1 - 2 * odd
        rows = target.shape[1]
        unit = rows // 6

        def part(start, count):
            return pl.ds(pl.multiple_of(start * unit, unit), count * unit)

        def send(k, block, owner, where, **device):
            return pltpu.make_async_remote_copy(
                block, target.at[owner, where], send_sems.at[k], recv_sems.at[k],
                device_id=device, device_id_type=MESH,
            )

        def forward(k, owner, where, **device):
            return send(k, target.at[owner, where], owner, where, **device)

        outer, inner = part(4 * odd, 2), part(4 * (1 - odd), 2)
        middle = part(2, 2)
        self.copies = [
            send(0, source.at[outer], me, outer, expert=side),
            send(1, source.at[middle], me, middle, expert=side),
            send(2, source.at[inner], me, inner, expert=above),
            send(3, source.at[middle], me, middle, expert=above),
            forward(4, side, outer, expert=above),
            forward(5, side, part(2 + odd, 1), expert=above),
            forward(6, above, inner, expert=side),
            forward(7, above, part(3 - odd, 1), expert=side),
            forward(8, side, outer, dp=partner),
            forward(9, above, inner, dp=partner),
            send(10, source, me, part(0, 6), expert=core),
            forward(11, side, part(2 * odd, 4), expert=core),
            forward(12, above, part(2 - 2 * odd, 4), expert=core),
            forward(13, side, inner, expert=core),
            forward(14, above, outer, expert=core),
            forward(15, far, part(0, 6), expert=core),
        ]
        self.local = pltpu.make_async_copy(source, target.at[me], local_sem)

    def step(self, number):
        copies = self.copies
        for k in ((), (0, 2), (1, 3), (8, 9), (4, 5, 6, 7), (10, 11, 12, 13, 14, 15))[number]:
            copies[k].wait_recv()
        for k in ((0, 2, 1, 3, 10), (4, 6, 8, 9), (5, 7, 11, 12), (13, 14), (15,), ())[number]:
            copies[k].start()
        if number == 0:
            self.local.start()
        if number == 5:
            self.local.wait()
            for copy in copies:
                copy.wait_send()


class Near:
    def __init__(self, own, target, send_sems, recv_sems):
        self.place = lax.axis_index("dp")
        self.last = lax.axis_size("dp") - 1
        self.right = pltpu.make_async_remote_copy(
            own, target, send_sems.at[0], recv_sems.at[0],
            device_id={"dp": jnp.minimum(self.place + 1, self.last)}, device_id_type=MESH,
        )
        self.left = pltpu.make_async_remote_copy(
            own, target, send_sems.at[1], recv_sems.at[1],
            device_id={"dp": jnp.maximum(self.place - 1, 0)}, device_id_type=MESH,
        )

    def start(self):
        pl.when(self.place < self.last)(lambda: self.right.start())
        pl.when(self.place == 1)(lambda: self.left.start())

    def wait(self):
        pl.when(self.place < self.last)(lambda: self.right.wait_send())
        pl.when(self.place == 1)(lambda: self.left.wait_send())
        pl.when(self.place > 0)(lambda: self.right.wait_recv())
        pl.when(self.place == 0)(lambda: self.left.wait_recv())


DMA = pltpu.SemaphoreType.DMA
FAR = pl.BlockSpec(memory_space=pl.ANY)


def remote_params(collective_id):
    return pltpu.CompilerParams(
        vmem_limit_bytes=VMEM_LIMIT, collective_id=collective_id, has_side_effects=True
    )


def columns_of(proj_ref, first, state, target):
    turned = proj_ref[...].T[first : first + state]
    for block in range(proj_ref.shape[0] // BLOCK):
        target[block * state : (block + 1) * state, 0:BLOCK] = turned[
            :, block * BLOCK : (block + 1) * BLOCK
        ]


def diagonals_of(proj_ref, first, state, high_ref, low_ref):
    rows, width = proj_ref.shape
    big = BLOCK * state
    place = (iota((width, big), 0) == first + iota((width, big), 1) % state).astype(BF16)
    own = iota((rows, big), 0) % BLOCK == iota((rows, big), 1) // state
    for part, target in zip(two_parts(proj_ref[...]), (high_ref, low_ref)):
        target[...] = jnp.where(own, product(part, place), 0.0).astype(BF16)


def block_of(ref, block, size):
    return ref[pl.ds(pl.multiple_of(block * size, size), size), :]


def forward_kernel(
    tokens_ref, in_ref, scan_ref, step_w_ref, decay_ref, conv_ref, bias_ref, dbias_ref, skip_ref,
    norm_ref, norm_two_ref, router_ref, outw_ref,
    normed_ref, xin_ref, u_out, gate_out, proj_ref, step_ref, mixed_ref, gated_ref, mid_ref,
    step_full, vec_ref, router_full, gains_ref, scan_full, in_full, outw_all, normed_all, hist_hbm,
    columns, widths, columns_all, widths_all, scan_here, in_here, u_all, gate_all, b_cols, c_high, c_low, du,
    scanned, gated_all, outw_here, ring,
    send_sems, recv_sems, local_sems, ring_sems,
):
    step = pl.program_id(0)
    devices, rank, part = columns_all.shape[0], step_w_ref.shape[0], step_w_ref.shape[1]
    state, taps, experts = decay_ref.shape[0], conv_ref.shape[0], router_ref.shape[0]
    slice_w = widths.shape[1]
    rows, tile = xin_ref.shape
    width = tokens_ref.shape[1]
    big = BLOCK * state
    turns = ring.shape[0]
    last = rows // BLOCK - 1
    small = [
        PlaneGather(source, target, send_sems.at[k], recv_sems.at[k], local_sems.at[k])
        for k, (source, target) in enumerate(
            [(columns, columns_all), (widths, widths_all), (scan_ref, scan_here)]
        )
    ]
    big_gather = WideGather(in_ref, in_here, send_sems.at[3], recv_sems.at[3], local_sems.at[3])
    gather = WideGather(outw_ref, outw_here, send_sems.at[4], recv_sems.at[4], local_sems.at[4])
    normed_gather = PlaneGather(
        normed_ref, normed_all, send_sems.at[5], recv_sems.at[5], local_sems.at[5]
    )
    keep = pltpu.make_async_copy(outw_here, outw_all, local_sems.at[6])
    keep_in = pltpu.make_async_copy(in_here, in_full, local_sems.at[7])
    half = step % 2
    lanes = pl.ds(pl.multiple_of(half * tile, tile), tile)

    @pl.when(step == 0)
    def _():
        greet_send()
        spare = columns.shape[0] - rank - state - taps - 3
        columns[...] = jnp.concatenate(
            [
                step_w_ref[...].astype(F32), decay_ref[...].astype(F32), conv_ref[...].astype(F32),
                *(ref[...].astype(F32)[None] for ref in (bias_ref, dbias_ref, skip_ref)),
                jnp.zeros((spare, part), F32),
            ],
            0,
        ).astype(BF16)
        widths[...] = jnp.concatenate(
            [
                router_ref[...].astype(F32),
                *(ref[...].astype(F32)[None] for ref in (norm_ref, norm_two_ref)),
                jnp.zeros((widths.shape[0] - experts - 2, slice_w), F32),
            ],
            0,
        ).astype(BF16)
        greet_wait()
        for number in range(3):
            for one in small:
                one.step(number)
            big_gather.step(number)
        for number in (3, 4):
            for one in small:
                one.step(number)
        big_gather.step(3)
        gather.step(0)
        table = jnp.concatenate([columns_all[k].astype(F32) for k in range(devices)], 1)
        step_full[...] = table[:rank].astype(BF16)
        scan_full[...] = scan_here[...]
        rest = table[rank:]
        vec_ref[0:state, :] = -jnp.exp(rest[:state])
        vec_ref[state : state + 8, :] = rest[state : state + 8]
        across = jnp.concatenate([widths_all[k].astype(F32) for k in range(devices)], 1)
        router_full[...] = across[:experts].astype(BF16)
        gains_ref[...] = across[experts : experts + 8]
        values = tokens_ref[...].astype(F32)
        scale = lax.rsqrt(jnp.mean(values * values, -1, keepdims=True) + 1e-05)
        normed_ref[...] = (values * scale * gains_ref[0:1, :]).astype(BF16)
        proj_ref[...] = jnp.zeros_like(proj_ref)
        big_gather.step(4)
        big_gather.step(5)
        keep_in.start()
        gather.step(1)

    @pl.when(step < 2)
    def _():
        misc = vec_ref[state : state + 8, lanes]
        normed = normed_ref[...]
        own = devices // 4

        def weights(first):
            rows_here = in_here.shape[1]
            return in_here[pl.ds(first + half * own, own)].reshape(own * rows_here, width)

        x_inner = times_transpose(normed, weights(0))
        gate_in = times_transpose(normed, weights(devices // 2))
        gate_out[...] = gate_in
        gate_all[:, lanes] = gate_in
        xin_ref[...] = x_inner
        summed = misc[taps : taps + 1] + misc[taps - 1 : taps] * x_inner
        for back in range(1, taps):
            tap = taps - 1 - back
            summed = summed + misc[tap : tap + 1] * shift_rows(x_inner, back)
        u_act = summed * sigmoid(summed)
        u_out[...] = u_act
        u_all[:, lanes] = u_act
        parts = devices // 2
        scan_rows_here = scan_here[pl.ds(half * parts, parts)].reshape(tile, scan_here.shape[2])
        proj_ref[...] += product(u_act.astype(BF16), scan_rows_here)

    @pl.when(step == 1)
    def _():
        gather.step(2)
        normed_gather.step(0)
        columns_of(proj_ref, rank, state, b_cols)
        diagonals_of(proj_ref, rank + state, state, c_high, c_low)

    def store(spot, block):
        start = pl.multiple_of((block * BLOCK + 1) * state, state)
        return pltpu.make_async_copy(
            ring.at[spot], hist_hbm.at[pl.ds(start, big), lanes], ring_sems.at[spot]
        )

    def sum_states(spot, block):
        high, low = block_of(c_high, block, BLOCK), block_of(c_low, block, BLOCK)
        both = product(jnp.concatenate([high, low], 0), ring[spot])
        return both[:BLOCK] + both[BLOCK:]

    def between(position):
        if position == 1:
            gather.step(3)
            gather.step(4)
        if position == 4:
            gather.step(5)
            keep.start()
            normed_gather.step(1)
            normed_gather.step(2)
        if position == 7:
            normed_gather.step(3)

    @pl.when(step >= 2)
    def _():
        misc = vec_ref[state : state + 8, lanes]
        u_act = u_all[:, lanes]
        step_size = softplus(
            product(proj_ref[:, :rank].astype(BF16), step_full[:, lanes])
            + misc[taps + 1 : taps + 2]
        )
        step_ref[...] = step_size
        du[...] = step_size * u_act
        decay = vec_ref[0:state, lanes] * LOG2E
        ring[turns - 1] = jnp.zeros((big, tile), BF16)
        zero_row = pltpu.make_async_copy(
            ring.at[turns - 1, pl.ds(0, state)], hist_hbm.at[pl.ds(0, state), lanes],
            ring_sems.at[turns],
        )
        zero_row.start()
        zero_row.wait()

        def run_blocks(quarter, held):
            for spot in range(turns):
                block = quarter * turns + spot
                pl.when(quarter > 0)(lambda: store(spot, block).wait())
                base = pl.multiple_of(block * BLOCK, BLOCK)
                before = (spot - 1) % turns
                scanned[pl.ds(base, BLOCK), :] = sum_states(before, jnp.maximum(block - 1, 0))
                steps_now, du_now = block_of(step_ref, block, BLOCK), block_of(du, block, BLOCK)
                b_now = block_of(b_cols, block, state)
                for t in range(BLOCK):
                    b_wide = jnp.broadcast_to(b_now[:, t : t + 1], (state, tile))
                    fade = jnp.exp2(steps_now[t : t + 1, :] * decay)
                    held = fade * held + du_now[t : t + 1, :] * b_wide
                    ring[spot, t * state : (t + 1) * state, :] = held.astype(BF16)
                store(spot, block).start()
            for turn in range(2):
                for count in range(rows // BLOCK // turns):

                    @pl.when((step == turn + 2) & (quarter == count))
                    def _():
                        between(turn * 4 + count)

            return held

        quarters = rows // BLOCK // turns
        lax.fori_loop(0, quarters, run_blocks, jnp.zeros((state, tile), F32))
        scanned[pl.ds(rows, BLOCK), :] = sum_states(turns - 1, last)
        mixed = scanned[pl.ds(BLOCK, rows), :] + misc[taps + 2 : taps + 3] * u_act
        mixed_ref[...] = mixed
        gate_in = gate_all[:, lanes]
        gated = (mixed * (gate_in * sigmoid(gate_in))).astype(BF16)
        gated_ref[...] = gated.T.reshape(gated_ref.shape)
        gated_all[:, lanes] = gated
        for spot in range(turns):
            store(spot, last - turns + 1 + spot).wait()

    @pl.when(step == 3)
    def _():
        weights = outw_here[...].reshape(devices * part, width)
        mid_ref[...] = tokens_ref[...].astype(F32) + product(gated_all[...], weights)
        keep.wait()
        keep_in.wait()
        normed_gather.step(4)


def forward_plane(
    tokens, in_t, scan_w, step_w, decay_t, conv, bias, dbias, skip, norm, norm_two, router_t, out_w
):
    rows, width = tokens.shape
    rank, part = step_w.shape
    cols = scan_w.shape[1]
    devices = lax.axis_size("expert")
    channels = devices * part
    state, experts, slice_w = decay_t.shape[0], router_t.shape[0], router_t.shape[1]
    tile = channels // 2
    hist_rows = (rows + 1) * state
    first = lambda i: jnp.minimum(i, 1)
    second = lambda i: jnp.maximum(i - 2, 0)

    def whole(shape):
        return pl.BlockSpec(shape, lambda i: (0,) * len(shape), pipeline_mode=pl.Buffered(1))

    def kept(shape):
        return pl.BlockSpec(shape, lambda i: (0,) * len(shape))

    def halves(index):
        return pl.BlockSpec((rows, tile), lambda i: (0, index(i)))

    inputs = (
        tokens, in_t, scan_w, step_w, decay_t, conv, bias, dbias, skip, norm, norm_two, router_t
    )
    fixed = [
        ((rank, channels), BF16), ((state + 8, channels), F32), ((experts, width), BF16),
        ((8, width), F32), ((devices, part, cols), BF16),
    ]
    return pl.pallas_call(
        forward_kernel,
        grid=(4,),
        in_specs=[whole(value.shape) for value in inputs] + [FAR],
        out_specs=[
            kept((rows, width)),
            halves(first),
            halves(first),
            halves(first),
            kept((rows, cols)),
            halves(second),
            halves(second),
            pl.BlockSpec((devices // 2, part, rows), lambda i: (second(i), 0, 0)),
            kept((rows, width)),
        ] + [kept(shape) for shape, _ in fixed] + [FAR] * 4,
        out_shape=[
            jax.ShapeDtypeStruct((rows, width), BF16),
            jax.ShapeDtypeStruct((rows, channels), F32),
            jax.ShapeDtypeStruct((rows, channels), F32),
            jax.ShapeDtypeStruct((rows, channels), F32),
            jax.ShapeDtypeStruct((rows, cols), F32),
            jax.ShapeDtypeStruct((rows, channels), F32),
            jax.ShapeDtypeStruct((rows, channels), F32),
            jax.ShapeDtypeStruct((devices, part, rows), BF16),
            jax.ShapeDtypeStruct((rows, width), F32),
        ] + [jax.ShapeDtypeStruct(shape, kind) for shape, kind in fixed] + [
            jax.ShapeDtypeStruct((devices,) + in_t.shape, BF16),
            jax.ShapeDtypeStruct((devices, part, width), BF16),
            jax.ShapeDtypeStruct((devices, rows, width), BF16),
            jax.ShapeDtypeStruct((hist_rows, channels), BF16),
        ],
        scratch_shapes=[
            pltpu.VMEM((rank + state + 8, part), BF16),
            pltpu.VMEM((32, slice_w), BF16),
            pltpu.VMEM((devices, rank + state + 8, part), BF16),
            pltpu.VMEM((devices, 32, slice_w), BF16),
            pltpu.VMEM((devices, part, cols), BF16),
            pltpu.VMEM((devices,) + in_t.shape, BF16),
            pltpu.VMEM((rows, channels), F32),
            pltpu.VMEM((rows, channels), F32),
            pltpu.VMEM((rows // BLOCK * state, 128), F32),
            pltpu.VMEM((rows, BLOCK * state), BF16),
            pltpu.VMEM((rows, BLOCK * state), BF16),
            pltpu.VMEM((rows, tile), F32),
            pltpu.VMEM((rows + BLOCK, tile), F32),
            pltpu.VMEM((rows, channels), BF16),
            pltpu.VMEM((devices, part, width), BF16),
            pltpu.VMEM((4, BLOCK * state, tile), BF16),
            DMA((6, 16)), DMA((6, 16)), DMA((8,)), DMA((5,)),
        ],
        compiler_params=remote_params(3),
        name="mixer_forward",
    )(*inputs, out_w)


def prepare_sends(raw, goal, sends):
    experts, cap, width = sends.shape[1:]
    matrix = dispatch_matrix(goal, experts)
    for part in range(2):
        values = product(matrix, raw[part]).astype(BF16)
        sends[part] = values.reshape(experts, cap, width)


def pick(choices, raw, goal, sems):
    place = lax.axis_index("dp")
    for where, (source, source_goal) in enumerate(choices):

        @pl.when(place == where)
        def _():
            copies = [
                pltpu.make_async_copy(source, raw, sems.at[0]),
                pltpu.make_async_copy(source_goal, goal, sems.at[1]),
            ]
            for copy in copies:
                copy.start()
            for copy in copies:
                copy.wait()


def fold_rows(got_ref, width):
    return fold_value(jnp.sum(got_ref[...].astype(F32), 0), width)


def fold_value(total, width):
    quarter = total.shape[0] // 4
    folded = jnp.concatenate([total[k * quarter : (k + 1) * quarter] for k in range(4)], 1)
    return jnp.concatenate([folded, jnp.zeros((32 - quarter, width), F32)], 0).astype(BF16)


def backward_kernel(
    proj_ref, stepw_ref, decay_ref, misc_ref, u_ref, gate_ref, outw_ref, gradmix_ref, step_ref,
    mixed_ref, scanw_ref, xin_ref, misc_x_ref, wx_ref, wg_ref, u_x_ref, tokens_ref, gains_ref,
    widths_ref,
    gradmid_hbm, gated_hbm, normed_hbm, hist_hbm, rows_0, grads_0, left_1, right_1, left_2, right_2, goal_l1,
    goal_r1, goal_l2, goal_r2,
    gradtok_hbm, totals_hbm, back_hbm, tail_hbm, rows_1, grads_1, left_3, right_3, goal_l3, goal_r3, sends_hbm,
    c_cols, b_high, b_low, b_sums, c_sums, gy, du, grad_du, grad_step, ring, g_ring, w_ring,
    gradproj, gradu_all, gate_all, send_in, got_in, everyone, gated_all, send_scan, got_scan,
    pack_back, send_back, send_tail, totals, raw, goal, send_grads,
    g_send, g_recv, x_send, x_recv, l_send, l_recv, local_sems, ring_sems, load_sems,
):
    step = pl.program_id(0)
    devices, me = lax.axis_size("expert"), lax.axis_index("expert")
    half = devices // 2
    rank, state = stepw_ref.shape[0], decay_ref.shape[0]
    rows, cols = proj_ref.shape
    tile, small_tile, width = u_ref.shape[1], xin_ref.shape[1], tokens_ref.shape[1]
    blocks, big = rows // BLOCK, BLOCK * state
    turns = ring.shape[0]
    quarters = blocks // turns
    in_part = send_in.shape[0] // devices
    channels = half * in_part
    steps_x = channels // small_tile
    mix = PlaneGather(gradmix_ref, everyone, g_send, g_recv, local_sems.at[0])
    gated = Exchange(gated_hbm, gated_all, x_send.at[0], x_recv.at[0], local_sems.at[1])
    scan = Exchange(send_scan, got_scan, x_send.at[1], x_recv.at[1], local_sems.at[2])
    near_grads = Exchange(send_grads, grads_1, x_send.at[2], x_recv.at[2], local_sems.at[3])

    def input_part(device):
        return send_in.at[pl.ds(pl.multiple_of(device * in_part, in_part), in_part)]

    input_copies = [
        pltpu.make_async_remote_copy(
            input_part((me + k) % devices), got_in.at[me], x_send.at[3, k], x_recv.at[3, k],
            device_id={"expert": (me + k) % devices}, device_id_type=MESH,
        )
        for k in range(1, devices)
    ]
    input_local = pltpu.make_async_copy(input_part(me), got_in.at[me], local_sems.at[4])

    def start_some(copies, local, first, last):
        for k, copy in enumerate(copies):
            peer = (me + k + 1) % devices
            pl.when((peer >= first) & (peer < last))(lambda copy=copy: copy.start())
        pl.when((me >= first) & (me < last))(lambda: local.start())

    def start_inputs(first, last):
        start_some(input_copies, input_local, first, last)

    lines = [
        Line(3, left_2, right_2, left_3, right_3, l_send.at[0], l_recv.at[0]),
        Line(3, goal_l2, goal_r2, goal_l3, goal_r3, l_send.at[1], l_recv.at[1]),
        Near(rows_0, rows_1, l_send.at[2], l_recv.at[2]),
        Near(
            grads_0.at[pl.ds(half, half)], grads_1.at[pl.ds(half, half)], l_send.at[3], l_recv.at[3]
        ),
    ]
    load_normed = pltpu.make_async_copy(normed_hbm, everyone, load_sems.at[0])
    load_mid = pltpu.make_async_copy(gradmid_hbm, gy, load_sems.at[1])
    store_back = pltpu.make_async_copy(send_back, back_hbm, load_sems.at[8])
    store_tail = pltpu.make_async_copy(send_tail, tail_hbm, load_sems.at[9])
    store_sends = [
        pltpu.make_async_copy(source, sends_hbm.at[k], load_sems.at[6 + k])
        for k, source in enumerate((g_ring, w_ring))
    ]
    x_spot = (jnp.maximum(step - 2, 0) % steps_x) // (steps_x // 2)
    x_lanes = pl.ds(
        pl.multiple_of((jnp.maximum(step - 2, 0) % (steps_x // 2)) * small_tile, small_tile),
        small_tile,
    )
    lanes = pl.ds(pl.multiple_of(jnp.minimum(step, 1) * tile, tile), tile)

    def load(spot, block):
        start = pl.multiple_of(block * big, big)
        return pltpu.make_async_copy(
            hist_hbm.at[pl.ds(start, big + state), lanes], ring.at[spot], ring_sems.at[spot]
        )

    @pl.when(step < 2)
    def _():
        for spot in range(turns - 1):
            load(spot, blocks - 1 - spot).start()

    @pl.when(step == 0)
    def _():
        greet()
        mix.step(0)
        for line in lines:
            line.start()
        near_l, near_r = (left_1, goal_l1), (right_1, goal_r1)
        pick((near_r, near_l, near_l, near_l), raw, goal, load_sems.at[pl.ds(4, 2)])
        matrix = dispatch_matrix(goal, devices)
        send_grads[...] = product(matrix, raw[1]).astype(BF16).reshape(send_grads.shape)
        gradproj[...] = jnp.zeros_like(gradproj)
        b_sums[...] = jnp.zeros_like(b_sums)
        c_sums[...] = jnp.zeros_like(c_sums)
        columns_of(proj_ref, rank + state, state, c_cols)
        diagonals_of(proj_ref, rank, state, b_high, b_low)

    def between(position):
        if position == 1:
            pl.when(me < half)(lambda: near_grads.start())
        if position == 2:
            mix.step(1)
            mix.step(2)
            gated.start()
        if position == 5:
            mix.step(3)
        if position == 7:
            mix.step(4)
            gated.wait()

    @pl.when(step < 2)
    def _():
        skip_ref = scan_rows(misc_ref)[1]
        grad_gated = times_transpose(gradmix_ref[...], outw_ref[...])
        gate_in = gate_ref[...]
        gate_sig = sigmoid(gate_in)
        grad_mixed = grad_gated * (gate_in * gate_sig)
        grad_gate = (
            grad_gated * mixed_ref[...] * (gate_sig * (1.0 + gate_in * (1.0 - gate_sig)))
        ).astype(BF16)
        gate_all[:, lanes] = grad_gate
        start = pl.multiple_of(channels + step * tile, tile)
        send_in[pl.ds(start, tile), :] = grad_gate.T
        u_act = u_ref[...]
        step_size = step_ref[...]
        gy[...] = grad_mixed
        du[0:rows, :] = step_size * u_act
        du[rows:, :] = jnp.zeros((BLOCK, tile), F32)
        grad_skip = jnp.sum(grad_mixed * u_act, 0, keepdims=True)
        rate = decay_ref[...]
        decay = rate * LOG2E
        sums = (iota((BLOCK, big), 0) == iota((BLOCK, big), 1) // state).astype(BF16)
        g_ring[1] = jnp.zeros((big, tile), BF16)
        w_ring[1] = jnp.zeros((big, tile), BF16)

        def reduce_block(spot, block):
            grads = g_ring[spot]
            source = jnp.minimum(block, blocks - 1)
            high, low = block_of(b_high, source, BLOCK), block_of(b_low, source, BLOCK)
            both = product(jnp.concatenate([high, low], 0), grads)
            base = pl.ds(pl.multiple_of(block * BLOCK, BLOCK), BLOCK)
            grad_du[base, :] = both[:BLOCK] + both[BLOCK:]
            grad_step[base, :] = product(sums, w_ring[spot])
            b_sums[base, :] += times_transpose(du[base, :].astype(BF16), grads)

        def run_blocks(quarter, carry):
            carried, log_sum = carry
            for spot in range(turns):
                turn = quarter * turns + spot
                block = blocks - 1 - turn
                later = (spot + turns - 1) % turns
                if spot == 0:
                    load(later, block - turns + 1).start()
                else:
                    pl.when(quarter < quarters - 1)(
                        lambda: load(later, block - turns + 1).start()
                    )
                load(spot, block).wait()
                here, before = spot % 2, (spot + 1) % 2
                reduce_block(before, block + 1)
                base = pl.ds(pl.multiple_of(block * BLOCK, BLOCK), BLOCK)
                steps_now, gy_now = step_ref[base, :], gy[base, :]
                c_now = block_of(c_cols, block, state)
                c_sums[base, :] += times_transpose(gy_now.astype(BF16), ring[spot, state:, :])
                for t in range(BLOCK - 1, -1, -1):
                    at = slice(t * state, (t + 1) * state)
                    c_wide = jnp.broadcast_to(c_now[:, t : t + 1], (state, tile))
                    step_now = steps_now[t : t + 1, :]
                    fade = jnp.exp2(step_now * decay)
                    grad = gy_now[t : t + 1, :] * c_wide + carried
                    g_ring[here, at, :] = grad.astype(BF16)
                    carried = fade * grad
                    weighted = carried * ring[spot, at, :].astype(F32) * rate
                    w_ring[here, at, :] = weighted.astype(BF16)
                    log_sum = log_sum + weighted * step_now
            for turn in range(2):
                for part in range(quarters):

                    @pl.when((step == turn) & (quarter == part))
                    def _():
                        between(turn * 4 + part)

            return carried, log_sum

        zeros = jnp.zeros((state, tile), F32)
        _, log_sum = lax.fori_loop(0, quarters, run_blocks, (zeros, zeros))
        reduce_block(1, 0)
        full_du = grad_du[0:rows, :]
        gradu_all[:, lanes] = full_du * step_size + skip_ref[...] * gy[...]
        grad_size = grad_step[0:rows, :] + full_du * u_act
        grad_pre = grad_size * (1.0 - jnp.exp(-step_size))
        grad_low = grad_pre.astype(BF16)
        grad_step_w = contract_rows(proj_ref[:, :rank].astype(BF16), grad_low)
        packed = jnp.concatenate(
            [grad_step_w, log_sum, jnp.sum(grad_pre, 0, keepdims=True), grad_skip, zeros[:6]], 0
        ).astype(BF16)
        for turn in range(2):

            @pl.when(step == turn)
            def _():
                split_lanes(send_scan.at[pl.ds(turn * half, half)], packed)
                start_some(scan.copies, scan.local, turn * half, (turn + 1) * half)
                start_inputs(half + turn * half // 2, half + (turn + 1) * half // 2)

        gradproj[:, :rank] += times_transpose(grad_low, stepw_ref[...])

    @pl.when(step == 1)
    def _():
        own = iota((rows, big), 0) % BLOCK == iota((rows, big), 1) // state
        lane = iota((big, cols), 1)
        slot = iota((big, cols), 0) % state
        total = gradproj[...]
        for sums_here, first in ((b_sums[0:rows, :], rank), (c_sums[...], rank + state)):
            place = (lane == first + slot).astype(F32)
            total = total + exact_product(jnp.where(own, sums_here, 0.0), place)
        gradproj[...] = total

    @pl.when(step == 2)
    def _():
        load_mid.start()
        grad_du[...] = jnp.zeros_like(grad_du)

    @pl.when(step == steps_x + 2)
    def _():
        split_lanes(send_back, pack_back[...])
        store_back.start()
        lhs = jnp.concatenate([gated_all[k] for k in range(devices)], 1)
        totals[2 * gated_all.shape[1] : 3 * gated_all.shape[1], :] = product(
            lhs, everyone[...].reshape(devices * rows, width)
        ).astype(BF16)
        load_normed.start()

    here = pl.ds(
        pl.multiple_of((jnp.maximum(step - 2, 0) % steps_x) * small_tile, small_tile), small_tile
    )

    @pl.when((step >= 2) & (step < steps_x + 2))
    def _():
        conv_ref, bias_ref = conv_rows(misc_x_ref)
        grad_proj = gradproj[...].astype(BF16)
        grad_u = gradu_all[:, here] + times_transpose(grad_proj, scanw_ref[...])
        pieces = [contract_rows(grad_proj, u_x_ref[...].astype(BF16))]
        x_inner = xin_ref[...]
        taps = conv_ref.shape[0]
        shifted = [shift_rows(x_inner, taps - 1 - tap) for tap in range(taps)]
        summed = bias_ref[...]
        for tap in range(taps):
            summed = summed + conv_ref[tap : tap + 1, :] * shifted[tap]
        sig = sigmoid(summed)
        grad_sum = grad_u * (sig * (1.0 + summed * (1.0 - sig)))
        grad_x = jnp.zeros_like(x_inner)
        for tap in range(taps):
            pieces.append(jnp.sum(grad_sum * shifted[tap], 0, keepdims=True))
            grad_x = grad_x + conv_ref[tap : tap + 1, :] * shift_rows(grad_sum, tap + 1 - taps)
        pieces.append(jnp.sum(grad_sum, 0, keepdims=True))
        pieces.append(jnp.zeros((pack_back.shape[0] - cols - taps - 1, small_tile), F32))
        pack_back[:, here] = jnp.concatenate(pieces, 0).astype(BF16)
        grad_x = grad_x.astype(BF16)
        send_in[here, :] = grad_x.T
        ring[x_spot, 0:rows, x_lanes] = grad_x
        for part in range(half):
            done = -(-(part + 1) * in_part // small_tile) + 1
            pl.when(step == done)(lambda: start_inputs(part, part + 1))

    @pl.when(step >= steps_x + 2)
    def _():
        grad_du[0:rows, :] += product(ring[x_spot, 0:rows, x_lanes], wx_ref[...]) + product(
            gate_all[:, here], wg_ref[...]
        )

    @pl.when(step == steps_x + 3)
    def _():
        next_to = [(left_2, goal_l2), (right_2, goal_r2), (right_1, goal_r1)]
        pick(
            (next_to[1], next_to[2], next_to[2], next_to[0]), raw, goal, load_sems.at[pl.ds(4, 2)]
        )
        matrix = dispatch_matrix(goal, devices)
        for part, (target, store) in enumerate(zip((g_ring, w_ring), store_sends)):
            target[...] = product(matrix, raw[part]).astype(BF16).reshape(target.shape)
            store.start()

    @pl.when(step == 2 * steps_x + 1)
    def _():
        values = tokens_ref[...].astype(F32)
        scale = lax.rsqrt(jnp.mean(values * values, -1, keepdims=True) + 1e-05)
        unit = values * scale
        grad = grad_du[0:rows, :]
        widths = jnp.concatenate([widths_ref[...], jnp.sum(grad * unit, 0, keepdims=True)], 0)
        widths = jnp.concatenate(
            [widths, jnp.zeros((send_tail.shape[1] - widths.shape[0], width), F32)], 0
        )
        split_lanes(send_tail, widths.astype(BF16))
        store_tail.start()
        inner = grad * gains_ref[0:1, :]
        load_mid.wait()
        gy[...] += scale * (inner - unit * jnp.mean(inner * unit, -1, keepdims=True))
        store_tokens = pltpu.make_async_copy(gy, gradtok_hbm, load_sems.at[2])
        store_tokens.start()
        at = 3 * gated_all.shape[1]
        scan.wait()
        totals[at : at + 32, :] = fold_rows(got_scan, width)
        load_normed.wait()
        input_local.wait()
        for copy in input_copies:
            copy.wait()
        lhs = jnp.concatenate([got_in[k] for k in range(devices)], 1)
        totals[0:in_part, :] = product(
            lhs, everyone[...].reshape(devices * rows, width)
        ).astype(BF16)
        store_totals = pltpu.make_async_copy(totals, totals_hbm, load_sems.at[3])
        store_totals.start()
        for line in lines:
            line.wait()
        for k, copy in enumerate(near_grads.copies):
            pl.when(me < half)(lambda copy=copy: copy.wait_send())
            source = (me + devices - k - 1) % devices
            pl.when(source < half)(lambda copy=copy: copy.wait_recv())
        pl.when(me < half)(lambda: near_grads.local.wait())
        store_back.wait()
        store_tail.wait()
        store_tokens.wait()
        store_totals.wait()
        for store in store_sends:
            store.wait()


def backward_plane(
    proj, step_w, vec, u_act, gate_in, out_w, grad_mix, step_size, mixed, scan_w, x_inner, in_t,
    tokens, gains, grad_widths, grad_mid, gated, normed_all, hist, rows_0, grads_0, raws,
    goals,
):
    rows, channels = u_act.shape
    width = grad_mix.shape[1]
    cols = proj.shape[1]
    rank, state = step_w.shape[0], vec.shape[0] - 8
    devices = lax.axis_size("expert")
    part = channels // devices
    tile, small = channels // 2, channels // 6
    big = BLOCK * state
    pack_rows, tail_rows = cols + 8, grad_widths.shape[0] + 7
    fixed = lambda i: (0, 0)
    first = lambda i: jnp.minimum(i, 1)
    second = lambda i: jnp.clip(i - 2, 0, 5)
    once = pl.Buffered(1)
    slots = jax.ShapeDtypeStruct(rows_0.shape, BF16)
    raw = jax.ShapeDtypeStruct(raws[0].shape, BF16)
    goal = jax.ShapeDtypeStruct(goals[0].shape, jnp.int32)
    total_rows = 3 * part + 32
    pair = jax.ShapeDtypeStruct((2, 2, big, tile), BF16)
    third = lambda i: jnp.maximum(i - 8, 0)
    scan_pack = (devices, rank + state + 8, part)
    back_pack = (devices, pack_rows, part)
    tail_pack = (devices, tail_rows, width // devices)
    return pl.pallas_call(
        backward_kernel,
        grid=(14,),
        in_specs=[
            pl.BlockSpec((rows, cols), fixed),
            pl.BlockSpec((rank, tile), lambda i: (0, first(i))),
            pl.BlockSpec((state, tile), lambda i: (0, first(i))),
            pl.BlockSpec((8, tile), lambda i: (state // 8, first(i))),
            pl.BlockSpec((rows, tile), lambda i: (0, first(i))),
            pl.BlockSpec((rows, tile), lambda i: (0, first(i))),
            pl.BlockSpec((tile, width), lambda i: (first(i), 0), pipeline_mode=once),
            pl.BlockSpec((rows, width), fixed, pipeline_mode=once),
            pl.BlockSpec((rows, tile), lambda i: (0, first(i))),
            pl.BlockSpec((rows, tile), lambda i: (0, first(i))),
            pl.BlockSpec((small, cols), lambda i: (second(i), 0)),
            pl.BlockSpec((rows, small), lambda i: (0, second(i))),
            pl.BlockSpec((8, small), lambda i: (state // 8, second(i))),
            pl.BlockSpec((small, width), lambda i: (third(i), 0)),
            pl.BlockSpec((small, width), lambda i: (third(i) + 6, 0)),
            pl.BlockSpec((rows, small), lambda i: (0, second(i))),
            pl.BlockSpec((rows, width), fixed, pipeline_mode=once),
            pl.BlockSpec(gains.shape, fixed),
            pl.BlockSpec(grad_widths.shape, fixed),
        ] + [FAR] * 14,
        out_specs=[FAR] * 11,
        out_shape=[
            jax.ShapeDtypeStruct((rows, width), F32),
            jax.ShapeDtypeStruct((total_rows, width), BF16),
            jax.ShapeDtypeStruct(back_pack, BF16),
            jax.ShapeDtypeStruct(tail_pack, BF16),
            slots, slots, raw, raw, goal, goal, pair,
        ],
        scratch_shapes=[
            pltpu.VMEM((rows // BLOCK * state, 128), F32),
            pltpu.VMEM((rows, big), BF16),
            pltpu.VMEM((rows, big), BF16),
            pltpu.VMEM((rows + BLOCK, big), F32),
            pltpu.VMEM((rows, big), F32),
            pltpu.VMEM((rows, tile), F32),
            pltpu.VMEM((rows + BLOCK, tile), F32),
            pltpu.VMEM((rows + BLOCK, tile), F32),
            pltpu.VMEM((rows + BLOCK, tile), F32),
            pltpu.VMEM((4, big + state, tile), BF16),
            pltpu.VMEM((2, big, tile), BF16),
            pltpu.VMEM((2, big, tile), BF16),
            pltpu.VMEM((rows, cols), F32),
            pltpu.VMEM((rows, channels), F32),
            pltpu.VMEM((rows, channels), BF16),
            pltpu.VMEM((2 * channels, rows), BF16),
            pltpu.VMEM((devices, 2 * part, rows), BF16),
            pltpu.VMEM((devices, rows, width), BF16),
            pltpu.VMEM(gated.shape, BF16),
            pltpu.VMEM(scan_pack, BF16),
            pltpu.VMEM(scan_pack, BF16),
            pltpu.VMEM((pack_rows, channels), BF16),
            pltpu.VMEM(back_pack, BF16),
            pltpu.VMEM(tail_pack, BF16),
            pltpu.VMEM((total_rows, width), BF16),
            pltpu.VMEM(raw.shape, BF16),
            pltpu.VMEM(goal.shape, jnp.int32),
            pltpu.VMEM(slots.shape, BF16),
            DMA((10,)), DMA((10,)), DMA((4, devices)), DMA((4, devices)), DMA((4, 2)), DMA((4, 2)),
            DMA((5,)), DMA((4,)), DMA((10,)),
        ],
        compiler_params=pltpu.CompilerParams(
            vmem_limit_bytes=VMEM_LIMIT, collective_id=4, has_side_effects=True
        ),
        name="mixer_backward",
    )(
        proj, step_w, vec, vec, u_act, gate_in, out_w, grad_mix, step_size, mixed, scan_w, x_inner,
        vec, in_t, in_t, u_act, tokens, gains, grad_widths, grad_mid, gated, normed_all, hist,
        rows_0, grads_0, *raws, *goals,
    )


def add_groups(rows, grads, rows_t, up_ref, down_ref):
    activated, slope = gelu_parts(product(rows, up_ref[...]))
    grad_pre = (times_transpose(grads, down_ref[...]) * slope).astype(BF16)
    return product(rows_t, grad_pre), contract_rows(activated.astype(BF16), grads)


def flat_rows(refs):
    experts, cap, width = refs[0].shape
    values = [ref[...].reshape(ref.shape[0] * cap, width) for ref in refs]
    return values[0] if len(values) == 1 else jnp.concatenate(values, 0)


def two_grads_kernel(
    up_ref, down_ref, gup_in, gdown_in, rows_1, grads_1, sends_2, left_2, left_3, right_2, right_3,
    goal_l2, goal_l3, goal_r2, goal_r3, back_hbm, tail_hbm,
    gup_ref, gdown_ref, rows_3, grads_3, small_ref,
    rows_t, gup_all, gdown_all, rows_2, grads_2, raw, goal, sends_3, own_back, pair_back, pair_sum,
    far_back, got_tail, small_here, small_all, z_send, z_recv, b_send, b_recv, x_send, x_recv,
    local_sems, load_sems, back_sems,
):
    step = pl.program_id(0)
    tiles = gup_all.shape[0]
    spot = step % tiles
    seconds, thirds = (
        [
            Exchange(
                source.at[k], out, x_send.at[first + k], x_recv.at[first + k],
                local_sems.at[first + k],
            )
            for k, out in enumerate(targets)
        ]
        for first, source, targets in (
            (0, sends_2, (rows_2, grads_2)), (2, sends_3, (rows_3, grads_3))
        )
    )

    small_tail = Exchange(
        tail_hbm, got_tail, x_send.at[4], x_recv.at[4], local_sems.at[4]
    )
    me = lax.axis_index("expert")
    core, chip = me % 2, me // 2
    chips = pair_sum.shape[0]
    to_core = [
        pltpu.make_async_remote_copy(
            back_hbm.at[2 * k + 1 - core], pair_back.at[k], b_send.at[k], b_recv.at[k],
            device_id={"expert": neighbour(1)}, device_id_type=MESH,
        )
        for k in range(chips)
    ]
    own_loads = [
        pltpu.make_async_copy(back_hbm.at[2 * k + core], own_back.at[k], back_sems.at[k])
        for k in range(chips)
    ]
    to_chips = [
        pltpu.make_async_remote_copy(
            pair_sum.at[(chip + k) % chips], far_back.at[k - 1], b_send.at[chips + k - 1],
            b_recv.at[chips + k - 1], device_id={"expert": 2 * ((chip + k) % chips) + core},
            device_id_type=MESH,
        )
        for k in range(1, chips)
    ]
    place, copies = lax.axis_index("dp"), lax.axis_size("dp")
    to_copies = [
        pltpu.make_async_remote_copy(
            small_here, small_all.at[k - 1], z_send.at[k - 1], z_recv.at[k - 1],
            device_id={"dp": (place + k) % copies}, device_id_type=MESH,
        )
        for k in range(1, copies)
    ]

    @pl.when(step == 0)
    def _():
        greet_all()
        for way in seconds:
            way.start()
        for copy in to_core + own_loads:
            copy.start()
        rows_t[...] = flat_rows((rows_1,)).T

    @pl.when(step == 1)
    def _():
        pick(
            ((right_3, goal_r3), (right_2, goal_r2), (left_2, goal_l2), (left_3, goal_l3)), raw,
            goal, load_sems,
        )
        prepare_sends(raw, goal, sends_3)

    @pl.when(step == tiles - 2)
    def _():
        for copy in to_core + own_loads:
            copy.wait()
        pair_sum[...] = (own_back[...].astype(F32) + pair_back[...].astype(F32)).astype(BF16)
        for copy in to_chips:
            copy.start()
        small_tail.start()
        for way in thirds:
            way.start()

    @pl.when(step == 2 * tiles - 3)
    def _():
        small_tail.wait()
        for copy in to_chips:
            copy.wait()
        width = small_here.shape[1]
        back = pair_sum[chip].astype(F32) + jnp.sum(far_back[...].astype(F32), 0)
        small_here[0:32, :] = fold_value(back, width)
        tail = jnp.sum(got_tail[...].astype(F32), 0)
        tail = jnp.concatenate([tail, jnp.zeros((tail.shape[0], width - tail.shape[1]), F32)], 1)
        small_here[32:48, :] = tail.astype(BF16)
        for copy in to_copies:
            copy.start()

    @pl.when(step < tiles)
    def _():
        grad_up, grad_down = add_groups(
            flat_rows((rows_1,)), flat_rows((grads_1,)), rows_t[...], up_ref, down_ref
        )
        gup_all[spot] = (gup_in[...].astype(F32) + grad_up).astype(BF16)
        gdown_all[spot] = (gdown_in[...].astype(F32) + grad_down).astype(BF16)

    @pl.when(step == tiles)
    def _():
        for way in seconds:
            way.wait()
        rows_t[...] = flat_rows((rows_2,)).T

    @pl.when(step >= tiles)
    def _():
        grad_up, grad_down = add_groups(
            flat_rows((rows_2,)), flat_rows((grads_2,)), rows_t[...], up_ref, down_ref
        )
        gup_ref[...] = (gup_all[spot].astype(F32) + grad_up).astype(BF16)
        gdown_ref[...] = (gdown_all[spot].astype(F32) + grad_down).astype(BF16)

    @pl.when(step == 2 * tiles - 1)
    def _():
        for copy in to_copies:
            copy.wait()
        small_ref[...] = small_here[...].astype(F32) + jnp.sum(small_all[...].astype(F32), 0)
        for way in thirds:
            way.wait()


def last_grads_kernel(
    up_ref, down_ref, gup_in, gdown_in, rows_ref, grads_ref, gup_ref, gdown_ref, rows_t
):
    rows, grads = flat_rows((rows_ref,)), flat_rows((grads_ref,))

    @pl.when(pl.program_id(0) == 0)
    def _():
        rows_t[...] = rows.T

    grad_up, grad_down = add_groups(rows, grads, rows_t[...], up_ref, down_ref)
    gup_ref[...] = gup_in[...].astype(F32) + grad_up
    gdown_ref[...] = gdown_in[...].astype(F32) + grad_down


def expert_grads_plane(
    up, down, grad_up, grad_down, rows, grads, sends, raws, goals, back, tail, tile
):
    width, hidden = up.shape
    devices, cap = grads.shape[:2]
    slots = jax.ShapeDtypeStruct(grads.shape, BF16)
    pair = jax.ShapeDtypeStruct(sends.shape, BF16)
    whole = pl.BlockSpec(grads.shape, lambda i: (0, 0, 0))

    def tiles(size):
        return [
            pl.BlockSpec((width, size), lambda i: (0, i)),
            pl.BlockSpec((size, width), lambda i: (i, 0)),
        ]

    def shapes(kind):
        return [
            jax.ShapeDtypeStruct((width, hidden), kind), jax.ShapeDtypeStruct((hidden, width), kind)
        ]

    turned = pltpu.VMEM((width, devices * cap), BF16)
    count = hidden // tile
    again = [
        pl.BlockSpec((width, tile), lambda i: (0, i % count)),
        pl.BlockSpec((tile, width), lambda i: (i % count, 0)),
    ]
    early = [
        pl.BlockSpec((width, tile), lambda i: (0, jnp.minimum(i, count - 1))),
        pl.BlockSpec((tile, width), lambda i: (jnp.minimum(i, count - 1), 0)),
    ]
    late = [
        pl.BlockSpec((width, tile), lambda i: (0, jnp.maximum(i - count, 0))),
        pl.BlockSpec((tile, width), lambda i: (jnp.maximum(i - count, 0), 0)),
    ]
    small = (48, width)
    grad_up, grad_down, rows, grads, small_total = pl.pallas_call(
        two_grads_kernel,
        grid=(2 * count,),
        in_specs=again + early + [whole] * 2 + [FAR] * 11,
        out_specs=late + [FAR] * 2 + [pl.BlockSpec(small, lambda i: (0, 0))],
        out_shape=shapes(BF16) + [slots] * 2 + [jax.ShapeDtypeStruct(small, F32)],
        scratch_shapes=[
            turned,
            pltpu.VMEM((count, width, tile), BF16),
            pltpu.VMEM((count, tile, width), BF16),
            pltpu.VMEM(slots.shape, BF16),
            pltpu.VMEM(slots.shape, BF16),
            pltpu.VMEM(raws[0].shape, BF16),
            pltpu.VMEM(goals[0].shape, jnp.int32),
            pltpu.VMEM(pair.shape, BF16),
            pltpu.VMEM((devices // 2,) + back.shape[1:], BF16),
            pltpu.VMEM((devices // 2,) + back.shape[1:], BF16),
            pltpu.VMEM((devices // 2,) + back.shape[1:], BF16),
            pltpu.VMEM((devices // 2 - 1,) + back.shape[1:], BF16),
            pltpu.VMEM(tail.shape, BF16),
            pltpu.VMEM(small, BF16),
            pltpu.VMEM((3,) + small, BF16),
            DMA((3,)), DMA((3,)), DMA((devices - 1,)), DMA((devices - 1,)), DMA((5, devices)),
            DMA((5, devices)), DMA((5,)), DMA((2,)), DMA((devices // 2,)),
        ],
        compiler_params=remote_params(6),
        name="expert_grads_12",
    )(up, down, grad_up, grad_down, rows, grads, sends, *raws, *goals, back, tail)
    grad_up, grad_down = pl.pallas_call(
        last_grads_kernel,
        grid=(hidden // 768,),
        in_specs=tiles(768) * 2 + [whole] * 2,
        out_specs=tiles(768),
        out_shape=shapes(F32),
        scratch_shapes=[turned],
        compiler_params=pltpu.CompilerParams(vmem_limit_bytes=VMEM_LIMIT),
        name="expert_grads_3",
    )(up, down, grad_up, grad_down, rows, grads)
    return grad_up, grad_down, small_total


def finish_kernel(
    totals_ref, small_ref, in_ref, out_ref, scanw_ref, stepw_ref, decay_ref, conv_ref, router_ref, bias_ref,
    dbias_ref, skip_ref, norm_two_ref, norm_ref,
):
    in_rows, part = in_ref.shape[0], out_ref.shape[0]
    cols, rank, state, taps = (
        scanw_ref.shape[1], stepw_ref.shape[0], decay_ref.shape[0], conv_ref.shape[0]
    )
    experts, slice_w = router_ref.shape
    in_ref[...] = totals_ref[0:in_rows, :].astype(F32)
    out_ref[...] = totals_ref[in_rows : in_rows + part, :].astype(F32)
    at = in_rows + part
    unfolded = []
    for block, quarter in (
        (totals_ref[at : at + 32, :].astype(F32), (rank + state + 8) // 4),
        (small_ref[0:32, :], (cols + 8) // 4),
    ):
        unfolded.append(
            jnp.concatenate(
                [block[:quarter, k * part : (k + 1) * part] for k in range(4)], 0
            )
        )
    scan, back = unfolded
    stepw_ref[...] = scan[:rank]
    decay_ref[...] = scan[rank : rank + state]
    scanw_ref[...] = back[:cols].T
    conv_ref[...] = back[cols : cols + taps]
    bias_ref[...] = back[cols + taps]
    dbias_ref[...] = scan[rank + state]
    skip_ref[...] = scan[rank + state + 1]
    tail = small_ref[32:48, :][:, :slice_w]
    router_ref[...] = tail[:experts]
    norm_two_ref[...] = tail[experts]
    norm_ref[...] = tail[experts + 1]


def finish(totals, small, in_rows, part, cols, rank, state, taps, experts, slice_w):
    here = pl.BlockSpec(memory_space=pltpu.VMEM)
    return pl.pallas_call(
        finish_kernel,
        in_specs=[here] * 2,
        out_specs=[here] * 12,
        out_shape=[
            jax.ShapeDtypeStruct(shape, F32)
            for shape in (
                (in_rows, totals.shape[1]), (part, totals.shape[1]), (part, cols), (rank, part),
                (state, part), (taps, part), (experts, slice_w), (part,), (part,), (part,),
                (slice_w,), (slice_w,),
            )
        ],
        compiler_params=pltpu.CompilerParams(vmem_limit_bytes=VMEM_LIMIT),
        name="finish",
    )(totals, small)


def gather(value):
    return lax.all_gather(value, "expert", axis=0, tiled=True)


def exchange(value):
    return lax.all_to_all(value, "expert", split_axis=0, concat_axis=0, tiled=True)


def shards(
    tokens, lengths, routes, slot_index, mixer_norm, in_weight, conv_weight, conv_bias,
    scan_weight, step_weight, step_bias, decay_log, skip_gain, out_weight, moe_norm, router_weight,
    up_weight, down_weight, cotangent,
):
    devices = lax.axis_size("expert")
    rows, width = tokens.shape[1:]
    part = out_weight.shape[0]
    channels = part * devices
    cols = scan_weight.shape[1]
    rank, state, taps = step_weight.shape[0], decay_log.shape[1], conv_weight.shape[0]
    experts = router_weight.shape[1]
    split = devices // experts
    slice_w = width // devices
    tile = channels // 2

    on_plane = devices == 8 and split == 1 and lax.axis_size("dp") == 4
    in_t, decay_t, router_t = in_weight.T, decay_log.T, router_weight.T
    up, down = up_weight[0], down_weight[0]
    hidden = up.shape[1]
    if on_plane:
        (
            normed_low, x_inner, u_act, gate_in, proj, step_size, mixed, gated, mid, step_full, vec,
            router_t, gains, scan_full, in_t, out_full, normed_all, hist,
        ) = forward_plane(
            tokens[0], in_t, scan_weight, step_weight, decay_t, conv_weight, conv_bias, step_bias,
            skip_gain, mixer_norm, moe_norm, router_t, out_weight,
        )
        in_t = in_t.reshape(2 * channels, width)
        scan_full = scan_full.reshape(channels, cols)
        out_full = out_full.reshape(channels, width)
        layer_out, grad_mid, grad_mix, grad_widths, rows_0, grads_0, *line = expert_layer(
            lengths, mid, gains, router_t, routes, slot_index, cotangent[0], up, down
        )
        raws, goals, grad_up, grad_down = line[:4], line[4:8], line[8], line[9]
        (
            tokens_grad, totals, back_parts, tail_parts, rows_1, grads_1, left_3, right_3, goal_l3,
            goal_r3, sends,
        ) = backward_plane(
            proj, step_full, vec, u_act, gate_in, out_full, grad_mix, step_size, mixed, scan_full,
            x_inner, in_t, tokens[0], gains, grad_widths, grad_mid, gated, normed_all, hist, rows_0,
            grads_0, raws, goals,
        )
        totals = lax.psum(totals, "dp")
        grad_up, grad_down, small_total = expert_grads_plane(
            up, down, grad_up, grad_down, rows_1, grads_1,
            sends.reshape((2,) + rows_1.shape), (raws[2], left_3, raws[3], right_3),
            (goals[2], goal_l3, goals[3], goal_r3), back_parts, tail_parts, 512,
        )
        in_total, out_total, scan_w_total, step_w_total, decay_total, conv_total, *rest = finish(
            totals, small_total, 2 * part, part, cols, rank, state, taps, experts, slice_w
        )
        router_total, vector_totals, norm_totals = rest[0], rest[1:4], rest[4:]
    else:
        vectors = jnp.stack([conv_bias, step_bias, skip_gain])
        norms = jnp.stack([mixer_norm, moe_norm])
        spare = jnp.zeros((8 - taps - 3, part), BF16)
        columns = jnp.concatenate([step_weight, decay_t, conv_weight, vectors, spare], 0)
        across = jnp.concatenate([router_t, norms, jnp.zeros((6, slice_w), BF16)], 0)
        in_t, scan_full, columns, across = (
            lax.all_gather(value, "expert") for value in (in_t, scan_weight, columns, across)
        )
        columns = columns.transpose(1, 0, 2).reshape(columns.shape[1], channels)
        across = across.transpose(1, 0, 2).reshape(across.shape[1], width)
        step_full, rest = columns[:rank], columns[rank:].astype(F32)
        vec = jnp.concatenate([-jnp.exp(rest[:state]), rest[state:]], 0)
        router_t, gains = across[:experts], across[experts:].astype(F32)
        in_t = in_t.reshape(2 * channels, width)
        scan_full = scan_full.reshape(channels, cols)
        normed_low, x_inner, u_act, gate_in, proj = front(
            tokens[0], gains, in_t, vec, scan_full, tile
        )
        live = (jnp.arange(rows, dtype=jnp.int32) < lengths[0]).astype(F32)[:, None]
        routes_col, slots_col = routes[0][:, None], slot_index[0][:, None]
        router, gain_second = router_t.T, gains[1:2]
        out_full = gather(out_weight)
        step_size, mixed, gated, hist, mid = scan_forward(
            proj, step_full, vec, u_act, gate_in, out_full, tokens[0], tile
        )
        send_rows, send_grads, normed_two, probs = router_step(
            mid, gain_second, router, routes_col, routes, slot_index, live, cotangent[0]
        )

        def to_pieces(value):
            wide = jnp.broadcast_to(value[:, None], (experts, split) + value.shape[1:])
            return exchange(wide.reshape(devices, CAP, width))

        def from_pieces(value):
            value = exchange(value).reshape(experts, split, CAP, width)
            if split == 1:
                return value[:, 0]
            return jnp.sum(value.astype(F32), 1).astype(BF16)

        some = min(512, hidden // 3)
        rows_in = to_pieces(send_rows)
        grads_in = to_pieces(send_grads)
        partial_out, slope = expert_out(rows_in, up, down, some)
        back_rows = from_pieces(partial_out)
        back_grads = from_pieces(expert_back(grads_in, up, down, slope, some))
        all_rows = lax.all_gather(rows_in, "dp")
        layer_out, grad_mid, grad_mix, grad_widths = combine_step(
            mid, gain_second, router, routes_col, slots_col, live, cotangent[0], probs, normed_two,
            back_rows, back_grads,
        )
        grad_mix, all_rows = lax.optimization_barrier((grad_mix, all_rows))
        all_grads = lax.all_gather(grads_in, "dp")
        out_parts = contract_rows(gated, grad_mix).astype(BF16).reshape(devices, part, width)
        grad_out_w = jnp.sum(exchange(out_parts).astype(F32), 0).astype(BF16)
        grad_u, grad_gate, scan_parts, grad_proj = scan_backward(
            proj, step_full, vec, u_act, gate_in, out_full, grad_mix, step_size, mixed, hist, tile,
            devices,
        )
        scan_small = jnp.sum(exchange(scan_parts).astype(F32), 0).astype(BF16)
        grad_x, back_parts, width_parts, tokens_grad = mixer_back(
            grad_proj, scan_full, grad_u, x_inner, vec, grad_gate, in_t, u_act, tokens[0], gains,
            grad_mid, grad_widths, tile, devices,
        )
        back_small = jnp.sum(exchange(back_parts).astype(F32), 0).astype(BF16)
        width_small = jnp.sum(exchange(width_parts).astype(F32), 0).astype(BF16)
        normed_all = gather(normed_low)
        grad_in_parts = exchange(jnp.concatenate([grad_x, grad_gate], 0))
        grad_in_w = contract_rows(
            grad_in_parts.reshape(devices * rows, 2 * part), normed_all
        ).astype(BF16)
        totals = (grad_in_w, grad_out_w, scan_small, back_small, width_small)
        totals, all_grads = lax.optimization_barrier((totals, all_grads))
        totals = lax.psum(totals, "dp")
        in_total, out_total, scan_small, back_small, width_small = (
            t.astype(F32) for t in totals
        )
        grad_up, grad_down = expert_grads(all_rows, all_grads, up, down, min(256, hidden))
        scan_w_total, conv_total = back_small[:cols].T, back_small[cols : cols + taps]
        step_w_total, decay_total = scan_small[:rank], scan_small[rank : rank + state]
        vector_totals = (
            back_small[cols + taps], scan_small[rank + state], scan_small[rank + state + 1]
        )
        router_total = width_small[:experts]
        norm_totals = (width_small[experts], width_small[experts + 1])
    return (
        layer_out[None],
        tokens_grad[None],
        norm_totals[1],
        in_total.T,
        conv_total,
        vector_totals[0],
        scan_w_total,
        step_w_total,
        vector_totals[1],
        decay_total.T,
        vector_totals[2],
        out_total,
        norm_totals[0],
        router_total.T,
        grad_up[None],
        grad_down[None],
    )


def solution(mesh):
    in_specs = (
        P(("dp", "expert"), None, None),
        P(("dp", "expert")),
        P(("dp", "expert"), None),
        P(("dp", "expert"), None),
        P("expert"),
        P(None, "expert"),
        P(None, "expert"),
        P("expert"),
        P("expert", None),
        P(None, "expert"),
        P("expert"),
        P("expert", None),
        P("expert"),
        P("expert", None),
        P("expert"),
        P("expert", None),
        P("expert", None, None),
        P("expert", None, None),
        P(("dp", "expert"), None, None),
    )
    out_specs = (
        P(("dp", "expert"), None, None),
        P(("dp", "expert"), None, None),
        P("expert"),
        P(None, "expert"),
        P(None, "expert"),
        P("expert"),
        P("expert", None),
        P(None, "expert"),
        P("expert"),
        P("expert", None),
        P("expert"),
        P("expert", None),
        P("expert"),
        P("expert", None),
        P("expert", None, None),
        P("expert", None, None),
    )
    return jax.shard_map(shards, mesh=mesh, in_specs=in_specs, out_specs=out_specs, check_vma=False)
```
